32 devices in a mesh: dp: 4 (over x, core), fsdp: 8 (over z, y).
Axes of the slice: x: 2, y: 2, z: 4, core: 2. Of those that a mesh axis runs over, the one named last changes fastest.
Arguments:
- tokens: bfloat16 [32768, 768], P(('dp', 'fsdp')), may hold values from -6 to 6
- segment_index: int32 [64, 512], P(('dp', 'fsdp')), may hold values from 0 to 7, never falling along the last dimension, each value on 1 to 128 neighbouring positions
- start_vectors: bfloat16 [64, 8, 768], P(('dp', 'fsdp')), may hold values from -6 to 6
- first_gain: bfloat16 [768], P('fsdp'), may hold values from 0.5 to 1.5
- query_weight: bfloat16 [768, 768], P('fsdp'), may hold values from -0.109375 to 0.109375
- key_weight: bfloat16 [768, 768], P('fsdp'), may hold values from -0.109375 to 0.109375
- value_weight: bfloat16 [768, 768], P('fsdp'), may hold values from -0.21875 to 0.21875
- output_weight: bfloat16 [768, 768], P('fsdp'), may hold values from -0.4375 to 0.4375
- position_table: float32 [32, 12], replicated, may hold values from -4 to 4
- second_gain: bfloat16 [768], P('fsdp'), may hold values from 0.5 to 1.5
- inner_weight: bfloat16 [768, 3072], P('fsdp'), may hold values from -0.21875 to 0.21875
- outer_weight: bfloat16 [3072, 768], P('fsdp'), may hold values from -0.15625 to 0.15625
- start_gain: bfloat16 [768], P('fsdp'), may hold values from 0.5 to 1.5
- self_value: bfloat16 [768, 768], P('fsdp'), may hold values from -0.21875 to 0.21875
- self_output: bfloat16 [768, 768], P('fsdp'), may hold values from -0.21875 to 0.21875
- middle_gain: bfloat16 [768], P('fsdp'), may hold values from 0.5 to 1.5
- cross_query: bfloat16 [768, 768], P('fsdp'), may hold values from -0.109375 to 0.109375
- cross_key: bfloat16 [768, 768], P('fsdp'), may hold values from -0.078125 to 0.078125
- cross_value: bfloat16 [768, 768], P('fsdp'), may hold values from -0.21875 to 0.21875
- cross_output: bfloat16 [768, 768], P('fsdp'), may hold values from -0.4375 to 0.4375
- final_gain: bfloat16 [768], P('fsdp'), may hold values from 0.5 to 1.5
- decoder_inner: bfloat16 [768, 3072], P('fsdp'), may hold values from -0.21875 to 0.21875
- decoder_outer: bfloat16 [3072, 768], P('fsdp'), may hold values from -0.15625 to 0.15625
- encoded_cotangent: bfloat16 [32768, 768], P(('dp', 'fsdp')), may hold values from -6 to 6
- decoded_cotangent: bfloat16 [64, 8, 768], P(('dp', 'fsdp')), may hold values from -6 to 6
Outputs:
- encoded: bfloat16 [32768, 768], P(('dp', 'fsdp'))
- decoded: bfloat16 [64, 8, 768], P(('dp', 'fsdp'))
- tokens_grad: float32 [32768, 768], P(('dp', 'fsdp'))
- start_grad: float32 [64, 8, 768], P(('dp', 'fsdp'))
- first_gain_grad: float32 [768], P('fsdp')
- query_weight_grad: float32 [768, 768], P('fsdp')
- key_weight_grad: float32 [768, 768], P('fsdp')
- value_weight_grad: float32 [768, 768], P('fsdp')
- output_weight_grad: float32 [768, 768], P('fsdp')
- position_table_grad: float32 [32, 12], replicated
- second_gain_grad: float32 [768], P('fsdp')
- inner_weight_grad: float32 [768, 3072], P('fsdp')
- outer_weight_grad: float32 [3072, 768], P('fsdp')
- start_gain_grad: float32 [768], P('fsdp')
- self_value_grad: float32 [768, 768], P('fsdp')
- self_output_grad: float32 [768, 768], P('fsdp')
- middle_gain_grad: float32 [768], P('fsdp')
- cross_query_grad: float32 [768, 768], P('fsdp')
- cross_key_grad: float32 [768, 768], P('fsdp')
- cross_value_grad: float32 [768, 768], P('fsdp')
- cross_output_grad: float32 [768, 768], P('fsdp')
- final_gain_grad: float32 [768], P('fsdp')
- decoder_inner_grad: float32 [768, 3072], P('fsdp')
- decoder_outer_grad: float32 [3072, 768], P('fsdp')
The draws below stay inside these ranges and needn't reach their ends.
Inputs may be any that keep to these rules, and one draw needn't show every extreme that they name: `segment_index`: within each row of 512 tokens the pair numbers never fall, and each of the 8 numbers holds 1 to 128 consecutive tokens, one exactly 128.
All inputs are finite; a program needn't handle non-finite values.
Results may differ from the reference program's by a relative error of at most 0.025.
Values may be sent and summed in bfloat16 or wider, within the bound.
A program may use at most 320 MiB of HBM per device.

```python
import math
import jax
import jax.numpy as jnp
import numpy as np
from jax import lax

D = 768
HEADS = 12
KV = 64
FF = 3072
BUCKETS = 32
SEQ = 512
SLOTS = 8
SEG_MOST = 128
INNER = 768
ROWS = 64
TOKENS = 32768


def block_scale(key, dims, shards, smallest, largest):
    level, own = 1.0, jax.random.fold_in(key, 6)
    for axis_at, shards_of in shards:
        steps = jnp.exp(jax.random.uniform(jax.random.fold_in(own, axis_at), (shards_of,), jnp.float32, smallest / len(shards), largest / len(shards)))
        level = level * jnp.repeat(steps, dims[axis_at] // shards_of).reshape([-1 if axis == axis_at else 1 for axis in range(len(dims))])
    return level


def split_up(number_of, total, reach, slope):
    portions = [(1 << 20) // math.isqrt(standing ** slope) + 1 for standing in range(2, number_of + 1)]
    spare, given = total - reach - (number_of - 1), [1] * (number_of - 1)
    while spare > 0:
        free = [i for i in range(number_of - 1) if given[i] < reach]
        whole, remaining = sum([portions[i] for i in free]), spare
        for i in free:
            more = min(reach - given[i], max(1, remaining * portions[i] // whole), spare)
            given[i] = given[i] + more
            spare = spare - more
    return np.array([reach] + given)


def ragged_sizes(rng, number_of, total, most, skew):
    if number_of == 2:
        one = jax.random.randint(rng, (), max(1, total - most), min(most, total - 1) + 1)
        return jnp.stack([one, total - one])
    lengths = jnp.asarray(split_up(number_of, total, most, skew), jnp.int32)
    twos = (number_of - 1) // 2
    source_of, sink = lengths[1:1 + 2 * twos:2], lengths[2:2 + 2 * twos:2]
    margin = jnp.minimum(source_of - 1, most - sink)
    moved = jax.random.randint(jax.random.fold_in(rng, 1), (twos,), 0, 1 << 20) % (margin + 1)
    lengths = lengths.at[1:1 + 2 * twos:2].set(source_of - moved).at[2:2 + 2 * twos:2].set(sink + moved)
    return lengths[jax.random.permutation(jax.random.fold_in(rng, 2), number_of)]


def bell_draw(stream_key, dims, spread, most, pieces=(), kind=jnp.bfloat16):
    result = spread * jax.random.normal(stream_key, dims, jnp.float32)
    if pieces:
        result = result * block_scale(stream_key, dims, pieces, -0.22, 0.18)
    return jnp.clip(result, -most, most).astype(kind)


def setup_inputs(seed: int = 0) -> dict:
    streams_of = jax.random.split(jax.random.key(seed), 26)
    return {
        "tokens": bell_draw(streams_of[0], (TOKENS, D), 1.0, 6.0, ((0, 32),)),
        "segment_index": jax.vmap(lambda own: jnp.searchsorted(jnp.cumsum(ragged_sizes(own, SLOTS, SEQ, SEG_MOST, 1)), jnp.arange(SEQ), side="right"))(jax.random.split(streams_of[1], ROWS)).reshape((ROWS, SEQ)).astype(jnp.int32),
        "start_vectors": bell_draw(streams_of[2], (ROWS, SLOTS, D), 1.0, 6.0, ((0, 32),)),
        "first_gain": jnp.clip(1.0 + 0.1 * jax.random.normal(streams_of[3], (D,), jnp.float32), 0.5, 1.5).astype(jnp.bfloat16),
        "query_weight": bell_draw(streams_of[4], (D, INNER), (4 * D) ** -0.5, 0.109375, ((0, 8),)),
        "key_weight": bell_draw(streams_of[5], (D, INNER), (4 * D) ** -0.5, 0.109375, ((0, 8),)),
        "value_weight": bell_draw(streams_of[6], (D, INNER), D ** -0.5, 0.21875, ((0, 8),)),
        "output_weight": bell_draw(streams_of[7], (INNER, D), (INNER // 4) ** -0.5, 0.4375, ((0, 8),)),
        "position_table": bell_draw(streams_of[8], (BUCKETS, HEADS), 1.0, 4.0, (), jnp.float32),
        "second_gain": jnp.clip(1.0 + 0.1 * jax.random.normal(streams_of[9], (D,), jnp.float32), 0.5, 1.5).astype(jnp.bfloat16),
        "inner_weight": bell_draw(streams_of[10], (D, FF), D ** -0.5, 0.21875, ((0, 8),)),
        "outer_weight": bell_draw(streams_of[11], (FF, D), (FF // 2) ** -0.5, 0.15625, ((0, 8),)),
        "start_gain": jnp.clip(1.0 + 0.1 * jax.random.normal(streams_of[12], (D,), jnp.float32), 0.5, 1.5).astype(jnp.bfloat16),
        "self_value": bell_draw(streams_of[13], (D, INNER), D ** -0.5, 0.21875, ((0, 8),)),
        "self_output": bell_draw(streams_of[14], (INNER, D), INNER ** -0.5, 0.21875, ((0, 8),)),
        "middle_gain": jnp.clip(1.0 + 0.1 * jax.random.normal(streams_of[15], (D,), jnp.float32), 0.5, 1.5).astype(jnp.bfloat16),
        "cross_query": bell_draw(streams_of[16], (D, INNER), (4 * D) ** -0.5, 0.109375, ((0, 8),)),
        "cross_key": bell_draw(streams_of[17], (D, INNER), (8 * D) ** -0.5, 0.078125, ((0, 8),)),
        "cross_value": bell_draw(streams_of[18], (D, INNER), D ** -0.5, 0.21875, ((0, 8),)),
        "cross_output": bell_draw(streams_of[19], (INNER, D), (INNER // 4) ** -0.5, 0.4375, ((0, 8),)),
        "final_gain": jnp.clip(1.0 + 0.1 * jax.random.normal(streams_of[20], (D,), jnp.float32), 0.5, 1.5).astype(jnp.bfloat16),
        "decoder_inner": bell_draw(streams_of[21], (D, FF), D ** -0.5, 0.21875, ((0, 8),)),
        "decoder_outer": bell_draw(streams_of[22], (FF, D), (FF // 2) ** -0.5, 0.15625, ((0, 8),)),
        "encoded_cotangent": bell_draw(streams_of[23], (TOKENS, D), 1.0, 6.0, ((0, 32),)),
        "decoded_cotangent": bell_draw(streams_of[24], (ROWS, SLOTS, D), 1.0, 6.0, ((0, 32),)),
    }


@jax.custom_vjp
def low(v):
    return lax.optimization_barrier(v.astype(jnp.bfloat16)).astype(jnp.float32)

@jax.custom_vjp
def low_back(v):
    return v

def low_keep(v):
    return (low(v), None)

def low_pass(kept, grad):
    return (grad,)

def back_keep(v):
    return (v, None)

def back_low(kept, grad):
    return (low(grad),)
low.defvjp(low_keep, low_pass)
low_back.defvjp(back_keep, back_low)
epsilon = 1e-06
negative_fill = -1e+30
bucket_edges = (12, 16, 23, 32, 46, 64, 91)

def relative_buckets(length):
    places = jnp.arange(length, dtype=jnp.int32)
    offset = places[None, :] - places[:, None]
    distance = jnp.abs(offset)
    far_bucket = 8 + sum(((distance >= boundary).astype(jnp.int32) for boundary in bucket_edges))
    near_bucket = jnp.where(distance < 8, distance, far_bucket)
    return (jnp.where(offset > 0, 16, 0) + near_bucket).astype(jnp.int32)

def rms_scale(field, gain):
    return field * lax.rsqrt(lax.optimization_barrier(jnp.mean(field * field, axis=-1, keepdims=True)) + epsilon) * gain

def highest(left, right):
    return jnp.dot(left, right, precision=lax.Precision.HIGHEST)

def rounded(value):
    return low(low_back(value))

def attend(asking, key_rows, value_rows, extra, allowed):
    count = asking.shape[0]
    heads_query = asking.reshape(count, HEADS, KV)
    heads_key = key_rows.reshape(key_rows.shape[0], HEADS, KV)
    heads_value = value_rows.reshape(value_rows.shape[0], HEADS, KV)
    scores = low_back(jnp.einsum('qhd,khd->hqk', heads_query, heads_key, precision=lax.Precision.HIGHEST)) + extra
    scores = jnp.where(allowed[None], scores, negative_fill)
    shares = jax.nn.softmax(scores, axis=-1)
    mixed = jnp.einsum('hqk,khd->qhd', low(shares), heads_value, precision=lax.Precision.HIGHEST)
    return rounded(mixed.reshape(count, HEADS * KV))

def row_forward(weights, token_row, start_row, segment_row):
    first_gain, query_weight, key_weight, value_weight, output_weight, position_table, second_gain, inner_weight, outer_weight, start_gain, self_value, self_output, middle_gain, cross_query, cross_key, cross_value, cross_output, final_gain, decoder_inner, decoder_outer = weights
    length = token_row.shape[0]
    normed = low(rms_scale(token_row, first_gain))
    query = rounded(highest(normed, query_weight))
    key_rows = rounded(highest(normed, key_weight))
    value_rows = rounded(highest(normed, value_weight))
    extra = jnp.transpose(position_table[relative_buckets(length)], (2, 0, 1))
    allowed = segment_row[:, None] == segment_row[None, :]
    context = attend(query, key_rows, value_rows, extra, allowed)
    hidden = token_row + low_back(highest(context, output_weight))
    normed = low(rms_scale(hidden, second_gain))
    active = low(jax.nn.gelu(low_back(highest(normed, inner_weight))))
    encoded = hidden + low_back(highest(active, outer_weight))
    memory = low(encoded)
    normed = low(rms_scale(start_row, start_gain))
    own_value = rounded(highest(normed, self_value))
    first_field = start_row + low_back(highest(own_value, self_output))
    normed = low(rms_scale(first_field, middle_gain))
    asking = rounded(highest(normed, cross_query))
    cross_keys = rounded(highest(memory, cross_key))
    cross_values = rounded(highest(memory, cross_value))
    slot_index = jnp.arange(start_row.shape[0], dtype=jnp.int32)
    allowed = slot_index[:, None] == segment_row[None, :]
    context = attend(asking, cross_keys, cross_values, 0.0, allowed)
    second_field = first_field + low_back(highest(context, cross_output))
    normed = low(rms_scale(second_field, final_gain))
    active = low(jax.nn.gelu(low_back(highest(normed, decoder_inner))))
    decoded = second_field + low_back(highest(active, decoder_outer))
    return (encoded, decoded)

def reference(tokens, segment_index, start_vectors, first_gain, query_weight, key_weight, value_weight, output_weight, position_table, second_gain, inner_weight, outer_weight, start_gain, self_value, self_output, middle_gain, cross_query, cross_key, cross_value, cross_output, final_gain, decoder_inner, decoder_outer, encoded_cotangent, decoded_cotangent):
    weights = tuple((weight.astype(jnp.float32) for weight in (first_gain, query_weight, key_weight, value_weight, output_weight, position_table, second_gain, inner_weight, outer_weight, start_gain, self_value, self_output, middle_gain, cross_query, cross_key, cross_value, cross_output, final_gain, decoder_inner, decoder_outer)))
    token_rows = tokens.astype(jnp.float32).reshape(ROWS, SEQ, D)
    start_rows = start_vectors.astype(jnp.float32)
    encoded_rows = encoded_cotangent.astype(jnp.float32).reshape(ROWS, SEQ, D)
    decoded_rows = decoded_cotangent.astype(jnp.float32)

    def one_row(totals, packed):
        token_row, start_row, segment_row, encoded_grad, decoded_grad = packed

        def forward(weight_set, token_part, start_part):
            return row_forward(weight_set, token_part, start_part, segment_row)
        outputs, pullback = jax.vjp(forward, weights, token_row, start_row)
        weight_grads, token_grad, start_grad = pullback((encoded_grad, decoded_grad))
        totals = jax.tree.map(jnp.add, totals, weight_grads)
        return (totals, (outputs[0], outputs[1], token_grad, start_grad))
    zeros = jax.tree.map(jnp.zeros_like, weights)
    totals, (encoded, decoded, token_grads, start_grads) = lax.scan(one_row, zeros, (token_rows, start_rows, segment_index, encoded_rows, decoded_rows))
    return (encoded.reshape(TOKENS, D).astype(jnp.bfloat16), decoded.astype(jnp.bfloat16), token_grads.reshape(TOKENS, D), start_grads, totals[0], totals[1], totals[2], totals[3], totals[4], totals[5], totals[6], totals[7], totals[8], totals[9], totals[10], totals[11], totals[12], totals[13], totals[14], totals[15], totals[16], totals[17], totals[18], totals[19])
```

```python
import functools

import jax
import jax.numpy as jnp
from jax import lax
from jax.experimental import pallas as pl
from jax.experimental.pallas import tpu as pltpu
from jax.sharding import PartitionSpec as P

HEADS = 12
KV = 64


epsilon = 1e-06
negative_fill = -1e30
bucket_edges = (12, 16, 23, 32, 46, 64, 91)


MESH = pl.DeviceIdType.MESH
KINDS = (
    "square", "square", "square", "square", "wide", "tall", "square", "square",
    "square", "square", "square", "square", "wide", "tall", "small",
)


def ring_position(index, count):
    if count == 64:
        slow, rest = index // 32, index % 32
        row, column = rest // 8, rest % 8
        place = row * 8 + column + (row % 2) * (7 - 2 * column)
        return place + slow * (count - 1 - 2 * place)
    across, along = index % 2, index // 2
    return along + across * (count - 1 - 2 * along)


def ring_index(position, count):
    position = lax.rem(position, count)
    across = position // (count // 2)
    along = position + across * (count - 1 - 2 * position)
    if count == 64:
        row, column = along // 8, along % 8
        return across * 32 + row * 8 + column + (row % 2) * (7 - 2 * column)
    return 2 * along + across


class Spot:
    def __init__(self, count):
        self.count = count
        self.dp = lax.axis_index("dp")
        self.fsdp = lax.axis_index("fsdp")
        self.core = lax.rem(self.dp, 2)
        self.plane = self.dp // 2
        self.place = ring_position(self.fsdp, count)
        self.sibling = (self.dp + 1 - 2 * self.core, self.fsdp)
        self.opposite = (lax.rem(self.dp + 2, 4), self.fsdp)
        self.after = (self.dp, ring_index(self.place + 1, count))
        self.before = (self.dp, ring_index(self.place + count - 1, count))

    def greet(self, others=()):
        barrier = pltpu.get_barrier_semaphore()
        partners = (self.sibling, self.opposite, self.after, self.before) + tuple(others)
        for partner in partners:
            pl.semaphore_signal(barrier, inc=1, device_id=partner, device_id_type=MESH)
        pl.semaphore_wait(barrier, len(partners))


def cut(kind, ref, plane, core):
    rows, columns = ref.shape
    if kind == "small":
        return ref
    if kind == "square":
        half = columns // 2
        return ref.at[:, pl.ds(pl.multiple_of(core * half, 128), half)]
    if kind == "wide":
        quarter = columns // 4
        return ref.at[:, pl.ds(pl.multiple_of((core * 2 + plane) * quarter, 128), quarter)]
    half, upper = columns // 2, rows // 2
    return ref.at[
        pl.ds(pl.multiple_of(plane * upper, 8), upper),
        pl.ds(pl.multiple_of(core * half, 128), half),
    ]


def send(source, target, send_sem, recv_sem, device):
    return pltpu.make_async_remote_copy(
        src_ref=source,
        dst_ref=target,
        send_sem=send_sem,
        recv_sem=recv_sem,
        device_id=device,
        device_id_type=MESH,
    )


def gather_kernel(count, kinds, *refs):
    total = len(kinds)
    shards, fulls = refs[:total], refs[total : 2 * total]
    ring_out, ring_in, near_out, near_in, far_out, far_in, last_out, last_in, own_sem = refs[
        2 * total :
    ]
    spot = Spot(count)
    split = [i for i in range(total) if kinds[i] in ("wide", "tall")]

    window = min(count, 8)

    def slot_of(i, step):
        turn = step if i % 2 else count - step
        return ring_index(spot.place + turn, count)

    def ring_copy(i, step, source=None):
        here = cut(kinds[i], fulls[i].at[slot_of(i, step)], spot.plane, spot.core)
        return send(
            here if source is None else source,
            here,
            ring_out.at[i, lax.rem(step, window)],
            ring_in.at[i, step],
            spot.before if i % 2 else spot.after,
        )

    def near_copy(i, step):
        here = cut(kinds[i], fulls[i].at[slot_of(i, step)], spot.plane, spot.core)
        out = near_out.at[i, lax.rem(step, window)]
        return send(here, here, out, near_in.at[i, step], spot.sibling)

    def far_copy(i, step):
        here = cut(kinds[i], fulls[i].at[slot_of(i, step)], spot.plane, spot.core)
        at = split.index(i)
        out = far_out.at[at, lax.rem(step, window)]
        return send(here, here, out, far_in.at[at, step], spot.opposite)

    def last_copy(i, step):
        here = cut(kinds[i], fulls[i].at[slot_of(i, step)], 1 - spot.plane, spot.core)
        at = split.index(i)
        out = last_out.at[at, lax.rem(step, window)]
        return send(here, here, out, last_in.at[at, step], spot.sibling)

    def start(copy, i, step, first):
        if window < count:

            @pl.when(step >= first + window)
            def _():
                copy(i, step - window).wait_send()

        copy(i, step).start()

    def finish(copy, i, first, end):
        def one(step, carry):
            copy(i, step).wait_send()
            return carry

        lax.fori_loop(max(first, end - window), end, one, 0)

    owns = []
    for i in range(total):
        owns.append(pltpu.make_async_copy(shards[i], fulls[i].at[spot.fsdp], own_sem.at[i]))
        owns[-1].start()
    spot.greet()
    for i in range(total):
        ring_copy(i, 0, cut(kinds[i], shards[i], spot.plane, spot.core)).start()

    def one_step(step, carry):
        for i in range(total):
            ring_copy(i, step - 1).wait_recv()

            @pl.when(step < count - 1)
            def _():
                start(ring_copy, i, step, 0)

            if kinds[i] != "small":
                start(near_copy, i, step, 1)
            if i in split:
                start(far_copy, i, step, 1)

        @pl.when(step > 1)
        def _():
            for i in split:
                far_copy(i, step - 1).wait_recv()
                start(last_copy, i, step - 1, 1)

        return carry

    lax.fori_loop(1, count, one_step, 0)
    for i in split:
        far_copy(i, count - 1).wait_recv()
        start(last_copy, i, count - 1, 1)

    def settle(step, carry):
        for i in range(total):
            if kinds[i] != "small":
                near_copy(i, step).wait_recv()
            if i in split:
                last_copy(i, step).wait_recv()
        return carry

    lax.fori_loop(1, count, settle, 0)
    for i in range(total):
        finish(ring_copy, i, 0, count - 1)
        if kinds[i] != "small":
            finish(near_copy, i, 1, count)
        if i in split:
            finish(far_copy, i, 1, count)
            finish(last_copy, i, 1, count)
    for copy in owns:
        copy.wait()


def gather_weights(count, shards, kinds):
    total = len(shards)
    split = sum(kind in ("wide", "tall") for kind in kinds)
    window = min(count, 8)
    many, few = [
        [pltpu.SemaphoreType.DMA((rows, window)), pltpu.SemaphoreType.DMA((rows, count))] * 2
        for rows in (total, split)
    ]
    return pl.pallas_call(
        functools.partial(gather_kernel, count, kinds),
        out_shape=[jax.ShapeDtypeStruct((count,) + s.shape, s.dtype) for s in shards],
        in_specs=[pl.BlockSpec(memory_space=pl.ANY)] * total,
        out_specs=[pl.BlockSpec(memory_space=pl.ANY)] * total,
        scratch_shapes=many + few + [pltpu.SemaphoreType.DMA((total,))],
        compiler_params=pltpu.CompilerParams(collective_id=0, has_side_effects=True),
        name="gather_weights",
    )(*shards)

def plus(*terms):
    total = terms[0].astype(jnp.float32)
    for term in terms[1:]:
        total = total + term.astype(jnp.float32)
    return total


def half_of(core, columns):
    half = columns // 2
    return pl.ds(pl.multiple_of(core * half, 128), half)


def plane_part(kind, plane, rows, columns):
    if kind == "wide":
        return slice(None), pl.ds(pl.multiple_of(plane * (columns // 2), 128), columns // 2)
    if kind == "tall":
        return pl.ds(pl.multiple_of(plane * (rows // 2), 8), rows // 2), slice(None)
    return slice(None), slice(None)


ENCODER_KINDS = ("wide", "tall", "square", "square", "square", "square", "square", "square")


def reduce_kernel(count, kinds, spans, *refs):
    total, pairs = len(kinds), len(spans)
    refs = list(refs)

    def take(size):
        got = refs[:size]
        del refs[:size]
        return got

    grads = take(total)
    left_part, right_part, small = take(3)
    sums = take(total)
    pair_sums = take(pairs)
    (small_sum,) = take(1)
    half, work, final = take(total), take(total), take(total)
    split = [i for i in range(total) if kinds[i] != "square"]
    far = take(len(split))
    left_all, right_all = take(2)
    pair_half, pair_far, pair_work = take(pairs), take(pairs), take(pairs)
    small_near, small_mid, small_far, small_all = take(4)
    (
        near_sem, ring_out, ring_in, far_sem, end_sem, left_out, left_in,
        right_out, right_in, pair_sem, small_sem, small_out, small_in,
    ) = take(13)
    spot = Spot(count)
    core, plane = spot.core, spot.plane
    diagonal = (lax.rem(spot.dp + 2, 4) + 1 - 2 * core, spot.fsdp)

    def peer(k):
        return (spot.dp, lax.rem(spot.fsdp + k, count))

    barrier = pltpu.get_barrier_semaphore()
    for partner in (spot.sibling, spot.opposite, diagonal):
        pl.semaphore_signal(barrier, inc=1, device_id=partner, device_id_type=MESH)

    def greet(k, carry):
        pl.semaphore_signal(barrier, inc=1, device_id=peer(k), device_id_type=MESH)
        return carry

    lax.fori_loop(1, count, greet, 0)
    pl.semaphore_wait(barrier, count + 2)

    def near_copy(i):
        columns = grads[i].shape[2]
        return send(
            grads[i].at[:, :, half_of(1 - core, columns)], half[i],
            near_sem.at[0, i], near_sem.at[1, i], spot.sibling,
        )

    def slot_at(i, step):
        turn = step + 1 if i % 2 else count - 1 - step
        return ring_index(spot.place + turn, count)

    def far_copy(i, step):
        at = split.index(i)
        rows, columns = half[i].shape[1:]
        part = plane_part(kinds[i], 1 - plane, rows, columns)
        return send(
            half[i].at[(slot_at(i, step),) + part], far[at].at[step],
            far_sem.at[0, at, step], far_sem.at[1, at, step], spot.opposite,
        )

    def ring_copy(i, step):
        return send(
            work[i].at[step], work[i].at[step + 1], ring_out.at[i, step], ring_in.at[i, step],
            spot.before if i % 2 else spot.after,
        )

    def left_copy(k):
        other = lax.rem(spot.fsdp + k, count)
        return send(
            left_part.at[other], left_all.at[spot.fsdp], left_out.at[k], left_in.at[k], peer(k)
        )

    def right_copy(way, step):
        turn = step if way else count - step
        slot = ring_index(spot.place + turn, count)
        width = right_part.shape[1] // 2
        here = right_all.at[slot, :, way * width : (way + 1) * width]
        return send(
            here, here, right_out.at[way, step], right_in.at[way, step],
            spot.before if way else spot.after,
        )

    for i in range(total):
        near_copy(i).start()
    near_small = send(small, small_near, small_sem.at[0], small_sem.at[1], spot.sibling)
    near_small.start()

    def left_start(k, carry):
        left_copy(k).start()
        return carry

    lax.fori_loop(1, count, left_start, 0)
    right_all[spot.fsdp] = right_part[...]
    left_all[spot.fsdp] = left_part[spot.fsdp]
    for way in range(2):
        right_copy(way, 0).start()
    near_small.wait()
    small_mid[...] = small[...] + small_near[...]
    far_small = send(small_mid, small_far, small_sem.at[2], small_sem.at[3], spot.opposite)
    far_small.start()

    for i in range(total):
        near_copy(i).wait_recv()

        def join(slot, carry):
            mine = grads[i][slot, :, half_of(core, grads[i].shape[2])]
            half[i][slot] = plus(half[i][slot], mine).astype(jnp.bfloat16)
            return carry

        lax.fori_loop(0, count, join, 0)
        if i in split:

            def far_start(step, carry):
                far_copy(i, step).start()
                return carry

            lax.fori_loop(0, count, far_start, 0)

    far_small.wait()
    small_all[spot.fsdp] = small_mid[...] + small_far[...]

    def small_copy(k):
        here = small_all.at[spot.fsdp]
        return send(here, here, small_out.at[k], small_in.at[k], peer(k))

    def small_start(k, carry):
        small_copy(k).start()
        return carry

    lax.fori_loop(1, count, small_start, 0)

    def right_step(step, carry):
        for way in range(2):
            right_copy(way, step - 1).wait_recv()

            @pl.when(step < count - 1)
            def _():
                right_copy(way, step).start()

        return carry

    lax.fori_loop(1, count, right_step, 0)

    def left_wait(k, carry):
        left_copy(k).wait_recv()
        return carry

    lax.fori_loop(1, count, left_wait, 0)

    def pair_near(j):
        columns = pair_sums[j].shape[1]
        return send(
            pair_work[j].at[:, half_of(1 - core, columns)], pair_half[j],
            pair_sem.at[0, j], pair_sem.at[1, j], spot.sibling,
        )

    def pair_across(j):
        return send(
            pair_half[j], pair_far[j], pair_sem.at[2, j], pair_sem.at[3, j], spot.opposite
        )

    def pair_end(j):
        here = pair_sums[j].at[:, half_of(core, pair_sums[j].shape[1])]
        return send(here, here, pair_sem.at[4, j], pair_sem.at[5, j], spot.sibling)

    for j, (left_at, right_at) in enumerate(spans):
        rows, columns = pair_sums[j].shape
        span = -(-rows // 128) * 128
        left = left_all[:, :, left_at : left_at + span].reshape(-1, span)
        for begin in range(0, columns, 768):
            right = right_all[:, :, right_at + begin : right_at + begin + 768].reshape(-1, 768)
            block = lax.dot_general(
                left, right, (((0,), (0,)), ((), ())), preferred_element_type=jnp.float32
            )
            pair_work[j][:, begin : begin + 768] = block[:rows].astype(jnp.bfloat16)
        pair_near(j).start()
    for j in range(pairs):
        pair_near(j).wait()
        mine = pair_work[j][:, half_of(core, pair_sums[j].shape[1])]
        pair_half[j][...] = plus(pair_half[j][...], mine).astype(jnp.bfloat16)
        pair_across(j).start()

    def one_step(step, carry):
        for i in range(total):
            rows, columns = half[i].shape[1:]
            slot = slot_at(i, step)
            value = half[i][(slot,) + plane_part(kinds[i], plane, rows, columns)]
            value = value.astype(jnp.float32)
            if i in split:
                far_copy(i, step).wait_recv()
                value = value + far[split.index(i)][step].astype(jnp.float32)

            @pl.when(step > 0)
            def _():
                ring_copy(i, step - 1).wait_recv()
                work[i][step] = plus(value, work[i][step]).astype(jnp.bfloat16)

            @pl.when(step == 0)
            def _():
                work[i][step] = value.astype(jnp.bfloat16)

            @pl.when(step < count - 1)
            def _():
                ring_copy(i, step).start()

        return carry

    lax.fori_loop(0, count, one_step, 0)

    def end_across(i):
        return send(
            work[i].at[count - 1], final[i], end_sem.at[0, i], end_sem.at[1, i], spot.opposite
        )

    def end_piece(i, mine_plane):
        rows, columns = sums[i].shape
        wide = half_of(core, columns)
        if kinds[i] == "square":
            return sums[i].at[:, wide]
        return cut(kinds[i], sums[i], mine_plane, core)

    def end_copies(i):
        here = end_piece(i, plane)
        copies = [send(here, here, end_sem.at[2, i], end_sem.at[3, i], spot.sibling)]
        if i in split:
            copies.append(send(here, here, end_sem.at[4, i], end_sem.at[5, i], spot.opposite))
            copies.append(send(here, here, end_sem.at[6, i], end_sem.at[7, i], diagonal))
        return copies

    for i in range(total):
        if i not in split:
            end_across(i).start()
    for i in split:
        end_piece(i, plane)[...] = work[i][count - 1]
        for copy in end_copies(i):
            copy.start()
    for j in range(pairs):
        pair_across(j).wait()
        here = half_of(core, pair_sums[j].shape[1])
        pair_sums[j][:, here] = plus(pair_half[j][...], pair_far[j][...]).astype(jnp.bfloat16)
        pair_end(j).start()
    for i in range(total):
        if i not in split:
            end_across(i).wait()
            value = plus(work[i][count - 1], final[i][...]).astype(jnp.bfloat16)
            end_piece(i, plane)[...] = value
            for copy in end_copies(i):
                copy.start()

    def small_wait(k, carry):
        small_copy(k).wait_recv()
        return carry

    lax.fori_loop(1, count, small_wait, 0)
    small_sum[...] = lax.fori_loop(
        1, count, lambda k, so_far: so_far + small_all[k], small_all[0]
    )
    for i in range(total):
        for copy in end_copies(i):
            copy.wait()
    for j in range(pairs):
        pair_end(j).wait()
    for i in range(total):
        near_copy(i).wait_send()

    def drain(step, carry):
        for i in split:
            far_copy(i, step).wait_send()
        return carry

    lax.fori_loop(0, count, drain, 0)

    def drain_ring(step, carry):
        for i in range(total):
            ring_copy(i, step).wait_send()
        for way in range(2):
            right_copy(way, step).wait_send()
        left_copy(step + 1).wait_send()
        small_copy(step + 1).wait_send()
        return carry

    lax.fori_loop(0, count - 1, drain_ring, 0)


def reduce_grads(count, kinds, grads, left_part, right_part, pair_shapes, small):
    total, pairs = len(kinds), len(pair_shapes)
    spans, left_at, right_at = [], 0, 0
    for rows, columns in pair_shapes:
        spans.append((left_at, right_at))
        left_at, right_at = left_at + -(-rows // 128) * 128, right_at + columns
    narrow = jnp.bfloat16
    blocks = [g.shape[1:] for g in grads]
    pieces = []
    for kind, (rows, columns) in zip(kinds, blocks):
        if kind == "wide":
            pieces.append((rows, columns // 4))
        elif kind == "tall":
            pieces.append((rows // 2, columns // 2))
        else:
            pieces.append((rows, columns // 2))
    split = [i for i in range(total) if kinds[i] != "square"]
    dma = pltpu.SemaphoreType.DMA
    scratch = [pltpu.VMEM((count, r, c // 2), narrow) for r, c in blocks]
    scratch += [pltpu.VMEM((count, r, c), narrow) for r, c in pieces]
    scratch += [pltpu.VMEM((r, c), narrow) for r, c in pieces]
    scratch += [pltpu.VMEM((count,) + pieces[i], narrow) for i in split]
    scratch += [
        pltpu.VMEM(left_part.shape, narrow),
        pltpu.VMEM((count,) + right_part.shape, narrow),
    ]
    scratch += [pltpu.VMEM((r, c // 2), narrow) for r, c in pair_shapes] * 2
    scratch += [pltpu.VMEM((r, c), narrow) for r, c in pair_shapes]
    scratch += [pltpu.VMEM(small.shape, jnp.float32)] * 3
    scratch += [pltpu.VMEM((count,) + small.shape, jnp.float32)]
    scratch += [
        dma((2, total)), dma((total, count)), dma((total, count)), dma((2, len(split), count)),
        dma((8, total)), dma((count,)), dma((count,)), dma((2, count)), dma((2, count)),
        dma((6, pairs)), dma((4,)), dma((count,)), dma((count,)),
    ]
    outs = [jax.ShapeDtypeStruct(b, narrow) for b in blocks]
    outs += [jax.ShapeDtypeStruct(s, narrow) for s in pair_shapes]
    outs += [jax.ShapeDtypeStruct(small.shape, jnp.float32)]
    got = pl.pallas_call(
        functools.partial(reduce_kernel, count, kinds, spans),
        out_shape=outs,
        in_specs=[pl.BlockSpec(memory_space=pltpu.VMEM)] * (total + 3),
        out_specs=[pl.BlockSpec(memory_space=pltpu.VMEM)] * len(outs),
        scratch_shapes=scratch,
        compiler_params=pltpu.CompilerParams(
            collective_id=1, has_side_effects=True, vmem_limit_bytes=62 * 2**20
        ),
        name="reduce_grads",
    )(*grads, left_part, right_part, small)
    return got[:total], got[total : total + pairs], got[-1]


def relative_buckets(length):
    places = jnp.arange(length, dtype=jnp.int32)
    offset = places[None, :] - places[:, None]
    distance = jnp.abs(offset)
    far_bucket = 8 + sum(((distance >= boundary).astype(jnp.int32) for boundary in bucket_edges))
    near_bucket = jnp.where(distance < 8, distance, far_bucket)
    return jnp.where(offset > 0, 16, 0) + near_bucket


def bucket_onehot(length, bucket_count):
    flat_buckets = relative_buckets(length).reshape(length * length)
    choices_row = jnp.arange(bucket_count, dtype=jnp.int32)
    return (flat_buckets[:, None] == choices_row[None, :]).astype(jnp.float32)


def product(left, right):
    return jnp.dot(left, right, preferred_element_type=jnp.float32)


def product_left(left, right):
    return lax.dot_general(
        left, right, (((0,), (0,)), ((), ())), preferred_element_type=jnp.float32
    )


def product_right(left, right):
    return lax.dot_general(
        left, right, (((1,), (1,)), ((), ())), preferred_element_type=jnp.float32
    )


def gelu_back(before, grad_out):
    unused, pullback = jax.vjp(jax.nn.gelu, before)
    return pullback(grad_out)[0]


def root_scale(field):
    return lax.rsqrt(jnp.mean(field * field, axis=-1, keepdims=True) + epsilon)


def norm_back(grad_normed, field, scale, gain):
    gain_grad = jnp.sum(grad_normed * field * scale, axis=0)
    weighted = grad_normed * gain
    field_grad = scale * weighted - field * (scale * scale * scale) * jnp.mean(
        weighted * field, axis=-1, keepdims=True
    )
    return (field_grad, gain_grad)


def split_heads(matrix):
    return matrix.reshape(matrix.shape[0], HEADS, KV)


def masked_scores(asking, key_rows, extra, allowed):
    scores = (
        jnp.einsum(
            "qhd,khd->hqk",
            split_heads(asking),
            split_heads(key_rows),
            preferred_element_type=jnp.float32,
        )
        + extra
    )
    return jnp.where(allowed[None], scores, negative_fill)


def attend_forward(asking, key_rows, value_rows, extra, allowed):
    scores = masked_scores(asking, key_rows, extra, allowed)
    highest_score = jnp.max(scores, axis=-1, keepdims=True)
    log_total = highest_score + jnp.log(
        jnp.sum(jnp.exp(scores - highest_score), axis=-1, keepdims=True)
    )
    shares = jnp.exp(scores - log_total).astype(jnp.bfloat16)
    mixed = jnp.einsum(
        "hqk,khd->qhd", shares, split_heads(value_rows), preferred_element_type=jnp.float32
    )
    return (mixed.reshape(asking.shape[0], HEADS * KV).astype(jnp.bfloat16), log_total)


def attend_backward(asking, key_rows, value_rows, extra, allowed, log_total, grad_mixed):
    scores = masked_scores(asking, key_rows, extra, allowed)
    shares = jnp.exp(scores - log_total)
    grad_heads = split_heads(grad_mixed)
    grad_shares = jnp.einsum(
        "qhd,khd->hqk", grad_heads, split_heads(value_rows), preferred_element_type=jnp.float32
    )
    grad_value = jnp.einsum(
        "hqk,qhd->khd", shares.astype(jnp.bfloat16), grad_heads, preferred_element_type=jnp.float32
    )
    grad_scores = shares * (grad_shares - jnp.sum(shares * grad_shares, axis=-1, keepdims=True))
    narrow = grad_scores.astype(jnp.bfloat16)
    grad_query = jnp.einsum(
        "hqk,khd->qhd", narrow, split_heads(key_rows), preferred_element_type=jnp.float32
    )
    grad_key = jnp.einsum(
        "hqk,qhd->khd", narrow, split_heads(asking), preferred_element_type=jnp.float32
    )
    query_count = asking.shape[0]
    key_count = key_rows.shape[0]
    return (
        grad_query.reshape(query_count, HEADS * KV),
        grad_key.reshape(key_count, HEADS * KV),
        grad_value.reshape(key_count, HEADS * KV),
        grad_scores,
    )


def on_device(
    tokens,
    segment_index,
    start_vectors,
    first_gain,
    query_weight,
    key_weight,
    value_weight,
    output_weight,
    position_table,
    second_gain,
    inner_weight,
    outer_weight,
    start_gain,
    self_value,
    self_output,
    middle_gain,
    cross_query,
    cross_key,
    cross_value,
    cross_output,
    final_gain,
    decoder_inner,
    decoder_outer,
    encoded_cotangent,
    decoded_cotangent,
):
    row_count = segment_index.shape[0]
    length = segment_index.shape[1]
    slot_count = start_vectors.shape[1]
    width = tokens.shape[1]
    count = lax.axis_size("fsdp")
    depth = first_gain.shape[0]
    gains = jnp.stack([first_gain, second_gain, start_gain, middle_gain, final_gain])
    gains = jnp.pad(gains, ((0, 11), (0, 128 - depth)))
    whole = gather_weights(
        count,
        (
            query_weight, key_weight, value_weight, output_weight, inner_weight, outer_weight,
            cross_key, cross_value, self_value, self_output, cross_query, cross_output,
            decoder_inner, decoder_outer, gains,
        ),
        KINDS,
    )
    gain_parts = whole[14][:, :5, :depth]
    gain_set = [gain_parts[:, at].reshape(count * depth) for at in range(5)]
    (
        query_full, key_full, value_full, output_full, inner_full, outer_full, cross_key_full,
        cross_value_full, self_value_full, self_output_full, cross_query_full, cross_output_full,
        decoder_inner_full, decoder_outer_full,
    ) = [part.reshape(-1, part.shape[2]) for part in whole[:14]]
    gain_one, gain_two, start_full, middle_full, final_full = gain_set
    gain_one = gain_one.astype(jnp.float32)
    gain_two = gain_two.astype(jnp.float32)
    onehot = bucket_onehot(length, position_table.shape[0])
    extra = lax.dot_general(
        position_table, onehot, (((0,), (1,)), ((), ())), precision=lax.Precision.HIGHEST
    ).reshape(HEADS, length, length)
    field = tokens.astype(jnp.float32)
    scale_one = root_scale(field)
    normed_one = (field * scale_one * gain_one).astype(jnp.bfloat16)
    query_all = product(normed_one, query_full).astype(jnp.bfloat16)
    key_all = product(normed_one, key_full).astype(jnp.bfloat16)
    value_all = product(normed_one, value_full).astype(jnp.bfloat16)
    contexts = []
    kept_totals = []
    for row_index in range(row_count):
        row_begin = row_index * length
        row_end = row_begin + length
        segment_row = segment_index[row_index]
        allowed = segment_row[:, None] == segment_row[None, :]
        mixed, log_total = attend_forward(
            query_all[row_begin:row_end],
            key_all[row_begin:row_end],
            value_all[row_begin:row_end],
            extra,
            allowed,
        )
        contexts.append(mixed)
        kept_totals.append(log_total)
    context = jnp.concatenate(contexts, axis=0)
    hidden = field + product(context, output_full)
    scale_two = root_scale(hidden)
    normed_two = (hidden * scale_two * gain_two).astype(jnp.bfloat16)
    inner_before = product(normed_two, inner_full)
    active = jax.nn.gelu(inner_before).astype(jnp.bfloat16)
    encoded_full = hidden + product(active, outer_full)
    memory = encoded_full.astype(jnp.bfloat16)
    start_full = start_full.astype(jnp.float32)
    middle_full = middle_full.astype(jnp.float32)
    final_full = final_full.astype(jnp.float32)
    start_field = start_vectors.astype(jnp.float32).reshape(row_count * slot_count, width)
    scale_start = root_scale(start_field)
    normed_start = (start_field * scale_start * start_full).astype(jnp.bfloat16)
    own_value = product(normed_start, self_value_full).astype(jnp.bfloat16)
    first_field = start_field + product(own_value, self_output_full)
    scale_mid = root_scale(first_field)
    normed_mid = (first_field * scale_mid * middle_full).astype(jnp.bfloat16)
    asking = product(normed_mid, cross_query_full).astype(jnp.bfloat16)
    cross_keys = product(memory, cross_key_full).astype(jnp.bfloat16)
    cross_values = product(memory, cross_value_full).astype(jnp.bfloat16)
    slot_index = jnp.arange(slot_count, dtype=jnp.int32)
    cross_parts = []
    cross_totals = []
    for row_index in range(row_count):
        row_begin = row_index * length
        row_end = row_begin + length
        slot_begin = row_index * slot_count
        slot_end = slot_begin + slot_count
        allowed = slot_index[:, None] == segment_index[row_index][None, :]
        mixed, log_total = attend_forward(
            asking[slot_begin:slot_end],
            cross_keys[row_begin:row_end],
            cross_values[row_begin:row_end],
            0.0,
            allowed,
        )
        cross_parts.append(mixed)
        cross_totals.append(log_total)
    cross_context = jnp.concatenate(cross_parts, axis=0)
    second_field = first_field + product(cross_context, cross_output_full)
    scale_fin = root_scale(second_field)
    normed_fin = (second_field * scale_fin * final_full).astype(jnp.bfloat16)
    decoder_before = product(normed_fin, decoder_inner_full)
    decoder_active = jax.nn.gelu(decoder_before).astype(jnp.bfloat16)
    decoded_full = second_field + product(decoder_active, decoder_outer_full)
    back_start, back_middle, back_final = start_full, middle_full, final_full
    back_gain_one, back_gain_two = gain_one, gain_two
    back_query, back_key, back_value, back_output = query_full, key_full, value_full, output_full
    back_inner, back_outer = inner_full, outer_full
    back_self_value, back_self_output, back_cross_query = self_value_full, self_output_full, cross_query_full
    back_cross_key, back_cross_value, back_cross_output = cross_key_full, cross_value_full, cross_output_full
    back_decoder_inner, back_decoder_outer = decoder_inner_full, decoder_outer_full
    grad_second = decoded_cotangent.astype(jnp.float32).reshape(row_count * slot_count, width)
    grad_branch = grad_second.astype(jnp.bfloat16)
    last_branch = grad_branch
    grad_active = product_right(grad_branch, back_decoder_outer)
    grad_before = gelu_back(decoder_before, grad_active).astype(jnp.bfloat16)
    decoder_before_grad = grad_before
    grad_normed = product_right(grad_before, back_decoder_inner)
    field_part, grad_final = norm_back(
        grad_normed, second_field, scale_fin, back_final.astype(jnp.float32)
    )
    grad_second = grad_second + field_part
    grad_branch = grad_second.astype(jnp.bfloat16)
    cross_branch = grad_branch
    grad_cross_context = product_right(grad_branch, back_cross_output).astype(jnp.bfloat16)
    ask_parts = []
    key_parts = []
    value_parts = []
    for row_index in range(row_count):
        row_begin = row_index * length
        row_end = row_begin + length
        slot_begin = row_index * slot_count
        slot_end = slot_begin + slot_count
        allowed = slot_index[:, None] == segment_index[row_index][None, :]
        grad_ask_row, grad_key_row, grad_value_row, unused_scores = attend_backward(
            asking[slot_begin:slot_end],
            cross_keys[row_begin:row_end],
            cross_values[row_begin:row_end],
            0.0,
            allowed,
            cross_totals[row_index],
            grad_cross_context[slot_begin:slot_end],
        )
        ask_parts.append(grad_ask_row)
        key_parts.append(grad_key_row)
        value_parts.append(grad_value_row)
    grad_asking = jnp.concatenate(ask_parts, axis=0).astype(jnp.bfloat16)
    grad_cross_keys = jnp.concatenate(key_parts, axis=0).astype(jnp.bfloat16)
    grad_cross_values = jnp.concatenate(value_parts, axis=0).astype(jnp.bfloat16)
    grad_cross_key = product_left(memory, grad_cross_keys)
    grad_cross_value = product_left(memory, grad_cross_values)
    grad_memory = product_right(grad_cross_keys, back_cross_key) + product_right(
        grad_cross_values, back_cross_value
    )
    grad_normed = product_right(grad_asking, back_cross_query)
    field_part, grad_middle = norm_back(
        grad_normed, first_field, scale_mid, back_middle.astype(jnp.float32)
    )
    grad_first = grad_second + field_part
    grad_branch = grad_first.astype(jnp.bfloat16)
    self_branch = grad_branch
    grad_own = product_right(grad_branch, back_self_output).astype(jnp.bfloat16)
    grad_normed = product_right(grad_own, back_self_value)
    field_part, grad_start_gain = norm_back(
        grad_normed, start_field, scale_start, back_start.astype(jnp.float32)
    )
    start_grad = (grad_first + field_part).reshape(row_count, slot_count, width)
    grad_encoded = encoded_cotangent.astype(jnp.float32) + grad_memory
    grad_branch = grad_encoded.astype(jnp.bfloat16)
    grad_outer = product_left(active, grad_branch)
    grad_active = product_right(grad_branch, back_outer)
    grad_before = gelu_back(inner_before, grad_active).astype(jnp.bfloat16)
    grad_inner = product_left(normed_two, grad_before)
    grad_normed = product_right(grad_before, back_inner)
    field_part, grad_gain_two = norm_back(
        grad_normed, hidden, scale_two, back_gain_two.astype(jnp.float32)
    )
    grad_hidden = grad_encoded + field_part
    grad_branch = grad_hidden.astype(jnp.bfloat16)
    grad_output = product_left(context, grad_branch)
    grad_context = product_right(grad_branch, back_output).astype(jnp.bfloat16)
    query_parts = []
    key_parts = []
    value_parts = []
    bias_grad = jnp.zeros((HEADS, length, length), jnp.float32)
    for row_index in range(row_count):
        row_begin = row_index * length
        row_end = row_begin + length
        segment_row = segment_index[row_index]
        allowed = segment_row[:, None] == segment_row[None, :]
        grad_query_row, grad_key_row, grad_value_row, grad_scores = attend_backward(
            query_all[row_begin:row_end],
            key_all[row_begin:row_end],
            value_all[row_begin:row_end],
            extra,
            allowed,
            kept_totals[row_index],
            grad_context[row_begin:row_end],
        )
        query_parts.append(grad_query_row)
        key_parts.append(grad_key_row)
        value_parts.append(grad_value_row)
        bias_grad = bias_grad + grad_scores
    grad_query_all = jnp.concatenate(query_parts, axis=0).astype(jnp.bfloat16)
    grad_key_all = jnp.concatenate(key_parts, axis=0).astype(jnp.bfloat16)
    grad_value_all = jnp.concatenate(value_parts, axis=0).astype(jnp.bfloat16)
    grad_query = product_left(normed_one, grad_query_all)
    grad_key = product_left(normed_one, grad_key_all)
    grad_value = product_left(normed_one, grad_value_all)
    grad_normed = (
        product_right(grad_query_all, back_query)
        + product_right(grad_key_all, back_key)
        + product_right(grad_value_all, back_value)
    )
    field_part, grad_gain_one = norm_back(
        grad_normed, field, scale_one, back_gain_one.astype(jnp.float32)
    )
    tokens_grad = grad_hidden + field_part
    table_grad = lax.dot_general(
        onehot,
        bias_grad.reshape(HEADS, length * length),
        (((0,), (1,)), ((), ())),
        precision=lax.Precision.HIGHEST,
    )
    token_count = row_count * slot_count
    lefts = (normed_fin, decoder_active, normed_start, own_value, normed_mid, cross_context)
    rights = (decoder_before_grad, last_branch, grad_own, self_branch, grad_asking, cross_branch)
    pair_shapes = [(left.shape[1] // count, right.shape[1]) for left, right in zip(lefts, rights)]
    left_cols = []
    for left, (rows, unused) in zip(lefts, pair_shapes):
        columns = left.reshape(token_count, count, rows).transpose(1, 0, 2)
        left_cols.append(jnp.pad(columns, ((0, 0), (0, 0), (0, -rows % 128))))
    small = jnp.concatenate([
        jnp.stack([grad_gain_one, grad_gain_two, grad_start_gain, grad_middle, grad_final]),
        jnp.pad(table_grad.reshape(1, -1), ((0, 2), (0, width - table_grad.size))),
    ])
    encoder_grads = (
        grad_inner, grad_outer, grad_query, grad_key, grad_value, grad_output,
        grad_cross_key, grad_cross_value,
    )
    encoder_sums, decoder_sums, small_sum = reduce_grads(
        count,
        ENCODER_KINDS,
        [
            g.astype(jnp.bfloat16).reshape(count, g.shape[0] // count, g.shape[1])
            for g in encoder_grads
        ],
        jnp.concatenate(left_cols, axis=2),
        jnp.concatenate(rights, axis=1),
        pair_shapes,
        small,
    )
    (
        inner_weight_grad, outer_weight_grad, query_weight_grad, key_weight_grad,
        value_weight_grad, output_weight_grad, cross_key_grad, cross_value_grad,
    ) = [part.astype(jnp.float32) for part in encoder_sums]
    (
        decoder_inner_grad, decoder_outer_grad, self_value_grad, self_output_grad,
        cross_query_grad, cross_output_grad,
    ) = [part.astype(jnp.float32) for part in decoder_sums]
    own_gains = lax.dynamic_slice_in_dim(
        small_sum[:5], lax.axis_index("fsdp") * depth, depth, axis=1
    )
    first_gain_grad, second_gain_grad, start_gain_grad, middle_gain_grad, final_gain_grad = own_gains
    position_table_grad = small_sum[5, : table_grad.size].reshape(table_grad.shape)
    decoded = decoded_full.reshape(row_count, slot_count, width).astype(jnp.bfloat16)
    return (
        encoded_full.astype(jnp.bfloat16),
        decoded,
        tokens_grad,
        start_grad,
        first_gain_grad,
        query_weight_grad,
        key_weight_grad,
        value_weight_grad,
        output_weight_grad,
        position_table_grad,
        second_gain_grad,
        inner_weight_grad,
        outer_weight_grad,
        start_gain_grad,
        self_value_grad,
        self_output_grad,
        middle_gain_grad,
        cross_query_grad,
        cross_key_grad,
        cross_value_grad,
        cross_output_grad,
        final_gain_grad,
        decoder_inner_grad,
        decoder_outer_grad,
    )


def solution(mesh):
    placed = (
        P(("dp", "fsdp"), None),
        P(("dp", "fsdp"), None),
        P(("dp", "fsdp"), None, None),
        P("fsdp"),
        P("fsdp", None),
        P("fsdp", None),
        P("fsdp", None),
        P("fsdp", None),
        P(),
        P("fsdp"),
        P("fsdp", None),
        P("fsdp", None),
        P("fsdp"),
        P("fsdp", None),
        P("fsdp", None),
        P("fsdp"),
        P("fsdp", None),
        P("fsdp", None),
        P("fsdp", None),
        P("fsdp", None),
        P("fsdp"),
        P("fsdp", None),
        P("fsdp", None),
        P(("dp", "fsdp"), None),
        P(("dp", "fsdp"), None, None),
    )
    return jax.shard_map(
        on_device,
        mesh=mesh,
        in_specs=placed,
        out_specs=(
            P(("dp", "fsdp"), None),
            P(("dp", "fsdp"), None, None),
            P(("dp", "fsdp"), None),
            P(("dp", "fsdp"), None, None),
            P("fsdp"),
            P("fsdp", None),
            P("fsdp", None),
            P("fsdp", None),
            P("fsdp", None),
            P(),
            P("fsdp"),
            P("fsdp", None),
            P("fsdp", None),
            P("fsdp"),
            P("fsdp", None),
            P("fsdp", None),
            P("fsdp"),
            P("fsdp", None),
            P("fsdp", None),
            P("fsdp", None),
            P("fsdp", None),
            P("fsdp"),
            P("fsdp", None),
            P("fsdp", None),
        ),
        check_vma=False,
    )
```

```python
import functools

import jax
import jax.numpy as jnp
from jax import lax
from jax.experimental import pallas as pl
from jax.experimental.pallas import tpu as pltpu
from jax.sharding import PartitionSpec as P

HEADS = 12
KV = 64
BLOCK = 128


epsilon = 1e-06
negative_fill = -1e30
bucket_edges = (12, 16, 23, 32, 46, 64, 91)


MESH = pl.DeviceIdType.MESH
KINDS = (
    "square", "square", "square", "square", "wide", "tall", "square", "square",
    "square", "square", "square", "square", "wide", "tall", "small",
)


def ring_position(index, count):
    if count == 64:
        slow, rest = index // 32, index % 32
        row, column = rest // 8, rest % 8
        place = row * 8 + column + (row % 2) * (7 - 2 * column)
        return place + slow * (count - 1 - 2 * place)
    across, along = index % 2, index // 2
    return along + across * (count - 1 - 2 * along)


def ring_index(position, count):
    position = lax.rem(position, count)
    across = position // (count // 2)
    along = position + across * (count - 1 - 2 * position)
    if count == 64:
        row, column = along // 8, along % 8
        return across * 32 + row * 8 + column + (row % 2) * (7 - 2 * column)
    return 2 * along + across


class Spot:
    def __init__(self, count):
        self.count = count
        self.dp = lax.axis_index("dp")
        self.fsdp = lax.axis_index("fsdp")
        self.core = lax.rem(self.dp, 2)
        self.plane = self.dp // 2
        self.place = ring_position(self.fsdp, count)
        self.sibling = (self.dp + 1 - 2 * self.core, self.fsdp)
        self.opposite = (lax.rem(self.dp + 2, 4), self.fsdp)
        self.after = (self.dp, ring_index(self.place + 1, count))
        self.before = (self.dp, ring_index(self.place + count - 1, count))

    def greet(self, others=()):
        barrier = pltpu.get_barrier_semaphore()
        partners = (self.sibling, self.opposite, self.after, self.before) + tuple(others)
        for partner in partners:
            pl.semaphore_signal(barrier, inc=1, device_id=partner, device_id_type=MESH)
        pl.semaphore_wait(barrier, len(partners))


def cut(kind, ref, plane, core):
    rows, columns = ref.shape
    if kind == "small":
        return ref
    if kind == "square":
        half = columns // 2
        return ref.at[:, pl.ds(pl.multiple_of(core * half, 128), half)]
    if kind == "wide":
        quarter = columns // 4
        return ref.at[:, pl.ds(pl.multiple_of((core * 2 + plane) * quarter, 128), quarter)]
    half, upper = columns // 2, rows // 2
    return ref.at[
        pl.ds(pl.multiple_of(plane * upper, 8), upper),
        pl.ds(pl.multiple_of(core * half, 128), half),
    ]


def send(source, target, send_sem, recv_sem, device):
    return pltpu.make_async_remote_copy(
        src_ref=source,
        dst_ref=target,
        send_sem=send_sem,
        recv_sem=recv_sem,
        device_id=device,
        device_id_type=MESH,
    )


def gather_kernel(count, kinds, *refs):
    total = len(kinds)
    shards, fulls = refs[:total], refs[total : 2 * total]
    ring_out, ring_in, near_out, near_in, far_out, far_in, last_out, last_in, own_sem = refs[
        2 * total :
    ]
    spot = Spot(count)
    split = [i for i in range(total) if kinds[i] in ("wide", "tall")]

    window = min(count, 8)

    def slot_of(i, step):
        turn = step if i % 2 else count - step
        return ring_index(spot.place + turn, count)

    def ring_copy(i, step, source=None):
        here = cut(kinds[i], fulls[i].at[slot_of(i, step)], spot.plane, spot.core)
        return send(
            here if source is None else source,
            here,
            ring_out.at[i, lax.rem(step, window)],
            ring_in.at[i, step],
            spot.before if i % 2 else spot.after,
        )

    def near_copy(i, step):
        here = cut(kinds[i], fulls[i].at[slot_of(i, step)], spot.plane, spot.core)
        out = near_out.at[i, lax.rem(step, window)]
        return send(here, here, out, near_in.at[i, step], spot.sibling)

    def far_copy(i, step):
        here = cut(kinds[i], fulls[i].at[slot_of(i, step)], spot.plane, spot.core)
        at = split.index(i)
        out = far_out.at[at, lax.rem(step, window)]
        return send(here, here, out, far_in.at[at, step], spot.opposite)

    def last_copy(i, step):
        here = cut(kinds[i], fulls[i].at[slot_of(i, step)], 1 - spot.plane, spot.core)
        at = split.index(i)
        out = last_out.at[at, lax.rem(step, window)]
        return send(here, here, out, last_in.at[at, step], spot.sibling)

    def start(copy, i, step, first):
        if window < count:

            @pl.when(step >= first + window)
            def _():
                copy(i, step - window).wait_send()

        copy(i, step).start()

    def finish(copy, i, first, end):
        def one(step, carry):
            copy(i, step).wait_send()
            return carry

        lax.fori_loop(max(first, end - window), end, one, 0)

    owns = []
    for i in range(total):
        owns.append(pltpu.make_async_copy(shards[i], fulls[i].at[spot.fsdp], own_sem.at[i]))
        owns[-1].start()
    spot.greet()
    for i in range(total):
        ring_copy(i, 0, cut(kinds[i], shards[i], spot.plane, spot.core)).start()

    def one_step(step, carry):
        for i in range(total):
            ring_copy(i, step - 1).wait_recv()

            @pl.when(step < count - 1)
            def _():
                start(ring_copy, i, step, 0)

            if kinds[i] != "small":
                start(near_copy, i, step, 1)
            if i in split:
                start(far_copy, i, step, 1)

        @pl.when(step > 1)
        def _():
            for i in split:
                far_copy(i, step - 1).wait_recv()
                start(last_copy, i, step - 1, 1)

        return carry

    lax.fori_loop(1, count, one_step, 0)
    for i in split:
        far_copy(i, count - 1).wait_recv()
        start(last_copy, i, count - 1, 1)

    def settle(step, carry):
        for i in range(total):
            if kinds[i] != "small":
                near_copy(i, step).wait_recv()
            if i in split:
                last_copy(i, step).wait_recv()
        return carry

    lax.fori_loop(1, count, settle, 0)
    for i in range(total):
        finish(ring_copy, i, 0, count - 1)
        if kinds[i] != "small":
            finish(near_copy, i, 1, count)
        if i in split:
            finish(far_copy, i, 1, count)
            finish(last_copy, i, 1, count)
    for copy in owns:
        copy.wait()


def gather_weights(count, shards, kinds):
    total = len(shards)
    split = sum(kind in ("wide", "tall") for kind in kinds)
    window = min(count, 8)
    many, few = [
        [pltpu.SemaphoreType.DMA((rows, window)), pltpu.SemaphoreType.DMA((rows, count))] * 2
        for rows in (total, split)
    ]
    return pl.pallas_call(
        functools.partial(gather_kernel, count, kinds),
        out_shape=[jax.ShapeDtypeStruct((count,) + s.shape, s.dtype) for s in shards],
        in_specs=[pl.BlockSpec(memory_space=pl.ANY)] * total,
        out_specs=[pl.BlockSpec(memory_space=pl.ANY)] * total,
        scratch_shapes=many + few + [pltpu.SemaphoreType.DMA((total,))],
        compiler_params=pltpu.CompilerParams(collective_id=0, has_side_effects=True),
        name="gather_weights",
    )(*shards)

def plus(*terms):
    total = terms[0].astype(jnp.float32)
    for term in terms[1:]:
        total = total + term.astype(jnp.float32)
    return total


def half_of(core, columns):
    half = columns // 2
    return pl.ds(pl.multiple_of(core * half, 128), half)


def plane_part(kind, plane, rows, columns):
    if kind == "wide":
        return slice(None), pl.ds(pl.multiple_of(plane * (columns // 2), 128), columns // 2)
    if kind == "tall":
        return pl.ds(pl.multiple_of(plane * (rows // 2), 8), rows // 2), slice(None)
    return slice(None), slice(None)


ENCODER_KINDS = ("wide", "tall", "square", "square", "square", "square", "square", "square")


def reduce_kernel(count, kinds, spans, *refs):
    total, pairs = len(kinds), len(spans)
    refs = list(refs)

    def take(size):
        got = refs[:size]
        del refs[:size]
        return got

    grads = take(total)
    left_part, right_part, small = take(3)
    sums = take(total)
    pair_sums = take(pairs)
    (small_sum,) = take(1)
    half, work, final = take(total), take(total), take(total)
    split = [i for i in range(total) if kinds[i] != "square"]
    far = take(len(split))
    left_all, right_all = take(2)
    pair_half, pair_far, pair_work = take(pairs), take(pairs), take(pairs)
    small_near, small_mid, small_far, small_all = take(4)
    (
        near_sem, ring_out, ring_in, far_sem, end_sem, left_out, left_in,
        right_out, right_in, pair_sem, small_sem, small_out, small_in,
    ) = take(13)
    spot = Spot(count)
    core, plane = spot.core, spot.plane
    diagonal = (lax.rem(spot.dp + 2, 4) + 1 - 2 * core, spot.fsdp)

    def peer(k):
        return (spot.dp, lax.rem(spot.fsdp + k, count))

    barrier = pltpu.get_barrier_semaphore()
    for partner in (spot.sibling, spot.opposite, diagonal):
        pl.semaphore_signal(barrier, inc=1, device_id=partner, device_id_type=MESH)

    def greet(k, carry):
        pl.semaphore_signal(barrier, inc=1, device_id=peer(k), device_id_type=MESH)
        return carry

    lax.fori_loop(1, count, greet, 0)
    pl.semaphore_wait(barrier, count + 2)

    def near_copy(i):
        columns = grads[i].shape[2]
        return send(
            grads[i].at[:, :, half_of(1 - core, columns)], half[i],
            near_sem.at[0, i], near_sem.at[1, i], spot.sibling,
        )

    def slot_at(i, step):
        turn = step + 1 if i % 2 else count - 1 - step
        return ring_index(spot.place + turn, count)

    def far_copy(i, step):
        at = split.index(i)
        rows, columns = half[i].shape[1:]
        part = plane_part(kinds[i], 1 - plane, rows, columns)
        return send(
            half[i].at[(slot_at(i, step),) + part], far[at].at[step],
            far_sem.at[0, at, step], far_sem.at[1, at, step], spot.opposite,
        )

    def ring_copy(i, step):
        return send(
            work[i].at[step], work[i].at[step + 1], ring_out.at[i, step], ring_in.at[i, step],
            spot.before if i % 2 else spot.after,
        )

    def left_copy(k):
        other = lax.rem(spot.fsdp + k, count)
        return send(
            left_part.at[other], left_all.at[spot.fsdp], left_out.at[k], left_in.at[k], peer(k)
        )

    def right_copy(way, step):
        turn = step if way else count - step
        slot = ring_index(spot.place + turn, count)
        width = right_part.shape[1] // 2
        here = right_all.at[slot, :, way * width : (way + 1) * width]
        return send(
            here, here, right_out.at[way, step], right_in.at[way, step],
            spot.before if way else spot.after,
        )

    for i in range(total):
        near_copy(i).start()
    near_small = send(small, small_near, small_sem.at[0], small_sem.at[1], spot.sibling)
    near_small.start()

    def left_start(k, carry):
        left_copy(k).start()
        return carry

    lax.fori_loop(1, count, left_start, 0)
    right_all[spot.fsdp] = right_part[...]
    left_all[spot.fsdp] = left_part[spot.fsdp]
    for way in range(2):
        right_copy(way, 0).start()
    near_small.wait()
    small_mid[...] = small[...] + small_near[...]
    far_small = send(small_mid, small_far, small_sem.at[2], small_sem.at[3], spot.opposite)
    far_small.start()

    for i in range(total):
        near_copy(i).wait_recv()

        def join(slot, carry):
            mine = grads[i][slot, :, half_of(core, grads[i].shape[2])]
            half[i][slot] = plus(half[i][slot], mine).astype(jnp.bfloat16)
            return carry

        lax.fori_loop(0, count, join, 0)
        if i in split:

            def far_start(step, carry):
                far_copy(i, step).start()
                return carry

            lax.fori_loop(0, count, far_start, 0)

    far_small.wait()
    small_all[spot.fsdp] = small_mid[...] + small_far[...]

    def small_copy(k):
        here = small_all.at[spot.fsdp]
        return send(here, here, small_out.at[k], small_in.at[k], peer(k))

    def small_start(k, carry):
        small_copy(k).start()
        return carry

    lax.fori_loop(1, count, small_start, 0)

    def right_step(step, carry):
        for way in range(2):
            right_copy(way, step - 1).wait_recv()

            @pl.when(step < count - 1)
            def _():
                right_copy(way, step).start()

        return carry

    lax.fori_loop(1, count, right_step, 0)

    def left_wait(k, carry):
        left_copy(k).wait_recv()
        return carry

    lax.fori_loop(1, count, left_wait, 0)

    def pair_near(j):
        columns = pair_sums[j].shape[1]
        return send(
            pair_work[j].at[:, half_of(1 - core, columns)], pair_half[j],
            pair_sem.at[0, j], pair_sem.at[1, j], spot.sibling,
        )

    def pair_across(j):
        return send(
            pair_half[j], pair_far[j], pair_sem.at[2, j], pair_sem.at[3, j], spot.opposite
        )

    def pair_end(j):
        here = pair_sums[j].at[:, half_of(core, pair_sums[j].shape[1])]
        return send(here, here, pair_sem.at[4, j], pair_sem.at[5, j], spot.sibling)

    for j, (left_at, right_at) in enumerate(spans):
        rows, columns = pair_sums[j].shape
        span = -(-rows // 128) * 128
        left = left_all[:, :, left_at : left_at + span].reshape(-1, span)
        for begin in range(0, columns, 768):
            right = right_all[:, :, right_at + begin : right_at + begin + 768].reshape(-1, 768)
            block = lax.dot_general(
                left, right, (((0,), (0,)), ((), ())), preferred_element_type=jnp.float32
            )
            pair_work[j][:, begin : begin + 768] = block[:rows].astype(jnp.bfloat16)
        pair_near(j).start()
    for j in range(pairs):
        pair_near(j).wait()
        mine = pair_work[j][:, half_of(core, pair_sums[j].shape[1])]
        pair_half[j][...] = plus(pair_half[j][...], mine).astype(jnp.bfloat16)
        pair_across(j).start()

    def one_step(step, carry):
        for i in range(total):
            rows, columns = half[i].shape[1:]
            slot = slot_at(i, step)
            value = half[i][(slot,) + plane_part(kinds[i], plane, rows, columns)]
            value = value.astype(jnp.float32)
            if i in split:
                far_copy(i, step).wait_recv()
                value = value + far[split.index(i)][step].astype(jnp.float32)

            @pl.when(step > 0)
            def _():
                ring_copy(i, step - 1).wait_recv()
                work[i][step] = plus(value, work[i][step]).astype(jnp.bfloat16)

            @pl.when(step == 0)
            def _():
                work[i][step] = value.astype(jnp.bfloat16)

            @pl.when(step < count - 1)
            def _():
                ring_copy(i, step).start()

        return carry

    lax.fori_loop(0, count, one_step, 0)

    def end_across(i):
        return send(
            work[i].at[count - 1], final[i], end_sem.at[0, i], end_sem.at[1, i], spot.opposite
        )

    def end_piece(i, mine_plane):
        rows, columns = sums[i].shape
        wide = half_of(core, columns)
        if kinds[i] == "square":
            return sums[i].at[:, wide]
        return cut(kinds[i], sums[i], mine_plane, core)

    def end_copies(i):
        here = end_piece(i, plane)
        copies = [send(here, here, end_sem.at[2, i], end_sem.at[3, i], spot.sibling)]
        if i in split:
            copies.append(send(here, here, end_sem.at[4, i], end_sem.at[5, i], spot.opposite))
            copies.append(send(here, here, end_sem.at[6, i], end_sem.at[7, i], diagonal))
        return copies

    for i in range(total):
        if i not in split:
            end_across(i).start()
    for i in split:
        end_piece(i, plane)[...] = work[i][count - 1]
        for copy in end_copies(i):
            copy.start()
    for j in range(pairs):
        pair_across(j).wait()
        here = half_of(core, pair_sums[j].shape[1])
        pair_sums[j][:, here] = plus(pair_half[j][...], pair_far[j][...]).astype(jnp.bfloat16)
        pair_end(j).start()
    for i in range(total):
        if i not in split:
            end_across(i).wait()
            value = plus(work[i][count - 1], final[i][...]).astype(jnp.bfloat16)
            end_piece(i, plane)[...] = value
            for copy in end_copies(i):
                copy.start()

    def small_wait(k, carry):
        small_copy(k).wait_recv()
        return carry

    lax.fori_loop(1, count, small_wait, 0)
    small_sum[...] = lax.fori_loop(
        1, count, lambda k, so_far: so_far + small_all[k], small_all[0]
    )
    for i in range(total):
        for copy in end_copies(i):
            copy.wait()
    for j in range(pairs):
        pair_end(j).wait()
    for i in range(total):
        near_copy(i).wait_send()

    def drain(step, carry):
        for i in split:
            far_copy(i, step).wait_send()
        return carry

    lax.fori_loop(0, count, drain, 0)

    def drain_ring(step, carry):
        for i in range(total):
            ring_copy(i, step).wait_send()
        for way in range(2):
            right_copy(way, step).wait_send()
        left_copy(step + 1).wait_send()
        small_copy(step + 1).wait_send()
        return carry

    lax.fori_loop(0, count - 1, drain_ring, 0)


def reduce_grads(count, kinds, grads, left_part, right_part, pair_shapes, small):
    total, pairs = len(kinds), len(pair_shapes)
    spans, left_at, right_at = [], 0, 0
    for rows, columns in pair_shapes:
        spans.append((left_at, right_at))
        left_at, right_at = left_at + -(-rows // 128) * 128, right_at + columns
    narrow = jnp.bfloat16
    blocks = [g.shape[1:] for g in grads]
    pieces = []
    for kind, (rows, columns) in zip(kinds, blocks):
        if kind == "wide":
            pieces.append((rows, columns // 4))
        elif kind == "tall":
            pieces.append((rows // 2, columns // 2))
        else:
            pieces.append((rows, columns // 2))
    split = [i for i in range(total) if kinds[i] != "square"]
    dma = pltpu.SemaphoreType.DMA
    scratch = [pltpu.VMEM((count, r, c // 2), narrow) for r, c in blocks]
    scratch += [pltpu.VMEM((count, r, c), narrow) for r, c in pieces]
    scratch += [pltpu.VMEM((r, c), narrow) for r, c in pieces]
    scratch += [pltpu.VMEM((count,) + pieces[i], narrow) for i in split]
    scratch += [
        pltpu.VMEM(left_part.shape, narrow),
        pltpu.VMEM((count,) + right_part.shape, narrow),
    ]
    scratch += [pltpu.VMEM((r, c // 2), narrow) for r, c in pair_shapes] * 2
    scratch += [pltpu.VMEM((r, c), narrow) for r, c in pair_shapes]
    scratch += [pltpu.VMEM(small.shape, jnp.float32)] * 3
    scratch += [pltpu.VMEM((count,) + small.shape, jnp.float32)]
    scratch += [
        dma((2, total)), dma((total, count)), dma((total, count)), dma((2, len(split), count)),
        dma((8, total)), dma((count,)), dma((count,)), dma((2, count)), dma((2, count)),
        dma((6, pairs)), dma((4,)), dma((count,)), dma((count,)),
    ]
    outs = [jax.ShapeDtypeStruct(b, narrow) for b in blocks]
    outs += [jax.ShapeDtypeStruct(s, narrow) for s in pair_shapes]
    outs += [jax.ShapeDtypeStruct(small.shape, jnp.float32)]
    got = pl.pallas_call(
        functools.partial(reduce_kernel, count, kinds, spans),
        out_shape=outs,
        in_specs=[pl.BlockSpec(memory_space=pltpu.VMEM)] * (total + 3),
        out_specs=[pl.BlockSpec(memory_space=pltpu.VMEM)] * len(outs),
        scratch_shapes=scratch,
        compiler_params=pltpu.CompilerParams(
            collective_id=1, has_side_effects=True, vmem_limit_bytes=62 * 2**20
        ),
        name="reduce_grads",
    )(*grads, left_part, right_part, small)
    return got[:total], got[total : total + pairs], got[-1]


def product(left, right):
    return jnp.dot(left, right, preferred_element_type=jnp.float32)


def product_left(left, right):
    return lax.dot_general(
        left, right, (((0,), (0,)), ((), ())), preferred_element_type=jnp.float32
    )


def product_right(left, right):
    return lax.dot_general(
        left, right, (((1,), (1,)), ((), ())), preferred_element_type=jnp.float32
    )


def gelu_back(before, grad_out):
    unused, pullback = jax.vjp(jax.nn.gelu, before)
    return pullback(grad_out)[0]


def root_scale(field):
    return lax.rsqrt(jnp.mean(field * field, axis=-1, keepdims=True) + epsilon)


def norm_back(grad_normed, field, scale, gain):
    gain_grad = jnp.sum(grad_normed * field * scale, axis=0)
    weighted = grad_normed * gain
    field_grad = scale * weighted - field * (scale * scale * scale) * jnp.mean(
        weighted * field, axis=-1, keepdims=True
    )
    return (field_grad, gain_grad)


def wide_heads(block):
    first = lax.broadcasted_iota(jnp.int32, block.shape, 1) < KV
    none = jnp.zeros_like(block)
    return jnp.concatenate([jnp.where(first, block, none), jnp.where(first, none, block)], axis=0)


def narrow_heads(stacked):
    half = stacked.shape[0] // 2
    first = lax.broadcasted_iota(jnp.int32, (half, stacked.shape[1]), 1) < KV
    return jnp.where(first, stacked[:half], stacked[half:])


def reach(at, blocks):
    low, high = max(0, at - 1), min(blocks, at + 2)
    begin = (low - at + 1) * BLOCK
    return slice(low * BLOCK, high * BLOCK), slice(begin, begin + (high - low) * BLOCK)


def bias_block(base):
    heads = []
    for at in range(2):
        level = jnp.broadcast_to(base[at : at + 1], (BLOCK, base.shape[1]))
        heads.append(pltpu.roll(level, 0, axis=1, stride=1, stride_axis=0))
    return jnp.concatenate(heads, axis=0)


def offset_sums(block):
    rows, width = block.shape
    while rows > 8:
        rows = rows // 2
        block = block[:rows] + pltpu.roll(block[rows:], width - rows, axis=1)
    place = lax.broadcasted_iota(jnp.int32, block.shape, 0)
    for bit in (4, 2, 1):
        block = jnp.where((place & bit) > 0, pltpu.roll(block, width - bit, axis=1), block)
    return jnp.sum(block, axis=0, keepdims=True)


def attend_kernel(column_ref, row_ref, base_ref, query_ref, key_ref, value_ref, out_ref, share_ref):
    blocks = query_ref.shape[0] // BLOCK
    bias = bias_block(base_ref[0])
    for at in range(blocks):
        keys, places = reach(at, blocks)
        own = slice(at * BLOCK, (at + 1) * BLOCK)
        scores = product_right(wide_heads(query_ref[own]), key_ref[keys]) + bias[:, places]
        allowed = column_ref[own, :1] == row_ref[0, :1, keys]
        scores = jnp.where(jnp.concatenate([allowed, allowed], axis=0), scores, negative_fill)
        powers = jnp.exp(scores - jnp.max(scores, axis=1, keepdims=True))
        shares = powers * (1.0 / jnp.sum(powers, axis=1, keepdims=True))
        shares = shares.astype(jnp.bfloat16)
        share_ref[0, 0, at, :, places] = shares
        mixed = product(shares, value_ref[keys])
        out_ref[own] = narrow_heads(mixed).astype(jnp.bfloat16)


def attend_back_kernel(
    query_ref, key_ref, value_ref, grad_ref, share_ref,
    grad_query_ref, grad_key_ref, grad_value_ref, sums_ref, bias_acc, key_acc, value_acc,
):
    blocks = query_ref.shape[0] // BLOCK

    @pl.when(pl.program_id(1) == 0)
    def _():
        bias_acc[...] = jnp.zeros_like(bias_acc)

    key_acc[...] = jnp.zeros_like(key_acc)
    value_acc[...] = jnp.zeros_like(value_acc)
    for at in range(blocks):
        keys, places = reach(at, blocks)
        own = slice(at * BLOCK, (at + 1) * BLOCK)
        query, grad = wide_heads(query_ref[own]), wide_heads(grad_ref[own])
        narrow_shares = share_ref[0, 0, at, :, places]
        shares = narrow_shares.astype(jnp.float32)
        value_acc[keys] += product_left(narrow_shares, grad)
        moved = shares * product_right(grad, value_ref[keys])
        grad_scores = moved - shares * jnp.sum(moved, axis=1, keepdims=True)
        bias_acc[:, places] += grad_scores
        narrow = grad_scores.astype(jnp.bfloat16)
        grad_query_ref[own] = narrow_heads(product(narrow, key_ref[keys])).astype(jnp.bfloat16)
        key_acc[keys] += product_left(narrow, query)
    grad_key_ref[...] = key_acc[...].astype(jnp.bfloat16)
    grad_value_ref[...] = value_acc[...].astype(jnp.bfloat16)

    @pl.when(pl.program_id(1) == pl.num_programs(1) - 1)
    def _():
        sums_ref[0] = jnp.concatenate(
            [offset_sums(bias_acc[:BLOCK]), offset_sums(bias_acc[BLOCK:])], axis=0
        )


def offset_buckets():
    offset = jnp.arange(3 * BLOCK, dtype=jnp.int32) - BLOCK
    distance = jnp.abs(offset)
    far_bucket = 8 + sum(((distance >= boundary).astype(jnp.int32) for boundary in bucket_edges))
    near_bucket = jnp.where(distance < 8, distance, far_bucket)
    return jnp.where(offset > 0, 16, 0) + near_bucket


def attend_rows(rows, length, column, segment_index, base, query, key, value):
    pairs = HEADS // 2
    part = pl.BlockSpec((length, 2 * KV), lambda r, p: (r, p))
    return pl.pallas_call(
        attend_kernel,
        grid=(rows, pairs),
        out_shape=[
            jax.ShapeDtypeStruct(query.shape, jnp.bfloat16),
            jax.ShapeDtypeStruct(
                (rows, pairs, length // BLOCK, 2 * BLOCK, 3 * BLOCK), jnp.bfloat16
            ),
        ],
        in_specs=[
            pl.BlockSpec((length, BLOCK), lambda r, p: (r, 0)),
            pl.BlockSpec((1, 1, length), lambda r, p: (r, 0, 0)),
            pl.BlockSpec((1, 2, 3 * BLOCK), lambda r, p: (p, 0, 0)),
            part, part, part,
        ],
        out_specs=[
            part,
            pl.BlockSpec(
                (1, 1, length // BLOCK, 2 * BLOCK, 3 * BLOCK), lambda r, p: (r, p, 0, 0, 0)
            ),
        ],
        compiler_params=pltpu.CompilerParams(vmem_limit_bytes=48 * 2**20),
        name="attend",
    )(column, segment_index.reshape(rows, 1, length), base, query, key, value)


def attend_rows_back(rows, length, query, key, value, grad, shares):
    pairs = HEADS // 2
    part = pl.BlockSpec((length, 2 * KV), lambda p, r: (r, p))
    return pl.pallas_call(
        attend_back_kernel,
        grid=(pairs, rows),
        out_shape=[jax.ShapeDtypeStruct(query.shape, jnp.bfloat16)] * 3
        + [jax.ShapeDtypeStruct((pairs, 2, 3 * BLOCK), jnp.float32)],
        in_specs=[
            part, part, part, part,
            pl.BlockSpec(
                (1, 1, length // BLOCK, 2 * BLOCK, 3 * BLOCK), lambda p, r: (r, p, 0, 0, 0)
            ),
        ],
        out_specs=[part, part, part, pl.BlockSpec((1, 2, 3 * BLOCK), lambda p, r: (p, 0, 0))],
        scratch_shapes=[
            pltpu.VMEM((2 * BLOCK, 3 * BLOCK), jnp.float32),
            pltpu.VMEM((length, 2 * KV), jnp.float32),
            pltpu.VMEM((length, 2 * KV), jnp.float32),
        ],
        compiler_params=pltpu.CompilerParams(vmem_limit_bytes=48 * 2**20),
        name="attend_back",
    )(query, key, value, grad, shares)


def gelu_parts(before):
    slope = 0.7978845608028654
    square = before * before
    bend = jnp.tanh(slope * (before + 0.044715 * before * square))
    half = 0.5 * (1.0 + bend)
    rise = half + 0.5 * before * (1.0 - bend * bend) * slope * (1.0 + 3 * 0.044715 * square)
    return before * half, rise


def slots_of(stacked, count):
    rows, columns = stacked.shape
    own = lax.broadcasted_iota(jnp.int32, (rows, columns), 0) // count
    head = lax.broadcasted_iota(jnp.int32, (rows, columns), 1) // KV
    return jnp.where(own == head, stacked, 0.0)


def decoder_kernel(rows, slots, *refs):
    (
        segment_ref, start_ref, cotangent_ref, gain_ref, keys_ref, values_ref,
        self_value_hbm, self_output_hbm, cross_query_hbm, cross_output_hbm,
        inner_hbm, outer_hbm,
        decoded_ref, start_grad_ref, gain_grad_ref,
        normed_fin_ref, active_ref, normed_start_ref, own_ref, normed_mid_ref, context_ref,
        before_grad_ref, last_branch_ref, grad_own_ref, self_branch_ref, grad_asking_ref,
        cross_branch_ref, grad_keys_ref, grad_values_ref,
        self_value, self_output, cross_query, cross_output, inner, outer, sems,
    ) = refs
    loads = []
    for at, (source, target) in enumerate((
        (self_value_hbm, self_value), (self_output_hbm, self_output),
        (cross_query_hbm, cross_query), (cross_output_hbm, cross_output),
        (inner_hbm, inner), (outer_hbm, outer),
    )):
        loads.append(pltpu.make_async_copy(source, target, sems.at[at]))
        loads[-1].start()
    narrow = jnp.bfloat16
    length = keys_ref.shape[0] // rows
    start_gain, middle_gain, final_gain = gain_ref[0:1], gain_ref[1:2], gain_ref[2:3]

    start_field = start_ref[...].astype(jnp.float32)
    scale_start = root_scale(start_field)
    normed_start = (start_field * scale_start * start_gain).astype(narrow)
    normed_start_ref[...] = normed_start
    loads[0].wait()
    own = product(normed_start, self_value[...]).astype(narrow)
    own_ref[...] = own
    loads[1].wait()
    first_field = start_field + product(own, self_output[...])
    scale_mid = root_scale(first_field)
    normed_mid = (first_field * scale_mid * middle_gain).astype(narrow)
    normed_mid_ref[...] = normed_mid
    loads[2].wait()
    asking = product(normed_mid, cross_query[...]).astype(narrow).astype(jnp.float32)
    wides, all_shares, contexts = [], [], []
    for row in range(rows):
        part = asking[row * slots : (row + 1) * slots]
        wide = slots_of(jnp.concatenate([part] * HEADS, axis=0), slots).astype(narrow)
        span = slice(row * length, (row + 1) * length)
        scores = product_right(wide, keys_ref[span])
        slot = lax.rem(lax.broadcasted_iota(jnp.int32, scores.shape, 0), slots)
        scores = jnp.where(slot == segment_ref[row : row + 1], scores, negative_fill)
        powers = jnp.exp(scores - jnp.max(scores, axis=1, keepdims=True))
        shares = powers * (1.0 / jnp.sum(powers, axis=1, keepdims=True))
        mixed = slots_of(product(shares.astype(narrow), values_ref[span]), slots)
        contexts.append(jnp.sum(mixed.reshape(HEADS, slots, -1), axis=0))
        wides.append(wide)
        all_shares.append(shares)
    context = jnp.concatenate(contexts, axis=0).astype(narrow)
    context_ref[...] = context
    loads[3].wait()
    second_field = first_field + product(context, cross_output[...])
    scale_fin = root_scale(second_field)
    normed_fin = (second_field * scale_fin * final_gain).astype(narrow)
    normed_fin_ref[...] = normed_fin
    loads[4].wait()
    active, rise = gelu_parts(product(normed_fin, inner[...]))
    active = active.astype(narrow)
    active_ref[...] = active
    loads[5].wait()
    decoded_ref[...] = (second_field + product(active, outer[...])).astype(narrow)

    branch = cotangent_ref[...]
    last_branch_ref[...] = branch
    grad_second = branch.astype(jnp.float32)
    before_grad = (product_right(branch, outer[...]) * rise).astype(narrow)
    before_grad_ref[...] = before_grad
    grad_normed = product_right(before_grad, inner[...])
    moved, final_gain_grad = norm_back(grad_normed, second_field, scale_fin, final_gain)
    grad_second = grad_second + moved
    branch = grad_second.astype(narrow)
    cross_branch_ref[...] = branch
    grad_context = product_right(branch, cross_output[...]).astype(narrow).astype(jnp.float32)
    askings = []
    for row in range(rows):
        part = grad_context[row * slots : (row + 1) * slots]
        wide = slots_of(jnp.concatenate([part] * HEADS, axis=0), slots).astype(narrow)
        span = slice(row * length, (row + 1) * length)
        shares = all_shares[row]
        moved = shares * product_right(wide, values_ref[span])
        grad_scores = moved - shares * jnp.sum(moved, axis=1, keepdims=True)
        grad_scores = grad_scores.astype(narrow)
        grad_values_ref[span] = product_left(shares.astype(narrow), wide).astype(narrow)
        grad_keys_ref[span] = product_left(grad_scores, wides[row]).astype(narrow)
        mixed = slots_of(product(grad_scores, keys_ref[span]), slots)
        askings.append(jnp.sum(mixed.reshape(HEADS, slots, -1), axis=0))
    grad_asking = jnp.concatenate(askings, axis=0).astype(narrow)
    grad_asking_ref[...] = grad_asking
    grad_normed = product_right(grad_asking, cross_query[...])
    moved, middle_gain_grad = norm_back(grad_normed, first_field, scale_mid, middle_gain)
    grad_first = grad_second + moved
    branch = grad_first.astype(narrow)
    self_branch_ref[...] = branch
    grad_own = product_right(branch, self_output[...]).astype(narrow)
    grad_own_ref[...] = grad_own
    grad_normed = product_right(grad_own, self_value[...])
    moved, start_gain_grad = norm_back(grad_normed, start_field, scale_start, start_gain)
    start_grad_ref[...] = grad_first + moved
    gain_grad_ref[...] = jnp.concatenate(
        [start_gain_grad[None], middle_gain_grad[None], final_gain_grad[None]], axis=0
    )


def decode(segment_index, start, cotangent, gains, keys, values, weights):
    rows, tokens, width = segment_index.shape[0], start.shape[0], start.shape[1]
    narrow, hidden = jnp.bfloat16, weights[4].shape[1]
    few = jax.ShapeDtypeStruct((tokens, width), narrow)
    many = jax.ShapeDtypeStruct((tokens, hidden), narrow)
    outs = [
        few,
        jax.ShapeDtypeStruct((tokens, width), jnp.float32),
        jax.ShapeDtypeStruct((3, width), jnp.float32),
        few, many, few, few, few, few,
        many, few, few, few, few, few,
        jax.ShapeDtypeStruct(keys.shape, narrow),
        jax.ShapeDtypeStruct(values.shape, narrow),
    ]
    local = pl.BlockSpec(memory_space=pltpu.VMEM)
    return pl.pallas_call(
        functools.partial(decoder_kernel, rows, tokens // rows),
        out_shape=outs,
        in_specs=[local] * 6 + [pl.BlockSpec(memory_space=pl.ANY)] * 6,
        out_specs=[local] * len(outs),
        scratch_shapes=[pltpu.VMEM(w.shape, narrow) for w in weights]
        + [pltpu.SemaphoreType.DMA((6,))],
        compiler_params=pltpu.CompilerParams(vmem_limit_bytes=48 * 2**20),
        name="decode",
    )(segment_index, start, cotangent, gains, keys, values, *weights)


def on_device(
    tokens,
    segment_index,
    start_vectors,
    first_gain,
    query_weight,
    key_weight,
    value_weight,
    output_weight,
    position_table,
    second_gain,
    inner_weight,
    outer_weight,
    start_gain,
    self_value,
    self_output,
    middle_gain,
    cross_query,
    cross_key,
    cross_value,
    cross_output,
    final_gain,
    decoder_inner,
    decoder_outer,
    encoded_cotangent,
    decoded_cotangent,
):
    row_count = segment_index.shape[0]
    length = segment_index.shape[1]
    slot_count = start_vectors.shape[1]
    width = tokens.shape[1]
    count = lax.axis_size("fsdp")
    depth = first_gain.shape[0]
    gains = jnp.stack([first_gain, second_gain, start_gain, middle_gain, final_gain])
    gains = jnp.pad(gains, ((0, 11), (0, 128 - depth)))
    whole = gather_weights(
        count,
        (
            query_weight, key_weight, value_weight, output_weight, inner_weight, outer_weight,
            cross_key, cross_value, self_value, self_output, cross_query, cross_output,
            decoder_inner, decoder_outer, gains,
        ),
        KINDS,
    )
    gain_parts = whole[14][:, :5, :depth]
    gain_set = [gain_parts[:, at].reshape(count * depth) for at in range(5)]
    (
        query_full, key_full, value_full, output_full, inner_full, outer_full, cross_key_full,
        cross_value_full, self_value_full, self_output_full, cross_query_full, cross_output_full,
        decoder_inner_full, decoder_outer_full,
    ) = [part.reshape(-1, part.shape[2]) for part in whole[:14]]
    gain_one, gain_two, start_full, middle_full, final_full = gain_set
    gain_one = gain_one.astype(jnp.float32)
    gain_two = gain_two.astype(jnp.float32)
    choices = jnp.arange(position_table.shape[0], dtype=jnp.int32)
    onehot = (offset_buckets()[None, :] == choices[:, None]).astype(jnp.float32)
    base = jnp.dot(position_table.T, onehot, precision=lax.Precision.HIGHEST)
    base = base.reshape(HEADS // 2, 2, 3 * BLOCK)
    column = jnp.broadcast_to(segment_index.reshape(-1, 1), (row_count * length, BLOCK))
    field = tokens.astype(jnp.float32)
    scale_one = root_scale(field)
    normed_one = (field * scale_one * gain_one).astype(jnp.bfloat16)
    query_all = product(normed_one, query_full).astype(jnp.bfloat16)
    key_all = product(normed_one, key_full).astype(jnp.bfloat16)
    value_all = product(normed_one, value_full).astype(jnp.bfloat16)
    context, shares = attend_rows(
        row_count, length, column, segment_index, base, query_all, key_all, value_all
    )
    hidden = field + product(context, output_full)
    scale_two = root_scale(hidden)
    normed_two = (hidden * scale_two * gain_two).astype(jnp.bfloat16)
    inner_before = product(normed_two, inner_full)
    active = jax.nn.gelu(inner_before).astype(jnp.bfloat16)
    encoded_full = hidden + product(active, outer_full)
    memory = encoded_full.astype(jnp.bfloat16)
    start_full = start_full.astype(jnp.float32)
    middle_full = middle_full.astype(jnp.float32)
    final_full = final_full.astype(jnp.float32)
    cross_keys = product(memory, cross_key_full).astype(jnp.bfloat16)
    cross_values = product(memory, cross_value_full).astype(jnp.bfloat16)
    back_gain_one, back_gain_two = gain_one, gain_two
    back_query, back_key, back_value, back_output = query_full, key_full, value_full, output_full
    back_inner, back_outer = inner_full, outer_full
    back_cross_key, back_cross_value = cross_key_full, cross_value_full
    token_count = row_count * slot_count
    (
        decoded, start_grad, decoder_gain_grads,
        normed_fin, decoder_active, normed_start, own_value, normed_mid, cross_context,
        decoder_before_grad, last_branch, grad_own, self_branch, grad_asking, cross_branch,
        grad_cross_keys, grad_cross_values,
    ) = decode(
        segment_index,
        start_vectors.reshape(token_count, width),
        decoded_cotangent.reshape(token_count, width),
        jnp.stack([start_full, middle_full, final_full]),
        cross_keys,
        cross_values,
        (
            self_value_full, self_output_full, cross_query_full, cross_output_full,
            decoder_inner_full, decoder_outer_full,
        ),
    )
    grad_cross_key = product_left(memory, grad_cross_keys)
    grad_cross_value = product_left(memory, grad_cross_values)
    grad_memory = product_right(grad_cross_keys, back_cross_key) + product_right(
        grad_cross_values, back_cross_value
    )
    grad_encoded = encoded_cotangent.astype(jnp.float32) + grad_memory
    grad_branch = grad_encoded.astype(jnp.bfloat16)
    grad_outer = product_left(active, grad_branch)
    grad_active = product_right(grad_branch, back_outer)
    grad_before = gelu_back(inner_before, grad_active).astype(jnp.bfloat16)
    grad_inner = product_left(normed_two, grad_before)
    grad_normed = product_right(grad_before, back_inner)
    field_part, grad_gain_two = norm_back(
        grad_normed, hidden, scale_two, back_gain_two.astype(jnp.float32)
    )
    grad_hidden = grad_encoded + field_part
    grad_branch = grad_hidden.astype(jnp.bfloat16)
    grad_output = product_left(context, grad_branch)
    grad_context = product_right(grad_branch, back_output).astype(jnp.bfloat16)
    grad_query_all, grad_key_all, grad_value_all, bias_sums = attend_rows_back(
        row_count, length, query_all, key_all, value_all, grad_context, shares
    )
    grad_query = product_left(normed_one, grad_query_all)
    grad_key = product_left(normed_one, grad_key_all)
    grad_value = product_left(normed_one, grad_value_all)
    grad_normed = (
        product_right(grad_query_all, back_query)
        + product_right(grad_key_all, back_key)
        + product_right(grad_value_all, back_value)
    )
    field_part, grad_gain_one = norm_back(
        grad_normed, field, scale_one, back_gain_one.astype(jnp.float32)
    )
    tokens_grad = grad_hidden + field_part
    table_grad = lax.dot_general(
        onehot,
        bias_sums.reshape(HEADS, 3 * BLOCK),
        (((1,), (1,)), ((), ())),
        precision=lax.Precision.HIGHEST,
    )
    lefts = (normed_fin, decoder_active, normed_start, own_value, normed_mid, cross_context)
    rights = (decoder_before_grad, last_branch, grad_own, self_branch, grad_asking, cross_branch)
    pair_shapes = [(left.shape[1] // count, right.shape[1]) for left, right in zip(lefts, rights)]
    left_cols = []
    for left, (rows, unused) in zip(lefts, pair_shapes):
        columns = left.reshape(token_count, count, rows).transpose(1, 0, 2)
        left_cols.append(jnp.pad(columns, ((0, 0), (0, 0), (0, -rows % 128))))
    small = jnp.concatenate([
        jnp.stack([grad_gain_one, grad_gain_two]),
        decoder_gain_grads,
        jnp.pad(table_grad.reshape(1, -1), ((0, 2), (0, width - table_grad.size))),
    ])
    encoder_grads = (
        grad_inner, grad_outer, grad_query, grad_key, grad_value, grad_output,
        grad_cross_key, grad_cross_value,
    )
    encoder_sums, decoder_sums, small_sum = reduce_grads(
        count,
        ENCODER_KINDS,
        [
            g.astype(jnp.bfloat16).reshape(count, g.shape[0] // count, g.shape[1])
            for g in encoder_grads
        ],
        jnp.concatenate(left_cols, axis=2),
        jnp.concatenate(rights, axis=1),
        pair_shapes,
        small,
    )
    (
        inner_weight_grad, outer_weight_grad, query_weight_grad, key_weight_grad,
        value_weight_grad, output_weight_grad, cross_key_grad, cross_value_grad,
    ) = [part.astype(jnp.float32) for part in encoder_sums]
    (
        decoder_inner_grad, decoder_outer_grad, self_value_grad, self_output_grad,
        cross_query_grad, cross_output_grad,
    ) = [part.astype(jnp.float32) for part in decoder_sums]
    own_gains = lax.dynamic_slice_in_dim(
        small_sum[:5], lax.axis_index("fsdp") * depth, depth, axis=1
    )
    first_gain_grad, second_gain_grad, start_gain_grad, middle_gain_grad, final_gain_grad = own_gains
    position_table_grad = small_sum[5, : table_grad.size].reshape(table_grad.shape)
    decoded = decoded.reshape(start_vectors.shape)
    start_grad = start_grad.reshape(start_vectors.shape)
    return (
        encoded_full.astype(jnp.bfloat16),
        decoded,
        tokens_grad,
        start_grad,
        first_gain_grad,
        query_weight_grad,
        key_weight_grad,
        value_weight_grad,
        output_weight_grad,
        position_table_grad,
        second_gain_grad,
        inner_weight_grad,
        outer_weight_grad,
        start_gain_grad,
        self_value_grad,
        self_output_grad,
        middle_gain_grad,
        cross_query_grad,
        cross_key_grad,
        cross_value_grad,
        cross_output_grad,
        final_gain_grad,
        decoder_inner_grad,
        decoder_outer_grad,
    )


def solution(mesh):
    placed = (
        P(("dp", "fsdp"), None),
        P(("dp", "fsdp"), None),
        P(("dp", "fsdp"), None, None),
        P("fsdp"),
        P("fsdp", None),
        P("fsdp", None),
        P("fsdp", None),
        P("fsdp", None),
        P(),
        P("fsdp"),
        P("fsdp", None),
        P("fsdp", None),
        P("fsdp"),
        P("fsdp", None),
        P("fsdp", None),
        P("fsdp"),
        P("fsdp", None),
        P("fsdp", None),
        P("fsdp", None),
        P("fsdp", None),
        P("fsdp"),
        P("fsdp", None),
        P("fsdp", None),
        P(("dp", "fsdp"), None),
        P(("dp", "fsdp"), None, None),
    )
    return jax.shard_map(
        on_device,
        mesh=mesh,
        in_specs=placed,
        out_specs=(
            P(("dp", "fsdp"), None),
            P(("dp", "fsdp"), None, None),
            P(("dp", "fsdp"), None),
            P(("dp", "fsdp"), None, None),
            P("fsdp"),
            P("fsdp", None),
            P("fsdp", None),
            P("fsdp", None),
            P("fsdp", None),
            P(),
            P("fsdp"),
            P("fsdp", None),
            P("fsdp", None),
            P("fsdp"),
            P("fsdp", None),
            P("fsdp", None),
            P("fsdp"),
            P("fsdp", None),
            P("fsdp", None),
            P("fsdp", None),
            P("fsdp", None),
            P("fsdp"),
            P("fsdp", None),
            P("fsdp", None),
        ),
        check_vma=False,
    )
```

```python
import functools

import jax
import jax.numpy as jnp
from jax import lax
from jax.experimental import pallas as pl
from jax.experimental.pallas import tpu as pltpu
from jax.sharding import PartitionSpec as P

HEADS = 12
KV = 64
BLOCK = 128


epsilon = 1e-06
negative_fill = -1e30
bucket_edges = (12, 16, 23, 32, 46, 64, 91)


MESH = pl.DeviceIdType.MESH
KINDS = (
    "square", "square", "square", "square", "wide", "tall", "square", "square",
    "square", "square", "square", "square", "wide", "tall", "small",
)


def ring_position(index, count):
    if count == 64:
        slow, rest = index // 32, index % 32
        row, column = rest // 8, rest % 8
        place = row * 8 + column + (row % 2) * (7 - 2 * column)
        return place + slow * (count - 1 - 2 * place)
    across, along = index % 2, index // 2
    return along + across * (count - 1 - 2 * along)


def ring_index(position, count):
    position = lax.rem(position, count)
    across = position // (count // 2)
    along = position + across * (count - 1 - 2 * position)
    if count == 64:
        row, column = along // 8, along % 8
        return across * 32 + row * 8 + column + (row % 2) * (7 - 2 * column)
    return 2 * along + across


class Spot:
    def __init__(self, count):
        self.count = count
        self.dp = lax.axis_index("dp")
        self.fsdp = lax.axis_index("fsdp")
        self.core = lax.rem(self.dp, 2)
        self.plane = self.dp // 2
        self.place = ring_position(self.fsdp, count)
        self.sibling = (self.dp + 1 - 2 * self.core, self.fsdp)
        self.opposite = (lax.rem(self.dp + 2, 4), self.fsdp)
        self.after = (self.dp, ring_index(self.place + 1, count))
        self.before = (self.dp, ring_index(self.place + count - 1, count))

    def greet(self, others=()):
        barrier = pltpu.get_barrier_semaphore()
        partners = (self.sibling, self.opposite, self.after, self.before) + tuple(others)
        for partner in partners:
            pl.semaphore_signal(barrier, inc=1, device_id=partner, device_id_type=MESH)
        pl.semaphore_wait(barrier, len(partners))


def cut(kind, ref, plane, core):
    rows, columns = ref.shape
    if kind == "small":
        return ref
    if kind == "square":
        half = columns // 2
        return ref.at[:, pl.ds(pl.multiple_of(core * half, 128), half)]
    if kind == "wide":
        quarter = columns // 4
        return ref.at[:, pl.ds(pl.multiple_of((core * 2 + plane) * quarter, 128), quarter)]
    half, upper = columns // 2, rows // 2
    return ref.at[
        pl.ds(pl.multiple_of(plane * upper, 8), upper),
        pl.ds(pl.multiple_of(core * half, 128), half),
    ]


def send(source, target, send_sem, recv_sem, device):
    return pltpu.make_async_remote_copy(
        src_ref=source,
        dst_ref=target,
        send_sem=send_sem,
        recv_sem=recv_sem,
        device_id=device,
        device_id_type=MESH,
    )


def gather_kernel(count, kinds, *refs):
    total = len(kinds)
    shards, fulls = refs[:total], refs[total : 2 * total]
    ring_out, ring_in, near_out, near_in, far_out, far_in, last_out, last_in, own_sem = refs[
        2 * total :
    ]
    spot = Spot(count)
    split = [i for i in range(total) if kinds[i] in ("wide", "tall")]

    window = min(count, 8)

    def slot_of(i, step):
        turn = step if i % 2 else count - step
        return ring_index(spot.place + turn, count)

    def ring_copy(i, step, source=None):
        here = cut(kinds[i], fulls[i].at[slot_of(i, step)], spot.plane, spot.core)
        return send(
            here if source is None else source,
            here,
            ring_out.at[i, lax.rem(step, window)],
            ring_in.at[i, step],
            spot.before if i % 2 else spot.after,
        )

    def near_copy(i, step):
        here = cut(kinds[i], fulls[i].at[slot_of(i, step)], spot.plane, spot.core)
        out = near_out.at[i, lax.rem(step, window)]
        return send(here, here, out, near_in.at[i, step], spot.sibling)

    def far_copy(i, step):
        here = cut(kinds[i], fulls[i].at[slot_of(i, step)], spot.plane, spot.core)
        at = split.index(i)
        out = far_out.at[at, lax.rem(step, window)]
        return send(here, here, out, far_in.at[at, step], spot.opposite)

    def last_copy(i, step):
        here = cut(kinds[i], fulls[i].at[slot_of(i, step)], 1 - spot.plane, spot.core)
        at = split.index(i)
        out = last_out.at[at, lax.rem(step, window)]
        return send(here, here, out, last_in.at[at, step], spot.sibling)

    def start(copy, i, step, first):
        if window < count:

            @pl.when(step >= first + window)
            def _():
                copy(i, step - window).wait_send()

        copy(i, step).start()

    def finish(copy, i, first, end):
        def one(step, carry):
            copy(i, step).wait_send()
            return carry

        lax.fori_loop(max(first, end - window), end, one, 0)

    owns = []
    for i in range(total):
        owns.append(pltpu.make_async_copy(shards[i], fulls[i].at[spot.fsdp], own_sem.at[i]))
        owns[-1].start()
    spot.greet()
    for i in range(total):
        ring_copy(i, 0, cut(kinds[i], shards[i], spot.plane, spot.core)).start()

    def one_step(step, carry):
        for i in range(total):
            ring_copy(i, step - 1).wait_recv()

            @pl.when(step < count - 1)
            def _():
                start(ring_copy, i, step, 0)

            if kinds[i] != "small":
                start(near_copy, i, step, 1)
            if i in split:
                start(far_copy, i, step, 1)

        @pl.when(step > 1)
        def _():
            for i in split:
                far_copy(i, step - 1).wait_recv()
                start(last_copy, i, step - 1, 1)

        return carry

    lax.fori_loop(1, count, one_step, 0)
    for i in split:
        far_copy(i, count - 1).wait_recv()
        start(last_copy, i, count - 1, 1)

    def settle(step, carry):
        for i in range(total):
            if kinds[i] != "small":
                near_copy(i, step).wait_recv()
            if i in split:
                last_copy(i, step).wait_recv()
        return carry

    lax.fori_loop(1, count, settle, 0)
    for i in range(total):
        finish(ring_copy, i, 0, count - 1)
        if kinds[i] != "small":
            finish(near_copy, i, 1, count)
        if i in split:
            finish(far_copy, i, 1, count)
            finish(last_copy, i, 1, count)
    for copy in owns:
        copy.wait()


def gather_weights(count, shards, kinds):
    total = len(shards)
    split = sum(kind in ("wide", "tall") for kind in kinds)
    window = min(count, 8)
    many, few = [
        [pltpu.SemaphoreType.DMA((rows, window)), pltpu.SemaphoreType.DMA((rows, count))] * 2
        for rows in (total, split)
    ]
    return pl.pallas_call(
        functools.partial(gather_kernel, count, kinds),
        out_shape=[jax.ShapeDtypeStruct((count,) + s.shape, s.dtype) for s in shards],
        in_specs=[pl.BlockSpec(memory_space=pl.ANY)] * total,
        out_specs=[pl.BlockSpec(memory_space=pl.ANY)] * total,
        scratch_shapes=many + few + [pltpu.SemaphoreType.DMA((total,))],
        compiler_params=pltpu.CompilerParams(collective_id=0, has_side_effects=True),
        name="gather_weights",
    )(*shards)

def plus(*terms):
    total = terms[0].astype(jnp.float32)
    for term in terms[1:]:
        total = total + term.astype(jnp.float32)
    return total


def half_of(core, columns):
    half = columns // 2
    return pl.ds(pl.multiple_of(core * half, 128), half)


def plane_part(kind, plane, rows, columns):
    if kind == "wide":
        return slice(None), pl.ds(pl.multiple_of(plane * (columns // 2), 128), columns // 2)
    if kind == "tall":
        return pl.ds(pl.multiple_of(plane * (rows // 2), 8), rows // 2), slice(None)
    return slice(None), slice(None)


ENCODER_KINDS = ("wide", "tall", "square", "square", "square", "square", "square", "square")


def reduce_kernel(count, kinds, spans, *refs):
    total, pairs = len(kinds), len(spans)
    refs = list(refs)

    def take(size):
        got = refs[:size]
        del refs[:size]
        return got

    grads = take(total)
    left_part, right_part, small = take(3)
    sums = take(total)
    pair_sums = take(pairs)
    (small_sum,) = take(1)
    half, work, final = take(total), take(total), take(total)
    split = [i for i in range(total) if kinds[i] != "square"]
    far = take(len(split))
    left_all, right_all = take(2)
    pair_half, pair_far, pair_work = take(pairs), take(pairs), take(pairs)
    small_near, small_mid, small_far, small_all = take(4)
    (
        near_sem, ring_out, ring_in, far_sem, end_sem, left_out, left_in,
        right_out, right_in, pair_sem, small_sem, small_out, small_in,
    ) = take(13)
    spot = Spot(count)
    core, plane = spot.core, spot.plane
    diagonal = (lax.rem(spot.dp + 2, 4) + 1 - 2 * core, spot.fsdp)

    def peer(k):
        return (spot.dp, lax.rem(spot.fsdp + k, count))

    barrier = pltpu.get_barrier_semaphore()
    for partner in (spot.sibling, spot.opposite, diagonal):
        pl.semaphore_signal(barrier, inc=1, device_id=partner, device_id_type=MESH)

    def greet(k, carry):
        pl.semaphore_signal(barrier, inc=1, device_id=peer(k), device_id_type=MESH)
        return carry

    lax.fori_loop(1, count, greet, 0)
    pl.semaphore_wait(barrier, count + 2)

    def near_copy(i):
        columns = grads[i].shape[2]
        return send(
            grads[i].at[:, :, half_of(1 - core, columns)], half[i],
            near_sem.at[0, i], near_sem.at[1, i], spot.sibling,
        )

    def slot_at(i, step):
        turn = step + 1 if i % 2 else count - 1 - step
        return ring_index(spot.place + turn, count)

    def far_copy(i, step):
        at = split.index(i)
        rows, columns = half[i].shape[1:]
        part = plane_part(kinds[i], 1 - plane, rows, columns)
        return send(
            half[i].at[(slot_at(i, step),) + part], far[at].at[step],
            far_sem.at[0, at, step], far_sem.at[1, at, step], spot.opposite,
        )

    def ring_copy(i, step):
        return send(
            work[i].at[step], work[i].at[step + 1], ring_out.at[i, step], ring_in.at[i, step],
            spot.before if i % 2 else spot.after,
        )

    def left_copy(k):
        other = lax.rem(spot.fsdp + k, count)
        return send(
            left_part.at[other], left_all.at[spot.fsdp], left_out.at[k], left_in.at[k], peer(k)
        )

    def right_copy(way, step):
        turn = step if way else count - step
        slot = ring_index(spot.place + turn, count)
        width = right_part.shape[1] // 2
        here = right_all.at[slot, :, way * width : (way + 1) * width]
        return send(
            here, here, right_out.at[way, step], right_in.at[way, step],
            spot.before if way else spot.after,
        )

    for i in range(total):
        near_copy(i).start()
    near_small = send(small, small_near, small_sem.at[0], small_sem.at[1], spot.sibling)
    near_small.start()

    def left_start(k, carry):
        left_copy(k).start()
        return carry

    lax.fori_loop(1, count, left_start, 0)
    right_all[spot.fsdp] = right_part[...]
    left_all[spot.fsdp] = left_part[spot.fsdp]
    for way in range(2):
        right_copy(way, 0).start()
    near_small.wait()
    small_mid[...] = small[...] + small_near[...]
    far_small = send(small_mid, small_far, small_sem.at[2], small_sem.at[3], spot.opposite)
    far_small.start()

    for i in range(total):
        near_copy(i).wait_recv()

        def join(slot, carry):
            mine = grads[i][slot, :, half_of(core, grads[i].shape[2])]
            half[i][slot] = plus(half[i][slot], mine).astype(jnp.bfloat16)
            return carry

        lax.fori_loop(0, count, join, 0)
        if i in split:

            def far_start(step, carry):
                far_copy(i, step).start()
                return carry

            lax.fori_loop(0, count, far_start, 0)

    far_small.wait()
    small_all[spot.fsdp] = small_mid[...] + small_far[...]

    def small_copy(k):
        here = small_all.at[spot.fsdp]
        return send(here, here, small_out.at[k], small_in.at[k], peer(k))

    def small_start(k, carry):
        small_copy(k).start()
        return carry

    lax.fori_loop(1, count, small_start, 0)

    def right_step(step, carry):
        for way in range(2):
            right_copy(way, step - 1).wait_recv()

            @pl.when(step < count - 1)
            def _():
                right_copy(way, step).start()

        return carry

    lax.fori_loop(1, count, right_step, 0)

    def left_wait(k, carry):
        left_copy(k).wait_recv()
        return carry

    lax.fori_loop(1, count, left_wait, 0)

    def pair_near(j):
        columns = pair_sums[j].shape[1]
        return send(
            pair_work[j].at[:, half_of(1 - core, columns)], pair_half[j],
            pair_sem.at[0, j], pair_sem.at[1, j], spot.sibling,
        )

    def pair_across(j):
        return send(
            pair_half[j], pair_far[j], pair_sem.at[2, j], pair_sem.at[3, j], spot.opposite
        )

    def pair_end(j):
        here = pair_sums[j].at[:, half_of(core, pair_sums[j].shape[1])]
        return send(here, here, pair_sem.at[4, j], pair_sem.at[5, j], spot.sibling)

    for j, (left_at, right_at) in enumerate(spans):
        rows, columns = pair_sums[j].shape
        span = -(-rows // 128) * 128
        left = left_all[:, :, left_at : left_at + span].reshape(-1, span)
        for begin in range(0, columns, 768):
            right = right_all[:, :, right_at + begin : right_at + begin + 768].reshape(-1, 768)
            block = lax.dot_general(
                left, right, (((0,), (0,)), ((), ())), preferred_element_type=jnp.float32
            )
            pair_work[j][:, begin : begin + 768] = block[:rows].astype(jnp.bfloat16)
        pair_near(j).start()
    for j in range(pairs):
        pair_near(j).wait()
        mine = pair_work[j][:, half_of(core, pair_sums[j].shape[1])]
        pair_half[j][...] = plus(pair_half[j][...], mine).astype(jnp.bfloat16)
        pair_across(j).start()

    def one_step(step, carry):
        for i in range(total):
            rows, columns = half[i].shape[1:]
            slot = slot_at(i, step)
            value = half[i][(slot,) + plane_part(kinds[i], plane, rows, columns)]
            value = value.astype(jnp.float32)
            if i in split:
                far_copy(i, step).wait_recv()
                value = value + far[split.index(i)][step].astype(jnp.float32)

            @pl.when(step > 0)
            def _():
                ring_copy(i, step - 1).wait_recv()
                work[i][step] = plus(value, work[i][step]).astype(jnp.bfloat16)

            @pl.when(step == 0)
            def _():
                work[i][step] = value.astype(jnp.bfloat16)

            @pl.when(step < count - 1)
            def _():
                ring_copy(i, step).start()

        return carry

    lax.fori_loop(0, count, one_step, 0)

    def end_across(i):
        return send(
            work[i].at[count - 1], final[i], end_sem.at[0, i], end_sem.at[1, i], spot.opposite
        )

    def end_piece(i, mine_plane):
        rows, columns = sums[i].shape
        wide = half_of(core, columns)
        if kinds[i] == "square":
            return sums[i].at[:, wide]
        return cut(kinds[i], sums[i], mine_plane, core)

    def end_copies(i):
        here = end_piece(i, plane)
        copies = [send(here, here, end_sem.at[2, i], end_sem.at[3, i], spot.sibling)]
        if i in split:
            copies.append(send(here, here, end_sem.at[4, i], end_sem.at[5, i], spot.opposite))
            copies.append(send(here, here, end_sem.at[6, i], end_sem.at[7, i], diagonal))
        return copies

    for i in range(total):
        if i not in split:
            end_across(i).start()
    for i in split:
        end_piece(i, plane)[...] = work[i][count - 1]
        for copy in end_copies(i):
            copy.start()
    for j in range(pairs):
        pair_across(j).wait()
        here = half_of(core, pair_sums[j].shape[1])
        pair_sums[j][:, here] = plus(pair_half[j][...], pair_far[j][...]).astype(jnp.bfloat16)
        pair_end(j).start()
    for i in range(total):
        if i not in split:
            end_across(i).wait()
            value = plus(work[i][count - 1], final[i][...]).astype(jnp.bfloat16)
            end_piece(i, plane)[...] = value
            for copy in end_copies(i):
                copy.start()

    def small_wait(k, carry):
        small_copy(k).wait_recv()
        return carry

    lax.fori_loop(1, count, small_wait, 0)
    small_sum[...] = lax.fori_loop(
        1, count, lambda k, so_far: so_far + small_all[k], small_all[0]
    )
    for i in range(total):
        for copy in end_copies(i):
            copy.wait()
    for j in range(pairs):
        pair_end(j).wait()
    for i in range(total):
        near_copy(i).wait_send()

    def drain(step, carry):
        for i in split:
            far_copy(i, step).wait_send()
        return carry

    lax.fori_loop(0, count, drain, 0)

    def drain_ring(step, carry):
        for i in range(total):
            ring_copy(i, step).wait_send()
        for way in range(2):
            right_copy(way, step).wait_send()
        left_copy(step + 1).wait_send()
        small_copy(step + 1).wait_send()
        return carry

    lax.fori_loop(0, count - 1, drain_ring, 0)


def reduce_grads(count, kinds, grads, left_part, right_part, pair_shapes, small):
    total, pairs = len(kinds), len(pair_shapes)
    spans, left_at, right_at = [], 0, 0
    for rows, columns in pair_shapes:
        spans.append((left_at, right_at))
        left_at, right_at = left_at + -(-rows // 128) * 128, right_at + columns
    narrow = jnp.bfloat16
    blocks = [g.shape[1:] for g in grads]
    pieces = []
    for kind, (rows, columns) in zip(kinds, blocks):
        if kind == "wide":
            pieces.append((rows, columns // 4))
        elif kind == "tall":
            pieces.append((rows // 2, columns // 2))
        else:
            pieces.append((rows, columns // 2))
    split = [i for i in range(total) if kinds[i] != "square"]
    dma = pltpu.SemaphoreType.DMA
    scratch = [pltpu.VMEM((count, r, c // 2), narrow) for r, c in blocks]
    scratch += [pltpu.VMEM((count, r, c), narrow) for r, c in pieces]
    scratch += [pltpu.VMEM((r, c), narrow) for r, c in pieces]
    scratch += [pltpu.VMEM((count,) + pieces[i], narrow) for i in split]
    scratch += [
        pltpu.VMEM(left_part.shape, narrow),
        pltpu.VMEM((count,) + right_part.shape, narrow),
    ]
    scratch += [pltpu.VMEM((r, c // 2), narrow) for r, c in pair_shapes] * 2
    scratch += [pltpu.VMEM((r, c), narrow) for r, c in pair_shapes]
    scratch += [pltpu.VMEM(small.shape, jnp.float32)] * 3
    scratch += [pltpu.VMEM((count,) + small.shape, jnp.float32)]
    scratch += [
        dma((2, total)), dma((total, count)), dma((total, count)), dma((2, len(split), count)),
        dma((8, total)), dma((count,)), dma((count,)), dma((2, count)), dma((2, count)),
        dma((6, pairs)), dma((4,)), dma((count,)), dma((count,)),
    ]
    outs = [jax.ShapeDtypeStruct(b, narrow) for b in blocks]
    outs += [jax.ShapeDtypeStruct(s, narrow) for s in pair_shapes]
    outs += [jax.ShapeDtypeStruct(small.shape, jnp.float32)]
    got = pl.pallas_call(
        functools.partial(reduce_kernel, count, kinds, spans),
        out_shape=outs,
        in_specs=[pl.BlockSpec(memory_space=pltpu.VMEM)] * (total + 3),
        out_specs=[pl.BlockSpec(memory_space=pltpu.VMEM)] * len(outs),
        scratch_shapes=scratch,
        compiler_params=pltpu.CompilerParams(
            collective_id=1, has_side_effects=True, vmem_limit_bytes=62 * 2**20
        ),
        name="reduce_grads",
    )(*grads, left_part, right_part, small)
    return got[:total], got[total : total + pairs], got[-1]


def product(left, right):
    return jnp.dot(left, right, preferred_element_type=jnp.float32)


def product_left(left, right):
    return lax.dot_general(
        left, right, (((0,), (0,)), ((), ())), preferred_element_type=jnp.float32
    )


def product_right(left, right):
    return lax.dot_general(
        left, right, (((1,), (1,)), ((), ())), preferred_element_type=jnp.float32
    )


def root_scale(field):
    return lax.rsqrt(jnp.mean(field * field, axis=-1, keepdims=True) + epsilon)


def norm_back(grad_normed, field, scale, gain):
    gain_grad = jnp.sum(grad_normed * field * scale, axis=0)
    weighted = grad_normed * gain
    field_grad = scale * weighted - field * (scale * scale * scale) * jnp.mean(
        weighted * field, axis=-1, keepdims=True
    )
    return (field_grad, gain_grad)


def wide_heads(block):
    first = lax.broadcasted_iota(jnp.int32, block.shape, 1) < KV
    none = jnp.zeros_like(block)
    return jnp.concatenate([jnp.where(first, block, none), jnp.where(first, none, block)], axis=0)


def narrow_heads(stacked):
    half = stacked.shape[0] // 2
    first = lax.broadcasted_iota(jnp.int32, (half, stacked.shape[1]), 1) < KV
    return jnp.where(first, stacked[:half], stacked[half:])


def reach(at, blocks):
    low, high = max(0, at - 1), min(blocks, at + 2)
    begin = (low - at + 1) * BLOCK
    return slice(low * BLOCK, high * BLOCK), slice(begin, begin + (high - low) * BLOCK)


def bias_block(base):
    heads = []
    for at in range(2):
        level = jnp.broadcast_to(base[at : at + 1], (BLOCK, base.shape[1]))
        heads.append(pltpu.roll(level, 0, axis=1, stride=1, stride_axis=0))
    return jnp.concatenate(heads, axis=0)


def offset_sums(block):
    rows, width = block.shape
    while rows > 8:
        rows = rows // 2
        block = block[:rows] + pltpu.roll(block[rows:], width - rows, axis=1)
    place = lax.broadcasted_iota(jnp.int32, block.shape, 0)
    for bit in (4, 2, 1):
        block = jnp.where((place & bit) > 0, pltpu.roll(block, width - bit, axis=1), block)
    return jnp.sum(block, axis=0, keepdims=True)


def attend_kernel(column_ref, row_ref, base_ref, query_ref, key_ref, value_ref, out_ref, share_ref):
    blocks = query_ref.shape[0] // BLOCK
    bias = bias_block(base_ref[0])
    for at in range(blocks):
        keys, places = reach(at, blocks)
        own = slice(at * BLOCK, (at + 1) * BLOCK)
        scores = product_right(wide_heads(query_ref[own]), key_ref[keys]) + bias[:, places]
        allowed = column_ref[own, :1] == row_ref[0, :1, keys]
        scores = jnp.where(jnp.concatenate([allowed, allowed], axis=0), scores, negative_fill)
        powers = jnp.exp(scores - jnp.max(scores, axis=1, keepdims=True))
        shares = powers * (1.0 / jnp.sum(powers, axis=1, keepdims=True))
        shares = shares.astype(jnp.bfloat16)
        share_ref[0, 0, at, :, places] = shares
        mixed = product(shares, value_ref[keys])
        out_ref[own] = narrow_heads(mixed).astype(jnp.bfloat16)


def attend_back_kernel(
    query_ref, key_ref, value_ref, grad_ref, share_ref,
    grad_query_ref, grad_key_ref, grad_value_ref, sums_ref, bias_acc, key_acc, value_acc,
):
    blocks = query_ref.shape[0] // BLOCK

    @pl.when(pl.program_id(1) == 0)
    def _():
        bias_acc[...] = jnp.zeros_like(bias_acc)

    key_acc[...] = jnp.zeros_like(key_acc)
    value_acc[...] = jnp.zeros_like(value_acc)
    for at in range(blocks):
        keys, places = reach(at, blocks)
        own = slice(at * BLOCK, (at + 1) * BLOCK)
        query, grad = wide_heads(query_ref[own]), wide_heads(grad_ref[own])
        narrow_shares = share_ref[0, 0, at, :, places]
        shares = narrow_shares.astype(jnp.float32)
        value_acc[keys] += product_left(narrow_shares, grad)
        moved = shares * product_right(grad, value_ref[keys])
        grad_scores = moved - shares * jnp.sum(moved, axis=1, keepdims=True)
        bias_acc[:, places] += grad_scores
        narrow = grad_scores.astype(jnp.bfloat16)
        grad_query_ref[own] = narrow_heads(product(narrow, key_ref[keys])).astype(jnp.bfloat16)
        key_acc[keys] += product_left(narrow, query)
    grad_key_ref[...] = key_acc[...].astype(jnp.bfloat16)
    grad_value_ref[...] = value_acc[...].astype(jnp.bfloat16)

    @pl.when(pl.program_id(1) == pl.num_programs(1) - 1)
    def _():
        sums_ref[0] = jnp.concatenate(
            [offset_sums(bias_acc[:BLOCK]), offset_sums(bias_acc[BLOCK:])], axis=0
        )


def offset_buckets():
    offset = jnp.arange(3 * BLOCK, dtype=jnp.int32) - BLOCK
    distance = jnp.abs(offset)
    far_bucket = 8 + sum(((distance >= boundary).astype(jnp.int32) for boundary in bucket_edges))
    near_bucket = jnp.where(distance < 8, distance, far_bucket)
    return jnp.where(offset > 0, 16, 0) + near_bucket


def attend_rows(rows, length, column, segment_index, base, query, key, value):
    pairs = HEADS // 2
    part = pl.BlockSpec((length, 2 * KV), lambda r, p: (r, p))
    return pl.pallas_call(
        attend_kernel,
        grid=(rows, pairs),
        out_shape=[
            jax.ShapeDtypeStruct(query.shape, jnp.bfloat16),
            jax.ShapeDtypeStruct(
                (rows, pairs, length // BLOCK, 2 * BLOCK, 3 * BLOCK), jnp.bfloat16
            ),
        ],
        in_specs=[
            pl.BlockSpec((length, BLOCK), lambda r, p: (r, 0)),
            pl.BlockSpec((1, 1, length), lambda r, p: (r, 0, 0)),
            pl.BlockSpec((1, 2, 3 * BLOCK), lambda r, p: (p, 0, 0)),
            part, part, part,
        ],
        out_specs=[
            part,
            pl.BlockSpec(
                (1, 1, length // BLOCK, 2 * BLOCK, 3 * BLOCK), lambda r, p: (r, p, 0, 0, 0)
            ),
        ],
        compiler_params=pltpu.CompilerParams(vmem_limit_bytes=48 * 2**20),
        name="attend",
    )(column, segment_index.reshape(rows, 1, length), base, query, key, value)


def attend_rows_back(rows, length, query, key, value, grad, shares):
    pairs = HEADS // 2
    part = pl.BlockSpec((length, 2 * KV), lambda p, r: (r, p))
    return pl.pallas_call(
        attend_back_kernel,
        grid=(pairs, rows),
        out_shape=[jax.ShapeDtypeStruct(query.shape, jnp.bfloat16)] * 3
        + [jax.ShapeDtypeStruct((pairs, 2, 3 * BLOCK), jnp.float32)],
        in_specs=[
            part, part, part, part,
            pl.BlockSpec(
                (1, 1, length // BLOCK, 2 * BLOCK, 3 * BLOCK), lambda p, r: (r, p, 0, 0, 0)
            ),
        ],
        out_specs=[part, part, part, pl.BlockSpec((1, 2, 3 * BLOCK), lambda p, r: (p, 0, 0))],
        scratch_shapes=[
            pltpu.VMEM((2 * BLOCK, 3 * BLOCK), jnp.float32),
            pltpu.VMEM((length, 2 * KV), jnp.float32),
            pltpu.VMEM((length, 2 * KV), jnp.float32),
        ],
        compiler_params=pltpu.CompilerParams(vmem_limit_bytes=48 * 2**20),
        name="attend_back",
    )(query, key, value, grad, shares)


def gelu_parts(before):
    slope = 0.7978845608028654
    square = before * before
    bend = jnp.tanh(slope * (before + 0.044715 * before * square))
    half = 0.5 * (1.0 + bend)
    rise = half + 0.5 * before * (1.0 - bend * bend) * slope * (1.0 + 3 * 0.044715 * square)
    return before * half, rise


def slots_of(stacked, count):
    rows, columns = stacked.shape
    own = lax.broadcasted_iota(jnp.int32, (rows, columns), 0) // count
    head = lax.broadcasted_iota(jnp.int32, (rows, columns), 1) // KV
    return jnp.where(own == head, stacked, 0.0)


def decoder_kernel(rows, slots, *refs):
    (
        segment_ref, start_ref, cotangent_ref, gain_ref, keys_ref, values_ref,
        self_value_hbm, self_output_hbm, cross_query_hbm, cross_output_hbm,
        inner_hbm, outer_hbm,
        decoded_ref, start_grad_ref, gain_grad_ref,
        normed_fin_ref, active_ref, normed_start_ref, own_ref, normed_mid_ref, context_ref,
        before_grad_ref, last_branch_ref, grad_own_ref, self_branch_ref, grad_asking_ref,
        cross_branch_ref, grad_keys_ref, grad_values_ref,
        self_value, self_output, cross_query, cross_output, inner, outer, sems,
    ) = refs
    loads = []
    for at, (source, target) in enumerate((
        (self_value_hbm, self_value), (self_output_hbm, self_output),
        (cross_query_hbm, cross_query), (cross_output_hbm, cross_output),
        (inner_hbm, inner), (outer_hbm, outer),
    )):
        loads.append(pltpu.make_async_copy(source, target, sems.at[at]))
        loads[-1].start()
    narrow = jnp.bfloat16
    length = keys_ref.shape[0] // rows
    start_gain, middle_gain, final_gain = gain_ref[0:1], gain_ref[1:2], gain_ref[2:3]

    start_field = start_ref[...].astype(jnp.float32)
    scale_start = root_scale(start_field)
    normed_start = (start_field * scale_start * start_gain).astype(narrow)
    normed_start_ref[...] = normed_start
    loads[0].wait()
    own = product(normed_start, self_value[...]).astype(narrow)
    own_ref[...] = own
    loads[1].wait()
    first_field = start_field + product(own, self_output[...])
    scale_mid = root_scale(first_field)
    normed_mid = (first_field * scale_mid * middle_gain).astype(narrow)
    normed_mid_ref[...] = normed_mid
    loads[2].wait()
    asking = product(normed_mid, cross_query[...]).astype(narrow).astype(jnp.float32)
    wides, all_shares, contexts = [], [], []
    for row in range(rows):
        part = asking[row * slots : (row + 1) * slots]
        wide = slots_of(jnp.concatenate([part] * HEADS, axis=0), slots).astype(narrow)
        span = slice(row * length, (row + 1) * length)
        scores = product_right(wide, keys_ref[span])
        slot = lax.rem(lax.broadcasted_iota(jnp.int32, scores.shape, 0), slots)
        scores = jnp.where(slot == segment_ref[row : row + 1], scores, negative_fill)
        powers = jnp.exp(scores - jnp.max(scores, axis=1, keepdims=True))
        shares = powers * (1.0 / jnp.sum(powers, axis=1, keepdims=True))
        mixed = slots_of(product(shares.astype(narrow), values_ref[span]), slots)
        contexts.append(jnp.sum(mixed.reshape(HEADS, slots, -1), axis=0))
        wides.append(wide)
        all_shares.append(shares)
    context = jnp.concatenate(contexts, axis=0).astype(narrow)
    context_ref[...] = context
    loads[3].wait()
    second_field = first_field + product(context, cross_output[...])
    scale_fin = root_scale(second_field)
    normed_fin = (second_field * scale_fin * final_gain).astype(narrow)
    normed_fin_ref[...] = normed_fin
    loads[4].wait()
    active, rise = gelu_parts(product(normed_fin, inner[...]))
    active = active.astype(narrow)
    active_ref[...] = active
    loads[5].wait()
    decoded_ref[...] = (second_field + product(active, outer[...])).astype(narrow)

    branch = cotangent_ref[...]
    last_branch_ref[...] = branch
    grad_second = branch.astype(jnp.float32)
    before_grad = (product_right(branch, outer[...]) * rise).astype(narrow)
    before_grad_ref[...] = before_grad
    grad_normed = product_right(before_grad, inner[...])
    moved, final_gain_grad = norm_back(grad_normed, second_field, scale_fin, final_gain)
    grad_second = grad_second + moved
    branch = grad_second.astype(narrow)
    cross_branch_ref[...] = branch
    grad_context = product_right(branch, cross_output[...]).astype(narrow).astype(jnp.float32)
    askings = []
    for row in range(rows):
        part = grad_context[row * slots : (row + 1) * slots]
        wide = slots_of(jnp.concatenate([part] * HEADS, axis=0), slots).astype(narrow)
        span = slice(row * length, (row + 1) * length)
        shares = all_shares[row]
        moved = shares * product_right(wide, values_ref[span])
        grad_scores = moved - shares * jnp.sum(moved, axis=1, keepdims=True)
        grad_scores = grad_scores.astype(narrow)
        grad_values_ref[span] = product_left(shares.astype(narrow), wide).astype(narrow)
        grad_keys_ref[span] = product_left(grad_scores, wides[row]).astype(narrow)
        mixed = slots_of(product(grad_scores, keys_ref[span]), slots)
        askings.append(jnp.sum(mixed.reshape(HEADS, slots, -1), axis=0))
    grad_asking = jnp.concatenate(askings, axis=0).astype(narrow)
    grad_asking_ref[...] = grad_asking
    grad_normed = product_right(grad_asking, cross_query[...])
    moved, middle_gain_grad = norm_back(grad_normed, first_field, scale_mid, middle_gain)
    grad_first = grad_second + moved
    branch = grad_first.astype(narrow)
    self_branch_ref[...] = branch
    grad_own = product_right(branch, self_output[...]).astype(narrow)
    grad_own_ref[...] = grad_own
    grad_normed = product_right(grad_own, self_value[...])
    moved, start_gain_grad = norm_back(grad_normed, start_field, scale_start, start_gain)
    start_grad_ref[...] = grad_first + moved
    gain_grad_ref[...] = jnp.concatenate(
        [start_gain_grad[None], middle_gain_grad[None], final_gain_grad[None]], axis=0
    )


def decode(segment_index, start, cotangent, gains, keys, values, weights):
    rows, tokens, width = segment_index.shape[0], start.shape[0], start.shape[1]
    narrow, hidden = jnp.bfloat16, weights[4].shape[1]
    few = jax.ShapeDtypeStruct((tokens, width), narrow)
    many = jax.ShapeDtypeStruct((tokens, hidden), narrow)
    outs = [
        few,
        jax.ShapeDtypeStruct((tokens, width), jnp.float32),
        jax.ShapeDtypeStruct((3, width), jnp.float32),
        few, many, few, few, few, few,
        many, few, few, few, few, few,
        jax.ShapeDtypeStruct(keys.shape, narrow),
        jax.ShapeDtypeStruct(values.shape, narrow),
    ]
    local = pl.BlockSpec(memory_space=pltpu.VMEM)
    return pl.pallas_call(
        functools.partial(decoder_kernel, rows, tokens // rows),
        out_shape=outs,
        in_specs=[local] * 6 + [pl.BlockSpec(memory_space=pl.ANY)] * 6,
        out_specs=[local] * len(outs),
        scratch_shapes=[pltpu.VMEM(w.shape, narrow) for w in weights]
        + [pltpu.SemaphoreType.DMA((6,))],
        compiler_params=pltpu.CompilerParams(vmem_limit_bytes=48 * 2**20),
        name="decode",
    )(segment_index, start, cotangent, gains, keys, values, *weights)


TILE = 256


def rows_of(at, size=TILE):
    return pl.ds(pl.multiple_of(at * size, size), size)


class Gather:
    def __init__(self, spot, kinds, shards, fulls, sems):
        self.spot, self.kinds, self.shards, self.fulls = spot, kinds, shards, fulls
        (
            self.ring_out, self.ring_in, self.near_out, self.near_in,
            self.far_out, self.far_in, self.last_out, self.last_in, self.own_sem,
        ) = sems
        self.split = [i for i in range(len(kinds)) if kinds[i] in ("wide", "tall")]

    def piece(self, i, step, plane):
        count = self.spot.count
        slot = ring_index(self.spot.place + (step if i % 2 else count - step), count)
        rows = self.shards[i].shape[0]
        block = self.fulls[i].at[pl.ds(pl.multiple_of(slot * rows, 16), rows)]
        return cut(self.kinds[i], block, plane, self.spot.core)

    def own_copy(self, i):
        rows = self.shards[i].shape[0]
        block = self.fulls[i].at[pl.ds(pl.multiple_of(self.spot.fsdp * rows, 16), rows)]
        return pltpu.make_async_copy(self.shards[i], block, self.own_sem.at[i])

    def ring_copy(self, i, step, source=None):
        here = self.piece(i, step, self.spot.plane)
        return send(
            here if source is None else source, here,
            self.ring_out.at[i, step], self.ring_in.at[i, step],
            self.spot.before if i % 2 else self.spot.after,
        )

    def near_copy(self, i, step):
        here = self.piece(i, step, self.spot.plane)
        return send(
            here, here, self.near_out.at[i, step], self.near_in.at[i, step], self.spot.sibling
        )

    def far_copy(self, i, step):
        here, at = self.piece(i, step, self.spot.plane), self.split.index(i)
        return send(
            here, here, self.far_out.at[at, step], self.far_in.at[at, step], self.spot.opposite
        )

    def last_copy(self, i, step):
        here, at = self.piece(i, step, 1 - self.spot.plane), self.split.index(i)
        return send(
            here, here, self.last_out.at[at, step], self.last_in.at[at, step], self.spot.sibling
        )

    def start(self, group):
        for i in group:
            source = cut(self.kinds[i], self.shards[i], self.spot.plane, self.spot.core)
            self.ring_copy(i, 0, source).start()

    def advance(self, group, step):
        count = self.spot.count

        @pl.when(step < count)
        def _():
            for i in group:
                self.ring_copy(i, step - 1).wait_recv()

                @pl.when(step < count - 1)
                def _():
                    self.ring_copy(i, step).start()

                if self.kinds[i] != "small":
                    self.near_copy(i, step).start()
                if i in self.split:
                    self.far_copy(i, step).start()

        @pl.when(step > 1)
        def _():
            for i in group:
                if i in self.split:
                    self.far_copy(i, step - 1).wait_recv()
                    self.last_copy(i, step - 1).start()

    def arrive(self, group):
        def one(step, carry):
            for i in group:
                if self.kinds[i] != "small":
                    self.near_copy(i, step).wait_recv()
                if i in self.split:
                    self.last_copy(i, step).wait_recv()
            return carry

        lax.fori_loop(1, self.spot.count, one, 0)
        for i in group:
            self.own_copy(i).wait()

    def settle(self, group):
        def one(step, carry):
            for i in group:
                self.ring_copy(i, step - 1).wait_send()
                if self.kinds[i] != "small":
                    self.near_copy(i, step).wait_send()
                if i in self.split:
                    self.far_copy(i, step).wait_send()
                    self.last_copy(i, step).wait_send()
            return carry

        lax.fori_loop(1, self.spot.count, one, 0)


FIRST, SECOND, THIRD = (0, 1, 2, 3, 14), (4, 5, 6, 7), (8, 9, 10, 11, 12, 13)


def forward_kernel(count, rows, *refs):
    refs = list(refs)

    def take(size):
        got = refs[:size]
        del refs[:size]
        return got

    shards = take(15)
    tokens, column, segment, base = take(4)
    weight_outs = take(14)
    (gain_out,) = take(1)
    (
        query_out, key_out, value_out, share_out, context_out, hidden_out, normed_two_out,
        active_out, rise_out, memory_out, cross_key_out, cross_value_out, normed_one_out,
    ) = take(13)
    held = take(8)
    gain_all, normed_one, query, key, value, context = take(6)
    hidden, normed_two, active, rise, memory, cross_keys, cross_values, shares = take(8)
    gather_sems = take(9)
    save_sem, share_sem = take(2)
    spot = Spot(count)
    fulls = held + weight_outs[8:] + [gain_all]
    gather = Gather(spot, KINDS, shards, fulls, gather_sems)
    tiles = tokens.shape[0] // TILE
    length = tokens.shape[0] // rows
    blocks, pairs = length // BLOCK, HEADS // 2
    narrow = jnp.bfloat16
    saves = []

    def save(source, target):
        copy = pltpu.make_async_copy(source, target, save_sem.at[len(saves)])
        copy.start()
        saves.append(copy)

    def each_tile(body):
        def one(at, carry):
            body(rows_of(at), at)
            return carry

        lax.fori_loop(0, tiles, one, 0)

    def run(group, first, last):
        def one(step, carry):
            gather.advance(group, step)
            return carry

        lax.fori_loop(first, last, one, 0)

    for i in FIRST:
        gather.own_copy(i).start()
    spot.greet()
    gather.start(FIRST)
    for i in SECOND + THIRD:
        gather.own_copy(i).start()
    run(FIRST, 1, count - 1)
    gather.start(SECOND)
    run(FIRST, count - 1, count + 1)
    gather.arrive(FIRST)
    gain = jnp.zeros((16, gain_all.shape[1]), jnp.float32)
    for slot in range(count):
        gain = gain + gain_all[slot * 16 : (slot + 1) * 16].astype(jnp.float32)
    gain_out[...] = gain
    query_weight, key_weight, value_weight, output_weight = held[:4]
    inner_weight, outer_weight, cross_key_weight, cross_value_weight = held[4:]

    def first_norm(span, at):
        field = tokens[span].astype(jnp.float32)
        normed_one[span] = (field * root_scale(field) * gain_out[0:1]).astype(narrow)

    each_tile(first_norm)

    def project(target, weight):
        def body(span, at):
            target[span] = product(normed_one[span], weight[...]).astype(narrow)

        each_tile(body)

    project(query, query_weight)
    gather.advance(SECOND, 1)
    project(key, key_weight)
    project(value, value_weight)
    gather.advance(SECOND, 2)
    for source, target in (
        (normed_one, normed_one_out), (query, query_out), (key, key_out), (value, value_out),
    ):
        save(source, target)
    for i in range(4):
        save(held[i], weight_outs[i])

    def share_copy(at):
        return pltpu.make_async_copy(
            shares.at[lax.rem(at, 2)],
            share_out.at[at // pairs, lax.rem(at, pairs)],
            share_sem.at[lax.rem(at, 2)],
        )

    def attend_pair(at, carry):
        row, pair, buffer = at // pairs, lax.rem(at, pairs), lax.rem(at, 2)

        @pl.when(lax.rem(at, 3) == 0)
        def _():
            gather.advance(SECOND, 3 + at // 3)

        @pl.when(at >= 2)
        def _():
            share_copy(at - 2).wait()

        bias = bias_block(base[pair])
        columns = rows_of(pair, 2 * KV)

        def span(begin, size):
            return pl.ds(pl.multiple_of(row * length + begin, BLOCK), size)

        for block in range(blocks):
            keys, places = reach(block, blocks)
            own = span(block * BLOCK, BLOCK)
            near = span(keys.start, keys.stop - keys.start)
            scores = product_right(wide_heads(query[own, columns]), key[near, columns])
            scores = scores + bias[:, places]
            allowed = column[own, :1] == segment[row, :, keys]
            scores = jnp.where(jnp.concatenate([allowed, allowed], axis=0), scores, negative_fill)
            powers = jnp.exp(scores - jnp.max(scores, axis=1, keepdims=True))
            part = powers * (1.0 / jnp.sum(powers, axis=1, keepdims=True))
            part = part.astype(narrow)
            shares[buffer, block, :, places] = part
            mixed = product(part, value[near, columns])
            context[own, columns] = narrow_heads(mixed).astype(narrow)
        share_copy(at).start()
        return carry

    lax.fori_loop(0, rows * pairs, attend_pair, 0)
    save(context, context_out)
    gather.advance(SECOND, 7)
    gather.start(THIRD)
    gather.advance(SECOND, 8)

    def second_norm(span, at):
        field = tokens[span].astype(jnp.float32) + product(context[span], output_weight[...])
        hidden[span] = field
        normed_two[span] = (field * root_scale(field) * gain_out[1:2]).astype(narrow)

    each_tile(second_norm)
    save(hidden, hidden_out)
    save(normed_two, normed_two_out)
    gather.arrive(SECOND)
    for i in range(4, 8):
        save(held[i], weight_outs[i])
    chunk = tokens.shape[1]

    def feed(span, at):
        gather.advance(THIRD, at + 1)
        for begin in range(0, active.shape[1], chunk):
            part = slice(begin, begin + chunk)
            level, slope = gelu_parts(product(normed_two[span], inner_weight[:, part]))
            active[span, part] = level.astype(narrow)
            rise[span, part] = slope.astype(narrow)
        full = hidden[span] + product(active[span], outer_weight[...])
        memory[span] = full.astype(narrow)

    each_tile(feed)
    save(active, active_out)
    save(rise, rise_out)
    save(memory, memory_out)
    gather.advance(THIRD, tiles + 1)

    def cross(span, at):
        cross_keys[span] = product(memory[span], cross_key_weight[...]).astype(narrow)
        cross_values[span] = product(memory[span], cross_value_weight[...]).astype(narrow)

    each_tile(cross)
    save(cross_keys, cross_key_out)
    save(cross_values, cross_value_out)
    run(THIRD, tiles + 2, count + 1)
    gather.arrive(THIRD)
    for group in (FIRST, SECOND, THIRD):
        gather.settle(group)
    for copy in saves:
        copy.wait()
    for at in range(rows * pairs - 2, rows * pairs):
        share_copy(at).wait()


def forward(count, shards, tokens, column, segment_index, base):
    rows, length = segment_index.shape
    many, width = tokens.shape
    hidden_width = shards[4].shape[1]
    narrow, wide = jnp.bfloat16, jnp.float32
    pairs, total = HEADS // 2, len(shards)
    split = sum(kind in ("wide", "tall") for kind in KINDS)
    weights = [(count * s.shape[0], s.shape[1]) for s in shards]
    few, much = (many, width), (many, hidden_width)
    share_shape = (rows, pairs, length // BLOCK, 2 * BLOCK, 3 * BLOCK)
    shapes = [(w, narrow) for w in weights[:14]] + [((16, width), wide)]
    shapes += [
        (few, narrow), (few, narrow), (few, narrow), (share_shape, narrow), (few, narrow),
        (few, wide), (few, narrow), (much, narrow), (much, narrow), (few, narrow), (few, narrow),
        (few, narrow), (few, narrow),
    ]
    dma = pltpu.SemaphoreType.DMA
    scratch = [pltpu.VMEM(w, narrow) for w in weights[:8]] + [pltpu.VMEM(weights[14], narrow)]
    scratch += [pltpu.VMEM(few, narrow)] * 5
    scratch += [
        pltpu.VMEM(few, wide), pltpu.VMEM(few, narrow), pltpu.VMEM(much, narrow),
        pltpu.VMEM(much, narrow), pltpu.VMEM(few, narrow), pltpu.VMEM(few, narrow),
        pltpu.VMEM(few, narrow), pltpu.VMEM((2,) + share_shape[2:], narrow),
    ]
    scratch += [dma((total, count))] * 4 + [dma((split, count))] * 4
    scratch += [dma((total,)), dma((24,)), dma((2,))]
    anywhere = pl.BlockSpec(memory_space=pl.ANY)
    local = pl.BlockSpec(memory_space=pltpu.VMEM)
    got = pl.pallas_call(
        functools.partial(forward_kernel, count, rows),
        out_shape=[jax.ShapeDtypeStruct(s, d) for s, d in shapes],
        in_specs=[anywhere] * total + [local] * 4,
        out_specs=[anywhere] * 14 + [local] + [anywhere] * 13,
        scratch_shapes=scratch,
        compiler_params=pltpu.CompilerParams(
            collective_id=2, has_side_effects=True, vmem_limit_bytes=62 * 2**20
        ),
        name="forward",
    )(*shards, tokens, column, segment_index.reshape(rows, 1, length), base)
    return got[:14], got[14], got[15:]


def forward_apart(count, shards, tokens, column, segment_index, base):
    rows, length = segment_index.shape
    narrow = jnp.bfloat16
    whole = gather_weights(count, shards, KINDS)
    gains = jnp.sum(whole[14].astype(jnp.float32), axis=0)
    whole = [part.reshape(-1, part.shape[2]) for part in whole[:14]]
    field = tokens.astype(jnp.float32)
    normed_one = (field * root_scale(field) * gains[0]).astype(narrow)
    query, key, value = [product(normed_one, weight).astype(narrow) for weight in whole[:3]]
    context, shares = attend_rows(
        rows, length, column, segment_index, base, query, key, value
    )
    hidden = field + product(context, whole[3])
    normed_two = (hidden * root_scale(hidden) * gains[1]).astype(narrow)
    active, rise = gelu_parts(product(normed_two, whole[4]))
    active = active.astype(narrow)
    memory = (hidden + product(active, whole[5])).astype(narrow)
    cross_keys, cross_values = [product(memory, weight).astype(narrow) for weight in whole[6:8]]
    return whole, gains, (
        query, key, value, shares, context, hidden, normed_two,
        active, rise, memory, cross_keys, cross_values, normed_one,
    )


def on_device(
    tokens,
    segment_index,
    start_vectors,
    first_gain,
    query_weight,
    key_weight,
    value_weight,
    output_weight,
    position_table,
    second_gain,
    inner_weight,
    outer_weight,
    start_gain,
    self_value,
    self_output,
    middle_gain,
    cross_query,
    cross_key,
    cross_value,
    cross_output,
    final_gain,
    decoder_inner,
    decoder_outer,
    encoded_cotangent,
    decoded_cotangent,
):
    row_count = segment_index.shape[0]
    length = segment_index.shape[1]
    slot_count = start_vectors.shape[1]
    width = tokens.shape[1]
    count = lax.axis_size("fsdp")
    depth = first_gain.shape[0]
    choices = jnp.arange(position_table.shape[0], dtype=jnp.int32)
    onehot = (offset_buckets()[None, :] == choices[:, None]).astype(jnp.float32)
    base = jnp.dot(position_table.T, onehot, precision=lax.Precision.HIGHEST)
    base = base.reshape(HEADS // 2, 2, 3 * BLOCK)
    column = jnp.broadcast_to(segment_index.reshape(-1, 1), (row_count * length, BLOCK))
    gains = jnp.stack([first_gain, second_gain, start_gain, middle_gain, final_gain])
    place = jnp.arange(width, dtype=jnp.int32) // depth
    gains = jnp.where(place == lax.axis_index("fsdp"), jnp.tile(gains, (1, count)), 0)
    shards = (
        query_weight, key_weight, value_weight, output_weight, inner_weight, outer_weight,
        cross_key, cross_value, self_value, self_output, cross_query, cross_output,
        decoder_inner, decoder_outer, jnp.pad(gains, ((0, 11), (0, 0))),
    )
    fused = count == 8 and depth % 32 == 0 and (row_count, length) == (2, 512)
    plan = forward if fused else forward_apart
    whole, all_gains, kept = plan(count, shards, tokens, column, segment_index, base)
    (
        query_full, key_full, value_full, output_full, inner_full, outer_full, cross_key_full,
        cross_value_full, self_value_full, self_output_full, cross_query_full, cross_output_full,
        decoder_inner_full, decoder_outer_full,
    ) = whole
    (
        query_all, key_all, value_all, shares, context, hidden, normed_two,
        active, rise, memory, cross_keys, cross_values, normed_one,
    ) = kept
    gain_one, gain_two = all_gains[0], all_gains[1]
    field = tokens.astype(jnp.float32)
    scale_one, scale_two = root_scale(field), root_scale(hidden)
    token_count = row_count * slot_count
    (
        decoded, start_grad, decoder_gain_grads,
        normed_fin, decoder_active, normed_start, own_value, normed_mid, cross_context,
        decoder_before_grad, last_branch, grad_own, self_branch, grad_asking, cross_branch,
        grad_cross_keys, grad_cross_values,
    ) = decode(
        segment_index,
        start_vectors.reshape(token_count, width),
        decoded_cotangent.reshape(token_count, width),
        all_gains[2:5],
        cross_keys,
        cross_values,
        (
            self_value_full, self_output_full, cross_query_full, cross_output_full,
            decoder_inner_full, decoder_outer_full,
        ),
    )
    grad_cross_key = product_left(memory, grad_cross_keys)
    grad_cross_value = product_left(memory, grad_cross_values)
    grad_memory = product_right(grad_cross_keys, cross_key_full) + product_right(
        grad_cross_values, cross_value_full
    )
    grad_encoded = encoded_cotangent.astype(jnp.float32) + grad_memory
    grad_branch = grad_encoded.astype(jnp.bfloat16)
    grad_outer = product_left(active, grad_branch)
    grad_active = product_right(grad_branch, outer_full)
    grad_before = (grad_active * rise).astype(jnp.bfloat16)
    grad_inner = product_left(normed_two, grad_before)
    grad_normed = product_right(grad_before, inner_full)
    field_part, grad_gain_two = norm_back(
        grad_normed, hidden, scale_two, gain_two
    )
    grad_hidden = grad_encoded + field_part
    grad_branch = grad_hidden.astype(jnp.bfloat16)
    grad_output = product_left(context, grad_branch)
    grad_context = product_right(grad_branch, output_full).astype(jnp.bfloat16)
    grad_query_all, grad_key_all, grad_value_all, bias_sums = attend_rows_back(
        row_count, length, query_all, key_all, value_all, grad_context, shares
    )
    grad_query = product_left(normed_one, grad_query_all)
    grad_key = product_left(normed_one, grad_key_all)
    grad_value = product_left(normed_one, grad_value_all)
    grad_normed = (
        product_right(grad_query_all, query_full)
        + product_right(grad_key_all, key_full)
        + product_right(grad_value_all, value_full)
    )
    field_part, grad_gain_one = norm_back(
        grad_normed, field, scale_one, gain_one
    )
    tokens_grad = grad_hidden + field_part
    table_grad = lax.dot_general(
        onehot,
        bias_sums.reshape(HEADS, 3 * BLOCK),
        (((1,), (1,)), ((), ())),
        precision=lax.Precision.HIGHEST,
    )
    lefts = (normed_fin, decoder_active, normed_start, own_value, normed_mid, cross_context)
    rights = (decoder_before_grad, last_branch, grad_own, self_branch, grad_asking, cross_branch)
    pair_shapes = [(left.shape[1] // count, right.shape[1]) for left, right in zip(lefts, rights)]
    left_cols = []
    for left, (rows, unused) in zip(lefts, pair_shapes):
        columns = left.reshape(token_count, count, rows).transpose(1, 0, 2)
        left_cols.append(jnp.pad(columns, ((0, 0), (0, 0), (0, -rows % 128))))
    small = jnp.concatenate([
        jnp.stack([grad_gain_one, grad_gain_two]),
        decoder_gain_grads,
        jnp.pad(table_grad.reshape(1, -1), ((0, 2), (0, width - table_grad.size))),
    ])
    encoder_grads = (
        grad_inner, grad_outer, grad_query, grad_key, grad_value, grad_output,
        grad_cross_key, grad_cross_value,
    )
    encoder_sums, decoder_sums, small_sum = reduce_grads(
        count,
        ENCODER_KINDS,
        [
            g.astype(jnp.bfloat16).reshape(count, g.shape[0] // count, g.shape[1])
            for g in encoder_grads
        ],
        jnp.concatenate(left_cols, axis=2),
        jnp.concatenate(rights, axis=1),
        pair_shapes,
        small,
    )
    (
        inner_weight_grad, outer_weight_grad, query_weight_grad, key_weight_grad,
        value_weight_grad, output_weight_grad, cross_key_grad, cross_value_grad,
    ) = [part.astype(jnp.float32) for part in encoder_sums]
    (
        decoder_inner_grad, decoder_outer_grad, self_value_grad, self_output_grad,
        cross_query_grad, cross_output_grad,
    ) = [part.astype(jnp.float32) for part in decoder_sums]
    own_gains = lax.dynamic_slice_in_dim(
        small_sum[:5], lax.axis_index("fsdp") * depth, depth, axis=1
    )
    first_gain_grad, second_gain_grad, start_gain_grad, middle_gain_grad, final_gain_grad = own_gains
    position_table_grad = small_sum[5, : table_grad.size].reshape(table_grad.shape)
    decoded = decoded.reshape(start_vectors.shape)
    start_grad = start_grad.reshape(start_vectors.shape)
    return (
        memory,
        decoded,
        tokens_grad,
        start_grad,
        first_gain_grad,
        query_weight_grad,
        key_weight_grad,
        value_weight_grad,
        output_weight_grad,
        position_table_grad,
        second_gain_grad,
        inner_weight_grad,
        outer_weight_grad,
        start_gain_grad,
        self_value_grad,
        self_output_grad,
        middle_gain_grad,
        cross_query_grad,
        cross_key_grad,
        cross_value_grad,
        cross_output_grad,
        final_gain_grad,
        decoder_inner_grad,
        decoder_outer_grad,
    )


def solution(mesh):
    placed = (
        P(("dp", "fsdp"), None),
        P(("dp", "fsdp"), None),
        P(("dp", "fsdp"), None, None),
        P("fsdp"),
        P("fsdp", None),
        P("fsdp", None),
        P("fsdp", None),
        P("fsdp", None),
        P(),
        P("fsdp"),
        P("fsdp", None),
        P("fsdp", None),
        P("fsdp"),
        P("fsdp", None),
        P("fsdp", None),
        P("fsdp"),
        P("fsdp", None),
        P("fsdp", None),
        P("fsdp", None),
        P("fsdp", None),
        P("fsdp"),
        P("fsdp", None),
        P("fsdp", None),
        P(("dp", "fsdp"), None),
        P(("dp", "fsdp"), None, None),
    )
    return jax.shard_map(
        on_device,
        mesh=mesh,
        in_specs=placed,
        out_specs=(
            P(("dp", "fsdp"), None),
            P(("dp", "fsdp"), None, None),
            P(("dp", "fsdp"), None),
            P(("dp", "fsdp"), None, None),
            P("fsdp"),
            P("fsdp", None),
            P("fsdp", None),
            P("fsdp", None),
            P("fsdp", None),
            P(),
            P("fsdp"),
            P("fsdp", None),
            P("fsdp", None),
            P("fsdp"),
            P("fsdp", None),
            P("fsdp", None),
            P("fsdp"),
            P("fsdp", None),
            P("fsdp", None),
            P("fsdp", None),
            P("fsdp", None),
            P("fsdp"),
            P("fsdp", None),
            P("fsdp", None),
        ),
        check_vma=False,
    )
```

```python
import functools

import jax
import jax.numpy as jnp
from jax import lax
from jax.experimental import pallas as pl
from jax.experimental.pallas import tpu as pltpu
from jax.sharding import PartitionSpec as P

HEADS = 12
KV = 64
BLOCK = 128


epsilon = 1e-06
negative_fill = -1e30
bucket_edges = (12, 16, 23, 32, 46, 64, 91)


MESH = pl.DeviceIdType.MESH
KINDS = (
    "square", "square", "square", "square", "wide", "tall", "square", "square",
    "square", "square", "square", "square", "wide", "tall", "small",
)


def ring_position(index, count):
    if count == 64:
        slow, rest = index // 32, index % 32
        row, column = rest // 8, rest % 8
        place = row * 8 + column + (row % 2) * (7 - 2 * column)
        return place + slow * (count - 1 - 2 * place)
    across, along = index % 2, index // 2
    return along + across * (count - 1 - 2 * along)


def ring_index(position, count):
    position = lax.rem(position, count)
    across = position // (count // 2)
    along = position + across * (count - 1 - 2 * position)
    if count == 64:
        row, column = along // 8, along % 8
        return across * 32 + row * 8 + column + (row % 2) * (7 - 2 * column)
    return 2 * along + across


class Spot:
    def __init__(self, count):
        self.count = count
        self.dp = lax.axis_index("dp")
        self.fsdp = lax.axis_index("fsdp")
        self.core = lax.rem(self.dp, 2)
        self.plane = self.dp // 2
        self.place = ring_position(self.fsdp, count)
        self.sibling = (self.dp + 1 - 2 * self.core, self.fsdp)
        self.opposite = (lax.rem(self.dp + 2, 4), self.fsdp)
        self.after = (self.dp, ring_index(self.place + 1, count))
        self.before = (self.dp, ring_index(self.place + count - 1, count))

    def greet(self, others=()):
        barrier = pltpu.get_barrier_semaphore()
        partners = (self.sibling, self.opposite, self.after, self.before) + tuple(others)
        for partner in partners:
            pl.semaphore_signal(barrier, inc=1, device_id=partner, device_id_type=MESH)
        pl.semaphore_wait(barrier, len(partners))


def cut(kind, ref, plane, core):
    rows, columns = ref.shape
    if kind == "small":
        return ref
    if kind == "square":
        half = columns // 2
        return ref.at[:, pl.ds(pl.multiple_of(core * half, 128), half)]
    if kind == "wide":
        quarter = columns // 4
        return ref.at[:, pl.ds(pl.multiple_of((core * 2 + plane) * quarter, 128), quarter)]
    half, upper = columns // 2, rows // 2
    return ref.at[
        pl.ds(pl.multiple_of(plane * upper, 8), upper),
        pl.ds(pl.multiple_of(core * half, 128), half),
    ]


def send(source, target, send_sem, recv_sem, device):
    return pltpu.make_async_remote_copy(
        src_ref=source,
        dst_ref=target,
        send_sem=send_sem,
        recv_sem=recv_sem,
        device_id=device,
        device_id_type=MESH,
    )


def gather_kernel(count, kinds, *refs):
    total = len(kinds)
    shards, fulls = refs[:total], refs[total : 2 * total]
    ring_out, ring_in, near_out, near_in, far_out, far_in, last_out, last_in, own_sem = refs[
        2 * total :
    ]
    spot = Spot(count)
    split = [i for i in range(total) if kinds[i] in ("wide", "tall")]

    window = min(count, 8)

    def slot_of(i, step):
        turn = step if i % 2 else count - step
        return ring_index(spot.place + turn, count)

    def ring_copy(i, step, source=None):
        here = cut(kinds[i], fulls[i].at[slot_of(i, step)], spot.plane, spot.core)
        return send(
            here if source is None else source,
            here,
            ring_out.at[i, lax.rem(step, window)],
            ring_in.at[i, step],
            spot.before if i % 2 else spot.after,
        )

    def near_copy(i, step):
        here = cut(kinds[i], fulls[i].at[slot_of(i, step)], spot.plane, spot.core)
        out = near_out.at[i, lax.rem(step, window)]
        return send(here, here, out, near_in.at[i, step], spot.sibling)

    def far_copy(i, step):
        here = cut(kinds[i], fulls[i].at[slot_of(i, step)], spot.plane, spot.core)
        at = split.index(i)
        out = far_out.at[at, lax.rem(step, window)]
        return send(here, here, out, far_in.at[at, step], spot.opposite)

    def last_copy(i, step):
        here = cut(kinds[i], fulls[i].at[slot_of(i, step)], 1 - spot.plane, spot.core)
        at = split.index(i)
        out = last_out.at[at, lax.rem(step, window)]
        return send(here, here, out, last_in.at[at, step], spot.sibling)

    def start(copy, i, step, first):
        if window < count:

            @pl.when(step >= first + window)
            def _():
                copy(i, step - window).wait_send()

        copy(i, step).start()

    def finish(copy, i, first, end):
        def one(step, carry):
            copy(i, step).wait_send()
            return carry

        lax.fori_loop(max(first, end - window), end, one, 0)

    owns = []
    for i in range(total):
        owns.append(pltpu.make_async_copy(shards[i], fulls[i].at[spot.fsdp], own_sem.at[i]))
        owns[-1].start()
    spot.greet()
    for i in range(total):
        ring_copy(i, 0, cut(kinds[i], shards[i], spot.plane, spot.core)).start()

    def one_step(step, carry):
        for i in range(total):
            ring_copy(i, step - 1).wait_recv()

            @pl.when(step < count - 1)
            def _():
                start(ring_copy, i, step, 0)

            if kinds[i] != "small":
                start(near_copy, i, step, 1)
            if i in split:
                start(far_copy, i, step, 1)

        @pl.when(step > 1)
        def _():
            for i in split:
                far_copy(i, step - 1).wait_recv()
                start(last_copy, i, step - 1, 1)

        return carry

    lax.fori_loop(1, count, one_step, 0)
    for i in split:
        far_copy(i, count - 1).wait_recv()
        start(last_copy, i, count - 1, 1)

    def settle(step, carry):
        for i in range(total):
            if kinds[i] != "small":
                near_copy(i, step).wait_recv()
            if i in split:
                last_copy(i, step).wait_recv()
        return carry

    lax.fori_loop(1, count, settle, 0)
    for i in range(total):
        finish(ring_copy, i, 0, count - 1)
        if kinds[i] != "small":
            finish(near_copy, i, 1, count)
        if i in split:
            finish(far_copy, i, 1, count)
            finish(last_copy, i, 1, count)
    for copy in owns:
        copy.wait()


def gather_weights(count, shards, kinds):
    total = len(shards)
    split = sum(kind in ("wide", "tall") for kind in kinds)
    window = min(count, 8)
    many, few = [
        [pltpu.SemaphoreType.DMA((rows, window)), pltpu.SemaphoreType.DMA((rows, count))] * 2
        for rows in (total, split)
    ]
    return pl.pallas_call(
        functools.partial(gather_kernel, count, kinds),
        out_shape=[jax.ShapeDtypeStruct((count,) + s.shape, s.dtype) for s in shards],
        in_specs=[pl.BlockSpec(memory_space=pl.ANY)] * total,
        out_specs=[pl.BlockSpec(memory_space=pl.ANY)] * total,
        scratch_shapes=many + few + [pltpu.SemaphoreType.DMA((total,))],
        compiler_params=pltpu.CompilerParams(collective_id=0, has_side_effects=True),
        name="gather_weights",
    )(*shards)

def plus(*terms):
    total = terms[0].astype(jnp.float32)
    for term in terms[1:]:
        total = total + term.astype(jnp.float32)
    return total


def half_of(core, columns):
    half = columns // 2
    return pl.ds(pl.multiple_of(core * half, 128), half)


def plane_part(kind, plane, rows, columns):
    if kind == "wide":
        return slice(None), pl.ds(pl.multiple_of(plane * (columns // 2), 128), columns // 2)
    if kind == "tall":
        return pl.ds(pl.multiple_of(plane * (rows // 2), 8), rows // 2), slice(None)
    return slice(None), slice(None)


ENCODER_KINDS = ("wide", "tall", "square", "square", "square", "square", "square", "square")


def reduce_kernel(count, kinds, spans, *refs):
    total, pairs = len(kinds), len(spans)
    refs = list(refs)

    def take(size):
        got = refs[:size]
        del refs[:size]
        return got

    grads = take(total)
    left_part, right_part, small = take(3)
    sums = take(total)
    pair_sums = take(pairs)
    (small_sum,) = take(1)
    half, work, final = take(total), take(total), take(total)
    split = [i for i in range(total) if kinds[i] != "square"]
    far = take(len(split))
    left_all, right_all = take(2)
    pair_half, pair_far, pair_work = take(pairs), take(pairs), take(pairs)
    small_near, small_mid, small_far, small_all = take(4)
    (
        near_sem, ring_out, ring_in, far_sem, end_sem, left_out, left_in,
        right_out, right_in, pair_sem, small_sem, small_out, small_in,
    ) = take(13)
    spot = Spot(count)
    core, plane = spot.core, spot.plane
    diagonal = (lax.rem(spot.dp + 2, 4) + 1 - 2 * core, spot.fsdp)

    def peer(k):
        return (spot.dp, lax.rem(spot.fsdp + k, count))

    barrier = pltpu.get_barrier_semaphore()
    for partner in (spot.sibling, spot.opposite, diagonal):
        pl.semaphore_signal(barrier, inc=1, device_id=partner, device_id_type=MESH)

    def greet(k, carry):
        pl.semaphore_signal(barrier, inc=1, device_id=peer(k), device_id_type=MESH)
        return carry

    lax.fori_loop(1, count, greet, 0)
    pl.semaphore_wait(barrier, count + 2)

    def near_copy(i):
        columns = grads[i].shape[2]
        return send(
            grads[i].at[:, :, half_of(1 - core, columns)], half[i],
            near_sem.at[0, i], near_sem.at[1, i], spot.sibling,
        )

    def slot_at(i, step):
        turn = step + 1 if i % 2 else count - 1 - step
        return ring_index(spot.place + turn, count)

    def far_copy(i, step):
        at = split.index(i)
        rows, columns = half[i].shape[1:]
        part = plane_part(kinds[i], 1 - plane, rows, columns)
        return send(
            half[i].at[(slot_at(i, step),) + part], far[at].at[step],
            far_sem.at[0, at, step], far_sem.at[1, at, step], spot.opposite,
        )

    def ring_copy(i, step):
        return send(
            work[i].at[step], work[i].at[step + 1], ring_out.at[i, step], ring_in.at[i, step],
            spot.before if i % 2 else spot.after,
        )

    def left_copy(k):
        other = lax.rem(spot.fsdp + k, count)
        return send(
            left_part.at[other], left_all.at[spot.fsdp], left_out.at[k], left_in.at[k], peer(k)
        )

    def right_copy(way, step):
        turn = step if way else count - step
        slot = ring_index(spot.place + turn, count)
        width = right_part.shape[1] // 2
        here = right_all.at[slot, :, way * width : (way + 1) * width]
        return send(
            here, here, right_out.at[way, step], right_in.at[way, step],
            spot.before if way else spot.after,
        )

    for i in range(total):
        near_copy(i).start()
    near_small = send(small, small_near, small_sem.at[0], small_sem.at[1], spot.sibling)
    near_small.start()

    def left_start(k, carry):
        left_copy(k).start()
        return carry

    lax.fori_loop(1, count, left_start, 0)
    right_all[spot.fsdp] = right_part[...]
    left_all[spot.fsdp] = left_part[spot.fsdp]
    for way in range(2):
        right_copy(way, 0).start()
    near_small.wait()
    small_mid[...] = small[...] + small_near[...]
    far_small = send(small_mid, small_far, small_sem.at[2], small_sem.at[3], spot.opposite)
    far_small.start()

    for i in range(total):
        near_copy(i).wait_recv()

        def join(slot, carry):
            mine = grads[i][slot, :, half_of(core, grads[i].shape[2])]
            half[i][slot] = plus(half[i][slot], mine).astype(jnp.bfloat16)
            return carry

        lax.fori_loop(0, count, join, 0)
        if i in split:

            def far_start(step, carry):
                far_copy(i, step).start()
                return carry

            lax.fori_loop(0, count, far_start, 0)

    far_small.wait()
    small_all[spot.fsdp] = small_mid[...] + small_far[...]

    def small_copy(k):
        here = small_all.at[spot.fsdp]
        return send(here, here, small_out.at[k], small_in.at[k], peer(k))

    def small_start(k, carry):
        small_copy(k).start()
        return carry

    lax.fori_loop(1, count, small_start, 0)

    def right_step(step, carry):
        for way in range(2):
            right_copy(way, step - 1).wait_recv()

            @pl.when(step < count - 1)
            def _():
                right_copy(way, step).start()

        return carry

    lax.fori_loop(1, count, right_step, 0)

    def left_wait(k, carry):
        left_copy(k).wait_recv()
        return carry

    lax.fori_loop(1, count, left_wait, 0)

    def pair_near(j):
        columns = pair_sums[j].shape[1]
        return send(
            pair_work[j].at[:, half_of(1 - core, columns)], pair_half[j],
            pair_sem.at[0, j], pair_sem.at[1, j], spot.sibling,
        )

    def pair_across(j):
        return send(
            pair_half[j], pair_far[j], pair_sem.at[2, j], pair_sem.at[3, j], spot.opposite
        )

    def pair_end(j):
        here = pair_sums[j].at[:, half_of(core, pair_sums[j].shape[1])]
        return send(here, here, pair_sem.at[4, j], pair_sem.at[5, j], spot.sibling)

    for j, (left_at, right_at) in enumerate(spans):
        rows, columns = pair_sums[j].shape
        span = -(-rows // 128) * 128
        left = left_all[:, :, left_at : left_at + span].reshape(-1, span)
        for begin in range(0, columns, 768):
            right = right_all[:, :, right_at + begin : right_at + begin + 768].reshape(-1, 768)
            block = lax.dot_general(
                left, right, (((0,), (0,)), ((), ())), preferred_element_type=jnp.float32
            )
            pair_work[j][:, begin : begin + 768] = block[:rows].astype(jnp.bfloat16)
        pair_near(j).start()
    for j in range(pairs):
        pair_near(j).wait()
        mine = pair_work[j][:, half_of(core, pair_sums[j].shape[1])]
        pair_half[j][...] = plus(pair_half[j][...], mine).astype(jnp.bfloat16)
        pair_across(j).start()

    def one_step(step, carry):
        for i in range(total):
            rows, columns = half[i].shape[1:]
            slot = slot_at(i, step)
            value = half[i][(slot,) + plane_part(kinds[i], plane, rows, columns)]
            value = value.astype(jnp.float32)
            if i in split:
                far_copy(i, step).wait_recv()
                value = value + far[split.index(i)][step].astype(jnp.float32)

            @pl.when(step > 0)
            def _():
                ring_copy(i, step - 1).wait_recv()
                work[i][step] = plus(value, work[i][step]).astype(jnp.bfloat16)

            @pl.when(step == 0)
            def _():
                work[i][step] = value.astype(jnp.bfloat16)

            @pl.when(step < count - 1)
            def _():
                ring_copy(i, step).start()

        return carry

    lax.fori_loop(0, count, one_step, 0)

    def end_across(i):
        return send(
            work[i].at[count - 1], final[i], end_sem.at[0, i], end_sem.at[1, i], spot.opposite
        )

    def end_piece(i, mine_plane):
        rows, columns = sums[i].shape
        wide = half_of(core, columns)
        if kinds[i] == "square":
            return sums[i].at[:, wide]
        return cut(kinds[i], sums[i], mine_plane, core)

    def end_copies(i):
        here = end_piece(i, plane)
        copies = [send(here, here, end_sem.at[2, i], end_sem.at[3, i], spot.sibling)]
        if i in split:
            copies.append(send(here, here, end_sem.at[4, i], end_sem.at[5, i], spot.opposite))
            copies.append(send(here, here, end_sem.at[6, i], end_sem.at[7, i], diagonal))
        return copies

    for i in range(total):
        if i not in split:
            end_across(i).start()
    for i in split:
        end_piece(i, plane)[...] = work[i][count - 1]
        for copy in end_copies(i):
            copy.start()
    for j in range(pairs):
        pair_across(j).wait()
        here = half_of(core, pair_sums[j].shape[1])
        pair_sums[j][:, here] = plus(pair_half[j][...], pair_far[j][...]).astype(jnp.bfloat16)
        pair_end(j).start()
    for i in range(total):
        if i not in split:
            end_across(i).wait()
            value = plus(work[i][count - 1], final[i][...]).astype(jnp.bfloat16)
            end_piece(i, plane)[...] = value
            for copy in end_copies(i):
                copy.start()

    def small_wait(k, carry):
        small_copy(k).wait_recv()
        return carry

    lax.fori_loop(1, count, small_wait, 0)
    small_sum[...] = lax.fori_loop(
        1, count, lambda k, so_far: so_far + small_all[k], small_all[0]
    )
    for i in range(total):
        for copy in end_copies(i):
            copy.wait()
    for j in range(pairs):
        pair_end(j).wait()
    for i in range(total):
        near_copy(i).wait_send()

    def drain(step, carry):
        for i in split:
            far_copy(i, step).wait_send()
        return carry

    lax.fori_loop(0, count, drain, 0)

    def drain_ring(step, carry):
        for i in range(total):
            ring_copy(i, step).wait_send()
        for way in range(2):
            right_copy(way, step).wait_send()
        left_copy(step + 1).wait_send()
        small_copy(step + 1).wait_send()
        return carry

    lax.fori_loop(0, count - 1, drain_ring, 0)


def reduce_grads(count, kinds, grads, left_part, right_part, pair_shapes, small):
    total, pairs = len(kinds), len(pair_shapes)
    spans, left_at, right_at = [], 0, 0
    for rows, columns in pair_shapes:
        spans.append((left_at, right_at))
        left_at, right_at = left_at + -(-rows // 128) * 128, right_at + columns
    narrow = jnp.bfloat16
    blocks = [g.shape[1:] for g in grads]
    pieces = []
    for kind, (rows, columns) in zip(kinds, blocks):
        if kind == "wide":
            pieces.append((rows, columns // 4))
        elif kind == "tall":
            pieces.append((rows // 2, columns // 2))
        else:
            pieces.append((rows, columns // 2))
    split = [i for i in range(total) if kinds[i] != "square"]
    dma = pltpu.SemaphoreType.DMA
    scratch = [pltpu.VMEM((count, r, c // 2), narrow) for r, c in blocks]
    scratch += [pltpu.VMEM((count, r, c), narrow) for r, c in pieces]
    scratch += [pltpu.VMEM((r, c), narrow) for r, c in pieces]
    scratch += [pltpu.VMEM((count,) + pieces[i], narrow) for i in split]
    scratch += [
        pltpu.VMEM(left_part.shape, narrow),
        pltpu.VMEM((count,) + right_part.shape, narrow),
    ]
    scratch += [pltpu.VMEM((r, c // 2), narrow) for r, c in pair_shapes] * 2
    scratch += [pltpu.VMEM((r, c), narrow) for r, c in pair_shapes]
    scratch += [pltpu.VMEM(small.shape, jnp.float32)] * 3
    scratch += [pltpu.VMEM((count,) + small.shape, jnp.float32)]
    scratch += [
        dma((2, total)), dma((total, count)), dma((total, count)), dma((2, len(split), count)),
        dma((8, total)), dma((count,)), dma((count,)), dma((2, count)), dma((2, count)),
        dma((6, pairs)), dma((4,)), dma((count,)), dma((count,)),
    ]
    outs = [jax.ShapeDtypeStruct(b, narrow) for b in blocks]
    outs += [jax.ShapeDtypeStruct(s, narrow) for s in pair_shapes]
    outs += [jax.ShapeDtypeStruct(small.shape, jnp.float32)]
    got = pl.pallas_call(
        functools.partial(reduce_kernel, count, kinds, spans),
        out_shape=outs,
        in_specs=[pl.BlockSpec(memory_space=pltpu.VMEM)] * (total + 3),
        out_specs=[pl.BlockSpec(memory_space=pltpu.VMEM)] * len(outs),
        scratch_shapes=scratch,
        compiler_params=pltpu.CompilerParams(
            collective_id=1, has_side_effects=True, vmem_limit_bytes=62 * 2**20
        ),
        name="reduce_grads",
    )(*grads, left_part, right_part, small)
    return got[:total], got[total : total + pairs], got[-1]


def product(left, right):
    return jnp.dot(left, right, preferred_element_type=jnp.float32)


def product_left(left, right):
    return lax.dot_general(
        left, right, (((0,), (0,)), ((), ())), preferred_element_type=jnp.float32
    )


def product_right(left, right):
    return lax.dot_general(
        left, right, (((1,), (1,)), ((), ())), preferred_element_type=jnp.float32
    )


def root_scale(field):
    return lax.rsqrt(jnp.mean(field * field, axis=-1, keepdims=True) + epsilon)


def norm_back(grad_normed, field, scale, gain):
    gain_grad = jnp.sum(grad_normed * field * scale, axis=0)
    weighted = grad_normed * gain
    field_grad = scale * weighted - field * (scale * scale * scale) * jnp.mean(
        weighted * field, axis=-1, keepdims=True
    )
    return (field_grad, gain_grad)


def wide_heads(block):
    first = lax.broadcasted_iota(jnp.int32, block.shape, 1) < KV
    none = jnp.zeros_like(block)
    return jnp.concatenate([jnp.where(first, block, none), jnp.where(first, none, block)], axis=0)


def narrow_heads(stacked):
    half = stacked.shape[0] // 2
    first = lax.broadcasted_iota(jnp.int32, (half, stacked.shape[1]), 1) < KV
    return jnp.where(first, stacked[:half], stacked[half:])


def reach(at, blocks):
    low, high = max(0, at - 1), min(blocks, at + 2)
    begin = (low - at + 1) * BLOCK
    return slice(low * BLOCK, high * BLOCK), slice(begin, begin + (high - low) * BLOCK)


def bias_block(base):
    heads = []
    for at in range(2):
        level = jnp.broadcast_to(base[at : at + 1], (BLOCK, base.shape[1]))
        heads.append(pltpu.roll(level, 0, axis=1, stride=1, stride_axis=0))
    return jnp.concatenate(heads, axis=0)


def offset_sums(block):
    rows, width = block.shape
    while rows > 8:
        rows = rows // 2
        block = block[:rows] + pltpu.roll(block[rows:], width - rows, axis=1)
    place = lax.broadcasted_iota(jnp.int32, block.shape, 0)
    for bit in (4, 2, 1):
        block = jnp.where((place & bit) > 0, pltpu.roll(block, width - bit, axis=1), block)
    return jnp.sum(block, axis=0, keepdims=True)


def attend_kernel(column_ref, row_ref, base_ref, query_ref, key_ref, value_ref, out_ref, share_ref):
    blocks = query_ref.shape[0] // BLOCK
    bias = bias_block(base_ref[0])
    for at in range(blocks):
        keys, places = reach(at, blocks)
        own = slice(at * BLOCK, (at + 1) * BLOCK)
        scores = product_right(wide_heads(query_ref[own]), key_ref[keys]) + bias[:, places]
        allowed = column_ref[own, :1] == row_ref[0, :1, keys]
        scores = jnp.where(jnp.concatenate([allowed, allowed], axis=0), scores, negative_fill)
        powers = jnp.exp(scores - jnp.max(scores, axis=1, keepdims=True))
        shares = powers * (1.0 / jnp.sum(powers, axis=1, keepdims=True))
        shares = shares.astype(jnp.bfloat16)
        share_ref[0, 0, at, :, places] = shares
        mixed = product(shares, value_ref[keys])
        out_ref[own] = narrow_heads(mixed).astype(jnp.bfloat16)


def attend_back_kernel(
    query_ref, key_ref, value_ref, grad_ref, share_ref,
    grad_query_ref, grad_key_ref, grad_value_ref, sums_ref, bias_acc, key_acc, value_acc,
):
    blocks = query_ref.shape[0] // BLOCK

    @pl.when(pl.program_id(1) == 0)
    def _():
        bias_acc[...] = jnp.zeros_like(bias_acc)

    key_acc[...] = jnp.zeros_like(key_acc)
    value_acc[...] = jnp.zeros_like(value_acc)
    for at in range(blocks):
        keys, places = reach(at, blocks)
        own = slice(at * BLOCK, (at + 1) * BLOCK)
        query, grad = wide_heads(query_ref[own]), wide_heads(grad_ref[own])
        narrow_shares = share_ref[0, 0, at, :, places]
        shares = narrow_shares.astype(jnp.float32)
        value_acc[keys] += product_left(narrow_shares, grad)
        moved = shares * product_right(grad, value_ref[keys])
        grad_scores = moved - shares * jnp.sum(moved, axis=1, keepdims=True)
        bias_acc[:, places] += grad_scores
        narrow = grad_scores.astype(jnp.bfloat16)
        grad_query_ref[own] = narrow_heads(product(narrow, key_ref[keys])).astype(jnp.bfloat16)
        key_acc[keys] += product_left(narrow, query)
    grad_key_ref[...] = key_acc[...].astype(jnp.bfloat16)
    grad_value_ref[...] = value_acc[...].astype(jnp.bfloat16)

    @pl.when(pl.program_id(1) == pl.num_programs(1) - 1)
    def _():
        sums_ref[0] = jnp.concatenate(
            [offset_sums(bias_acc[:BLOCK]), offset_sums(bias_acc[BLOCK:])], axis=0
        )


def offset_buckets():
    offset = jnp.arange(3 * BLOCK, dtype=jnp.int32) - BLOCK
    distance = jnp.abs(offset)
    far_bucket = 8 + sum(((distance >= boundary).astype(jnp.int32) for boundary in bucket_edges))
    near_bucket = jnp.where(distance < 8, distance, far_bucket)
    return jnp.where(offset > 0, 16, 0) + near_bucket


def attend_rows(rows, length, column, segment_index, base, query, key, value):
    pairs = HEADS // 2
    part = pl.BlockSpec((length, 2 * KV), lambda r, p: (r, p))
    return pl.pallas_call(
        attend_kernel,
        grid=(rows, pairs),
        out_shape=[
            jax.ShapeDtypeStruct(query.shape, jnp.bfloat16),
            jax.ShapeDtypeStruct(
                (rows, pairs, length // BLOCK, 2 * BLOCK, 3 * BLOCK), jnp.bfloat16
            ),
        ],
        in_specs=[
            pl.BlockSpec((length, BLOCK), lambda r, p: (r, 0)),
            pl.BlockSpec((1, 1, length), lambda r, p: (r, 0, 0)),
            pl.BlockSpec((1, 2, 3 * BLOCK), lambda r, p: (p, 0, 0)),
            part, part, part,
        ],
        out_specs=[
            part,
            pl.BlockSpec(
                (1, 1, length // BLOCK, 2 * BLOCK, 3 * BLOCK), lambda r, p: (r, p, 0, 0, 0)
            ),
        ],
        compiler_params=pltpu.CompilerParams(vmem_limit_bytes=48 * 2**20),
        name="attend",
    )(column, segment_index.reshape(rows, 1, length), base, query, key, value)


def attend_rows_back(rows, length, query, key, value, grad, shares):
    pairs = HEADS // 2
    part = pl.BlockSpec((length, 2 * KV), lambda p, r: (r, p))
    return pl.pallas_call(
        attend_back_kernel,
        grid=(pairs, rows),
        out_shape=[jax.ShapeDtypeStruct(query.shape, jnp.bfloat16)] * 3
        + [jax.ShapeDtypeStruct((pairs, 2, 3 * BLOCK), jnp.float32)],
        in_specs=[
            part, part, part, part,
            pl.BlockSpec(
                (1, 1, length // BLOCK, 2 * BLOCK, 3 * BLOCK), lambda p, r: (r, p, 0, 0, 0)
            ),
        ],
        out_specs=[part, part, part, pl.BlockSpec((1, 2, 3 * BLOCK), lambda p, r: (p, 0, 0))],
        scratch_shapes=[
            pltpu.VMEM((2 * BLOCK, 3 * BLOCK), jnp.float32),
            pltpu.VMEM((length, 2 * KV), jnp.float32),
            pltpu.VMEM((length, 2 * KV), jnp.float32),
        ],
        compiler_params=pltpu.CompilerParams(vmem_limit_bytes=48 * 2**20),
        name="attend_back",
    )(query, key, value, grad, shares)


def gelu_parts(before):
    slope = 0.7978845608028654
    square = before * before
    bend = jnp.tanh(slope * (before + 0.044715 * before * square))
    half = 0.5 * (1.0 + bend)
    rise = half + 0.5 * before * (1.0 - bend * bend) * slope * (1.0 + 3 * 0.044715 * square)
    return before * half, rise


def slots_of(stacked, count):
    rows, columns = stacked.shape
    own = lax.broadcasted_iota(jnp.int32, (rows, columns), 0) // count
    head = lax.broadcasted_iota(jnp.int32, (rows, columns), 1) // KV
    return jnp.where(own == head, stacked, 0.0)


def decoder_kernel(rows, slots, *refs):
    (
        segment_ref, start_ref, cotangent_ref, gain_ref, keys_ref, values_ref,
        self_value_hbm, self_output_hbm, cross_query_hbm, cross_output_hbm,
        inner_hbm, outer_hbm,
        decoded_ref, start_grad_ref, gain_grad_ref,
        normed_fin_ref, active_ref, normed_start_ref, own_ref, normed_mid_ref, context_ref,
        before_grad_ref, last_branch_ref, grad_own_ref, self_branch_ref, grad_asking_ref,
        cross_branch_ref, grad_keys_ref, grad_values_ref,
        self_value, self_output, cross_query, cross_output, inner, outer, sems,
    ) = refs
    loads = []
    for at, (source, target) in enumerate((
        (self_value_hbm, self_value), (self_output_hbm, self_output),
        (cross_query_hbm, cross_query), (cross_output_hbm, cross_output),
        (inner_hbm, inner), (outer_hbm, outer),
    )):
        loads.append(pltpu.make_async_copy(source, target, sems.at[at]))
        loads[-1].start()
    narrow = jnp.bfloat16
    length = keys_ref.shape[0] // rows
    start_gain, middle_gain, final_gain = gain_ref[0:1], gain_ref[1:2], gain_ref[2:3]

    start_field = start_ref[...].astype(jnp.float32)
    scale_start = root_scale(start_field)
    normed_start = (start_field * scale_start * start_gain).astype(narrow)
    normed_start_ref[...] = normed_start
    loads[0].wait()
    own = product(normed_start, self_value[...]).astype(narrow)
    own_ref[...] = own
    loads[1].wait()
    first_field = start_field + product(own, self_output[...])
    scale_mid = root_scale(first_field)
    normed_mid = (first_field * scale_mid * middle_gain).astype(narrow)
    normed_mid_ref[...] = normed_mid
    loads[2].wait()
    asking = product(normed_mid, cross_query[...]).astype(narrow).astype(jnp.float32)
    wides, all_shares, contexts = [], [], []
    for row in range(rows):
        part = asking[row * slots : (row + 1) * slots]
        wide = slots_of(jnp.concatenate([part] * HEADS, axis=0), slots).astype(narrow)
        span = slice(row * length, (row + 1) * length)
        scores = product_right(wide, keys_ref[span])
        slot = lax.rem(lax.broadcasted_iota(jnp.int32, scores.shape, 0), slots)
        scores = jnp.where(slot == segment_ref[row : row + 1], scores, negative_fill)
        powers = jnp.exp(scores - jnp.max(scores, axis=1, keepdims=True))
        shares = powers * (1.0 / jnp.sum(powers, axis=1, keepdims=True))
        mixed = slots_of(product(shares.astype(narrow), values_ref[span]), slots)
        contexts.append(jnp.sum(mixed.reshape(HEADS, slots, -1), axis=0))
        wides.append(wide)
        all_shares.append(shares)
    context = jnp.concatenate(contexts, axis=0).astype(narrow)
    context_ref[...] = context
    loads[3].wait()
    second_field = first_field + product(context, cross_output[...])
    scale_fin = root_scale(second_field)
    normed_fin = (second_field * scale_fin * final_gain).astype(narrow)
    normed_fin_ref[...] = normed_fin
    loads[4].wait()
    active, rise = gelu_parts(product(normed_fin, inner[...]))
    active = active.astype(narrow)
    active_ref[...] = active
    loads[5].wait()
    decoded_ref[...] = (second_field + product(active, outer[...])).astype(narrow)

    branch = cotangent_ref[...]
    last_branch_ref[...] = branch
    grad_second = branch.astype(jnp.float32)
    before_grad = (product_right(branch, outer[...]) * rise).astype(narrow)
    before_grad_ref[...] = before_grad
    grad_normed = product_right(before_grad, inner[...])
    moved, final_gain_grad = norm_back(grad_normed, second_field, scale_fin, final_gain)
    grad_second = grad_second + moved
    branch = grad_second.astype(narrow)
    cross_branch_ref[...] = branch
    grad_context = product_right(branch, cross_output[...]).astype(narrow).astype(jnp.float32)
    askings = []
    for row in range(rows):
        part = grad_context[row * slots : (row + 1) * slots]
        wide = slots_of(jnp.concatenate([part] * HEADS, axis=0), slots).astype(narrow)
        span = slice(row * length, (row + 1) * length)
        shares = all_shares[row]
        moved = shares * product_right(wide, values_ref[span])
        grad_scores = moved - shares * jnp.sum(moved, axis=1, keepdims=True)
        grad_scores = grad_scores.astype(narrow)
        grad_values_ref[span] = product_left(shares.astype(narrow), wide).astype(narrow)
        grad_keys_ref[span] = product_left(grad_scores, wides[row]).astype(narrow)
        mixed = slots_of(product(grad_scores, keys_ref[span]), slots)
        askings.append(jnp.sum(mixed.reshape(HEADS, slots, -1), axis=0))
    grad_asking = jnp.concatenate(askings, axis=0).astype(narrow)
    grad_asking_ref[...] = grad_asking
    grad_normed = product_right(grad_asking, cross_query[...])
    moved, middle_gain_grad = norm_back(grad_normed, first_field, scale_mid, middle_gain)
    grad_first = grad_second + moved
    branch = grad_first.astype(narrow)
    self_branch_ref[...] = branch
    grad_own = product_right(branch, self_output[...]).astype(narrow)
    grad_own_ref[...] = grad_own
    grad_normed = product_right(grad_own, self_value[...])
    moved, start_gain_grad = norm_back(grad_normed, start_field, scale_start, start_gain)
    start_grad_ref[...] = grad_first + moved
    gain_grad_ref[...] = jnp.concatenate(
        [start_gain_grad[None], middle_gain_grad[None], final_gain_grad[None]], axis=0
    )


def decode(segment_index, start, cotangent, gains, keys, values, weights):
    rows, tokens, width = segment_index.shape[0], start.shape[0], start.shape[1]
    narrow, hidden = jnp.bfloat16, weights[4].shape[1]
    few = jax.ShapeDtypeStruct((tokens, width), narrow)
    many = jax.ShapeDtypeStruct((tokens, hidden), narrow)
    outs = [
        few,
        jax.ShapeDtypeStruct((tokens, width), jnp.float32),
        jax.ShapeDtypeStruct((3, width), jnp.float32),
        few, many, few, few, few, few,
        many, few, few, few, few, few,
        jax.ShapeDtypeStruct(keys.shape, narrow),
        jax.ShapeDtypeStruct(values.shape, narrow),
    ]
    local = pl.BlockSpec(memory_space=pltpu.VMEM)
    return pl.pallas_call(
        functools.partial(decoder_kernel, rows, tokens // rows),
        out_shape=outs,
        in_specs=[local] * 6 + [pl.BlockSpec(memory_space=pl.ANY)] * 6,
        out_specs=[local] * len(outs),
        scratch_shapes=[pltpu.VMEM(w.shape, narrow) for w in weights]
        + [pltpu.SemaphoreType.DMA((6,))],
        compiler_params=pltpu.CompilerParams(vmem_limit_bytes=48 * 2**20),
        name="decode",
    )(segment_index, start, cotangent, gains, keys, values, *weights)


TILE = 256


def rows_of(at, size=TILE):
    return pl.ds(pl.multiple_of(at * size, size), size)


class Gather:
    def __init__(self, spot, kinds, shards, fulls, sems):
        self.spot, self.kinds, self.shards, self.fulls = spot, kinds, shards, fulls
        (
            self.ring_out, self.ring_in, self.near_out, self.near_in,
            self.far_out, self.far_in, self.last_out, self.last_in, self.own_sem,
        ) = sems
        self.split = [i for i in range(len(kinds)) if kinds[i] in ("wide", "tall")]

    def piece(self, i, step, plane):
        count = self.spot.count
        slot = ring_index(self.spot.place + (step if i % 2 else count - step), count)
        rows = self.shards[i].shape[0]
        block = self.fulls[i].at[pl.ds(pl.multiple_of(slot * rows, 16), rows)]
        return cut(self.kinds[i], block, plane, self.spot.core)

    def own_copy(self, i):
        rows = self.shards[i].shape[0]
        block = self.fulls[i].at[pl.ds(pl.multiple_of(self.spot.fsdp * rows, 16), rows)]
        return pltpu.make_async_copy(self.shards[i], block, self.own_sem.at[i])

    def ring_copy(self, i, step, source=None):
        here = self.piece(i, step, self.spot.plane)
        return send(
            here if source is None else source, here,
            self.ring_out.at[i, step], self.ring_in.at[i, step],
            self.spot.before if i % 2 else self.spot.after,
        )

    def near_copy(self, i, step):
        here = self.piece(i, step, self.spot.plane)
        return send(
            here, here, self.near_out.at[i, step], self.near_in.at[i, step], self.spot.sibling
        )

    def far_copy(self, i, step):
        here, at = self.piece(i, step, self.spot.plane), self.split.index(i)
        return send(
            here, here, self.far_out.at[at, step], self.far_in.at[at, step], self.spot.opposite
        )

    def last_copy(self, i, step):
        here, at = self.piece(i, step, 1 - self.spot.plane), self.split.index(i)
        return send(
            here, here, self.last_out.at[at, step], self.last_in.at[at, step], self.spot.sibling
        )

    def start(self, group):
        for i in group:
            source = cut(self.kinds[i], self.shards[i], self.spot.plane, self.spot.core)
            self.ring_copy(i, 0, source).start()

    def advance(self, group, step):
        count = self.spot.count

        @pl.when(step < count)
        def _():
            for i in group:
                self.ring_copy(i, step - 1).wait_recv()

                @pl.when(step < count - 1)
                def _():
                    self.ring_copy(i, step).start()

                if self.kinds[i] != "small":
                    self.near_copy(i, step).start()
                if i in self.split:
                    self.far_copy(i, step).start()

        @pl.when(step > 1)
        def _():
            for i in group:
                if i in self.split:
                    self.far_copy(i, step - 1).wait_recv()
                    self.last_copy(i, step - 1).start()

    def arrive(self, group):
        def one(step, carry):
            for i in group:
                if self.kinds[i] != "small":
                    self.near_copy(i, step).wait_recv()
                if i in self.split:
                    self.last_copy(i, step).wait_recv()
            return carry

        lax.fori_loop(1, self.spot.count, one, 0)
        for i in group:
            self.own_copy(i).wait()

    def settle(self, group):
        def one(step, carry):
            for i in group:
                self.ring_copy(i, step - 1).wait_send()
                if self.kinds[i] != "small":
                    self.near_copy(i, step).wait_send()
                if i in self.split:
                    self.far_copy(i, step).wait_send()
                    self.last_copy(i, step).wait_send()
            return carry

        lax.fori_loop(1, self.spot.count, one, 0)


FIRST, SECOND, THIRD = (0, 1, 2, 3, 14), (4, 5, 6, 7), (8, 9, 10, 11, 12, 13)


def forward_kernel(count, rows, *refs):
    refs = list(refs)

    def take(size):
        got = refs[:size]
        del refs[:size]
        return got

    shards = take(15)
    tokens, column, segment, base = take(4)
    weight_outs = take(14)
    (gain_out,) = take(1)
    (
        query_out, key_out, value_out, share_out, context_out, hidden_out, normed_two_out,
        active_out, rise_out, memory_out, cross_key_out, cross_value_out, normed_one_out,
    ) = take(13)
    held = take(8)
    gain_all, normed_one, query, key, value, context = take(6)
    hidden, normed_two, active, rise, memory, cross_keys, cross_values, shares = take(8)
    gather_sems = take(9)
    save_sem, share_sem = take(2)
    spot = Spot(count)
    fulls = held + weight_outs[8:] + [gain_all]
    gather = Gather(spot, KINDS, shards, fulls, gather_sems)
    tiles = tokens.shape[0] // TILE
    length = tokens.shape[0] // rows
    blocks, pairs = length // BLOCK, HEADS // 2
    narrow = jnp.bfloat16
    saves = []

    def save(source, target):
        copy = pltpu.make_async_copy(source, target, save_sem.at[len(saves)])
        copy.start()
        saves.append(copy)

    def each_tile(body):
        def one(at, carry):
            body(rows_of(at), at)
            return carry

        lax.fori_loop(0, tiles, one, 0)

    def run(group, first, last):
        def one(step, carry):
            gather.advance(group, step)
            return carry

        lax.fori_loop(first, last, one, 0)

    for i in FIRST:
        gather.own_copy(i).start()
    spot.greet()
    gather.start(FIRST)
    for i in SECOND + THIRD:
        gather.own_copy(i).start()
    run(FIRST, 1, count - 1)
    gather.start(SECOND)
    run(FIRST, count - 1, count + 1)
    gather.arrive(FIRST)
    gain = jnp.zeros((16, gain_all.shape[1]), jnp.float32)
    for slot in range(count):
        gain = gain + gain_all[slot * 16 : (slot + 1) * 16].astype(jnp.float32)
    gain_out[...] = gain
    query_weight, key_weight, value_weight, output_weight = held[:4]
    inner_weight, outer_weight, cross_key_weight, cross_value_weight = held[4:]

    def first_norm(span, at):
        field = tokens[span].astype(jnp.float32)
        normed_one[span] = (field * root_scale(field) * gain_out[0:1]).astype(narrow)

    each_tile(first_norm)

    def project(target, weight):
        def body(span, at):
            target[span] = product(normed_one[span], weight[...]).astype(narrow)

        each_tile(body)

    project(query, query_weight)
    gather.advance(SECOND, 1)
    project(key, key_weight)
    project(value, value_weight)
    gather.advance(SECOND, 2)
    for source, target in (
        (normed_one, normed_one_out), (query, query_out), (key, key_out), (value, value_out),
    ):
        save(source, target)
    for i in range(4):
        save(held[i], weight_outs[i])

    def share_copy(at):
        return pltpu.make_async_copy(
            shares.at[lax.rem(at, 2)],
            share_out.at[at // pairs, lax.rem(at, pairs)],
            share_sem.at[lax.rem(at, 2)],
        )

    def attend_pair(at, carry):
        row, pair, buffer = at // pairs, lax.rem(at, pairs), lax.rem(at, 2)

        @pl.when(lax.rem(at, 3) == 0)
        def _():
            gather.advance(SECOND, 3 + at // 3)

        @pl.when(at >= 2)
        def _():
            share_copy(at - 2).wait()

        bias = bias_block(base[pair])
        columns = rows_of(pair, 2 * KV)

        def span(begin, size):
            return pl.ds(pl.multiple_of(row * length + begin, BLOCK), size)

        for block in range(blocks):
            keys, places = reach(block, blocks)
            own = span(block * BLOCK, BLOCK)
            near = span(keys.start, keys.stop - keys.start)
            scores = product_right(wide_heads(query[own, columns]), key[near, columns])
            scores = scores + bias[:, places]
            allowed = column[own, :1] == segment[row, :, keys]
            scores = jnp.where(jnp.concatenate([allowed, allowed], axis=0), scores, negative_fill)
            powers = jnp.exp(scores - jnp.max(scores, axis=1, keepdims=True))
            part = powers * (1.0 / jnp.sum(powers, axis=1, keepdims=True))
            part = part.astype(narrow)
            shares[buffer, block, :, places] = part
            mixed = product(part, value[near, columns])
            context[own, columns] = narrow_heads(mixed).astype(narrow)
        share_copy(at).start()
        return carry

    lax.fori_loop(0, rows * pairs, attend_pair, 0)
    save(context, context_out)
    gather.advance(SECOND, 7)
    gather.start(THIRD)
    gather.advance(SECOND, 8)

    def second_norm(span, at):
        field = tokens[span].astype(jnp.float32) + product(context[span], output_weight[...])
        hidden[span] = field
        normed_two[span] = (field * root_scale(field) * gain_out[1:2]).astype(narrow)

    each_tile(second_norm)
    save(hidden, hidden_out)
    save(normed_two, normed_two_out)
    gather.arrive(SECOND)
    for i in range(4, 8):
        save(held[i], weight_outs[i])
    chunk = tokens.shape[1]

    def feed(span, at):
        gather.advance(THIRD, at + 1)
        for begin in range(0, active.shape[1], chunk):
            part = slice(begin, begin + chunk)
            level, slope = gelu_parts(product(normed_two[span], inner_weight[:, part]))
            active[span, part] = level.astype(narrow)
            rise[span, part] = slope.astype(narrow)
        full = hidden[span] + product(active[span], outer_weight[...])
        memory[span] = full.astype(narrow)

    each_tile(feed)
    save(active, active_out)
    save(rise, rise_out)
    save(memory, memory_out)
    gather.advance(THIRD, tiles + 1)

    def cross(span, at):
        cross_keys[span] = product(memory[span], cross_key_weight[...]).astype(narrow)
        cross_values[span] = product(memory[span], cross_value_weight[...]).astype(narrow)

    each_tile(cross)
    save(cross_keys, cross_key_out)
    save(cross_values, cross_value_out)
    run(THIRD, tiles + 2, count + 1)
    gather.arrive(THIRD)
    for group in (FIRST, SECOND, THIRD):
        gather.settle(group)
    for copy in saves:
        copy.wait()
    for at in range(rows * pairs - 2, rows * pairs):
        share_copy(at).wait()


def forward(count, shards, tokens, column, segment_index, base):
    rows, length = segment_index.shape
    many, width = tokens.shape
    hidden_width = shards[4].shape[1]
    narrow, wide = jnp.bfloat16, jnp.float32
    pairs, total = HEADS // 2, len(shards)
    split = sum(kind in ("wide", "tall") for kind in KINDS)
    weights = [(count * s.shape[0], s.shape[1]) for s in shards]
    few, much = (many, width), (many, hidden_width)
    share_shape = (rows, pairs, length // BLOCK, 2 * BLOCK, 3 * BLOCK)
    shapes = [(w, narrow) for w in weights[:14]] + [((16, width), wide)]
    shapes += [
        (few, narrow), (few, narrow), (few, narrow), (share_shape, narrow), (few, narrow),
        (few, wide), (few, narrow), (much, narrow), (much, narrow), (few, narrow), (few, narrow),
        (few, narrow), (few, narrow),
    ]
    dma = pltpu.SemaphoreType.DMA
    scratch = [pltpu.VMEM(w, narrow) for w in weights[:8]] + [pltpu.VMEM(weights[14], narrow)]
    scratch += [pltpu.VMEM(few, narrow)] * 5
    scratch += [
        pltpu.VMEM(few, wide), pltpu.VMEM(few, narrow), pltpu.VMEM(much, narrow),
        pltpu.VMEM(much, narrow), pltpu.VMEM(few, narrow), pltpu.VMEM(few, narrow),
        pltpu.VMEM(few, narrow), pltpu.VMEM((2,) + share_shape[2:], narrow),
    ]
    scratch += [dma((total, count))] * 4 + [dma((split, count))] * 4
    scratch += [dma((total,)), dma((24,)), dma((2,))]
    anywhere = pl.BlockSpec(memory_space=pl.ANY)
    local = pl.BlockSpec(memory_space=pltpu.VMEM)
    got = pl.pallas_call(
        functools.partial(forward_kernel, count, rows),
        out_shape=[jax.ShapeDtypeStruct(s, d) for s, d in shapes],
        in_specs=[anywhere] * total + [local] * 4,
        out_specs=[anywhere] * 14 + [local] + [anywhere] * 13,
        scratch_shapes=scratch,
        compiler_params=pltpu.CompilerParams(
            collective_id=2, has_side_effects=True, vmem_limit_bytes=62 * 2**20
        ),
        name="forward",
    )(*shards, tokens, column, segment_index.reshape(rows, 1, length), base)
    return got[:14], got[14], got[15:]


def forward_apart(count, shards, tokens, column, segment_index, base):
    rows, length = segment_index.shape
    narrow = jnp.bfloat16
    whole = gather_weights(count, shards, KINDS)
    gains = jnp.sum(whole[14].astype(jnp.float32), axis=0)
    whole = [part.reshape(-1, part.shape[2]) for part in whole[:14]]
    field = tokens.astype(jnp.float32)
    normed_one = (field * root_scale(field) * gains[0]).astype(narrow)
    query, key, value = [product(normed_one, weight).astype(narrow) for weight in whole[:3]]
    context, shares = attend_rows(
        rows, length, column, segment_index, base, query, key, value
    )
    hidden = field + product(context, whole[3])
    normed_two = (hidden * root_scale(hidden) * gains[1]).astype(narrow)
    active, rise = gelu_parts(product(normed_two, whole[4]))
    active = active.astype(narrow)
    memory = (hidden + product(active, whole[5])).astype(narrow)
    cross_keys, cross_values = [product(memory, weight).astype(narrow) for weight in whole[6:8]]
    return whole, gains, (
        query, key, value, shares, context, hidden, normed_two,
        active, rise, memory, cross_keys, cross_values, normed_one,
    )


INNER, OUTER = 0, 1
SQUARES = (2, 3, 4, 5, 6, 7)


def backward_kernel(count, rows, spans, *refs):
    refs = list(refs)

    def take(size):
        got = refs[:size]
        del refs[:size]
        return got

    (
        inner_hbm, outer_hbm, query_weight_hbm, key_weight_hbm, value_weight_hbm,
        output_weight_hbm, cross_key_weight_hbm, cross_value_weight_hbm,
        active_hbm, rise_hbm, normed_two_hbm, context_hbm, query_hbm, key_hbm, value_hbm,
        normed_one_hbm, tokens_hbm, memory_hbm, grad_keys_hbm, grad_values_hbm, cotangent_hbm,
        hidden_hbm, shares_hbm,
    ) = take(23)
    left_part, right_part, gain, decoder_gains = take(4)
    sums, pairs = take(8), len(spans)
    pair_sums = take(pairs)
    small_sum, tokens_grad_hbm = take(2)
    big, flat, half, work, final, far = take(1)[0], take(2), take(8), take(8), take(6), take(2)
    left_all, right_all = take(2)
    pair_work, pair_half, pair_far = take(pairs), take(pairs), take(pairs)
    small, small_near, small_mid, small_far, small_all = take(5)
    pool, level, weights, shares, bias_acc, key_acc, value_acc = take(7)
    (
        near_sem, ring_out, ring_in, far_sem, end_sem, left_out, left_in,
        right_out, right_in, pair_sem, small_sem, small_out, small_in, load_sem, share_sem,
    ) = take(15)
    spot = Spot(count)
    core, plane = spot.core, spot.plane
    diagonal = (lax.rem(spot.dp + 2, 4) + 1 - 2 * core, spot.fsdp)
    narrow = jnp.bfloat16
    many, width = level.shape[1:]
    tiles, length = many // TILE, many // rows
    blocks = length // BLOCK
    depth = width // count
    products = {2: big.at[0], 3: big.at[1], 4: big.at[2], 5: flat[0], 6: flat[0], 7: flat[1]}

    def peer(k):
        return (spot.dp, lax.rem(spot.fsdp + k, count))

    def slot_at(i, step):
        turn = step + 1 if i % 2 else count - 1 - step
        return ring_index(spot.place + turn, count)

    def near_copy(i):
        if i == INNER:
            source = big.at[pl.ds(2 * (1 - core), 2)]
        elif i == OUTER:
            source = big.at[:, :, half_of(1 - core, width)]
        else:
            source = products[i].at[:, half_of(1 - core, width)]
        return send(source, half[i], near_sem.at[0, i], near_sem.at[1, i], spot.sibling)

    def part_of(i, slot, side):
        if i == INNER:
            return half[i].at[side, pl.ds(pl.multiple_of(slot * depth, 16), depth)]
        if i == OUTER:
            own = 4 * depth
            begin = lax.rem(slot, 2) * own + side * (own // 2)
            return half[i].at[slot // 2, pl.ds(pl.multiple_of(begin, 16), own // 2)]
        return half[i].at[pl.ds(pl.multiple_of(slot * depth, 16), depth)]

    def far_copy(i, step):
        return send(
            part_of(i, slot_at(i, step), 1 - plane), far[i].at[step],
            far_sem.at[0, i, step], far_sem.at[1, i, step], spot.opposite,
        )

    def join(i):
        near_copy(i).wait()
        if i == INNER:

            def one(at, carry):
                side, span = at // 3, rows_of(lax.rem(at, 3))
                mine = big[2 * core + side, span]
                half[i][side, span] = plus(half[i][side, span], mine).astype(narrow)
                return carry

            lax.fori_loop(0, 6, one, 0)
        elif i == OUTER:

            def one(at, carry):
                side, span = at // 3, rows_of(lax.rem(at, 3))
                mine = big[side, span, half_of(core, width)]
                half[i][side, span] = plus(half[i][side, span], mine).astype(narrow)
                return carry

            lax.fori_loop(0, 12, one, 0)
        else:

            def one(at, carry):
                span = rows_of(at)
                mine = products[i][span, half_of(core, width)]
                half[i][span] = plus(half[i][span], mine).astype(narrow)
                return carry

            lax.fori_loop(0, 3, one, 0)
        if i in (INNER, OUTER):

            def far_start(step, carry):
                far_copy(i, step).start()
                return carry

            lax.fori_loop(0, count, far_start, 0)

    def ring_copy(i, step):
        return send(
            work[i].at[step], work[i].at[step + 1], ring_out.at[i, step], ring_in.at[i, step],
            spot.before if i % 2 else spot.after,
        )

    def advance(group, step):
        for i in group:
            value = part_of(i, slot_at(i, step), plane)[...].astype(jnp.float32)
            if i in (INNER, OUTER):
                far_copy(i, step).wait_recv()
                value = value + far[i][step].astype(jnp.float32)

            @pl.when(step > 0)
            def _():
                ring_copy(i, step - 1).wait_recv()
                work[i][step] = plus(value, work[i][step]).astype(narrow)

            @pl.when(step == 0)
            def _():
                work[i][step] = value.astype(narrow)

            @pl.when(step < count - 1)
            def _():
                ring_copy(i, step).start()

    def run(group, first, last):
        def one(step, carry):
            advance(group, step)
            return carry

        lax.fori_loop(first, last, one, 0)

    def end_across(i):
        return send(
            work[i].at[count - 1], final[i - 2], end_sem.at[0, i], end_sem.at[1, i], spot.opposite
        )

    def end_piece(i):
        if i == INNER:
            return cut("wide", sums[i], plane, core)
        if i == OUTER:
            return cut("tall", sums[i], plane, core)
        return sums[i].at[:, half_of(core, width)]

    def end_copies(i):
        here = end_piece(i)
        copies = [send(here, here, end_sem.at[2, i], end_sem.at[3, i], spot.sibling)]
        if i in (INNER, OUTER):
            copies.append(send(here, here, end_sem.at[4, i], end_sem.at[5, i], spot.opposite))
            copies.append(send(here, here, end_sem.at[6, i], end_sem.at[7, i], diagonal))
        return copies

    def close(i):
        if i in (INNER, OUTER):
            end_piece(i)[...] = work[i][count - 1]
        else:
            end_across(i).wait()
            end_piece(i)[...] = plus(work[i][count - 1], final[i - 2][...]).astype(narrow)
        for copy in end_copies(i):
            copy.start()

    def left_copy(k):
        other = lax.rem(spot.fsdp + k, count)
        return send(
            left_part.at[other], left_all.at[spot.fsdp], left_out.at[k], left_in.at[k], peer(k)
        )

    def right_copy(way, step):
        turn = step if way else count - step
        slot = ring_index(spot.place + turn, count)
        wide = right_part.shape[1] // 2
        here = right_all.at[slot, :, way * wide : (way + 1) * wide]
        return send(
            here, here, right_out.at[way, step], right_in.at[way, step],
            spot.before if way else spot.after,
        )

    def right_step(step):
        for way in range(2):
            right_copy(way, step - 1).wait_recv()
            if step < count - 1:
                right_copy(way, step).start()

    def pair_near(j):
        columns = pair_sums[j].shape[1]
        return send(
            pair_work[j].at[:, half_of(1 - core, columns)], pair_half[j],
            pair_sem.at[0, j], pair_sem.at[1, j], spot.sibling,
        )

    def pair_across(j):
        return send(
            pair_half[j], pair_far[j], pair_sem.at[2, j], pair_sem.at[3, j], spot.opposite
        )

    def pair_end(j):
        here = pair_sums[j].at[:, half_of(core, pair_sums[j].shape[1])]
        return send(here, here, pair_sem.at[4, j], pair_sem.at[5, j], spot.sibling)

    def small_copy(k):
        here = small_all.at[spot.fsdp]
        return send(here, here, small_out.at[k], small_in.at[k], peer(k))

    def each_peer(body):
        def one(k, carry):
            body(k)
            return carry

        lax.fori_loop(1, count, one, 0)

    def each_tile(body):
        def one(at, carry):
            body(rows_of(at))
            return carry

        lax.fori_loop(0, tiles, one, 0)

    used = []

    def load(source, target):
        copy = pltpu.make_async_copy(source, target, load_sem.at[len(used)])
        copy.start()
        used.append(copy)
        return copy

    def fold(target, left, right):
        def one(at, carry):
            span = rows_of(at)
            target[span] = product_left(left[:, span], right[...]).astype(narrow)
            return carry

        lax.fori_loop(0, width // TILE, one, 0)

    loads = [
        load(grad_keys_hbm, pool.at[4]), load(cross_key_weight_hbm, weights.at[0]),
        load(grad_values_hbm, pool.at[5]), load(cross_value_weight_hbm, weights.at[1]),
        load(cotangent_hbm, pool.at[2]), load(memory_hbm, pool.at[1]),
    ]

    def chunk_of(source, at):
        return source.at[:, pl.ds(at * width, width)]

    active_loads = {1: load(chunk_of(active_hbm, 1), pool.at[3])}
    hidden_load = load(hidden_hbm, level.at[2])
    out_loads = {0: load(outer_hbm.at[pl.ds(0, width)], weights.at[2])}
    barrier = pltpu.get_barrier_semaphore()
    for partner in (spot.sibling, spot.opposite, diagonal):
        pl.semaphore_signal(barrier, inc=1, device_id=partner, device_id_type=MESH)
    each_peer(
        lambda k: pl.semaphore_signal(barrier, inc=1, device_id=peer(k), device_id_type=MESH)
    )
    pl.semaphore_wait(barrier, count + 2)
    each_peer(lambda k: left_copy(k).start())
    right_all[spot.fsdp] = right_part[...]
    left_all[spot.fsdp] = left_part[spot.fsdp]
    for way in range(2):
        right_copy(way, 0).start()
    small[...] = jnp.zeros_like(small)
    small[2:5] = decoder_gains[...]
    for copy in loads:
        copy.wait()

    def enter(span):
        value = pool[2, span].astype(jnp.float32)
        value = value + product_right(pool[4, span], weights[0])
        value = value + product_right(pool[5, span], weights[1])
        level[0, span] = value
        pool[0, span] = value.astype(narrow)

    each_tile(enter)
    active_loads[0] = load(chunk_of(active_hbm, 0), pool.at[2])
    in_loads = {
        at: load(chunk_of(inner_hbm, at), weights.at[at]) for at in range(2)
    }
    fold(flat[0], pool.at[1], pool.at[4])
    near_copy(6).start()
    fold(flat[1], pool.at[1], pool.at[5])
    near_copy(7).start()
    normed_load = load(normed_two_hbm, pool.at[1])
    context_load = load(context_hbm, pool.at[4])
    right_step(1)

    rise_loads = {}
    for at in range(4):
        buffer = 2 + at % 2
        active_loads[at].wait()
        fold(big.at[at], pool.at[buffer], pool.at[0])
        if at < 2:
            active_loads[at + 2] = load(chunk_of(active_hbm, at + 2), pool.at[buffer])
        else:
            rise_loads[at - 2] = load(chunk_of(rise_hbm, at - 2), pool.at[buffer])
        right_step(at + 2)
        if at == 1:
            join(6)
            join(7)
        if at >= 1:
            advance((6, 7), at - 1)
    near_copy(OUTER).start()
    out_loads[1] = load(outer_hbm.at[pl.ds(width, width)], weights.at[3])

    normed_load.wait()
    for at in range(4):
        buffer = 2 + at % 2
        rise_loads[at].wait()
        out_loads[at].wait()
        in_loads[at].wait()

        def back(span):
            before = product_right(pool[0, span], weights[2 + at % 2])
            before = (before * pool[buffer, span].astype(jnp.float32)).astype(narrow)
            pool[buffer, span] = before
            moved = product_right(before, weights[at % 2])
            level[1, span] = moved if at == 0 else level[1, span] + moved

        each_tile(back)
        if at < 2:
            span = pl.ds((at + 2) * width, width)
            out_loads[at + 2] = load(outer_hbm.at[span], weights.at[2 + at % 2])
            in_loads[at + 2] = load(chunk_of(inner_hbm, at + 2), weights.at[at % 2])
        if at == 0:
            right_step(6)
            advance((6, 7), 3)
            join(OUTER)
        fold(big.at[at], pool.at[1], pool.at[buffer])
        if at < 2:
            rise_loads[at + 2] = load(chunk_of(rise_hbm, at + 2), pool.at[buffer])
        if at == 0:
            right_step(7)
            each_peer(lambda k: left_copy(k).wait_recv())
            advance((6, 7), 4)
            for j, (left_at, right_at) in enumerate(spans):
                own, columns = pair_sums[j].shape
                wide = -(-own // 128) * 128
                left = left_all[:, :, left_at : left_at + wide].reshape(-1, wide)
                for begin in range(0, columns, width):
                    right = right_all[:, :, right_at + begin : right_at + begin + width]
                    right = right.reshape(-1, width)
                    block = product_left(left, right)
                    pair_work[j][:, begin : begin + width] = block[:own].astype(narrow)
                pair_near(j).start()
        elif at == 1:
            advance((6, 7), 5)
            advance((OUTER,), 0)
            advance((OUTER,), 1)
        elif at == 2:
            advance((6, 7), 6)
            advance((OUTER,), 2)
            advance((OUTER,), 3)
            for j in range(pairs):
                pair_near(j).wait()
                mine = pair_work[j][:, half_of(core, pair_sums[j].shape[1])]
                pair_half[j][...] = plus(pair_half[j][...], mine).astype(narrow)
                pair_across(j).start()
        else:
            advance((6, 7), 7)
            advance((OUTER,), 4)
            for i in (6, 7):
                end_across(i).start()
    near_copy(INNER).start()
    query_load = load(query_hbm, pool.at[1])
    key_load, value_load = load(key_hbm, pool.at[2]), load(value_hbm, pool.at[3])
    late_loads = [
        load(query_weight_hbm, weights.at[0]), load(key_weight_hbm, weights.at[1]),
        load(value_weight_hbm, weights.at[2]),
    ]
    output_load = load(output_weight_hbm, weights.at[3])

    def back_norm(field, moved, gain_row, at):
        scale = root_scale(field)
        small[at : at + 1] += jnp.sum(moved * field * scale, axis=0, keepdims=True)
        weighted = moved * gain_row
        mean = jnp.mean(weighted * field, axis=-1, keepdims=True)
        return scale * weighted - field * (scale * scale * scale) * mean

    hidden_load.wait()

    def second(span):
        value = level[0, span] + back_norm(level[2, span], level[1, span], gain[1:2], 1)
        level[0, span] = value
        pool[0, span] = value.astype(narrow)

    each_tile(second)
    advance((OUTER,), 5)
    context_load.wait()
    fold(flat[0], pool.at[4], pool.at[0])
    near_copy(5).start()
    normed_one_load = load(normed_one_hbm, pool.at[4])
    advance((OUTER,), 6)
    output_load.wait()

    def third(span):
        pool[5, span] = product_right(pool[0, span], weights[3]).astype(narrow)

    each_tile(third)
    tokens_load = load(tokens_hbm, pool.at[0])
    advance((OUTER,), 7)
    join(INNER)
    join(5)
    for copy in (query_load, key_load, value_load):
        copy.wait()

    def share_copy(at):
        return pltpu.make_async_copy(
            shares_hbm.at[lax.rem(at, rows), at // rows],
            shares.at[lax.rem(at, 2)],
            share_sem.at[lax.rem(at, 2)],
        )

    turns = rows * (HEADS // 2)
    share_copy(0).start()

    def attend_pair(at, carry):
        pair, row, buffer = at // rows, lax.rem(at, rows), lax.rem(at, 2)
        share_copy(at).wait()

        @pl.when(at + 1 < turns)
        def _():
            share_copy(at + 1).start()

        @pl.when((at >= 1) & (at < count + 1))
        def _():
            advance((5,), at - 1)

        @pl.when((at >= 3) & (at < count + 3))
        def _():
            advance((INNER,), at - 3)

        @pl.when(row == 0)
        def _():
            bias_acc[...] = jnp.zeros_like(bias_acc)

        key_acc[...] = jnp.zeros_like(key_acc)
        value_acc[...] = jnp.zeros_like(value_acc)
        columns = rows_of(pair, 2 * KV)

        def span(begin, size):
            return pl.ds(pl.multiple_of(row * length + begin, BLOCK), size)

        for block in range(blocks):
            keys, places = reach(block, blocks)
            own = span(block * BLOCK, BLOCK)
            near = span(keys.start, keys.stop - keys.start)
            query, grad = wide_heads(pool[1, own, columns]), wide_heads(pool[5, own, columns])
            narrow_shares = shares[buffer, block, :, places]
            part = narrow_shares.astype(jnp.float32)
            value_acc[keys] += product_left(narrow_shares, grad)
            moved = part * product_right(grad, pool[3, near, columns])
            grad_scores = moved - part * jnp.sum(moved, axis=1, keepdims=True)
            bias_acc[:, places] += grad_scores
            low = grad_scores.astype(narrow)
            key_acc[keys] += product_left(low, query)
            mixed = product(low, pool[2, near, columns])
            pool[1, own, columns] = narrow_heads(mixed).astype(narrow)
        pool[2, span(0, length), columns] = key_acc[...].astype(narrow)
        pool[3, span(0, length), columns] = value_acc[...].astype(narrow)

        @pl.when(row == rows - 1)
        def _():
            for head in range(2):
                block = bias_acc[head * BLOCK : (head + 1) * BLOCK]
                place = slice(head * 3 * BLOCK, (head + 1) * 3 * BLOCK)
                small[pl.ds(5 + pair, 1), place] = offset_sums(block)

        return carry

    lax.fori_loop(0, turns, attend_pair, 0)
    end_across(5).start()
    normed_one_load.wait()
    for i, at in ((2, 1), (3, 2), (4, 3)):
        fold(big.at[i - 2], pool.at[4], pool.at[at])
        near_copy(i).start()
    close(INNER)
    close(OUTER)
    for i in (5, 6, 7):
        close(i)
    for i in (2, 3, 4):
        join(i)
    advance((2, 3, 4), 0)
    tokens_load.wait()
    for copy in late_loads:
        copy.wait()

    def save(at):
        span = rows_of(at)
        return pltpu.make_async_copy(
            level.at[1, span], tokens_grad_hbm.at[span], share_sem.at[2 + at]
        )

    def last(at, carry):
        span = rows_of(at)
        moved = product_right(pool[1, span], weights[0])
        moved = moved + product_right(pool[2, span], weights[1])
        moved = moved + product_right(pool[3, span], weights[2])
        field = pool[0, span].astype(jnp.float32)
        level[1, span] = level[0, span] + back_norm(field, moved, gain[0:1], 0)
        save(at).start()
        advance((2, 3, 4), at + 1)
        return carry

    lax.fori_loop(0, tiles, last, 0)
    near_small = send(small, small_near, small_sem.at[0], small_sem.at[1], spot.sibling)
    near_small.start()
    for j in range(pairs):
        pair_across(j).wait()
        here = half_of(core, pair_sums[j].shape[1])
        pair_sums[j][:, here] = plus(pair_half[j][...], pair_far[j][...]).astype(narrow)
        pair_end(j).start()
    advance((2, 3, 4), tiles + 1)
    near_small.wait()
    small_mid[...] = small[...] + small_near[...]
    far_small = send(small_mid, small_far, small_sem.at[2], small_sem.at[3], spot.opposite)
    far_small.start()
    advance((2, 3, 4), tiles + 2)
    far_small.wait()
    small_all[spot.fsdp] = small_mid[...] + small_far[...]
    each_peer(lambda k: small_copy(k).start())
    run((2, 3, 4), tiles + 3, count)
    for i in (2, 3, 4):
        end_across(i).start()
    each_peer(lambda k: small_copy(k).wait_recv())
    small_sum[...] = lax.fori_loop(
        1, count, lambda k, so_far: so_far + small_all[k], small_all[0]
    )
    for i in (2, 3, 4):
        close(i)
    for i in range(8):
        for copy in end_copies(i):
            copy.wait()
    for j in range(pairs):
        pair_end(j).wait()
    for at in range(tiles):
        save(at).wait()

    def drain(step, carry):
        for i in (INNER, OUTER):
            far_copy(i, step).wait_send()
        return carry

    lax.fori_loop(0, count, drain, 0)

    def drain_ring(step, carry):
        for i in range(8):
            ring_copy(i, step).wait_send()
        for way in range(2):
            right_copy(way, step).wait_send()
        left_copy(step + 1).wait_send()
        small_copy(step + 1).wait_send()
        return carry

    lax.fori_loop(0, count - 1, drain_ring, 0)


def backward(
    count, rows, whole, kept, tokens, cotangent, grad_keys, grad_values,
    left_part, right_part, pair_shapes, gains, decoder_gains,
):
    (
        query, key, value, shares, context, hidden, normed_two,
        active, rise, memory, unused_keys, unused_values, normed_one,
    ) = kept
    many, width = tokens.shape
    depth, narrow, wide = width // count, jnp.bfloat16, jnp.float32
    pairs = len(pair_shapes)
    spans, left_at, right_at = [], 0, 0
    for own, columns in pair_shapes:
        spans.append((left_at, right_at))
        left_at, right_at = left_at + -(-own // 128) * 128, right_at + columns
    dma, vmem = pltpu.SemaphoreType.DMA, pltpu.VMEM
    pieces = [(depth, width), (2 * depth, width // 2)] + [(depth, width // 2)] * 6
    outs = [(depth, 4 * width), (4 * depth, width)] + [(depth, width)] * 6
    little = (16, width)
    scratch = [vmem((4, width, width), narrow)] + [vmem((width, width), narrow)] * 2
    scratch += [vmem((2, width, width), narrow), vmem((4, width, width // 2), narrow)]
    scratch += [vmem((width, width // 2), narrow)] * 6
    scratch += [vmem((count,) + piece, narrow) for piece in pieces]
    scratch += [vmem(pieces[2], narrow)] * 6
    scratch += [vmem((count,) + piece, narrow) for piece in pieces[:2]]
    scratch += [vmem(left_part.shape, narrow), vmem((count,) + right_part.shape, narrow)]
    scratch += [vmem(s, narrow) for s in pair_shapes]
    scratch += [vmem((r, c // 2), narrow) for r, c in pair_shapes] * 2
    scratch += [vmem(little, wide)] * 4 + [vmem((count,) + little, wide)]
    scratch += [
        vmem((6, many, width), narrow), vmem((3, many, width), wide),
        vmem((4, width, width), narrow), vmem((2,) + shares.shape[2:], narrow),
        vmem((2 * BLOCK, 3 * BLOCK), wide),
    ]
    scratch += [vmem((many // rows, 2 * KV), wide)] * 2
    scratch += [
        dma((2, 8)), dma((8, count)), dma((8, count)), dma((2, 2, count)), dma((8, 8)),
        dma((count,)), dma((count,)), dma((2, count)), dma((2, count)), dma((6, pairs)),
        dma((4,)), dma((count,)), dma((count,)), dma((48,)), dma((2 + many // TILE,)),
    ]
    shapes = [jax.ShapeDtypeStruct(s, narrow) for s in outs + list(pair_shapes)]
    shapes += [jax.ShapeDtypeStruct(little, wide), jax.ShapeDtypeStruct((many, width), wide)]
    anywhere = pl.BlockSpec(memory_space=pl.ANY)
    local = pl.BlockSpec(memory_space=pltpu.VMEM)
    got = pl.pallas_call(
        functools.partial(backward_kernel, count, rows, spans),
        out_shape=shapes,
        in_specs=[anywhere] * 23 + [local] * 4,
        out_specs=[local] * (len(shapes) - 1) + [anywhere],
        scratch_shapes=scratch,
        compiler_params=pltpu.CompilerParams(
            collective_id=3, has_side_effects=True, vmem_limit_bytes=63 * 2**20
        ),
        name="backward",
    )(
        whole[4], whole[5], whole[0], whole[1], whole[2], whole[3], whole[6], whole[7],
        active, rise, normed_two, context, query, key, value, normed_one, tokens, memory,
        grad_keys, grad_values, cotangent, hidden, shares,
        left_part, right_part, gains, decoder_gains,
    )
    return got[:8], got[8 : 8 + pairs], got[-2], got[-1]


def backward_apart(
    count, rows, whole, kept, tokens, cotangent, grad_cross_keys, grad_cross_values,
    left_part, right_part, pair_shapes, gains, decoder_gains,
):
    (
        query_full, key_full, value_full, output_full, inner_full, outer_full, cross_key_full,
        cross_value_full,
    ) = whole[:8]
    (
        query_all, key_all, value_all, shares, context, hidden, normed_two,
        active, rise, memory, unused_keys, unused_values, normed_one,
    ) = kept
    row_count, length = rows, tokens.shape[0] // rows
    gain_one, gain_two = gains[0], gains[1]
    field = tokens.astype(jnp.float32)
    scale_one, scale_two = root_scale(field), root_scale(hidden)
    grad_cross_key = product_left(memory, grad_cross_keys)
    grad_cross_value = product_left(memory, grad_cross_values)
    grad_memory = product_right(grad_cross_keys, cross_key_full) + product_right(
        grad_cross_values, cross_value_full
    )
    grad_encoded = cotangent.astype(jnp.float32) + grad_memory
    grad_branch = grad_encoded.astype(jnp.bfloat16)
    grad_outer = product_left(active, grad_branch)
    grad_active = product_right(grad_branch, outer_full)
    grad_before = (grad_active * rise).astype(jnp.bfloat16)
    grad_inner = product_left(normed_two, grad_before)
    grad_normed = product_right(grad_before, inner_full)
    field_part, grad_gain_two = norm_back(
        grad_normed, hidden, scale_two, gain_two
    )
    grad_hidden = grad_encoded + field_part
    grad_branch = grad_hidden.astype(jnp.bfloat16)
    grad_output = product_left(context, grad_branch)
    grad_context = product_right(grad_branch, output_full).astype(jnp.bfloat16)
    grad_query_all, grad_key_all, grad_value_all, bias_sums = attend_rows_back(
        row_count, length, query_all, key_all, value_all, grad_context, shares
    )
    grad_query = product_left(normed_one, grad_query_all)
    grad_key = product_left(normed_one, grad_key_all)
    grad_value = product_left(normed_one, grad_value_all)
    grad_normed = (
        product_right(grad_query_all, query_full)
        + product_right(grad_key_all, key_full)
        + product_right(grad_value_all, value_full)
    )
    field_part, grad_gain_one = norm_back(
        grad_normed, field, scale_one, gain_one
    )
    tokens_grad = grad_hidden + field_part
    small = jnp.concatenate([
        jnp.stack([grad_gain_one, grad_gain_two]),
        decoder_gains,
        bias_sums.reshape(HEADS // 2, -1),
        jnp.zeros((5, tokens.shape[1]), jnp.float32),
    ])
    encoder_grads = (
        grad_inner, grad_outer, grad_query, grad_key, grad_value, grad_output,
        grad_cross_key, grad_cross_value,
    )
    encoder_sums, decoder_sums, small_sum = reduce_grads(
        count,
        ENCODER_KINDS,
        [
            g.astype(jnp.bfloat16).reshape(count, g.shape[0] // count, g.shape[1])
            for g in encoder_grads
        ],
        left_part,
        right_part,
        pair_shapes,
        small,
    )
    return encoder_sums, decoder_sums, small_sum, tokens_grad


def widen_kernel(*refs):
    half = len(refs) // 2
    for source, target in zip(refs[:half], refs[half:]):
        target[...] = source[...].astype(jnp.float32)


def widen(parts):
    local = pl.BlockSpec(memory_space=pltpu.VMEM)
    return pl.pallas_call(
        widen_kernel,
        out_shape=[jax.ShapeDtypeStruct(part.shape, jnp.float32) for part in parts],
        in_specs=[local] * len(parts),
        out_specs=[local] * len(parts),
        compiler_params=pltpu.CompilerParams(vmem_limit_bytes=48 * 2**20),
        name="widen",
    )(*parts)


def on_device(
    tokens,
    segment_index,
    start_vectors,
    first_gain,
    query_weight,
    key_weight,
    value_weight,
    output_weight,
    position_table,
    second_gain,
    inner_weight,
    outer_weight,
    start_gain,
    self_value,
    self_output,
    middle_gain,
    cross_query,
    cross_key,
    cross_value,
    cross_output,
    final_gain,
    decoder_inner,
    decoder_outer,
    encoded_cotangent,
    decoded_cotangent,
):
    row_count = segment_index.shape[0]
    length = segment_index.shape[1]
    slot_count = start_vectors.shape[1]
    width = tokens.shape[1]
    count = lax.axis_size("fsdp")
    depth = first_gain.shape[0]
    choices = jnp.arange(position_table.shape[0], dtype=jnp.int32)
    onehot = (offset_buckets()[None, :] == choices[:, None]).astype(jnp.float32)
    base = jnp.dot(position_table.T, onehot, precision=lax.Precision.HIGHEST)
    base = base.reshape(HEADS // 2, 2, 3 * BLOCK)
    column = jnp.broadcast_to(segment_index.reshape(-1, 1), (row_count * length, BLOCK))
    gains = jnp.stack([first_gain, second_gain, start_gain, middle_gain, final_gain])
    place = jnp.arange(width, dtype=jnp.int32) // depth
    gains = jnp.where(place == lax.axis_index("fsdp"), jnp.tile(gains, (1, count)), 0)
    shards = (
        query_weight, key_weight, value_weight, output_weight, inner_weight, outer_weight,
        cross_key, cross_value, self_value, self_output, cross_query, cross_output,
        decoder_inner, decoder_outer, jnp.pad(gains, ((0, 11), (0, 0))),
    )
    fused = count == 8 and depth % 32 == 0 and (row_count, length) == (2, 512)
    plan = forward if fused else forward_apart
    whole, all_gains, kept = plan(count, shards, tokens, column, segment_index, base)
    memory, cross_keys, cross_values = kept[9:12]
    token_count = row_count * slot_count
    (
        decoded, start_grad, decoder_gain_grads,
        normed_fin, decoder_active, normed_start, own_value, normed_mid, cross_context,
        decoder_before_grad, last_branch, grad_own, self_branch, grad_asking, cross_branch,
        grad_cross_keys, grad_cross_values,
    ) = decode(
        segment_index,
        start_vectors.reshape(token_count, width),
        decoded_cotangent.reshape(token_count, width),
        all_gains[2:5],
        cross_keys,
        cross_values,
        whole[8:14],
    )
    lefts = (normed_fin, decoder_active, normed_start, own_value, normed_mid, cross_context)
    rights = (decoder_before_grad, last_branch, grad_own, self_branch, grad_asking, cross_branch)
    pair_shapes = [(left.shape[1] // count, right.shape[1]) for left, right in zip(lefts, rights)]
    left_cols = []
    for left, (rows, unused) in zip(lefts, pair_shapes):
        columns = left.reshape(token_count, count, rows).transpose(1, 0, 2)
        left_cols.append(jnp.pad(columns, ((0, 0), (0, 0), (0, -rows % 128))))
    turn_back = backward if fused else backward_apart
    encoder_sums, decoder_sums, small_sum, tokens_grad = turn_back(
        count, row_count, whole, kept, tokens, encoded_cotangent,
        grad_cross_keys, grad_cross_values,
        jnp.concatenate(left_cols, axis=2),
        jnp.concatenate(rights, axis=1),
        pair_shapes, all_gains, decoder_gain_grads,
    )
    (
        inner_weight_grad, outer_weight_grad, query_weight_grad, key_weight_grad,
        value_weight_grad, output_weight_grad, cross_key_grad, cross_value_grad,
        decoder_inner_grad, decoder_outer_grad, self_value_grad, self_output_grad,
        cross_query_grad, cross_output_grad,
    ) = widen([*encoder_sums, *decoder_sums])
    position_table_grad = lax.dot_general(
        onehot,
        small_sum[5:11].reshape(HEADS, 3 * BLOCK),
        (((1,), (1,)), ((), ())),
        precision=lax.Precision.HIGHEST,
    )
    own_gains = lax.dynamic_slice_in_dim(
        small_sum[:5], lax.axis_index("fsdp") * depth, depth, axis=1
    )
    first_gain_grad, second_gain_grad, start_gain_grad, middle_gain_grad, final_gain_grad = own_gains
    decoded = decoded.reshape(start_vectors.shape)
    start_grad = start_grad.reshape(start_vectors.shape)
    return (
        memory,
        decoded,
        tokens_grad,
        start_grad,
        first_gain_grad,
        query_weight_grad,
        key_weight_grad,
        value_weight_grad,
        output_weight_grad,
        position_table_grad,
        second_gain_grad,
        inner_weight_grad,
        outer_weight_grad,
        start_gain_grad,
        self_value_grad,
        self_output_grad,
        middle_gain_grad,
        cross_query_grad,
        cross_key_grad,
        cross_value_grad,
        cross_output_grad,
        final_gain_grad,
        decoder_inner_grad,
        decoder_outer_grad,
    )


def solution(mesh):
    placed = (
        P(("dp", "fsdp"), None),
        P(("dp", "fsdp"), None),
        P(("dp", "fsdp"), None, None),
        P("fsdp"),
        P("fsdp", None),
        P("fsdp", None),
        P("fsdp", None),
        P("fsdp", None),
        P(),
        P("fsdp"),
        P("fsdp", None),
        P("fsdp", None),
        P("fsdp"),
        P("fsdp", None),
        P("fsdp", None),
        P("fsdp"),
        P("fsdp", None),
        P("fsdp", None),
        P("fsdp", None),
        P("fsdp", None),
        P("fsdp"),
        P("fsdp", None),
        P("fsdp", None),
        P(("dp", "fsdp"), None),
        P(("dp", "fsdp"), None, None),
    )
    return jax.shard_map(
        on_device,
        mesh=mesh,
        in_specs=placed,
        out_specs=(
            P(("dp", "fsdp"), None),
            P(("dp", "fsdp"), None, None),
            P(("dp", "fsdp"), None),
            P(("dp", "fsdp"), None, None),
            P("fsdp"),
            P("fsdp", None),
            P("fsdp", None),
            P("fsdp", None),
            P("fsdp", None),
            P(),
            P("fsdp"),
            P("fsdp", None),
            P("fsdp", None),
            P("fsdp"),
            P("fsdp", None),
            P("fsdp", None),
            P("fsdp"),
            P("fsdp", None),
            P("fsdp", None),
            P("fsdp", None),
            P("fsdp", None),
            P("fsdp"),
            P("fsdp", None),
            P("fsdp", None),
        ),
        check_vma=False,
    )
```

```python
import functools

import jax
import jax.numpy as jnp
from jax import lax
from jax.experimental import pallas as pl
from jax.experimental.pallas import tpu as pltpu
from jax.sharding import PartitionSpec as P

HEADS = 12
KV = 64
BLOCK = 128


epsilon = 1e-06
negative_fill = -1e30
bucket_edges = (12, 16, 23, 32, 46, 64, 91)


MESH = pl.DeviceIdType.MESH
KINDS = (
    "square", "square", "square", "square", "wide", "tall", "square", "square",
    "square", "square", "square", "square", "wide", "tall", "small",
)


def ring_position(index, count):
    if count == 64:
        slow, rest = index // 32, index % 32
        row, column = rest // 8, rest % 8
        place = row * 8 + column + (row % 2) * (7 - 2 * column)
        return place + slow * (count - 1 - 2 * place)
    across, along = index % 2, index // 2
    return along + across * (count - 1 - 2 * along)


def ring_index(position, count):
    position = lax.rem(position, count)
    across = position // (count // 2)
    along = position + across * (count - 1 - 2 * position)
    if count == 64:
        row, column = along // 8, along % 8
        return across * 32 + row * 8 + column + (row % 2) * (7 - 2 * column)
    return 2 * along + across


class Spot:
    def __init__(self, count):
        self.count = count
        self.dp = lax.axis_index("dp")
        self.fsdp = lax.axis_index("fsdp")
        self.core = lax.rem(self.dp, 2)
        self.plane = self.dp // 2
        self.place = ring_position(self.fsdp, count)
        self.sibling = (self.dp + 1 - 2 * self.core, self.fsdp)
        self.opposite = (lax.rem(self.dp + 2, 4), self.fsdp)
        self.after = (self.dp, ring_index(self.place + 1, count))
        self.before = (self.dp, ring_index(self.place + count - 1, count))

    def greet(self, others=()):
        barrier = pltpu.get_barrier_semaphore()
        partners = (self.sibling, self.opposite, self.after, self.before) + tuple(others)
        for partner in partners:
            pl.semaphore_signal(barrier, inc=1, device_id=partner, device_id_type=MESH)
        pl.semaphore_wait(barrier, len(partners))


def cut(kind, ref, plane, core):
    rows, columns = ref.shape
    if kind == "small":
        return ref
    if kind == "square":
        half = columns // 2
        return ref.at[:, pl.ds(pl.multiple_of(core * half, 128), half)]
    if kind == "wide":
        quarter = columns // 4
        return ref.at[:, pl.ds(pl.multiple_of((core * 2 + plane) * quarter, 128), quarter)]
    half, upper = columns // 2, rows // 2
    return ref.at[
        pl.ds(pl.multiple_of(plane * upper, 8), upper),
        pl.ds(pl.multiple_of(core * half, 128), half),
    ]


def send(source, target, send_sem, recv_sem, device):
    return pltpu.make_async_remote_copy(
        src_ref=source,
        dst_ref=target,
        send_sem=send_sem,
        recv_sem=recv_sem,
        device_id=device,
        device_id_type=MESH,
    )


def gather_kernel(count, kinds, *refs):
    total = len(kinds)
    shards, fulls = refs[:total], refs[total : 2 * total]
    ring_out, ring_in, near_out, near_in, far_out, far_in, last_out, last_in, own_sem = refs[
        2 * total :
    ]
    spot = Spot(count)
    split = [i for i in range(total) if kinds[i] in ("wide", "tall")]

    window = min(count, 8)

    def slot_of(i, step):
        turn = step if i % 2 else count - step
        return ring_index(spot.place + turn, count)

    def ring_copy(i, step, source=None):
        here = cut(kinds[i], fulls[i].at[slot_of(i, step)], spot.plane, spot.core)
        return send(
            here if source is None else source,
            here,
            ring_out.at[i, lax.rem(step, window)],
            ring_in.at[i, step],
            spot.before if i % 2 else spot.after,
        )

    def near_copy(i, step):
        here = cut(kinds[i], fulls[i].at[slot_of(i, step)], spot.plane, spot.core)
        out = near_out.at[i, lax.rem(step, window)]
        return send(here, here, out, near_in.at[i, step], spot.sibling)

    def far_copy(i, step):
        here = cut(kinds[i], fulls[i].at[slot_of(i, step)], spot.plane, spot.core)
        at = split.index(i)
        out = far_out.at[at, lax.rem(step, window)]
        return send(here, here, out, far_in.at[at, step], spot.opposite)

    def last_copy(i, step):
        here = cut(kinds[i], fulls[i].at[slot_of(i, step)], 1 - spot.plane, spot.core)
        at = split.index(i)
        out = last_out.at[at, lax.rem(step, window)]
        return send(here, here, out, last_in.at[at, step], spot.sibling)

    def start(copy, i, step, first):
        if window < count:

            @pl.when(step >= first + window)
            def _():
                copy(i, step - window).wait_send()

        copy(i, step).start()

    def finish(copy, i, first, end):
        def one(step, carry):
            copy(i, step).wait_send()
            return carry

        lax.fori_loop(max(first, end - window), end, one, 0)

    owns = []
    for i in range(total):
        owns.append(pltpu.make_async_copy(shards[i], fulls[i].at[spot.fsdp], own_sem.at[i]))
        owns[-1].start()
    spot.greet()
    for i in range(total):
        ring_copy(i, 0, cut(kinds[i], shards[i], spot.plane, spot.core)).start()

    def one_step(step, carry):
        for i in range(total):
            ring_copy(i, step - 1).wait_recv()

            @pl.when(step < count - 1)
            def _():
                start(ring_copy, i, step, 0)

            if kinds[i] != "small":
                start(near_copy, i, step, 1)
            if i in split:
                start(far_copy, i, step, 1)

        @pl.when(step > 1)
        def _():
            for i in split:
                far_copy(i, step - 1).wait_recv()
                start(last_copy, i, step - 1, 1)

        return carry

    lax.fori_loop(1, count, one_step, 0)
    for i in split:
        far_copy(i, count - 1).wait_recv()
        start(last_copy, i, count - 1, 1)

    def settle(step, carry):
        for i in range(total):
            if kinds[i] != "small":
                near_copy(i, step).wait_recv()
            if i in split:
                last_copy(i, step).wait_recv()
        return carry

    lax.fori_loop(1, count, settle, 0)
    for i in range(total):
        finish(ring_copy, i, 0, count - 1)
        if kinds[i] != "small":
            finish(near_copy, i, 1, count)
        if i in split:
            finish(far_copy, i, 1, count)
            finish(last_copy, i, 1, count)
    for copy in owns:
        copy.wait()


def gather_weights(count, shards, kinds):
    total = len(shards)
    split = sum(kind in ("wide", "tall") for kind in kinds)
    window = min(count, 8)
    many, few = [
        [pltpu.SemaphoreType.DMA((rows, window)), pltpu.SemaphoreType.DMA((rows, count))] * 2
        for rows in (total, split)
    ]
    return pl.pallas_call(
        functools.partial(gather_kernel, count, kinds),
        out_shape=[jax.ShapeDtypeStruct((count,) + s.shape, s.dtype) for s in shards],
        in_specs=[pl.BlockSpec(memory_space=pl.ANY)] * total,
        out_specs=[pl.BlockSpec(memory_space=pl.ANY)] * total,
        scratch_shapes=many + few + [pltpu.SemaphoreType.DMA((total,))],
        compiler_params=pltpu.CompilerParams(collective_id=0, has_side_effects=True),
        name="gather_weights",
    )(*shards)

def plus(*terms):
    total = terms[0].astype(jnp.float32)
    for term in terms[1:]:
        total = total + term.astype(jnp.float32)
    return total


def half_of(core, columns):
    half = columns // 2
    return pl.ds(pl.multiple_of(core * half, 128), half)


def plane_part(kind, plane, rows, columns):
    if kind == "wide":
        return slice(None), pl.ds(pl.multiple_of(plane * (columns // 2), 128), columns // 2)
    if kind == "tall":
        return pl.ds(pl.multiple_of(plane * (rows // 2), 8), rows // 2), slice(None)
    return slice(None), slice(None)


ENCODER_KINDS = ("wide", "tall", "square", "square", "square", "square", "square", "square")


def reduce_kernel(count, kinds, spans, *refs):
    total, pairs = len(kinds), len(spans)
    refs = list(refs)

    def take(size):
        got = refs[:size]
        del refs[:size]
        return got

    grads = take(total)
    left_part, right_part, small = take(3)
    sums = take(total)
    pair_sums = take(pairs)
    (small_sum,) = take(1)
    half, work, final = take(total), take(total), take(total)
    split = [i for i in range(total) if kinds[i] != "square"]
    far = take(len(split))
    left_all, right_all = take(2)
    pair_half, pair_far, pair_work = take(pairs), take(pairs), take(pairs)
    small_near, small_mid, small_far, small_all = take(4)
    (
        near_sem, ring_out, ring_in, far_sem, end_sem, left_out, left_in,
        right_out, right_in, pair_sem, small_sem, small_out, small_in,
    ) = take(13)
    spot = Spot(count)
    core, plane = spot.core, spot.plane
    diagonal = (lax.rem(spot.dp + 2, 4) + 1 - 2 * core, spot.fsdp)

    def peer(k):
        return (spot.dp, lax.rem(spot.fsdp + k, count))

    barrier = pltpu.get_barrier_semaphore()
    for partner in (spot.sibling, spot.opposite, diagonal):
        pl.semaphore_signal(barrier, inc=1, device_id=partner, device_id_type=MESH)

    def greet(k, carry):
        pl.semaphore_signal(barrier, inc=1, device_id=peer(k), device_id_type=MESH)
        return carry

    lax.fori_loop(1, count, greet, 0)
    pl.semaphore_wait(barrier, count + 2)

    def near_copy(i):
        columns = grads[i].shape[2]
        return send(
            grads[i].at[:, :, half_of(1 - core, columns)], half[i],
            near_sem.at[0, i], near_sem.at[1, i], spot.sibling,
        )

    def slot_at(i, step):
        turn = step + 1 if i % 2 else count - 1 - step
        return ring_index(spot.place + turn, count)

    def far_copy(i, step):
        at = split.index(i)
        rows, columns = half[i].shape[1:]
        part = plane_part(kinds[i], 1 - plane, rows, columns)
        return send(
            half[i].at[(slot_at(i, step),) + part], far[at].at[step],
            far_sem.at[0, at, step], far_sem.at[1, at, step], spot.opposite,
        )

    def ring_copy(i, step):
        return send(
            work[i].at[step], work[i].at[step + 1], ring_out.at[i, step], ring_in.at[i, step],
            spot.before if i % 2 else spot.after,
        )

    def left_copy(k):
        other = lax.rem(spot.fsdp + k, count)
        return send(
            left_part.at[other], left_all.at[spot.fsdp], left_out.at[k], left_in.at[k], peer(k)
        )

    def right_copy(way, step):
        turn = step if way else count - step
        slot = ring_index(spot.place + turn, count)
        width = right_part.shape[1] // 2
        here = right_all.at[slot, :, way * width : (way + 1) * width]
        return send(
            here, here, right_out.at[way, step], right_in.at[way, step],
            spot.before if way else spot.after,
        )

    for i in range(total):
        near_copy(i).start()
    near_small = send(small, small_near, small_sem.at[0], small_sem.at[1], spot.sibling)
    near_small.start()

    def left_start(k, carry):
        left_copy(k).start()
        return carry

    lax.fori_loop(1, count, left_start, 0)
    right_all[spot.fsdp] = right_part[...]
    left_all[spot.fsdp] = left_part[spot.fsdp]
    for way in range(2):
        right_copy(way, 0).start()
    near_small.wait()
    small_mid[...] = small[...] + small_near[...]
    far_small = send(small_mid, small_far, small_sem.at[2], small_sem.at[3], spot.opposite)
    far_small.start()

    for i in range(total):
        near_copy(i).wait_recv()

        def join(slot, carry):
            mine = grads[i][slot, :, half_of(core, grads[i].shape[2])]
            half[i][slot] = plus(half[i][slot], mine).astype(jnp.bfloat16)
            return carry

        lax.fori_loop(0, count, join, 0)
        if i in split:

            def far_start(step, carry):
                far_copy(i, step).start()
                return carry

            lax.fori_loop(0, count, far_start, 0)

    far_small.wait()
    small_all[spot.fsdp] = small_mid[...] + small_far[...]

    def small_copy(k):
        here = small_all.at[spot.fsdp]
        return send(here, here, small_out.at[k], small_in.at[k], peer(k))

    def small_start(k, carry):
        small_copy(k).start()
        return carry

    lax.fori_loop(1, count, small_start, 0)

    def right_step(step, carry):
        for way in range(2):
            right_copy(way, step - 1).wait_recv()

            @pl.when(step < count - 1)
            def _():
                right_copy(way, step).start()

        return carry

    lax.fori_loop(1, count, right_step, 0)

    def left_wait(k, carry):
        left_copy(k).wait_recv()
        return carry

    lax.fori_loop(1, count, left_wait, 0)

    def pair_near(j):
        columns = pair_sums[j].shape[1]
        return send(
            pair_work[j].at[:, half_of(1 - core, columns)], pair_half[j],
            pair_sem.at[0, j], pair_sem.at[1, j], spot.sibling,
        )

    def pair_across(j):
        return send(
            pair_half[j], pair_far[j], pair_sem.at[2, j], pair_sem.at[3, j], spot.opposite
        )

    def pair_end(j):
        here = pair_sums[j].at[:, half_of(core, pair_sums[j].shape[1])]
        return send(here, here, pair_sem.at[4, j], pair_sem.at[5, j], spot.sibling)

    for j, (left_at, right_at) in enumerate(spans):
        rows, columns = pair_sums[j].shape
        span = -(-rows // 128) * 128
        left = left_all[:, :, left_at : left_at + span].reshape(-1, span)
        for begin in range(0, columns, 768):
            right = right_all[:, :, right_at + begin : right_at + begin + 768].reshape(-1, 768)
            block = lax.dot_general(
                left, right, (((0,), (0,)), ((), ())), preferred_element_type=jnp.float32
            )
            pair_work[j][:, begin : begin + 768] = block[:rows].astype(jnp.bfloat16)
        pair_near(j).start()
    for j in range(pairs):
        pair_near(j).wait()
        mine = pair_work[j][:, half_of(core, pair_sums[j].shape[1])]
        pair_half[j][...] = plus(pair_half[j][...], mine).astype(jnp.bfloat16)
        pair_across(j).start()

    def one_step(step, carry):
        for i in range(total):
            rows, columns = half[i].shape[1:]
            slot = slot_at(i, step)
            value = half[i][(slot,) + plane_part(kinds[i], plane, rows, columns)]
            value = value.astype(jnp.float32)
            if i in split:
                far_copy(i, step).wait_recv()
                value = value + far[split.index(i)][step].astype(jnp.float32)

            @pl.when(step > 0)
            def _():
                ring_copy(i, step - 1).wait_recv()
                work[i][step] = plus(value, work[i][step]).astype(jnp.bfloat16)

            @pl.when(step == 0)
            def _():
                work[i][step] = value.astype(jnp.bfloat16)

            @pl.when(step < count - 1)
            def _():
                ring_copy(i, step).start()

        return carry

    lax.fori_loop(0, count, one_step, 0)

    def end_across(i):
        return send(
            work[i].at[count - 1], final[i], end_sem.at[0, i], end_sem.at[1, i], spot.opposite
        )

    def end_piece(i, mine_plane):
        rows, columns = sums[i].shape
        wide = half_of(core, columns)
        if kinds[i] == "square":
            return sums[i].at[:, wide]
        return cut(kinds[i], sums[i], mine_plane, core)

    def end_copies(i):
        here = end_piece(i, plane)
        copies = [send(here, here, end_sem.at[2, i], end_sem.at[3, i], spot.sibling)]
        if i in split:
            copies.append(send(here, here, end_sem.at[4, i], end_sem.at[5, i], spot.opposite))
            copies.append(send(here, here, end_sem.at[6, i], end_sem.at[7, i], diagonal))
        return copies

    for i in range(total):
        if i not in split:
            end_across(i).start()
    for i in split:
        end_piece(i, plane)[...] = work[i][count - 1]
        for copy in end_copies(i):
            copy.start()
    for j in range(pairs):
        pair_across(j).wait()
        here = half_of(core, pair_sums[j].shape[1])
        pair_sums[j][:, here] = plus(pair_half[j][...], pair_far[j][...]).astype(jnp.bfloat16)
        pair_end(j).start()
    for i in range(total):
        if i not in split:
            end_across(i).wait()
            value = plus(work[i][count - 1], final[i][...]).astype(jnp.bfloat16)
            end_piece(i, plane)[...] = value
            for copy in end_copies(i):
                copy.start()

    def small_wait(k, carry):
        small_copy(k).wait_recv()
        return carry

    lax.fori_loop(1, count, small_wait, 0)
    small_sum[...] = lax.fori_loop(
        1, count, lambda k, so_far: so_far + small_all[k], small_all[0]
    )
    for i in range(total):
        for copy in end_copies(i):
            copy.wait()
    for j in range(pairs):
        pair_end(j).wait()
    for i in range(total):
        near_copy(i).wait_send()

    def drain(step, carry):
        for i in split:
            far_copy(i, step).wait_send()
        return carry

    lax.fori_loop(0, count, drain, 0)

    def drain_ring(step, carry):
        for i in range(total):
            ring_copy(i, step).wait_send()
        for way in range(2):
            right_copy(way, step).wait_send()
        left_copy(step + 1).wait_send()
        small_copy(step + 1).wait_send()
        return carry

    lax.fori_loop(0, count - 1, drain_ring, 0)


def reduce_grads(count, kinds, grads, left_part, right_part, pair_shapes, small):
    total, pairs = len(kinds), len(pair_shapes)
    spans, left_at, right_at = [], 0, 0
    for rows, columns in pair_shapes:
        spans.append((left_at, right_at))
        left_at, right_at = left_at + -(-rows // 128) * 128, right_at + columns
    narrow = jnp.bfloat16
    blocks = [g.shape[1:] for g in grads]
    pieces = []
    for kind, (rows, columns) in zip(kinds, blocks):
        if kind == "wide":
            pieces.append((rows, columns // 4))
        elif kind == "tall":
            pieces.append((rows // 2, columns // 2))
        else:
            pieces.append((rows, columns // 2))
    split = [i for i in range(total) if kinds[i] != "square"]
    dma = pltpu.SemaphoreType.DMA
    scratch = [pltpu.VMEM((count, r, c // 2), narrow) for r, c in blocks]
    scratch += [pltpu.VMEM((count, r, c), narrow) for r, c in pieces]
    scratch += [pltpu.VMEM((r, c), narrow) for r, c in pieces]
    scratch += [pltpu.VMEM((count,) + pieces[i], narrow) for i in split]
    scratch += [
        pltpu.VMEM(left_part.shape, narrow),
        pltpu.VMEM((count,) + right_part.shape, narrow),
    ]
    scratch += [pltpu.VMEM((r, c // 2), narrow) for r, c in pair_shapes] * 2
    scratch += [pltpu.VMEM((r, c), narrow) for r, c in pair_shapes]
    scratch += [pltpu.VMEM(small.shape, jnp.float32)] * 3
    scratch += [pltpu.VMEM((count,) + small.shape, jnp.float32)]
    scratch += [
        dma((2, total)), dma((total, count)), dma((total, count)), dma((2, len(split), count)),
        dma((8, total)), dma((count,)), dma((count,)), dma((2, count)), dma((2, count)),
        dma((6, pairs)), dma((4,)), dma((count,)), dma((count,)),
    ]
    outs = [jax.ShapeDtypeStruct(b, narrow) for b in blocks]
    outs += [jax.ShapeDtypeStruct(s, narrow) for s in pair_shapes]
    outs += [jax.ShapeDtypeStruct(small.shape, jnp.float32)]
    got = pl.pallas_call(
        functools.partial(reduce_kernel, count, kinds, spans),
        out_shape=outs,
        in_specs=[pl.BlockSpec(memory_space=pltpu.VMEM)] * (total + 3),
        out_specs=[pl.BlockSpec(memory_space=pltpu.VMEM)] * len(outs),
        scratch_shapes=scratch,
        compiler_params=pltpu.CompilerParams(
            collective_id=1, has_side_effects=True, vmem_limit_bytes=62 * 2**20
        ),
        name="reduce_grads",
    )(*grads, left_part, right_part, small)
    return got[:total], got[total : total + pairs], got[-1]


def product(left, right):
    return jnp.dot(left, right, preferred_element_type=jnp.float32)


def product_left(left, right):
    return lax.dot_general(
        left, right, (((0,), (0,)), ((), ())), preferred_element_type=jnp.float32
    )


def product_right(left, right):
    return lax.dot_general(
        left, right, (((1,), (1,)), ((), ())), preferred_element_type=jnp.float32
    )


def root_scale(field):
    return lax.rsqrt(jnp.mean(field * field, axis=-1, keepdims=True) + epsilon)


def norm_back(grad_normed, field, scale, gain):
    gain_grad = jnp.sum(grad_normed * field * scale, axis=0)
    weighted = grad_normed * gain
    field_grad = scale * weighted - field * (scale * scale * scale) * jnp.mean(
        weighted * field, axis=-1, keepdims=True
    )
    return (field_grad, gain_grad)


def wide_heads(block):
    first = lax.broadcasted_iota(jnp.int32, block.shape, 1) < KV
    none = jnp.zeros_like(block)
    return jnp.concatenate([jnp.where(first, block, none), jnp.where(first, none, block)], axis=0)


def narrow_heads(stacked):
    half = stacked.shape[0] // 2
    first = lax.broadcasted_iota(jnp.int32, (half, stacked.shape[1]), 1) < KV
    return jnp.where(first, stacked[:half], stacked[half:])


def reach(at, blocks):
    low, high = max(0, at - 1), min(blocks, at + 2)
    begin = (low - at + 1) * BLOCK
    return slice(low * BLOCK, high * BLOCK), slice(begin, begin + (high - low) * BLOCK)


def bias_block(base):
    heads = []
    for at in range(2):
        level = jnp.broadcast_to(base[at : at + 1], (BLOCK, base.shape[1]))
        heads.append(pltpu.roll(level, 0, axis=1, stride=1, stride_axis=0))
    return jnp.concatenate(heads, axis=0)


def offset_sums(block):
    rows, width = block.shape
    while rows > 8:
        rows = rows // 2
        block = block[:rows] + pltpu.roll(block[rows:], width - rows, axis=1)
    place = lax.broadcasted_iota(jnp.int32, block.shape, 0)
    for bit in (4, 2, 1):
        block = jnp.where((place & bit) > 0, pltpu.roll(block, width - bit, axis=1), block)
    return jnp.sum(block, axis=0, keepdims=True)


def attend_kernel(column_ref, row_ref, base_ref, query_ref, key_ref, value_ref, out_ref, share_ref):
    blocks = query_ref.shape[0] // BLOCK
    bias = bias_block(base_ref[0])
    for at in range(blocks):
        keys, places = reach(at, blocks)
        own = slice(at * BLOCK, (at + 1) * BLOCK)
        scores = product_right(wide_heads(query_ref[own]), key_ref[keys]) + bias[:, places]
        allowed = column_ref[own, :1] == row_ref[0, :1, keys]
        scores = jnp.where(jnp.concatenate([allowed, allowed], axis=0), scores, negative_fill)
        powers = jnp.exp(scores - jnp.max(scores, axis=1, keepdims=True))
        shares = powers * (1.0 / jnp.sum(powers, axis=1, keepdims=True))
        shares = shares.astype(jnp.bfloat16)
        share_ref[0, 0, at, :, places] = shares
        mixed = product(shares, value_ref[keys])
        out_ref[own] = narrow_heads(mixed).astype(jnp.bfloat16)


def attend_back_kernel(
    query_ref, key_ref, value_ref, grad_ref, share_ref,
    grad_query_ref, grad_key_ref, grad_value_ref, sums_ref, bias_acc, key_acc, value_acc,
):
    blocks = query_ref.shape[0] // BLOCK

    @pl.when(pl.program_id(1) == 0)
    def _():
        bias_acc[...] = jnp.zeros_like(bias_acc)

    key_acc[...] = jnp.zeros_like(key_acc)
    value_acc[...] = jnp.zeros_like(value_acc)
    for at in range(blocks):
        keys, places = reach(at, blocks)
        own = slice(at * BLOCK, (at + 1) * BLOCK)
        query, grad = wide_heads(query_ref[own]), wide_heads(grad_ref[own])
        narrow_shares = share_ref[0, 0, at, :, places]
        shares = narrow_shares.astype(jnp.float32)
        value_acc[keys] += product_left(narrow_shares, grad)
        moved = shares * product_right(grad, value_ref[keys])
        grad_scores = moved - shares * jnp.sum(moved, axis=1, keepdims=True)
        bias_acc[:, places] += grad_scores
        narrow = grad_scores.astype(jnp.bfloat16)
        grad_query_ref[own] = narrow_heads(product(narrow, key_ref[keys])).astype(jnp.bfloat16)
        key_acc[keys] += product_left(narrow, query)
    grad_key_ref[...] = key_acc[...].astype(jnp.bfloat16)
    grad_value_ref[...] = value_acc[...].astype(jnp.bfloat16)

    @pl.when(pl.program_id(1) == pl.num_programs(1) - 1)
    def _():
        sums_ref[0] = jnp.concatenate(
            [offset_sums(bias_acc[:BLOCK]), offset_sums(bias_acc[BLOCK:])], axis=0
        )


def offset_buckets():
    offset = jnp.arange(3 * BLOCK, dtype=jnp.int32) - BLOCK
    distance = jnp.abs(offset)
    far_bucket = 8 + sum(((distance >= boundary).astype(jnp.int32) for boundary in bucket_edges))
    near_bucket = jnp.where(distance < 8, distance, far_bucket)
    return jnp.where(offset > 0, 16, 0) + near_bucket


def attend_rows(rows, length, column, segment_index, base, query, key, value):
    pairs = HEADS // 2
    part = pl.BlockSpec((length, 2 * KV), lambda r, p: (r, p))
    return pl.pallas_call(
        attend_kernel,
        grid=(rows, pairs),
        out_shape=[
            jax.ShapeDtypeStruct(query.shape, jnp.bfloat16),
            jax.ShapeDtypeStruct(
                (rows, pairs, length // BLOCK, 2 * BLOCK, 3 * BLOCK), jnp.bfloat16
            ),
        ],
        in_specs=[
            pl.BlockSpec((length, BLOCK), lambda r, p: (r, 0)),
            pl.BlockSpec((1, 1, length), lambda r, p: (r, 0, 0)),
            pl.BlockSpec((1, 2, 3 * BLOCK), lambda r, p: (p, 0, 0)),
            part, part, part,
        ],
        out_specs=[
            part,
            pl.BlockSpec(
                (1, 1, length // BLOCK, 2 * BLOCK, 3 * BLOCK), lambda r, p: (r, p, 0, 0, 0)
            ),
        ],
        compiler_params=pltpu.CompilerParams(vmem_limit_bytes=48 * 2**20),
        name="attend",
    )(column, segment_index.reshape(rows, 1, length), base, query, key, value)


def attend_rows_back(rows, length, query, key, value, grad, shares):
    pairs = HEADS // 2
    part = pl.BlockSpec((length, 2 * KV), lambda p, r: (r, p))
    return pl.pallas_call(
        attend_back_kernel,
        grid=(pairs, rows),
        out_shape=[jax.ShapeDtypeStruct(query.shape, jnp.bfloat16)] * 3
        + [jax.ShapeDtypeStruct((pairs, 2, 3 * BLOCK), jnp.float32)],
        in_specs=[
            part, part, part, part,
            pl.BlockSpec(
                (1, 1, length // BLOCK, 2 * BLOCK, 3 * BLOCK), lambda p, r: (r, p, 0, 0, 0)
            ),
        ],
        out_specs=[part, part, part, pl.BlockSpec((1, 2, 3 * BLOCK), lambda p, r: (p, 0, 0))],
        scratch_shapes=[
            pltpu.VMEM((2 * BLOCK, 3 * BLOCK), jnp.float32),
            pltpu.VMEM((length, 2 * KV), jnp.float32),
            pltpu.VMEM((length, 2 * KV), jnp.float32),
        ],
        compiler_params=pltpu.CompilerParams(vmem_limit_bytes=48 * 2**20),
        name="attend_back",
    )(query, key, value, grad, shares)


def gelu_parts(before):
    slope = 0.7978845608028654
    square = before * before
    bend = jnp.tanh(slope * (before + 0.044715 * before * square))
    half = 0.5 * (1.0 + bend)
    rise = half + 0.5 * before * (1.0 - bend * bend) * slope * (1.0 + 3 * 0.044715 * square)
    return before * half, rise


def slots_of(stacked, count):
    rows, columns = stacked.shape
    own = lax.broadcasted_iota(jnp.int32, (rows, columns), 0) // count
    head = lax.broadcasted_iota(jnp.int32, (rows, columns), 1) // KV
    return jnp.where(own == head, stacked, 0.0)


def decoder_kernel(rows, slots, *refs):
    (
        segment_ref, start_ref, cotangent_ref, gain_ref, keys_hbm, values_hbm, memory_hbm,
        self_value_hbm, self_output_hbm, cross_query_hbm, cross_output_hbm,
        inner_hbm, outer_hbm,
        decoded_ref, start_grad_ref, gain_grad_ref,
        normed_fin_ref, active_ref, normed_start_ref, own_ref, normed_mid_ref, context_ref,
        before_grad_ref, last_branch_ref, grad_own_ref, self_branch_ref, grad_asking_ref,
        cross_branch_ref, grad_keys_hbm, grad_values_hbm, encoded_hbm,
        keys_ref, values_ref, grad_keys_ref, grad_values_ref, memory_ref,
        self_value, self_output, cross_query, cross_output, inner, outer, sems,
    ) = refs
    loads = []
    for at, (source, target) in enumerate((
        (self_value_hbm, self_value), (self_output_hbm, self_output),
        (cross_query_hbm, cross_query), (cross_output_hbm, cross_output),
        (inner_hbm, inner), (outer_hbm, outer), (keys_hbm, keys_ref), (values_hbm, values_ref),
        (memory_hbm, memory_ref),
    )):
        loads.append(pltpu.make_async_copy(source, target, sems.at[at]))
        loads[-1].start()
    narrow = jnp.bfloat16
    length = keys_ref.shape[0] // rows
    start_gain, middle_gain, final_gain = gain_ref[2:3], gain_ref[3:4], gain_ref[4:5]

    start_field = start_ref[...].astype(jnp.float32)
    scale_start = root_scale(start_field)
    normed_start = (start_field * scale_start * start_gain).astype(narrow)
    normed_start_ref[...] = normed_start
    loads[0].wait()
    own = product(normed_start, self_value[...]).astype(narrow)
    own_ref[...] = own
    loads[1].wait()
    first_field = start_field + product(own, self_output[...])
    scale_mid = root_scale(first_field)
    normed_mid = (first_field * scale_mid * middle_gain).astype(narrow)
    normed_mid_ref[...] = normed_mid
    loads[2].wait()
    asking = product(normed_mid, cross_query[...]).astype(narrow).astype(jnp.float32)
    for copy in loads[6:]:
        copy.wait()
    stores = [pltpu.make_async_copy(memory_ref, encoded_hbm, sems.at[11])]
    stores[0].start()
    wides, all_shares, contexts = [], [], []
    for row in range(rows):
        part = asking[row * slots : (row + 1) * slots]
        wide = slots_of(jnp.concatenate([part] * HEADS, axis=0), slots).astype(narrow)
        span = slice(row * length, (row + 1) * length)
        scores = product_right(wide, keys_ref[span])
        slot = lax.rem(lax.broadcasted_iota(jnp.int32, scores.shape, 0), slots)
        scores = jnp.where(slot == segment_ref[row : row + 1], scores, negative_fill)
        powers = jnp.exp(scores - jnp.max(scores, axis=1, keepdims=True))
        shares = powers * (1.0 / jnp.sum(powers, axis=1, keepdims=True))
        mixed = slots_of(product(shares.astype(narrow), values_ref[span]), slots)
        contexts.append(jnp.sum(mixed.reshape(HEADS, slots, -1), axis=0))
        wides.append(wide)
        all_shares.append(shares)
    context = jnp.concatenate(contexts, axis=0).astype(narrow)
    context_ref[...] = context
    loads[3].wait()
    second_field = first_field + product(context, cross_output[...])
    scale_fin = root_scale(second_field)
    normed_fin = (second_field * scale_fin * final_gain).astype(narrow)
    normed_fin_ref[...] = normed_fin
    loads[4].wait()
    active, rise = gelu_parts(product(normed_fin, inner[...]))
    active = active.astype(narrow)
    active_ref[...] = active
    loads[5].wait()
    decoded_ref[...] = (second_field + product(active, outer[...])).astype(narrow)

    branch = cotangent_ref[...]
    last_branch_ref[...] = branch
    grad_second = branch.astype(jnp.float32)
    before_grad = (product_right(branch, outer[...]) * rise).astype(narrow)
    before_grad_ref[...] = before_grad
    grad_normed = product_right(before_grad, inner[...])
    moved, final_gain_grad = norm_back(grad_normed, second_field, scale_fin, final_gain)
    grad_second = grad_second + moved
    branch = grad_second.astype(narrow)
    cross_branch_ref[...] = branch
    grad_context = product_right(branch, cross_output[...]).astype(narrow).astype(jnp.float32)
    askings = []
    for row in range(rows):
        part = grad_context[row * slots : (row + 1) * slots]
        wide = slots_of(jnp.concatenate([part] * HEADS, axis=0), slots).astype(narrow)
        span = slice(row * length, (row + 1) * length)
        shares = all_shares[row]
        moved = shares * product_right(wide, values_ref[span])
        grad_scores = moved - shares * jnp.sum(moved, axis=1, keepdims=True)
        grad_scores = grad_scores.astype(narrow)
        grad_values_ref[span] = product_left(shares.astype(narrow), wide).astype(narrow)
        grad_keys_ref[span] = product_left(grad_scores, wides[row]).astype(narrow)
        mixed = slots_of(product(grad_scores, keys_ref[span]), slots)
        askings.append(jnp.sum(mixed.reshape(HEADS, slots, -1), axis=0))
    stores.append(pltpu.make_async_copy(grad_keys_ref, grad_keys_hbm, sems.at[9]))
    stores.append(pltpu.make_async_copy(grad_values_ref, grad_values_hbm, sems.at[10]))
    for copy in stores[1:]:
        copy.start()
    grad_asking = jnp.concatenate(askings, axis=0).astype(narrow)
    grad_asking_ref[...] = grad_asking
    grad_normed = product_right(grad_asking, cross_query[...])
    moved, middle_gain_grad = norm_back(grad_normed, first_field, scale_mid, middle_gain)
    grad_first = grad_second + moved
    branch = grad_first.astype(narrow)
    self_branch_ref[...] = branch
    grad_own = product_right(branch, self_output[...]).astype(narrow)
    grad_own_ref[...] = grad_own
    grad_normed = product_right(grad_own, self_value[...])
    moved, start_gain_grad = norm_back(grad_normed, start_field, scale_start, start_gain)
    start_grad_ref[...] = grad_first + moved
    gain_grad_ref[...] = jnp.concatenate(
        [start_gain_grad[None], middle_gain_grad[None], final_gain_grad[None]], axis=0
    )
    for copy in stores:
        copy.wait()


def decode(segment_index, start, cotangent, gains, keys, values, memory, weights):
    rows, tokens, width = segment_index.shape[0], start.shape[0], start.shape[1]
    narrow, hidden = jnp.bfloat16, weights[4].shape[1]
    few = jax.ShapeDtypeStruct((tokens, width), narrow)
    many = jax.ShapeDtypeStruct((tokens, hidden), narrow)
    outs = [
        few,
        jax.ShapeDtypeStruct((tokens, width), jnp.float32),
        jax.ShapeDtypeStruct((3, width), jnp.float32),
        few, many, few, few, few, few,
        many, few, few, few, few, few,
        jax.ShapeDtypeStruct(keys.shape, narrow),
        jax.ShapeDtypeStruct(values.shape, narrow),
        jax.ShapeDtypeStruct(memory.shape, narrow),
    ]
    anywhere = pl.BlockSpec(memory_space=pl.ANY)
    local = pl.BlockSpec(memory_space=pltpu.VMEM)
    return pl.pallas_call(
        functools.partial(decoder_kernel, rows, tokens // rows),
        out_shape=outs,
        in_specs=[local] * 4 + [anywhere] * 9,
        out_specs=[local] * (len(outs) - 3) + [anywhere] * 3,
        scratch_shapes=[pltpu.VMEM(keys.shape, narrow)] * 5
        + [pltpu.VMEM(w.shape, narrow) for w in weights]
        + [pltpu.SemaphoreType.DMA((12,))],
        compiler_params=pltpu.CompilerParams(vmem_limit_bytes=48 * 2**20),
        name="decode",
    )(segment_index, start, cotangent, gains, keys, values, memory, *weights)


TILE = 256


def rows_of(at, size=TILE):
    return pl.ds(pl.multiple_of(at * size, size), size)


FORWARD_KINDS = (
    "tall", "tall", "square", "square", "wide", "tall", "square", "square",
    "square", "square", "square", "square", "wide", "tall", "small",
)


class Gather:
    def __init__(self, spot, kinds, shards, fulls, staged, sems):
        self.spot, self.kinds, self.shards, self.fulls = spot, kinds, shards, fulls
        self.staged = staged
        (
            self.ring_out, self.ring_in, self.near_out, self.near_in,
            self.far_out, self.far_in, self.last_out, self.last_in, self.own_sem,
        ) = sems
        self.split = [i for i in range(len(kinds)) if kinds[i] in ("wide", "tall")]

    def piece(self, i, step, plane):
        count = self.spot.count
        slot = ring_index(self.spot.place + (step if i % 2 else count - step), count)
        rows = self.shards[i].shape[0]
        block = self.fulls[i].at[pl.ds(pl.multiple_of(slot * rows, 16), rows)]
        return cut(self.kinds[i], block, plane, self.spot.core)

    def own_copy(self, i):
        rows = self.shards[i].shape[0]
        block = self.fulls[i].at[pl.ds(pl.multiple_of(self.spot.fsdp * rows, 16), rows)]
        return pltpu.make_async_copy(self.staged.get(i, self.shards[i]), block, self.own_sem.at[i])

    def stage_copy(self, i):
        at = len(self.kinds) + list(self.staged).index(i)
        return pltpu.make_async_copy(self.shards[i], self.staged[i], self.own_sem.at[at])

    def ring_copy(self, i, step, source=None):
        here = self.piece(i, step, self.spot.plane)
        return send(
            here if source is None else source, here,
            self.ring_out.at[i, step], self.ring_in.at[i, step],
            self.spot.before if i % 2 else self.spot.after,
        )

    def near_copy(self, i, step):
        here = self.piece(i, step, self.spot.plane)
        return send(
            here, here, self.near_out.at[i, step], self.near_in.at[i, step], self.spot.sibling
        )

    def far_copy(self, i, step):
        here, at = self.piece(i, step, self.spot.plane), self.split.index(i)
        return send(
            here, here, self.far_out.at[at, step], self.far_in.at[at, step], self.spot.opposite
        )

    def last_copy(self, i, step):
        here, at = self.piece(i, step, 1 - self.spot.plane), self.split.index(i)
        return send(
            here, here, self.last_out.at[at, step], self.last_in.at[at, step], self.spot.sibling
        )

    def start(self, group):
        for i in group:
            source = cut(self.kinds[i], self.shards[i], self.spot.plane, self.spot.core)
            self.ring_copy(i, 0, source).start()

    def advance(self, group, step):
        count = self.spot.count
        for i in group:
            if step < count:
                self.ring_copy(i, step - 1).wait_recv()
                if step < count - 1:
                    self.ring_copy(i, step).start()
                if self.kinds[i] != "small":
                    self.near_copy(i, step).start()
                if i in self.split:
                    self.far_copy(i, step).start()
        for i in group:
            if step > 1 and i in self.split:
                self.far_copy(i, step - 1).wait_recv()
                self.last_copy(i, step - 1).start()

    def arrive(self, group):
        def one(step, carry):
            for i in group:
                if self.kinds[i] != "small":
                    self.near_copy(i, step).wait_recv()
                if i in self.split:
                    self.last_copy(i, step).wait_recv()
            return carry

        lax.fori_loop(1, self.spot.count, one, 0)
        for i in group:
            self.own_copy(i).wait()

    def settle(self, group):
        def one(step, carry):
            for i in group:
                self.ring_copy(i, step - 1).wait_send()
                if self.kinds[i] != "small":
                    self.near_copy(i, step).wait_send()
                if i in self.split:
                    self.far_copy(i, step).wait_send()
                    self.last_copy(i, step).wait_send()
            return carry

        lax.fori_loop(1, self.spot.count, one, 0)


FIRST, SECOND, THIRD = (0, 1, 2, 3, 14), (4, 5, 6, 7), (8, 9, 10, 11, 12, 13)


def forward_kernel(count, rows, *refs):
    refs = list(refs)

    def take(size):
        got = refs[:size]
        del refs[:size]
        return got

    shards = take(15)
    tokens, segment, base = take(3)
    weight_outs = take(14)
    (gain_out,) = take(1)
    (
        query_out, key_out, value_out, share_out, context_out, hidden_out, normed_two_out,
        active_out, rise_out, memory_out, cross_key_out, cross_value_out, normed_one_out,
    ) = take(13)
    held = take(8)
    gain_all, normed_one, query, key, value, context = take(6)
    hidden, normed_two, active, rise, memory, cross_keys, cross_values, shares = take(8)
    column, lines, bases = take(3)
    staged = dict(zip(THIRD, take(len(THIRD))))
    gather_sems = take(9)
    save_sem, share_sem = take(2)
    spot = Spot(count)
    fulls = held + weight_outs[8:] + [gain_all]
    gather = Gather(spot, FORWARD_KINDS, shards, fulls, staged, gather_sems)
    tiles = tokens.shape[0] // TILE
    length = tokens.shape[0] // rows
    blocks, pairs = length // BLOCK, HEADS // 2
    narrow = jnp.bfloat16
    saves = []

    def save(source, target):
        copy = pltpu.make_async_copy(source, target, save_sem.at[len(saves)])
        copy.start()
        saves.append(copy)

    def each_tile(body):
        def one(at, carry):
            body(rows_of(at), at)
            return carry

        lax.fori_loop(0, tiles, one, 0)

    for i in FIRST:
        gather.own_copy(i).start()
    spot.greet()
    gather.start(FIRST)
    for i in SECOND:
        gather.own_copy(i).start()
    for i in THIRD:
        gather.stage_copy(i).start()
    for pair in range(pairs):
        bases[pair, 0:2] = base[2 * pair : 2 * pair + 2]
    for row in range(rows):
        lines[row, 0:1] = segment[row : row + 1].astype(jnp.float32)
        for block in range(blocks):
            line = segment[row : row + 1, block * BLOCK : (block + 1) * BLOCK].astype(jnp.float32)
            begin = row * length + block * BLOCK
            column[begin : begin + BLOCK] = jnp.broadcast_to(line, (BLOCK, BLOCK)).T
    for step in range(1, 5):
        gather.advance(FIRST, step)
    gather.start(SECOND)
    for i in THIRD:
        gather.stage_copy(i).wait()
        gather.own_copy(i).start()
    for step in range(5, count):
        gather.advance(FIRST, step)
        gather.advance(SECOND, step - 4)
    gather.advance(FIRST, count)
    gather.arrive(FIRST)
    gain, width = jnp.zeros(gain_out.shape, jnp.float32), tokens.shape[1]
    depth = width // count
    lanes = lax.broadcasted_iota(jnp.int32, gain.shape, 1)
    for slot in range(count):
        part = gain_all[slot * 16 : (slot + 1) * 16].astype(jnp.float32)
        part = jnp.concatenate([part, jnp.zeros((16, width - part.shape[1]), jnp.float32)], axis=1)
        part = pltpu.roll(part, slot * depth, axis=1)
        gain = gain + jnp.where(lanes // depth == slot, part, 0.0)
    gain_out[...] = gain
    query_weight, key_weight, value_weight, output_weight = held[:4]
    inner_weight, outer_weight, cross_key_weight, cross_value_weight = held[4:]

    def first_norm(span, at):
        field = tokens[span].astype(jnp.float32)
        normed_one[span] = (field * root_scale(field) * gain_out[0:1]).astype(narrow)

    each_tile(first_norm)

    def project(target, weight):
        def body(span, at):
            target[span] = product(normed_one[span], weight[...]).astype(narrow)

        each_tile(body)

    project(query, query_weight)
    gather.advance(SECOND, 4)
    project(key, key_weight)
    gather.start(THIRD)
    project(value, value_weight)
    gather.advance(SECOND, 5)
    for source, target in (
        (normed_one, normed_one_out), (query, query_out), (key, key_out), (value, value_out),
    ):
        save(source, target)
    for i in range(4):
        save(held[i], weight_outs[i])

    def share_copy(at):
        return pltpu.make_async_copy(
            shares.at[lax.rem(at, 2)],
            share_out.at[at // pairs, lax.rem(at, pairs)],
            share_sem.at[lax.rem(at, 2)],
        )

    def attend_pair(at, carry):
        row, pair, buffer = at // pairs, lax.rem(at, pairs), lax.rem(at, 2)

        for turn, group, step in (
            (1, THIRD, 1), (2, SECOND, 6), (4, THIRD, 2), (5, SECOND, 7), (7, THIRD, 3),
            (8, SECOND, 8), (10, THIRD, 4),
        ):

            @pl.when(at == turn)
            def _():
                gather.advance(group, step)

        @pl.when(at >= 2)
        def _():
            share_copy(at - 2).wait()

        bias = bias_block(bases[pair, 0:2])
        columns = rows_of(pair, 2 * KV)

        def span(begin, size):
            return pl.ds(pl.multiple_of(row * length + begin, BLOCK), size)

        for block in range(blocks):
            keys, places = reach(block, blocks)
            own = span(block * BLOCK, BLOCK)
            near = span(keys.start, keys.stop - keys.start)
            scores = product_right(wide_heads(query[own, columns]), key[near, columns])
            scores = scores + bias[:, places]
            allowed = column[own, :1] == lines[row, 0:1, keys]
            scores = jnp.where(jnp.concatenate([allowed, allowed], axis=0), scores, negative_fill)
            powers = jnp.exp(scores - jnp.max(scores, axis=1, keepdims=True))
            part = powers * (1.0 / jnp.sum(powers, axis=1, keepdims=True))
            part = part.astype(narrow)
            shares[buffer, block, :, places] = part
            mixed = product(part, value[near, columns])
            context[own, columns] = narrow_heads(mixed).astype(narrow)
        share_copy(at).start()
        return carry

    lax.fori_loop(0, rows * pairs, attend_pair, 0)
    save(context, context_out)

    def second_norm(span, at):
        field = tokens[span].astype(jnp.float32) + product(context[span], output_weight[...])
        hidden[span] = field
        normed_two[span] = (field * root_scale(field) * gain_out[1:2]).astype(narrow)

    each_tile(second_norm)
    save(hidden, hidden_out)
    save(normed_two, normed_two_out)
    gather.advance(THIRD, 5)
    gather.arrive(SECOND)
    for i in range(4, 8):
        save(held[i], weight_outs[i])
    chunk = tokens.shape[1]

    def feed(span, at):
        @pl.when(at == 1)
        def _():
            gather.advance(THIRD, 6)

        @pl.when(at == 3)
        def _():
            gather.advance(THIRD, 7)

        for begin in range(0, active.shape[1], chunk):
            part = slice(begin, begin + chunk)
            level, slope = gelu_parts(product(normed_two[span], inner_weight[:, part]))
            active[span, part] = level.astype(narrow)
            rise[span, part] = slope.astype(narrow)
        full = hidden[span] + product(active[span], outer_weight[...])
        memory[span] = full.astype(narrow)

    each_tile(feed)
    save(active, active_out)
    save(rise, rise_out)
    save(memory, memory_out)

    def cross(span, at):
        cross_keys[span] = product(memory[span], cross_key_weight[...]).astype(narrow)
        cross_values[span] = product(memory[span], cross_value_weight[...]).astype(narrow)

    each_tile(cross)
    save(cross_keys, cross_key_out)
    save(cross_values, cross_value_out)
    gather.advance(THIRD, count)
    gather.arrive(THIRD)
    for group in (FIRST, SECOND, THIRD):
        gather.settle(group)
    for copy in saves:
        copy.wait()
    for at in range(rows * pairs - 2, rows * pairs):
        share_copy(at).wait()


def forward(count, shards, tokens, segment_index, base):
    rows, length = segment_index.shape
    many, width = tokens.shape
    hidden_width = shards[4].shape[1]
    narrow, wide = jnp.bfloat16, jnp.float32
    pairs, total = HEADS // 2, len(shards)
    split = sum(kind in ("wide", "tall") for kind in FORWARD_KINDS)
    weights = [(count * s.shape[0], s.shape[1]) for s in shards]
    few, much = (many, width), (many, hidden_width)
    share_shape = (rows, pairs, length // BLOCK, 2 * BLOCK, 3 * BLOCK)
    shapes = [(w, narrow) for w in weights[:14]] + [((16, width), wide)]
    shapes += [
        (few, narrow), (few, narrow), (few, narrow), (share_shape, narrow), (few, narrow),
        (few, wide), (few, narrow), (much, narrow), (much, narrow), (few, narrow), (few, narrow),
        (few, narrow), (few, narrow),
    ]
    dma = pltpu.SemaphoreType.DMA
    scratch = [pltpu.VMEM(w, narrow) for w in weights[:8]] + [pltpu.VMEM(weights[14], narrow)]
    scratch += [pltpu.VMEM(few, narrow)] * 5
    scratch += [
        pltpu.VMEM(few, wide), pltpu.VMEM(few, narrow), pltpu.VMEM(much, narrow),
        pltpu.VMEM(much, narrow), pltpu.VMEM(few, narrow), pltpu.VMEM(few, narrow),
        pltpu.VMEM(few, narrow), pltpu.VMEM((2,) + share_shape[2:], narrow),
    ]
    scratch += [pltpu.VMEM((many, BLOCK), wide), pltpu.VMEM((rows, 8, length), wide)]
    scratch += [pltpu.VMEM((pairs, 8, base.shape[1]), wide)]
    scratch += [pltpu.VMEM(shards[i].shape, narrow) for i in THIRD]
    scratch += [dma((total, count))] * 4 + [dma((split, count))] * 4
    scratch += [dma((total + len(THIRD),)), dma((24,)), dma((2,))]
    anywhere = pl.BlockSpec(memory_space=pl.ANY)
    local = pl.BlockSpec(memory_space=pltpu.VMEM)
    got = pl.pallas_call(
        functools.partial(forward_kernel, count, rows),
        out_shape=[jax.ShapeDtypeStruct(s, d) for s, d in shapes],
        in_specs=[anywhere] * total + [local] * 3,
        out_specs=[anywhere] * 14 + [local] + [anywhere] * 13,
        scratch_shapes=scratch,
        compiler_params=pltpu.CompilerParams(
            collective_id=2, has_side_effects=True, vmem_limit_bytes=62 * 2**20
        ),
        name="forward",
    )(*shards, tokens, segment_index, base)
    return got[:14], got[14], got[15:]


def forward_apart(count, shards, tokens, segment_index, base):
    rows, length = segment_index.shape
    narrow = jnp.bfloat16
    whole = gather_weights(count, shards, KINDS)
    depth, many = shards[0].shape[0], tokens.shape[0]
    gains = whole[14][:, :, :depth].astype(jnp.float32)
    gains = gains.transpose(1, 0, 2).reshape(16, count * depth)
    base = base.reshape(HEADS // 2, 2, 3 * BLOCK)
    column = jnp.broadcast_to(segment_index.reshape(-1, 1), (many, BLOCK))
    whole = [part.reshape(-1, part.shape[2]) for part in whole[:14]]
    field = tokens.astype(jnp.float32)
    normed_one = (field * root_scale(field) * gains[0]).astype(narrow)
    query, key, value = [product(normed_one, weight).astype(narrow) for weight in whole[:3]]
    context, shares = attend_rows(
        rows, length, column, segment_index, base, query, key, value
    )
    hidden = field + product(context, whole[3])
    normed_two = (hidden * root_scale(hidden) * gains[1]).astype(narrow)
    active, rise = gelu_parts(product(normed_two, whole[4]))
    active = active.astype(narrow)
    memory = (hidden + product(active, whole[5])).astype(narrow)
    cross_keys, cross_values = [product(memory, weight).astype(narrow) for weight in whole[6:8]]
    return whole, gains, (
        query, key, value, shares, context, hidden, normed_two,
        active, rise, memory, cross_keys, cross_values, normed_one,
    )


INNER, OUTER = 0, 1
SQUARES = (2, 3, 4, 5, 6, 7)


def backward_kernel(count, rows, spans, *refs):
    refs = list(refs)

    def take(size):
        got = refs[:size]
        del refs[:size]
        return got

    (
        inner_hbm, outer_hbm, query_weight_hbm, key_weight_hbm, value_weight_hbm,
        output_weight_hbm, cross_key_weight_hbm, cross_value_weight_hbm,
        active_hbm, rise_hbm, normed_two_hbm, context_hbm, query_hbm, key_hbm, value_hbm,
        normed_one_hbm, tokens_hbm, memory_hbm, grad_keys_hbm, grad_values_hbm, cotangent_hbm,
        hidden_hbm, shares_hbm,
    ) = take(23)
    left_part, right_part, gain, decoder_gains = take(4)
    sums, pairs = take(8), len(spans)
    pair_sums = take(pairs)
    small_sum, tokens_grad_hbm = take(2)
    big, flat, half, work, final, far = take(1)[0], take(2), take(8), take(8), take(6), take(2)
    left_all, right_all = take(2)
    pair_work, pair_half, pair_far = take(pairs), take(pairs), take(pairs)
    small, small_near, small_mid, small_far, small_all = take(5)
    pool, level, weights, shares, bias_acc, key_acc, value_acc = take(7)
    (
        near_sem, ring_out, ring_in, far_sem, end_sem, left_out, left_in,
        right_out, right_in, pair_sem, small_sem, small_out, small_in, load_sem, share_sem,
    ) = take(15)
    spot = Spot(count)
    core, plane = spot.core, spot.plane
    narrow = jnp.bfloat16
    many, width = level.shape[1:]
    tiles, length = many // TILE, many // rows
    blocks = length // BLOCK
    depth = width // count
    products = {2: big.at[0], 3: big.at[1], 4: big.at[2], 5: flat[0], 6: flat[0], 7: flat[1]}

    def peer(k):
        return (spot.dp, lax.rem(spot.fsdp + k, count))

    def slot_at(way, step):
        turn = step + 1 if way else count - 1 - step
        return ring_index(spot.place + turn, count)

    def near_copy(i):
        if i == INNER:
            source = big.at[pl.ds(2 * (1 - core), 2)]
        elif i == OUTER:
            source = big.at[:, :, half_of(1 - core, width)]
        else:
            source = products[i].at[:, half_of(1 - core, width)]
        return send(source, half[i], near_sem.at[0, i], near_sem.at[1, i], spot.sibling)

    def part_of(i, slot, side, way):
        rows_own = work[i].shape[2]
        if i == INNER:
            begin = slot * depth + way * rows_own
            return half[i].at[side, pl.ds(pl.multiple_of(begin, 16), rows_own)]
        if i == OUTER:
            begin = lax.rem(slot, 2) * 4 * depth + (2 * side + way) * rows_own
            return half[i].at[slot // 2, pl.ds(pl.multiple_of(begin, 16), rows_own)]
        begin = slot * depth + way * rows_own
        return half[i].at[pl.ds(pl.multiple_of(begin, 16), rows_own)]

    def far_copy(i, way, step):
        return send(
            part_of(i, slot_at(way, step), 1 - plane, way), far[i].at[way, step],
            far_sem.at[0, i, way, step], far_sem.at[1, i, way, step], spot.opposite,
        )

    def join(i):
        near_copy(i).wait()
        if i == INNER:

            def one(at, carry):
                side, span = at // 3, rows_of(lax.rem(at, 3))
                mine = big[2 * core + side, span]
                half[i][side, span] = plus(half[i][side, span], mine).astype(narrow)
                return carry

            lax.fori_loop(0, 6, one, 0)
        elif i == OUTER:

            def one(at, carry):
                side, span = at // 3, rows_of(lax.rem(at, 3))
                mine = big[side, span, half_of(core, width)]
                half[i][side, span] = plus(half[i][side, span], mine).astype(narrow)
                return carry

            lax.fori_loop(0, 12, one, 0)
        else:

            def one(at, carry):
                span = rows_of(at)
                mine = products[i][span, half_of(core, width)]
                half[i][span] = plus(half[i][span], mine).astype(narrow)
                return carry

            lax.fori_loop(0, 3, one, 0)
        if i in (INNER, OUTER):

            def far_start(step, carry):
                for way in range(2):
                    far_copy(i, way, step).start()
                return carry

            lax.fori_loop(0, count, far_start, 0)

    def ring_copy(i, way, step):
        return send(
            work[i].at[way, step], work[i].at[way, step + 1],
            ring_out.at[i, way, step], ring_in.at[i, way, step],
            spot.before if way else spot.after,
        )

    def advance(group, step):
        for i in group:
            for way in range(2):
                value = part_of(i, slot_at(way, step), plane, way)[...].astype(jnp.float32)
                if i in (INNER, OUTER):
                    far_copy(i, way, step).wait_recv()
                    value = value + far[i][way, step].astype(jnp.float32)

                @pl.when(step > 0)
                def _():
                    ring_copy(i, way, step - 1).wait_recv()
                    work[i][way, step] = plus(value, work[i][way, step]).astype(narrow)

                @pl.when(step == 0)
                def _():
                    work[i][way, step] = value.astype(narrow)

                @pl.when(step < count - 1)
                def _():
                    ring_copy(i, way, step).start()

    def run(group, first, last):
        def one(step, carry):
            advance(group, step)
            return carry

        lax.fori_loop(first, last, one, 0)

    def end_across(i):
        return send(
            work[i].at[:, count - 1], final[i - 2], end_sem.at[0, i], end_sem.at[1, i],
            spot.opposite,
        )

    def end_piece(i, side):
        if i == INNER:
            return cut("wide", sums[i], side, core)
        if i == OUTER:
            return cut("tall", sums[i], side, core)
        return sums[i].at[:, half_of(core, width)]

    def end_near(i):
        here = end_piece(i, plane)
        return send(here, here, end_sem.at[2, i], end_sem.at[3, i], spot.sibling)

    def end_far(i):
        here = end_piece(i, plane)
        return send(here, here, end_sem.at[4, i], end_sem.at[5, i], spot.opposite)

    def end_relay(i):
        here = end_piece(i, 1 - plane)
        return send(here, here, end_sem.at[6, i], end_sem.at[7, i], spot.sibling)

    def close(i):
        if i not in (INNER, OUTER):
            end_across(i).wait()
        here, rows_own = end_piece(i, plane), work[i].shape[2]
        for way in range(2):
            value = work[i][way, count - 1]
            if i not in (INNER, OUTER):
                value = plus(value, final[i - 2][way]).astype(narrow)
            here[way * rows_own : (way + 1) * rows_own] = value
        if i in (INNER, OUTER):
            end_far(i).start()
        end_near(i).start()

    def left_copy(k):
        other = lax.rem(spot.fsdp + k, count)
        return send(
            left_part.at[other], left_all.at[spot.fsdp], left_out.at[k], left_in.at[k], peer(k)
        )

    def right_copy(way, step):
        turn = step if way else count - step
        slot = ring_index(spot.place + turn, count)
        wide = right_part.shape[1] // 2
        here = right_all.at[slot, :, way * wide : (way + 1) * wide]
        return send(
            here, here, right_out.at[way, step], right_in.at[way, step],
            spot.before if way else spot.after,
        )

    def right_step(step):
        for way in range(2):
            right_copy(way, step - 1).wait_recv()
            if step < count - 1:
                right_copy(way, step).start()

    def pair_near(j):
        columns = pair_sums[j].shape[1]
        return send(
            pair_work[j].at[:, half_of(1 - core, columns)], pair_half[j],
            pair_sem.at[0, j], pair_sem.at[1, j], spot.sibling,
        )

    def pair_across(j):
        return send(
            pair_half[j], pair_far[j], pair_sem.at[2, j], pair_sem.at[3, j], spot.opposite
        )

    def pair_end(j):
        here = pair_sums[j].at[:, half_of(core, pair_sums[j].shape[1])]
        return send(here, here, pair_sem.at[4, j], pair_sem.at[5, j], spot.sibling)

    def small_copy(k):
        here = small_all.at[spot.fsdp]
        return send(here, here, small_out.at[k], small_in.at[k], peer(k))

    def each_peer(body):
        def one(k, carry):
            body(k)
            return carry

        lax.fori_loop(1, count, one, 0)

    def each_tile(body):
        def one(at, carry):
            body(rows_of(at))
            return carry

        lax.fori_loop(0, tiles, one, 0)

    used = []

    def load(source, target):
        copy = pltpu.make_async_copy(source, target, load_sem.at[len(used)])
        copy.start()
        used.append(copy)
        return copy

    def fold(target, left, right):
        def one(at, carry):
            span = rows_of(at)
            target[span] = product_left(left[:, span], right[...]).astype(narrow)
            return carry

        lax.fori_loop(0, width // TILE, one, 0)

    loads = [
        load(grad_keys_hbm, pool.at[4]), load(cross_key_weight_hbm, weights.at[0]),
        load(grad_values_hbm, pool.at[5]), load(cross_value_weight_hbm, weights.at[1]),
        load(cotangent_hbm, pool.at[2]), load(memory_hbm, pool.at[1]),
    ]

    def chunk_of(source, at):
        return source.at[:, pl.ds(at * width, width)]

    active_loads = {1: load(chunk_of(active_hbm, 1), pool.at[3])}
    hidden_load = load(hidden_hbm, level.at[2])
    out_loads = {0: load(outer_hbm.at[pl.ds(0, width)], weights.at[2])}
    barrier = pltpu.get_barrier_semaphore()
    for partner in (spot.sibling, spot.opposite):
        pl.semaphore_signal(barrier, inc=1, device_id=partner, device_id_type=MESH)
    each_peer(
        lambda k: pl.semaphore_signal(barrier, inc=1, device_id=peer(k), device_id_type=MESH)
    )
    pl.semaphore_wait(barrier, count + 1)
    each_peer(lambda k: left_copy(k).start())
    right_all[spot.fsdp] = right_part[...]
    left_all[spot.fsdp] = left_part[spot.fsdp]
    for way in range(2):
        right_copy(way, 0).start()
    small[...] = jnp.zeros_like(small)
    small[2:5] = decoder_gains[...]
    for copy in loads:
        copy.wait()

    def enter(span):
        value = pool[2, span].astype(jnp.float32)
        value = value + product_right(pool[4, span], weights[0])
        value = value + product_right(pool[5, span], weights[1])
        level[0, span] = value
        pool[0, span] = value.astype(narrow)

    each_tile(enter)
    active_loads[0] = load(chunk_of(active_hbm, 0), pool.at[2])
    in_loads = {
        at: load(chunk_of(inner_hbm, at), weights.at[at]) for at in range(2)
    }
    fold(flat[0], pool.at[1], pool.at[4])
    near_copy(6).start()
    fold(flat[1], pool.at[1], pool.at[5])
    near_copy(7).start()
    normed_load = load(normed_two_hbm, pool.at[1])
    context_load = load(context_hbm, pool.at[4])
    right_step(1)

    rise_loads = {}
    for at in range(4):
        buffer = 2 + at % 2
        active_loads[at].wait()
        fold(big.at[at], pool.at[buffer], pool.at[0])
        if at < 2:
            active_loads[at + 2] = load(chunk_of(active_hbm, at + 2), pool.at[buffer])
        else:
            rise_loads[at - 2] = load(chunk_of(rise_hbm, at - 2), pool.at[buffer])
        if at == 1:
            right_step(2)
            join(6)
            join(7)
        if at == 3:
            right_step(3)
        if at >= 2:
            advance((6, 7), at - 2)
    near_copy(OUTER).start()
    out_loads[1] = load(outer_hbm.at[pl.ds(width, width)], weights.at[3])

    normed_load.wait()
    for at in range(4):
        buffer = 2 + at % 2
        rise_loads[at].wait()
        out_loads[at].wait()
        in_loads[at].wait()

        def back(span):
            before = product_right(pool[0, span], weights[2 + at % 2])
            before = (before * pool[buffer, span].astype(jnp.float32)).astype(narrow)
            pool[buffer, span] = before
            moved = product_right(before, weights[at % 2])
            level[1, span] = moved if at == 0 else level[1, span] + moved

        each_tile(back)
        if at < 2:
            span = pl.ds((at + 2) * width, width)
            out_loads[at + 2] = load(outer_hbm.at[span], weights.at[2 + at % 2])
            in_loads[at + 2] = load(chunk_of(inner_hbm, at + 2), weights.at[at % 2])
        if at == 0:
            right_step(4)
            advance((6, 7), 2)
            join(OUTER)
        elif at == 1:
            right_step(6)
            advance((6, 7), 4)
            advance((OUTER,), 0)
        elif at == 2:
            advance((6, 7), 5)
            advance((OUTER,), 2)
        else:
            advance((6, 7), 7)
            for i in (6, 7):
                end_across(i).start()
            advance((OUTER,), 4)
        fold(big.at[at], pool.at[1], pool.at[buffer])
        if at < 2:
            rise_loads[at + 2] = load(chunk_of(rise_hbm, at + 2), pool.at[buffer])
        if at == 0:
            right_step(5)
            advance((6, 7), 3)
        elif at == 1:
            right_step(7)
            advance((OUTER,), 1)
        elif at == 2:
            advance((6, 7), 6)
            advance((OUTER,), 3)
        else:
            advance((OUTER,), 5)
    near_copy(INNER).start()
    query_load = load(query_hbm, pool.at[1])
    key_load, value_load = load(key_hbm, pool.at[2]), load(value_hbm, pool.at[3])
    late_loads = [
        load(query_weight_hbm, weights.at[0]), load(key_weight_hbm, weights.at[1]),
        load(value_weight_hbm, weights.at[2]),
    ]
    output_load = load(output_weight_hbm, weights.at[3])

    def back_norm(field, moved, gain_row, at):
        scale = root_scale(field)
        small[at : at + 1] += jnp.sum(moved * field * scale, axis=0, keepdims=True)
        weighted = moved * gain_row
        mean = jnp.mean(weighted * field, axis=-1, keepdims=True)
        return scale * weighted - field * (scale * scale * scale) * mean

    hidden_load.wait()

    def second(span):
        value = level[0, span] + back_norm(level[2, span], level[1, span], gain[1:2], 1)
        level[0, span] = value
        pool[0, span] = value.astype(narrow)

    each_tile(second)
    context_load.wait()
    fold(flat[0], pool.at[4], pool.at[0])
    near_copy(5).start()
    normed_one_load = load(normed_one_hbm, pool.at[4])
    advance((OUTER,), 6)
    output_load.wait()

    def third(span):
        pool[5, span] = product_right(pool[0, span], weights[3]).astype(narrow)

    each_tile(third)
    tokens_load = load(tokens_hbm, pool.at[0])
    advance((OUTER,), 7)
    join(INNER)
    join(5)
    for copy in (query_load, key_load, value_load):
        copy.wait()

    def pair_products():
        each_peer(lambda k: left_copy(k).wait_recv())
        for j, (left_at, right_at) in enumerate(spans):
            own, columns = pair_sums[j].shape
            wide = -(-own // 128) * 128
            left = left_all[:, :, left_at : left_at + wide].reshape(-1, wide)
            for begin in range(0, columns, width):
                right = right_all[:, :, right_at + begin : right_at + begin + width]
                block = product_left(left, right.reshape(-1, width))
                pair_work[j][:, begin : begin + width] = block[:own].astype(narrow)
            pair_near(j).start()

    def pair_cross():
        for j in range(pairs):
            pair_near(j).wait()
            mine = pair_work[j][:, half_of(core, pair_sums[j].shape[1])]
            pair_half[j][...] = plus(pair_half[j][...], mine).astype(narrow)
            pair_across(j).start()

    def share_copy(at):
        return pltpu.make_async_copy(
            shares_hbm.at[lax.rem(at, rows), at // rows],
            shares.at[lax.rem(at, 2)],
            share_sem.at[lax.rem(at, 2)],
        )

    turns = rows * (HEADS // 2)
    share_copy(0).start()

    def attend_pair(at, carry):
        pair, row, buffer = at // rows, lax.rem(at, rows), lax.rem(at, 2)
        share_copy(at).wait()

        @pl.when(at + 1 < turns)
        def _():
            share_copy(at + 1).start()

        @pl.when((at >= 2) & (at < count + 2))
        def _():
            advance((5,), at - 2)

        @pl.when((at >= 1) & (lax.rem(at, 3) != 2))
        def _():
            advance((INNER,), 2 * (at // 3) + lax.rem(at, 3) - 1)

        @pl.when(at == 2)
        def _():
            pair_products()

        @pl.when(at == 5)
        def _():
            pair_cross()

        @pl.when(row == 0)
        def _():
            bias_acc[...] = jnp.zeros_like(bias_acc)

        key_acc[...] = jnp.zeros_like(key_acc)
        value_acc[...] = jnp.zeros_like(value_acc)
        columns = rows_of(pair, 2 * KV)

        def span(begin, size):
            return pl.ds(pl.multiple_of(row * length + begin, BLOCK), size)

        for block in range(blocks):
            keys, places = reach(block, blocks)
            own = span(block * BLOCK, BLOCK)
            near = span(keys.start, keys.stop - keys.start)
            query, grad = wide_heads(pool[1, own, columns]), wide_heads(pool[5, own, columns])
            narrow_shares = shares[buffer, block, :, places]
            part = narrow_shares.astype(jnp.float32)
            value_acc[keys] += product_left(narrow_shares, grad)
            moved = part * product_right(grad, pool[3, near, columns])
            grad_scores = moved - part * jnp.sum(moved, axis=1, keepdims=True)
            bias_acc[:, places] += grad_scores
            low = grad_scores.astype(narrow)
            key_acc[keys] += product_left(low, query)
            mixed = product(low, pool[2, near, columns])
            pool[1, own, columns] = narrow_heads(mixed).astype(narrow)
        pool[2, span(0, length), columns] = key_acc[...].astype(narrow)
        pool[3, span(0, length), columns] = value_acc[...].astype(narrow)

        @pl.when(row == rows - 1)
        def _():
            for head in range(2):
                block = bias_acc[head * BLOCK : (head + 1) * BLOCK]
                place = slice(head * 3 * BLOCK, (head + 1) * 3 * BLOCK)
                small[pl.ds(5 + pair, 1), place] = offset_sums(block)

        return carry

    lax.fori_loop(0, turns, attend_pair, 0)
    end_across(5).start()
    normed_one_load.wait()
    for i, at in ((2, 1), (3, 2), (4, 3)):
        fold(big.at[i - 2], pool.at[4], pool.at[at])
        near_copy(i).start()
    advance((INNER,), count - 1)
    close(INNER)
    close(OUTER)
    for i in (2, 3, 4):
        join(i)
    advance((2, 3, 4), 0)
    for i in (5, 6, 7):
        close(i)
    tokens_load.wait()
    for copy in late_loads:
        copy.wait()

    def save(at):
        span = rows_of(at)
        return pltpu.make_async_copy(
            level.at[1, span], tokens_grad_hbm.at[span], share_sem.at[2 + at]
        )

    def last(at, carry):
        span = rows_of(at)
        moved = product_right(pool[1, span], weights[0])
        moved = moved + product_right(pool[2, span], weights[1])
        moved = moved + product_right(pool[3, span], weights[2])
        field = pool[0, span].astype(jnp.float32)
        level[1, span] = level[0, span] + back_norm(field, moved, gain[0:1], 0)
        save(at).start()
        advance((2, 3, 4), at + 1)
        return carry

    lax.fori_loop(0, tiles, last, 0)
    near_small = send(small, small_near, small_sem.at[0], small_sem.at[1], spot.sibling)
    near_small.start()
    for j in range(pairs):
        pair_across(j).wait()
        here = half_of(core, pair_sums[j].shape[1])
        pair_sums[j][:, here] = plus(pair_half[j][...], pair_far[j][...]).astype(narrow)
        pair_end(j).start()
    advance((2, 3, 4), tiles + 1)
    near_small.wait()
    small_mid[...] = small[...] + small_near[...]
    far_small = send(small_mid, small_far, small_sem.at[2], small_sem.at[3], spot.opposite)
    far_small.start()
    advance((2, 3, 4), tiles + 2)
    far_small.wait()
    small_all[spot.fsdp] = small_mid[...] + small_far[...]
    each_peer(lambda k: small_copy(k).start())
    run((2, 3, 4), tiles + 3, count)
    for i in (2, 3, 4):
        end_across(i).start()
    for i in (INNER, OUTER):
        end_far(i).wait()
        end_relay(i).start()
    each_peer(lambda k: small_copy(k).wait_recv())
    small_sum[...] = lax.fori_loop(
        1, count, lambda k, so_far: so_far + small_all[k], small_all[0]
    )
    for i in (2, 3, 4):
        close(i)
    for i in range(8):
        end_near(i).wait()
    for i in (INNER, OUTER):
        end_relay(i).wait()
    for j in range(pairs):
        pair_end(j).wait()
    for at in range(tiles):
        save(at).wait()

    def drain(step, carry):
        for i in (INNER, OUTER):
            for way in range(2):
                far_copy(i, way, step).wait_send()
        return carry

    lax.fori_loop(0, count, drain, 0)

    def drain_ring(step, carry):
        for way in range(2):
            for i in range(8):
                ring_copy(i, way, step).wait_send()
            right_copy(way, step).wait_send()
        left_copy(step + 1).wait_send()
        small_copy(step + 1).wait_send()
        return carry

    lax.fori_loop(0, count - 1, drain_ring, 0)


def backward(
    count, rows, whole, kept, tokens, cotangent, grad_keys, grad_values,
    left_part, right_part, pair_shapes, gains, decoder_gains,
):
    (
        query, key, value, shares, context, hidden, normed_two,
        active, rise, memory, unused_keys, unused_values, normed_one,
    ) = kept
    many, width = tokens.shape
    depth, narrow, wide = width // count, jnp.bfloat16, jnp.float32
    pairs = len(pair_shapes)
    spans, left_at, right_at = [], 0, 0
    for own, columns in pair_shapes:
        spans.append((left_at, right_at))
        left_at, right_at = left_at + -(-own // 128) * 128, right_at + columns
    dma, vmem = pltpu.SemaphoreType.DMA, pltpu.VMEM
    pieces = [(depth // 2, width), (depth, width // 2)] + [(depth // 2, width // 2)] * 6
    outs = [(depth, 4 * width), (4 * depth, width)] + [(depth, width)] * 6
    little = (16, width)
    scratch = [vmem((4, width, width), narrow)] + [vmem((width, width), narrow)] * 2
    scratch += [vmem((2, width, width), narrow), vmem((4, width, width // 2), narrow)]
    scratch += [vmem((width, width // 2), narrow)] * 6
    scratch += [vmem((2, count) + piece, narrow) for piece in pieces]
    scratch += [vmem((2,) + pieces[2], narrow)] * 6
    scratch += [vmem((2, count) + piece, narrow) for piece in pieces[:2]]
    scratch += [vmem(left_part.shape, narrow), vmem((count,) + right_part.shape, narrow)]
    scratch += [vmem(s, narrow) for s in pair_shapes]
    scratch += [vmem((r, c // 2), narrow) for r, c in pair_shapes] * 2
    scratch += [vmem(little, wide)] * 4 + [vmem((count,) + little, wide)]
    scratch += [
        vmem((6, many, width), narrow), vmem((3, many, width), wide),
        vmem((4, width, width), narrow), vmem((2,) + shares.shape[2:], narrow),
        vmem((2 * BLOCK, 3 * BLOCK), wide),
    ]
    scratch += [vmem((many // rows, 2 * KV), wide)] * 2
    scratch += [
        dma((2, 8)), dma((8, 2, count)), dma((8, 2, count)), dma((2, 2, 2, count)), dma((8, 8)),
        dma((count,)), dma((count,)), dma((2, count)), dma((2, count)), dma((6, pairs)),
        dma((4,)), dma((count,)), dma((count,)), dma((48,)), dma((2 + many // TILE,)),
    ]
    shapes = [jax.ShapeDtypeStruct(s, narrow) for s in outs + list(pair_shapes)]
    shapes += [jax.ShapeDtypeStruct(little, wide), jax.ShapeDtypeStruct((many, width), wide)]
    anywhere = pl.BlockSpec(memory_space=pl.ANY)
    local = pl.BlockSpec(memory_space=pltpu.VMEM)
    got = pl.pallas_call(
        functools.partial(backward_kernel, count, rows, spans),
        out_shape=shapes,
        in_specs=[anywhere] * 23 + [local] * 4,
        out_specs=[local] * (len(shapes) - 1) + [anywhere],
        scratch_shapes=scratch,
        compiler_params=pltpu.CompilerParams(
            collective_id=3, has_side_effects=True, vmem_limit_bytes=63 * 2**20
        ),
        name="backward",
    )(
        whole[4], whole[5], whole[0], whole[1], whole[2], whole[3], whole[6], whole[7],
        active, rise, normed_two, context, query, key, value, normed_one, tokens, memory,
        grad_keys, grad_values, cotangent, hidden, shares,
        left_part, right_part, gains, decoder_gains,
    )
    return got[:8], got[8 : 8 + pairs], got[-2], got[-1]


def backward_apart(
    count, rows, whole, kept, tokens, cotangent, grad_cross_keys, grad_cross_values,
    left_part, right_part, pair_shapes, gains, decoder_gains,
):
    (
        query_full, key_full, value_full, output_full, inner_full, outer_full, cross_key_full,
        cross_value_full,
    ) = whole[:8]
    (
        query_all, key_all, value_all, shares, context, hidden, normed_two,
        active, rise, memory, unused_keys, unused_values, normed_one,
    ) = kept
    row_count, length = rows, tokens.shape[0] // rows
    gain_one, gain_two = gains[0], gains[1]
    field = tokens.astype(jnp.float32)
    scale_one, scale_two = root_scale(field), root_scale(hidden)
    grad_cross_key = product_left(memory, grad_cross_keys)
    grad_cross_value = product_left(memory, grad_cross_values)
    grad_memory = product_right(grad_cross_keys, cross_key_full) + product_right(
        grad_cross_values, cross_value_full
    )
    grad_encoded = cotangent.astype(jnp.float32) + grad_memory
    grad_branch = grad_encoded.astype(jnp.bfloat16)
    grad_outer = product_left(active, grad_branch)
    grad_active = product_right(grad_branch, outer_full)
    grad_before = (grad_active * rise).astype(jnp.bfloat16)
    grad_inner = product_left(normed_two, grad_before)
    grad_normed = product_right(grad_before, inner_full)
    field_part, grad_gain_two = norm_back(
        grad_normed, hidden, scale_two, gain_two
    )
    grad_hidden = grad_encoded + field_part
    grad_branch = grad_hidden.astype(jnp.bfloat16)
    grad_output = product_left(context, grad_branch)
    grad_context = product_right(grad_branch, output_full).astype(jnp.bfloat16)
    grad_query_all, grad_key_all, grad_value_all, bias_sums = attend_rows_back(
        row_count, length, query_all, key_all, value_all, grad_context, shares
    )
    grad_query = product_left(normed_one, grad_query_all)
    grad_key = product_left(normed_one, grad_key_all)
    grad_value = product_left(normed_one, grad_value_all)
    grad_normed = (
        product_right(grad_query_all, query_full)
        + product_right(grad_key_all, key_full)
        + product_right(grad_value_all, value_full)
    )
    field_part, grad_gain_one = norm_back(
        grad_normed, field, scale_one, gain_one
    )
    tokens_grad = grad_hidden + field_part
    small = jnp.concatenate([
        jnp.stack([grad_gain_one, grad_gain_two]),
        decoder_gains,
        bias_sums.reshape(HEADS // 2, -1),
        jnp.zeros((5, tokens.shape[1]), jnp.float32),
    ])
    encoder_grads = (
        grad_inner, grad_outer, grad_query, grad_key, grad_value, grad_output,
        grad_cross_key, grad_cross_value,
    )
    encoder_sums, decoder_sums, small_sum = reduce_grads(
        count,
        ENCODER_KINDS,
        [
            g.astype(jnp.bfloat16).reshape(count, g.shape[0] // count, g.shape[1])
            for g in encoder_grads
        ],
        left_part,
        right_part,
        pair_shapes,
        small,
    )
    return encoder_sums, decoder_sums, small_sum, tokens_grad


def widen_kernel(total, *refs):
    sources, targets = refs[:total], refs[total : 2 * total]
    held, wide, sems = refs[2 * total : 3 * total], list(refs[3 * total : -1]), refs[-1]
    ready = [part if part.dtype == jnp.float32 else wide.pop(0) for part in held]
    loads = [pltpu.make_async_copy(sources[at], held[at], sems.at[at]) for at in range(total)]
    stores = [
        pltpu.make_async_copy(ready[at], targets[at], sems.at[total + at]) for at in range(total)
    ]
    for copy in loads:
        copy.start()
    for at in range(total):
        loads[at].wait()
        if held[at] is not ready[at]:
            ready[at][...] = held[at][...].astype(jnp.float32)
        stores[at].start()
    for copy in stores:
        copy.wait()


def widen(parts):
    anywhere, total = pl.BlockSpec(memory_space=pl.ANY), len(parts)
    return pl.pallas_call(
        functools.partial(widen_kernel, total),
        out_shape=[jax.ShapeDtypeStruct(part.shape, jnp.float32) for part in parts],
        in_specs=[anywhere] * total,
        out_specs=[anywhere] * total,
        scratch_shapes=[pltpu.VMEM(part.shape, part.dtype) for part in parts]
        + [
            pltpu.VMEM(part.shape, jnp.float32) for part in parts if part.dtype != jnp.float32
        ]
        + [pltpu.SemaphoreType.DMA((2 * total,))],
        compiler_params=pltpu.CompilerParams(vmem_limit_bytes=48 * 2**20),
        name="widen",
    )(*parts)


def on_device(
    tokens,
    segment_index,
    start_vectors,
    first_gain,
    query_weight,
    key_weight,
    value_weight,
    output_weight,
    position_table,
    second_gain,
    inner_weight,
    outer_weight,
    start_gain,
    self_value,
    self_output,
    middle_gain,
    cross_query,
    cross_key,
    cross_value,
    cross_output,
    final_gain,
    decoder_inner,
    decoder_outer,
    encoded_cotangent,
    decoded_cotangent,
):
    row_count = segment_index.shape[0]
    length = segment_index.shape[1]
    slot_count = start_vectors.shape[1]
    width = tokens.shape[1]
    count = lax.axis_size("fsdp")
    depth = first_gain.shape[0]
    choices = jnp.arange(position_table.shape[0], dtype=jnp.int32)
    onehot = (offset_buckets()[None, :] == choices[:, None]).astype(jnp.float32)
    base = jnp.dot(position_table.T, onehot, precision=lax.Precision.HIGHEST)
    gains = jnp.stack([first_gain, second_gain, start_gain, middle_gain, final_gain])
    gains = jnp.pad(gains, ((0, 11), (0, BLOCK - depth)))
    shards = (
        query_weight, key_weight, value_weight, output_weight, inner_weight, outer_weight,
        cross_key, cross_value, self_value, self_output, cross_query, cross_output,
        decoder_inner, decoder_outer, gains,
    )
    fused = count == 8 and depth % 32 == 0 and (row_count, length) == (2, 512)
    plan = forward if fused else forward_apart
    whole, all_gains, kept = plan(count, shards, tokens, segment_index, base)
    memory, cross_keys, cross_values = kept[9:12]
    token_count = row_count * slot_count
    (
        decoded, start_grad, decoder_gain_grads,
        normed_fin, decoder_active, normed_start, own_value, normed_mid, cross_context,
        decoder_before_grad, last_branch, grad_own, self_branch, grad_asking, cross_branch,
        grad_cross_keys, grad_cross_values, encoded,
    ) = decode(
        segment_index,
        start_vectors.reshape(token_count, width),
        decoded_cotangent.reshape(token_count, width),
        all_gains,
        cross_keys,
        cross_values,
        memory,
        whole[8:14],
    )
    lefts = (normed_fin, decoder_active, normed_start, own_value, normed_mid, cross_context)
    rights = (decoder_before_grad, last_branch, grad_own, self_branch, grad_asking, cross_branch)
    pair_shapes = [(left.shape[1] // count, right.shape[1]) for left, right in zip(lefts, rights)]
    left_cols = []
    for left, (rows, unused) in zip(lefts, pair_shapes):
        columns = left.reshape(token_count, count, rows).transpose(1, 0, 2)
        left_cols.append(jnp.pad(columns, ((0, 0), (0, 0), (0, -rows % 128))))
    turn_back = backward if fused else backward_apart
    encoder_sums, decoder_sums, small_sum, tokens_grad = turn_back(
        count, row_count, whole, kept, tokens, encoded_cotangent,
        grad_cross_keys, grad_cross_values,
        jnp.concatenate(left_cols, axis=2),
        jnp.concatenate(rights, axis=1),
        pair_shapes, all_gains, decoder_gain_grads,
    )
    (
        inner_weight_grad, outer_weight_grad, query_weight_grad, key_weight_grad,
        value_weight_grad, output_weight_grad, cross_key_grad, cross_value_grad,
        decoder_inner_grad, decoder_outer_grad, self_value_grad, self_output_grad,
        cross_query_grad, cross_output_grad, tokens_grad,
    ) = widen([*encoder_sums, *decoder_sums, tokens_grad])
    position_table_grad = lax.dot_general(
        onehot,
        small_sum[5:11].reshape(HEADS, 3 * BLOCK),
        (((1,), (1,)), ((), ())),
        precision=lax.Precision.HIGHEST,
    )
    own_gains = lax.dynamic_slice_in_dim(
        small_sum[:5], lax.axis_index("fsdp") * depth, depth, axis=1
    )
    first_gain_grad, second_gain_grad, start_gain_grad, middle_gain_grad, final_gain_grad = own_gains
    decoded = decoded.reshape(start_vectors.shape)
    start_grad = start_grad.reshape(start_vectors.shape)
    return (
        encoded,
        decoded,
        tokens_grad,
        start_grad,
        first_gain_grad,
        query_weight_grad,
        key_weight_grad,
        value_weight_grad,
        output_weight_grad,
        position_table_grad,
        second_gain_grad,
        inner_weight_grad,
        outer_weight_grad,
        start_gain_grad,
        self_value_grad,
        self_output_grad,
        middle_gain_grad,
        cross_query_grad,
        cross_key_grad,
        cross_value_grad,
        cross_output_grad,
        final_gain_grad,
        decoder_inner_grad,
        decoder_outer_grad,
    )


def solution(mesh):
    placed = (
        P(("dp", "fsdp"), None),
        P(("dp", "fsdp"), None),
        P(("dp", "fsdp"), None, None),
        P("fsdp"),
        P("fsdp", None),
        P("fsdp", None),
        P("fsdp", None),
        P("fsdp", None),
        P(),
        P("fsdp"),
        P("fsdp", None),
        P("fsdp", None),
        P("fsdp"),
        P("fsdp", None),
        P("fsdp", None),
        P("fsdp"),
        P("fsdp", None),
        P("fsdp", None),
        P("fsdp", None),
        P("fsdp", None),
        P("fsdp"),
        P("fsdp", None),
        P("fsdp", None),
        P(("dp", "fsdp"), None),
        P(("dp", "fsdp"), None, None),
    )
    return jax.shard_map(
        on_device,
        mesh=mesh,
        in_specs=placed,
        out_specs=(
            P(("dp", "fsdp"), None),
            P(("dp", "fsdp"), None, None),
            P(("dp", "fsdp"), None),
            P(("dp", "fsdp"), None, None),
            P("fsdp"),
            P("fsdp", None),
            P("fsdp", None),
            P("fsdp", None),
            P("fsdp", None),
            P(),
            P("fsdp"),
            P("fsdp", None),
            P("fsdp", None),
            P("fsdp"),
            P("fsdp", None),
            P("fsdp", None),
            P("fsdp"),
            P("fsdp", None),
            P("fsdp", None),
            P("fsdp", None),
            P("fsdp", None),
            P("fsdp"),
            P("fsdp", None),
            P("fsdp", None),
        ),
        check_vma=False,
    )
```

```python
import functools

import jax
import jax.numpy as jnp
from jax import lax
from jax.experimental import pallas as pl
from jax.experimental.pallas import tpu as pltpu
from jax.sharding import PartitionSpec as P

HEADS = 12
KV = 64
BLOCK = 128


epsilon = 1e-06
negative_fill = -1e30
bucket_edges = (12, 16, 23, 32, 46, 64, 91)


MESH = pl.DeviceIdType.MESH
KINDS = (
    "square", "square", "square", "square", "wide", "tall", "square", "square",
    "square", "square", "square", "square", "wide", "tall", "small",
)


def ring_position(index, count):
    if count == 64:
        slow, rest = index // 32, index % 32
        row, column = rest // 8, rest % 8
        place = row * 8 + column + (row % 2) * (7 - 2 * column)
        return place + slow * (count - 1 - 2 * place)
    across, along = index % 2, index // 2
    return along + across * (count - 1 - 2 * along)


def ring_index(position, count):
    position = lax.rem(position, count)
    across = position // (count // 2)
    along = position + across * (count - 1 - 2 * position)
    if count == 64:
        row, column = along // 8, along % 8
        return across * 32 + row * 8 + column + (row % 2) * (7 - 2 * column)
    return 2 * along + across


class Spot:
    def __init__(self, count):
        self.count = count
        self.dp = lax.axis_index("dp")
        self.fsdp = lax.axis_index("fsdp")
        self.core = lax.rem(self.dp, 2)
        self.plane = self.dp // 2
        self.place = ring_position(self.fsdp, count)
        self.sibling = (self.dp + 1 - 2 * self.core, self.fsdp)
        self.opposite = (lax.rem(self.dp + 2, 4), self.fsdp)
        self.after = (self.dp, ring_index(self.place + 1, count))
        self.before = (self.dp, ring_index(self.place + count - 1, count))

    def greet(self, others=()):
        barrier = pltpu.get_barrier_semaphore()
        partners = (self.sibling, self.opposite, self.after, self.before) + tuple(others)
        for partner in partners:
            pl.semaphore_signal(barrier, inc=1, device_id=partner, device_id_type=MESH)
        pl.semaphore_wait(barrier, len(partners))


def cut(kind, ref, plane, core):
    rows, columns = ref.shape
    if kind == "small":
        return ref
    if kind == "square":
        half = columns // 2
        return ref.at[:, pl.ds(pl.multiple_of(core * half, 128), half)]
    if kind == "wide":
        quarter = columns // 4
        return ref.at[:, pl.ds(pl.multiple_of((core * 2 + plane) * quarter, 128), quarter)]
    half, upper = columns // 2, rows // 2
    return ref.at[
        pl.ds(pl.multiple_of(plane * upper, 8), upper),
        pl.ds(pl.multiple_of(core * half, 128), half),
    ]


def send(source, target, send_sem, recv_sem, device):
    return pltpu.make_async_remote_copy(
        src_ref=source,
        dst_ref=target,
        send_sem=send_sem,
        recv_sem=recv_sem,
        device_id=device,
        device_id_type=MESH,
    )


def gather_kernel(count, kinds, *refs):
    total = len(kinds)
    shards, fulls = refs[:total], refs[total : 2 * total]
    ring_out, ring_in, near_out, near_in, far_out, far_in, last_out, last_in, own_sem = refs[
        2 * total :
    ]
    spot = Spot(count)
    split = [i for i in range(total) if kinds[i] in ("wide", "tall")]

    window = min(count, 8)

    def slot_of(i, step):
        turn = step if i % 2 else count - step
        return ring_index(spot.place + turn, count)

    def ring_copy(i, step, source=None):
        here = cut(kinds[i], fulls[i].at[slot_of(i, step)], spot.plane, spot.core)
        return send(
            here if source is None else source,
            here,
            ring_out.at[i, lax.rem(step, window)],
            ring_in.at[i, step],
            spot.before if i % 2 else spot.after,
        )

    def near_copy(i, step):
        here = cut(kinds[i], fulls[i].at[slot_of(i, step)], spot.plane, spot.core)
        out = near_out.at[i, lax.rem(step, window)]
        return send(here, here, out, near_in.at[i, step], spot.sibling)

    def far_copy(i, step):
        here = cut(kinds[i], fulls[i].at[slot_of(i, step)], spot.plane, spot.core)
        at = split.index(i)
        out = far_out.at[at, lax.rem(step, window)]
        return send(here, here, out, far_in.at[at, step], spot.opposite)

    def last_copy(i, step):
        here = cut(kinds[i], fulls[i].at[slot_of(i, step)], 1 - spot.plane, spot.core)
        at = split.index(i)
        out = last_out.at[at, lax.rem(step, window)]
        return send(here, here, out, last_in.at[at, step], spot.sibling)

    def start(copy, i, step, first):
        if window < count:

            @pl.when(step >= first + window)
            def _():
                copy(i, step - window).wait_send()

        copy(i, step).start()

    def finish(copy, i, first, end):
        def one(step, carry):
            copy(i, step).wait_send()
            return carry

        lax.fori_loop(max(first, end - window), end, one, 0)

    owns = []
    for i in range(total):
        owns.append(pltpu.make_async_copy(shards[i], fulls[i].at[spot.fsdp], own_sem.at[i]))
        owns[-1].start()
    spot.greet()
    for i in range(total):
        ring_copy(i, 0, cut(kinds[i], shards[i], spot.plane, spot.core)).start()

    def one_step(step, carry):
        for i in range(total):
            ring_copy(i, step - 1).wait_recv()

            @pl.when(step < count - 1)
            def _():
                start(ring_copy, i, step, 0)

            if kinds[i] != "small":
                start(near_copy, i, step, 1)
            if i in split:
                start(far_copy, i, step, 1)

        @pl.when(step > 1)
        def _():
            for i in split:
                far_copy(i, step - 1).wait_recv()
                start(last_copy, i, step - 1, 1)

        return carry

    lax.fori_loop(1, count, one_step, 0)
    for i in split:
        far_copy(i, count - 1).wait_recv()
        start(last_copy, i, count - 1, 1)

    def settle(step, carry):
        for i in range(total):
            if kinds[i] != "small":
                near_copy(i, step).wait_recv()
            if i in split:
                last_copy(i, step).wait_recv()
        return carry

    lax.fori_loop(1, count, settle, 0)
    for i in range(total):
        finish(ring_copy, i, 0, count - 1)
        if kinds[i] != "small":
            finish(near_copy, i, 1, count)
        if i in split:
            finish(far_copy, i, 1, count)
            finish(last_copy, i, 1, count)
    for copy in owns:
        copy.wait()


def gather_weights(count, shards, kinds):
    total = len(shards)
    split = sum(kind in ("wide", "tall") for kind in kinds)
    window = min(count, 8)
    many, few = [
        [pltpu.SemaphoreType.DMA((rows, window)), pltpu.SemaphoreType.DMA((rows, count))] * 2
        for rows in (total, split)
    ]
    return pl.pallas_call(
        functools.partial(gather_kernel, count, kinds),
        out_shape=[jax.ShapeDtypeStruct((count,) + s.shape, s.dtype) for s in shards],
        in_specs=[pl.BlockSpec(memory_space=pl.ANY)] * total,
        out_specs=[pl.BlockSpec(memory_space=pl.ANY)] * total,
        scratch_shapes=many + few + [pltpu.SemaphoreType.DMA((total,))],
        compiler_params=pltpu.CompilerParams(collective_id=0, has_side_effects=True),
        name="gather_weights",
    )(*shards)

def plus(*terms):
    total = terms[0].astype(jnp.float32)
    for term in terms[1:]:
        total = total + term.astype(jnp.float32)
    return total


def half_of(core, columns):
    half = columns // 2
    return pl.ds(pl.multiple_of(core * half, 128), half)


def plane_part(kind, plane, rows, columns):
    if kind == "wide":
        return slice(None), pl.ds(pl.multiple_of(plane * (columns // 2), 128), columns // 2)
    if kind == "tall":
        return pl.ds(pl.multiple_of(plane * (rows // 2), 8), rows // 2), slice(None)
    return slice(None), slice(None)


ENCODER_KINDS = ("wide", "tall", "square", "square", "square", "square", "square", "square")


def reduce_kernel(count, kinds, spans, *refs):
    total, pairs = len(kinds), len(spans)
    refs = list(refs)

    def take(size):
        got = refs[:size]
        del refs[:size]
        return got

    grads = take(total)
    left_part, right_part, small = take(3)
    sums = take(total)
    pair_sums = take(pairs)
    (small_sum,) = take(1)
    half, work, final = take(total), take(total), take(total)
    split = [i for i in range(total) if kinds[i] != "square"]
    far = take(len(split))
    left_all, right_all = take(2)
    pair_half, pair_far, pair_work = take(pairs), take(pairs), take(pairs)
    small_near, small_mid, small_far, small_all = take(4)
    (
        near_sem, ring_out, ring_in, far_sem, end_sem, left_out, left_in,
        right_out, right_in, pair_sem, small_sem, small_out, small_in,
    ) = take(13)
    spot = Spot(count)
    core, plane = spot.core, spot.plane
    diagonal = (lax.rem(spot.dp + 2, 4) + 1 - 2 * core, spot.fsdp)

    def peer(k):
        return (spot.dp, lax.rem(spot.fsdp + k, count))

    barrier = pltpu.get_barrier_semaphore()
    for partner in (spot.sibling, spot.opposite, diagonal):
        pl.semaphore_signal(barrier, inc=1, device_id=partner, device_id_type=MESH)

    def greet(k, carry):
        pl.semaphore_signal(barrier, inc=1, device_id=peer(k), device_id_type=MESH)
        return carry

    lax.fori_loop(1, count, greet, 0)
    pl.semaphore_wait(barrier, count + 2)

    def near_copy(i):
        columns = grads[i].shape[2]
        return send(
            grads[i].at[:, :, half_of(1 - core, columns)], half[i],
            near_sem.at[0, i], near_sem.at[1, i], spot.sibling,
        )

    def slot_at(i, step):
        turn = step + 1 if i % 2 else count - 1 - step
        return ring_index(spot.place + turn, count)

    def far_copy(i, step):
        at = split.index(i)
        rows, columns = half[i].shape[1:]
        part = plane_part(kinds[i], 1 - plane, rows, columns)
        return send(
            half[i].at[(slot_at(i, step),) + part], far[at].at[step],
            far_sem.at[0, at, step], far_sem.at[1, at, step], spot.opposite,
        )

    def ring_copy(i, step):
        return send(
            work[i].at[step], work[i].at[step + 1], ring_out.at[i, step], ring_in.at[i, step],
            spot.before if i % 2 else spot.after,
        )

    def left_copy(k):
        other = lax.rem(spot.fsdp + k, count)
        return send(
            left_part.at[other], left_all.at[spot.fsdp], left_out.at[k], left_in.at[k], peer(k)
        )

    def right_copy(way, step):
        turn = step if way else count - step
        slot = ring_index(spot.place + turn, count)
        width = right_part.shape[1] // 2
        here = right_all.at[slot, :, way * width : (way + 1) * width]
        return send(
            here, here, right_out.at[way, step], right_in.at[way, step],
            spot.before if way else spot.after,
        )

    for i in range(total):
        near_copy(i).start()
    near_small = send(small, small_near, small_sem.at[0], small_sem.at[1], spot.sibling)
    near_small.start()

    def left_start(k, carry):
        left_copy(k).start()
        return carry

    lax.fori_loop(1, count, left_start, 0)
    right_all[spot.fsdp] = right_part[...]
    left_all[spot.fsdp] = left_part[spot.fsdp]
    for way in range(2):
        right_copy(way, 0).start()
    near_small.wait()
    small_mid[...] = small[...] + small_near[...]
    far_small = send(small_mid, small_far, small_sem.at[2], small_sem.at[3], spot.opposite)
    far_small.start()

    for i in range(total):
        near_copy(i).wait_recv()

        def join(slot, carry):
            mine = grads[i][slot, :, half_of(core, grads[i].shape[2])]
            half[i][slot] = plus(half[i][slot], mine).astype(jnp.bfloat16)
            return carry

        lax.fori_loop(0, count, join, 0)
        if i in split:

            def far_start(step, carry):
                far_copy(i, step).start()
                return carry

            lax.fori_loop(0, count, far_start, 0)

    far_small.wait()
    small_all[spot.fsdp] = small_mid[...] + small_far[...]

    def small_copy(k):
        here = small_all.at[spot.fsdp]
        return send(here, here, small_out.at[k], small_in.at[k], peer(k))

    def small_start(k, carry):
        small_copy(k).start()
        return carry

    lax.fori_loop(1, count, small_start, 0)

    def right_step(step, carry):
        for way in range(2):
            right_copy(way, step - 1).wait_recv()

            @pl.when(step < count - 1)
            def _():
                right_copy(way, step).start()

        return carry

    lax.fori_loop(1, count, right_step, 0)

    def left_wait(k, carry):
        left_copy(k).wait_recv()
        return carry

    lax.fori_loop(1, count, left_wait, 0)

    def pair_near(j):
        columns = pair_sums[j].shape[1]
        return send(
            pair_work[j].at[:, half_of(1 - core, columns)], pair_half[j],
            pair_sem.at[0, j], pair_sem.at[1, j], spot.sibling,
        )

    def pair_across(j):
        return send(
            pair_half[j], pair_far[j], pair_sem.at[2, j], pair_sem.at[3, j], spot.opposite
        )

    def pair_end(j):
        here = pair_sums[j].at[:, half_of(core, pair_sums[j].shape[1])]
        return send(here, here, pair_sem.at[4, j], pair_sem.at[5, j], spot.sibling)

    for j, (left_at, right_at) in enumerate(spans):
        rows, columns = pair_sums[j].shape
        span = -(-rows // 128) * 128
        left = left_all[:, :, left_at : left_at + span].reshape(-1, span)
        for begin in range(0, columns, 768):
            right = right_all[:, :, right_at + begin : right_at + begin + 768].reshape(-1, 768)
            block = lax.dot_general(
                left, right, (((0,), (0,)), ((), ())), preferred_element_type=jnp.float32
            )
            pair_work[j][:, begin : begin + 768] = block[:rows].astype(jnp.bfloat16)
        pair_near(j).start()
    for j in range(pairs):
        pair_near(j).wait()
        mine = pair_work[j][:, half_of(core, pair_sums[j].shape[1])]
        pair_half[j][...] = plus(pair_half[j][...], mine).astype(jnp.bfloat16)
        pair_across(j).start()

    def one_step(step, carry):
        for i in range(total):
            rows, columns = half[i].shape[1:]
            slot = slot_at(i, step)
            value = half[i][(slot,) + plane_part(kinds[i], plane, rows, columns)]
            value = value.astype(jnp.float32)
            if i in split:
                far_copy(i, step).wait_recv()
                value = value + far[split.index(i)][step].astype(jnp.float32)

            @pl.when(step > 0)
            def _():
                ring_copy(i, step - 1).wait_recv()
                work[i][step] = plus(value, work[i][step]).astype(jnp.bfloat16)

            @pl.when(step == 0)
            def _():
                work[i][step] = value.astype(jnp.bfloat16)

            @pl.when(step < count - 1)
            def _():
                ring_copy(i, step).start()

        return carry

    lax.fori_loop(0, count, one_step, 0)

    def end_across(i):
        return send(
            work[i].at[count - 1], final[i], end_sem.at[0, i], end_sem.at[1, i], spot.opposite
        )

    def end_piece(i, mine_plane):
        rows, columns = sums[i].shape
        wide = half_of(core, columns)
        if kinds[i] == "square":
            return sums[i].at[:, wide]
        return cut(kinds[i], sums[i], mine_plane, core)

    def end_copies(i):
        here = end_piece(i, plane)
        copies = [send(here, here, end_sem.at[2, i], end_sem.at[3, i], spot.sibling)]
        if i in split:
            copies.append(send(here, here, end_sem.at[4, i], end_sem.at[5, i], spot.opposite))
            copies.append(send(here, here, end_sem.at[6, i], end_sem.at[7, i], diagonal))
        return copies

    for i in range(total):
        if i not in split:
            end_across(i).start()
    for i in split:
        end_piece(i, plane)[...] = work[i][count - 1]
        for copy in end_copies(i):
            copy.start()
    for j in range(pairs):
        pair_across(j).wait()
        here = half_of(core, pair_sums[j].shape[1])
        pair_sums[j][:, here] = plus(pair_half[j][...], pair_far[j][...]).astype(jnp.bfloat16)
        pair_end(j).start()
    for i in range(total):
        if i not in split:
            end_across(i).wait()
            value = plus(work[i][count - 1], final[i][...]).astype(jnp.bfloat16)
            end_piece(i, plane)[...] = value
            for copy in end_copies(i):
                copy.start()

    def small_wait(k, carry):
        small_copy(k).wait_recv()
        return carry

    lax.fori_loop(1, count, small_wait, 0)
    small_sum[...] = lax.fori_loop(
        1, count, lambda k, so_far: so_far + small_all[k], small_all[0]
    )
    for i in range(total):
        for copy in end_copies(i):
            copy.wait()
    for j in range(pairs):
        pair_end(j).wait()
    for i in range(total):
        near_copy(i).wait_send()

    def drain(step, carry):
        for i in split:
            far_copy(i, step).wait_send()
        return carry

    lax.fori_loop(0, count, drain, 0)

    def drain_ring(step, carry):
        for i in range(total):
            ring_copy(i, step).wait_send()
        for way in range(2):
            right_copy(way, step).wait_send()
        left_copy(step + 1).wait_send()
        small_copy(step + 1).wait_send()
        return carry

    lax.fori_loop(0, count - 1, drain_ring, 0)


def reduce_grads(count, kinds, grads, left_part, right_part, pair_shapes, small):
    total, pairs = len(kinds), len(pair_shapes)
    spans, left_at, right_at = [], 0, 0
    for rows, columns in pair_shapes:
        spans.append((left_at, right_at))
        left_at, right_at = left_at + -(-rows // 128) * 128, right_at + columns
    narrow = jnp.bfloat16
    blocks = [g.shape[1:] for g in grads]
    pieces = []
    for kind, (rows, columns) in zip(kinds, blocks):
        if kind == "wide":
            pieces.append((rows, columns // 4))
        elif kind == "tall":
            pieces.append((rows // 2, columns // 2))
        else:
            pieces.append((rows, columns // 2))
    split = [i for i in range(total) if kinds[i] != "square"]
    dma = pltpu.SemaphoreType.DMA
    scratch = [pltpu.VMEM((count, r, c // 2), narrow) for r, c in blocks]
    scratch += [pltpu.VMEM((count, r, c), narrow) for r, c in pieces]
    scratch += [pltpu.VMEM((r, c), narrow) for r, c in pieces]
    scratch += [pltpu.VMEM((count,) + pieces[i], narrow) for i in split]
    scratch += [
        pltpu.VMEM(left_part.shape, narrow),
        pltpu.VMEM((count,) + right_part.shape, narrow),
    ]
    scratch += [pltpu.VMEM((r, c // 2), narrow) for r, c in pair_shapes] * 2
    scratch += [pltpu.VMEM((r, c), narrow) for r, c in pair_shapes]
    scratch += [pltpu.VMEM(small.shape, jnp.float32)] * 3
    scratch += [pltpu.VMEM((count,) + small.shape, jnp.float32)]
    scratch += [
        dma((2, total)), dma((total, count)), dma((total, count)), dma((2, len(split), count)),
        dma((8, total)), dma((count,)), dma((count,)), dma((2, count)), dma((2, count)),
        dma((6, pairs)), dma((4,)), dma((count,)), dma((count,)),
    ]
    outs = [jax.ShapeDtypeStruct(b, narrow) for b in blocks]
    outs += [jax.ShapeDtypeStruct(s, narrow) for s in pair_shapes]
    outs += [jax.ShapeDtypeStruct(small.shape, jnp.float32)]
    got = pl.pallas_call(
        functools.partial(reduce_kernel, count, kinds, spans),
        out_shape=outs,
        in_specs=[pl.BlockSpec(memory_space=pltpu.VMEM)] * (total + 3),
        out_specs=[pl.BlockSpec(memory_space=pltpu.VMEM)] * len(outs),
        scratch_shapes=scratch,
        compiler_params=pltpu.CompilerParams(
            collective_id=1, has_side_effects=True, vmem_limit_bytes=62 * 2**20
        ),
        name="reduce_grads",
    )(*grads, left_part, right_part, small)
    return got[:total], got[total : total + pairs], got[-1]


def product(left, right):
    return jnp.dot(left, right, preferred_element_type=jnp.float32)


def product_left(left, right):
    return lax.dot_general(
        left, right, (((0,), (0,)), ((), ())), preferred_element_type=jnp.float32
    )


def product_right(left, right):
    return lax.dot_general(
        left, right, (((1,), (1,)), ((), ())), preferred_element_type=jnp.float32
    )


def root_scale(field):
    return lax.rsqrt(jnp.mean(field * field, axis=-1, keepdims=True) + epsilon)


def norm_back(grad_normed, field, scale, gain):
    gain_grad = jnp.sum(grad_normed * field * scale, axis=0)
    weighted = grad_normed * gain
    field_grad = scale * weighted - field * (scale * scale * scale) * jnp.mean(
        weighted * field, axis=-1, keepdims=True
    )
    return (field_grad, gain_grad)


def wide_heads(block):
    first = lax.broadcasted_iota(jnp.int32, block.shape, 1) < KV
    none = jnp.zeros_like(block)
    return jnp.concatenate([jnp.where(first, block, none), jnp.where(first, none, block)], axis=0)


def narrow_heads(stacked):
    half = stacked.shape[0] // 2
    first = lax.broadcasted_iota(jnp.int32, (half, stacked.shape[1]), 1) < KV
    return jnp.where(first, stacked[:half], stacked[half:])


def reach(at, blocks):
    low, high = max(0, at - 1), min(blocks, at + 2)
    begin = (low - at + 1) * BLOCK
    return slice(low * BLOCK, high * BLOCK), slice(begin, begin + (high - low) * BLOCK)


def bias_block(base):
    heads = []
    for at in range(2):
        level = jnp.broadcast_to(base[at : at + 1], (BLOCK, base.shape[1]))
        heads.append(pltpu.roll(level, 0, axis=1, stride=1, stride_axis=0))
    return jnp.concatenate(heads, axis=0)


def offset_sums(block):
    rows, width = block.shape
    while rows > 8:
        rows = rows // 2
        block = block[:rows] + pltpu.roll(block[rows:], width - rows, axis=1)
    place = lax.broadcasted_iota(jnp.int32, block.shape, 0)
    for bit in (4, 2, 1):
        block = jnp.where((place & bit) > 0, pltpu.roll(block, width - bit, axis=1), block)
    return jnp.sum(block, axis=0, keepdims=True)


def attend_kernel(column_ref, row_ref, base_ref, query_ref, key_ref, value_ref, out_ref, share_ref):
    blocks = query_ref.shape[0] // BLOCK
    bias = bias_block(base_ref[0])
    for at in range(blocks):
        keys, places = reach(at, blocks)
        own = slice(at * BLOCK, (at + 1) * BLOCK)
        scores = product_right(wide_heads(query_ref[own]), key_ref[keys]) + bias[:, places]
        allowed = column_ref[own, :1] == row_ref[0, :1, keys]
        scores = jnp.where(jnp.concatenate([allowed, allowed], axis=0), scores, negative_fill)
        powers = jnp.exp(scores - jnp.max(scores, axis=1, keepdims=True))
        shares = powers * (1.0 / jnp.sum(powers, axis=1, keepdims=True))
        shares = shares.astype(jnp.bfloat16)
        share_ref[0, 0, at, :, places] = shares
        mixed = product(shares, value_ref[keys])
        out_ref[own] = narrow_heads(mixed).astype(jnp.bfloat16)


def attend_back_kernel(
    query_ref, key_ref, value_ref, grad_ref, share_ref,
    grad_query_ref, grad_key_ref, grad_value_ref, sums_ref, bias_acc, key_acc, value_acc,
):
    blocks = query_ref.shape[0] // BLOCK

    @pl.when(pl.program_id(1) == 0)
    def _():
        bias_acc[...] = jnp.zeros_like(bias_acc)

    key_acc[...] = jnp.zeros_like(key_acc)
    value_acc[...] = jnp.zeros_like(value_acc)
    for at in range(blocks):
        keys, places = reach(at, blocks)
        own = slice(at * BLOCK, (at + 1) * BLOCK)
        query, grad = wide_heads(query_ref[own]), wide_heads(grad_ref[own])
        narrow_shares = share_ref[0, 0, at, :, places]
        shares = narrow_shares.astype(jnp.float32)
        value_acc[keys] += product_left(narrow_shares, grad)
        moved = shares * product_right(grad, value_ref[keys])
        grad_scores = moved - shares * jnp.sum(moved, axis=1, keepdims=True)
        bias_acc[:, places] += grad_scores
        narrow = grad_scores.astype(jnp.bfloat16)
        grad_query_ref[own] = narrow_heads(product(narrow, key_ref[keys])).astype(jnp.bfloat16)
        key_acc[keys] += product_left(narrow, query)
    grad_key_ref[...] = key_acc[...].astype(jnp.bfloat16)
    grad_value_ref[...] = value_acc[...].astype(jnp.bfloat16)

    @pl.when(pl.program_id(1) == pl.num_programs(1) - 1)
    def _():
        sums_ref[0] = jnp.concatenate(
            [offset_sums(bias_acc[:BLOCK]), offset_sums(bias_acc[BLOCK:])], axis=0
        )


def offset_buckets():
    offset = jnp.arange(3 * BLOCK, dtype=jnp.int32) - BLOCK
    distance = jnp.abs(offset)
    far_bucket = 8 + sum(((distance >= boundary).astype(jnp.int32) for boundary in bucket_edges))
    near_bucket = jnp.where(distance < 8, distance, far_bucket)
    return jnp.where(offset > 0, 16, 0) + near_bucket


def attend_rows(rows, length, column, segment_index, base, query, key, value):
    pairs = HEADS // 2
    part = pl.BlockSpec((length, 2 * KV), lambda r, p: (r, p))
    return pl.pallas_call(
        attend_kernel,
        grid=(rows, pairs),
        out_shape=[
            jax.ShapeDtypeStruct(query.shape, jnp.bfloat16),
            jax.ShapeDtypeStruct(
                (rows, pairs, length // BLOCK, 2 * BLOCK, 3 * BLOCK), jnp.bfloat16
            ),
        ],
        in_specs=[
            pl.BlockSpec((length, BLOCK), lambda r, p: (r, 0)),
            pl.BlockSpec((1, 1, length), lambda r, p: (r, 0, 0)),
            pl.BlockSpec((1, 2, 3 * BLOCK), lambda r, p: (p, 0, 0)),
            part, part, part,
        ],
        out_specs=[
            part,
            pl.BlockSpec(
                (1, 1, length // BLOCK, 2 * BLOCK, 3 * BLOCK), lambda r, p: (r, p, 0, 0, 0)
            ),
        ],
        compiler_params=pltpu.CompilerParams(vmem_limit_bytes=48 * 2**20),
        name="attend",
    )(column, segment_index.reshape(rows, 1, length), base, query, key, value)


def attend_rows_back(rows, length, query, key, value, grad, shares):
    pairs = HEADS // 2
    part = pl.BlockSpec((length, 2 * KV), lambda p, r: (r, p))
    return pl.pallas_call(
        attend_back_kernel,
        grid=(pairs, rows),
        out_shape=[jax.ShapeDtypeStruct(query.shape, jnp.bfloat16)] * 3
        + [jax.ShapeDtypeStruct((pairs, 2, 3 * BLOCK), jnp.float32)],
        in_specs=[
            part, part, part, part,
            pl.BlockSpec(
                (1, 1, length // BLOCK, 2 * BLOCK, 3 * BLOCK), lambda p, r: (r, p, 0, 0, 0)
            ),
        ],
        out_specs=[part, part, part, pl.BlockSpec((1, 2, 3 * BLOCK), lambda p, r: (p, 0, 0))],
        scratch_shapes=[
            pltpu.VMEM((2 * BLOCK, 3 * BLOCK), jnp.float32),
            pltpu.VMEM((length, 2 * KV), jnp.float32),
            pltpu.VMEM((length, 2 * KV), jnp.float32),
        ],
        compiler_params=pltpu.CompilerParams(vmem_limit_bytes=48 * 2**20),
        name="attend_back",
    )(query, key, value, grad, shares)


def gelu_parts(before):
    slope = 0.7978845608028654
    square = before * before
    bend = jnp.tanh(slope * (before + 0.044715 * before * square))
    half = 0.5 * (1.0 + bend)
    rise = half + 0.5 * before * (1.0 - bend * bend) * slope * (1.0 + 3 * 0.044715 * square)
    return before * half, rise


def slots_of(stacked, count):
    rows, columns = stacked.shape
    own = lax.broadcasted_iota(jnp.int32, (rows, columns), 0) // count
    head = lax.broadcasted_iota(jnp.int32, (rows, columns), 1) // KV
    return jnp.where(own == head, stacked, 0.0)


def decoder_kernel(rows, slots, *refs):
    (
        segment_ref, start_ref, cotangent_ref, gain_ref, keys_hbm, values_hbm, memory_hbm,
        self_value_hbm, self_output_hbm, cross_query_hbm, cross_output_hbm,
        inner_hbm, outer_hbm,
        decoded_ref, start_grad_ref, gain_grad_ref,
        normed_fin_ref, active_ref, normed_start_ref, own_ref, normed_mid_ref, context_ref,
        before_grad_ref, last_branch_ref, grad_own_ref, self_branch_ref, grad_asking_ref,
        cross_branch_ref, grad_keys_hbm, grad_values_hbm, encoded_hbm,
        keys_ref, values_ref, grad_keys_ref, grad_values_ref, memory_ref,
        self_value, self_output, cross_query, cross_output, inner, outer, sems,
    ) = refs
    loads = []
    for at, (source, target) in enumerate((
        (self_value_hbm, self_value), (self_output_hbm, self_output),
        (cross_query_hbm, cross_query), (cross_output_hbm, cross_output),
        (inner_hbm, inner), (outer_hbm, outer), (keys_hbm, keys_ref), (values_hbm, values_ref),
        (memory_hbm, memory_ref),
    )):
        loads.append(pltpu.make_async_copy(source, target, sems.at[at]))
    for at in (0, 1, 2, 6, 7):
        loads[at].start()
    narrow = jnp.bfloat16
    length = keys_ref.shape[0] // rows
    start_gain, middle_gain, final_gain = gain_ref[2:3], gain_ref[3:4], gain_ref[4:5]

    start_field = start_ref[...].astype(jnp.float32)
    scale_start = root_scale(start_field)
    normed_start = (start_field * scale_start * start_gain).astype(narrow)
    normed_start_ref[...] = normed_start
    loads[0].wait()
    for at in (3, 4, 5, 8):
        loads[at].start()
    own = product(normed_start, self_value[...]).astype(narrow)
    own_ref[...] = own
    loads[1].wait()
    first_field = start_field + product(own, self_output[...])
    scale_mid = root_scale(first_field)
    normed_mid = (first_field * scale_mid * middle_gain).astype(narrow)
    normed_mid_ref[...] = normed_mid
    loads[2].wait()
    asking = product(normed_mid, cross_query[...]).astype(narrow).astype(jnp.float32)
    loads[6].wait()
    loads[7].wait()
    wides, all_shares, contexts = [], [], []
    for row in range(rows):
        part = asking[row * slots : (row + 1) * slots]
        wide = slots_of(jnp.concatenate([part] * HEADS, axis=0), slots).astype(narrow)
        span = slice(row * length, (row + 1) * length)
        scores = product_right(wide, keys_ref[span])
        slot = lax.rem(lax.broadcasted_iota(jnp.int32, scores.shape, 0), slots)
        scores = jnp.where(slot == segment_ref[row : row + 1], scores, negative_fill)
        powers = jnp.exp(scores - jnp.max(scores, axis=1, keepdims=True))
        shares = powers * (1.0 / jnp.sum(powers, axis=1, keepdims=True))
        mixed = slots_of(product(shares.astype(narrow), values_ref[span]), slots)
        contexts.append(jnp.sum(mixed.reshape(HEADS, slots, -1), axis=0))
        wides.append(wide)
        all_shares.append(shares)
    context = jnp.concatenate(contexts, axis=0).astype(narrow)
    context_ref[...] = context
    loads[3].wait()
    second_field = first_field + product(context, cross_output[...])
    scale_fin = root_scale(second_field)
    normed_fin = (second_field * scale_fin * final_gain).astype(narrow)
    normed_fin_ref[...] = normed_fin
    loads[4].wait()
    active, rise = gelu_parts(product(normed_fin, inner[...]))
    active = active.astype(narrow)
    active_ref[...] = active
    loads[5].wait()
    decoded_ref[...] = (second_field + product(active, outer[...])).astype(narrow)

    branch = cotangent_ref[...]
    last_branch_ref[...] = branch
    grad_second = branch.astype(jnp.float32)
    before_grad = (product_right(branch, outer[...]) * rise).astype(narrow)
    before_grad_ref[...] = before_grad
    grad_normed = product_right(before_grad, inner[...])
    moved, final_gain_grad = norm_back(grad_normed, second_field, scale_fin, final_gain)
    grad_second = grad_second + moved
    branch = grad_second.astype(narrow)
    cross_branch_ref[...] = branch
    grad_context = product_right(branch, cross_output[...]).astype(narrow).astype(jnp.float32)
    askings = []
    for row in range(rows):
        part = grad_context[row * slots : (row + 1) * slots]
        wide = slots_of(jnp.concatenate([part] * HEADS, axis=0), slots).astype(narrow)
        span = slice(row * length, (row + 1) * length)
        shares = all_shares[row]
        moved = shares * product_right(wide, values_ref[span])
        grad_scores = moved - shares * jnp.sum(moved, axis=1, keepdims=True)
        grad_scores = grad_scores.astype(narrow)
        grad_values_ref[span] = product_left(shares.astype(narrow), wide).astype(narrow)
        grad_keys_ref[span] = product_left(grad_scores, wides[row]).astype(narrow)
        mixed = slots_of(product(grad_scores, keys_ref[span]), slots)
        askings.append(jnp.sum(mixed.reshape(HEADS, slots, -1), axis=0))
    loads[8].wait()
    stores = [pltpu.make_async_copy(memory_ref, encoded_hbm, sems.at[11])]
    stores.append(pltpu.make_async_copy(grad_keys_ref, grad_keys_hbm, sems.at[9]))
    stores.append(pltpu.make_async_copy(grad_values_ref, grad_values_hbm, sems.at[10]))
    for copy in stores:
        copy.start()
    grad_asking = jnp.concatenate(askings, axis=0).astype(narrow)
    grad_asking_ref[...] = grad_asking
    grad_normed = product_right(grad_asking, cross_query[...])
    moved, middle_gain_grad = norm_back(grad_normed, first_field, scale_mid, middle_gain)
    grad_first = grad_second + moved
    branch = grad_first.astype(narrow)
    self_branch_ref[...] = branch
    grad_own = product_right(branch, self_output[...]).astype(narrow)
    grad_own_ref[...] = grad_own
    grad_normed = product_right(grad_own, self_value[...])
    moved, start_gain_grad = norm_back(grad_normed, start_field, scale_start, start_gain)
    start_grad_ref[...] = grad_first + moved
    gain_grad_ref[...] = jnp.concatenate(
        [start_gain_grad[None], middle_gain_grad[None], final_gain_grad[None]], axis=0
    )
    for copy in stores:
        copy.wait()


def decode(segment_index, start, cotangent, gains, keys, values, memory, weights):
    rows, tokens, width = segment_index.shape[0], start.shape[0], start.shape[1]
    narrow, hidden = jnp.bfloat16, weights[4].shape[1]
    few = jax.ShapeDtypeStruct((tokens, width), narrow)
    many = jax.ShapeDtypeStruct((tokens, hidden), narrow)
    outs = [
        few,
        jax.ShapeDtypeStruct((tokens, width), jnp.float32),
        jax.ShapeDtypeStruct((3, width), jnp.float32),
        few, many, few, few, few, few,
        many, few, few, few, few, few,
        jax.ShapeDtypeStruct(keys.shape, narrow),
        jax.ShapeDtypeStruct(values.shape, narrow),
        jax.ShapeDtypeStruct(memory.shape, narrow),
    ]
    anywhere = pl.BlockSpec(memory_space=pl.ANY)
    local = pl.BlockSpec(memory_space=pltpu.VMEM)
    return pl.pallas_call(
        functools.partial(decoder_kernel, rows, tokens // rows),
        out_shape=outs,
        in_specs=[local] * 4 + [anywhere] * 9,
        out_specs=[local] * (len(outs) - 3) + [anywhere] * 3,
        scratch_shapes=[pltpu.VMEM(keys.shape, narrow)] * 5
        + [pltpu.VMEM(w.shape, narrow) for w in weights]
        + [pltpu.SemaphoreType.DMA((12,))],
        compiler_params=pltpu.CompilerParams(vmem_limit_bytes=63 * 2**20),
        name="decode",
    )(segment_index, start, cotangent, gains, keys, values, memory, *weights)


TILE = 256


def rows_of(at, size=TILE):
    return pl.ds(pl.multiple_of(at * size, size), size)


FORWARD_KINDS = (
    "tall", "tall", "square", "square", "wide", "tall", "square", "square",
    "square", "square", "square", "square", "wide", "tall", "small",
)


class Gather:
    def __init__(self, spot, kinds, shards, fulls, staged, sems):
        self.spot, self.kinds, self.shards, self.fulls = spot, kinds, shards, fulls
        self.staged = staged
        (
            self.ring_out, self.ring_in, self.near_out, self.near_in,
            self.far_out, self.far_in, self.last_out, self.last_in, self.own_sem,
        ) = sems
        self.split = [i for i in range(len(kinds)) if kinds[i] in ("wide", "tall")]

    def piece(self, i, step, plane):
        count = self.spot.count
        slot = ring_index(self.spot.place + (step if i % 2 else count - step), count)
        rows = self.shards[i].shape[0]
        block = self.fulls[i].at[pl.ds(pl.multiple_of(slot * rows, 16), rows)]
        return cut(self.kinds[i], block, plane, self.spot.core)

    def own_copy(self, i):
        rows = self.shards[i].shape[0]
        block = self.fulls[i].at[pl.ds(pl.multiple_of(self.spot.fsdp * rows, 16), rows)]
        return pltpu.make_async_copy(self.staged.get(i, self.shards[i]), block, self.own_sem.at[i])

    def stage_copy(self, i):
        at = len(self.kinds) + list(self.staged).index(i)
        return pltpu.make_async_copy(self.shards[i], self.staged[i], self.own_sem.at[at])

    def ring_copy(self, i, step, source=None):
        here = self.piece(i, step, self.spot.plane)
        return send(
            here if source is None else source, here,
            self.ring_out.at[i, step], self.ring_in.at[i, step],
            self.spot.before if i % 2 else self.spot.after,
        )

    def near_copy(self, i, step):
        here = self.piece(i, step, self.spot.plane)
        return send(
            here, here, self.near_out.at[i, step], self.near_in.at[i, step], self.spot.sibling
        )

    def far_copy(self, i, step):
        here, at = self.piece(i, step, self.spot.plane), self.split.index(i)
        return send(
            here, here, self.far_out.at[at, step], self.far_in.at[at, step], self.spot.opposite
        )

    def last_copy(self, i, step):
        here, at = self.piece(i, step, 1 - self.spot.plane), self.split.index(i)
        return send(
            here, here, self.last_out.at[at, step], self.last_in.at[at, step], self.spot.sibling
        )

    def start(self, group):
        for i in group:
            source = cut(self.kinds[i], self.shards[i], self.spot.plane, self.spot.core)
            self.ring_copy(i, 0, source).start()

    def advance(self, group, step):
        count = self.spot.count
        for i in group:
            if step < count:
                self.ring_copy(i, step - 1).wait_recv()
                if step < count - 1:
                    self.ring_copy(i, step).start()
                if self.kinds[i] != "small":
                    self.near_copy(i, step).start()
                if i in self.split:
                    self.far_copy(i, step).start()
        for i in group:
            if step > 1 and i in self.split:
                self.far_copy(i, step - 1).wait_recv()
                self.last_copy(i, step - 1).start()

    def arrive(self, group):
        def one(step, carry):
            for i in group:
                if self.kinds[i] != "small":
                    self.near_copy(i, step).wait_recv()
                if i in self.split:
                    self.last_copy(i, step).wait_recv()
            return carry

        lax.fori_loop(1, self.spot.count, one, 0)
        for i in group:
            self.own_copy(i).wait()

    def settle(self, group):
        def one(step, carry):
            for i in group:
                self.ring_copy(i, step - 1).wait_send()
                if self.kinds[i] != "small":
                    self.near_copy(i, step).wait_send()
                if i in self.split:
                    self.far_copy(i, step).wait_send()
                    self.last_copy(i, step).wait_send()
            return carry

        lax.fori_loop(1, self.spot.count, one, 0)


FIRST, SECOND, THIRD = (0, 1, 2, 3, 14), (4, 5, 6, 7), (8, 9, 10, 11, 12, 13)


def forward_kernel(count, rows, *refs):
    refs = list(refs)

    def take(size):
        got = refs[:size]
        del refs[:size]
        return got

    shards = take(15)
    tokens, segment, base = take(3)
    weight_outs = take(14)
    (gain_out,) = take(1)
    (
        query_out, key_out, value_out, share_out, context_out, hidden_out, normed_two_out,
        active_out, rise_out, memory_out, cross_key_out, cross_value_out, normed_one_out,
    ) = take(13)
    held = take(8)
    gain_all, normed_one, query, key, value, context = take(6)
    hidden, normed_two, active, rise, memory, cross_keys, cross_values, shares = take(8)
    column, lines, bases = take(3)
    staged = dict(zip(THIRD, take(len(THIRD))))
    gather_sems = take(9)
    save_sem, share_sem = take(2)
    spot = Spot(count)
    fulls = held + weight_outs[8:] + [gain_all]
    gather = Gather(spot, FORWARD_KINDS, shards, fulls, staged, gather_sems)
    tiles = tokens.shape[0] // TILE
    length = tokens.shape[0] // rows
    blocks, pairs = length // BLOCK, HEADS // 2
    narrow = jnp.bfloat16
    saves = []

    def save(source, target):
        copy = pltpu.make_async_copy(source, target, save_sem.at[len(saves)])
        copy.start()
        saves.append(copy)

    def each_tile(body):
        def one(at, carry):
            body(rows_of(at), at)
            return carry

        lax.fori_loop(0, tiles, one, 0)

    for i in FIRST:
        gather.own_copy(i).start()
    spot.greet()
    gather.start(FIRST)
    for i in SECOND:
        gather.own_copy(i).start()
    for i in THIRD:
        gather.stage_copy(i).start()
    for pair in range(pairs):
        bases[pair, 0:2] = base[2 * pair : 2 * pair + 2]
    for row in range(rows):
        lines[row, 0:1] = segment[row : row + 1].astype(jnp.float32)
        for block in range(blocks):
            line = segment[row : row + 1, block * BLOCK : (block + 1) * BLOCK].astype(jnp.float32)
            begin = row * length + block * BLOCK
            column[begin : begin + BLOCK] = jnp.broadcast_to(line, (BLOCK, BLOCK)).T
    for step in range(1, 5):
        gather.advance(FIRST, step)
    gather.start(SECOND)
    for i in THIRD:
        gather.stage_copy(i).wait()
        gather.own_copy(i).start()
    for step in range(5, count):
        gather.advance(FIRST, step)
        gather.advance(SECOND, step - 4)
    gather.advance(FIRST, count)
    gather.arrive(FIRST)
    gain, width = jnp.zeros(gain_out.shape, jnp.float32), tokens.shape[1]
    depth = width // count
    lanes = lax.broadcasted_iota(jnp.int32, gain.shape, 1)
    for slot in range(count):
        part = gain_all[slot * 16 : (slot + 1) * 16].astype(jnp.float32)
        part = jnp.concatenate([part, jnp.zeros((16, width - part.shape[1]), jnp.float32)], axis=1)
        part = pltpu.roll(part, slot * depth, axis=1)
        gain = gain + jnp.where(lanes // depth == slot, part, 0.0)
    gain_out[...] = gain
    query_weight, key_weight, value_weight, output_weight = held[:4]
    inner_weight, outer_weight, cross_key_weight, cross_value_weight = held[4:]

    def first_norm(span, at):
        field = tokens[span].astype(jnp.float32)
        normed_one[span] = (field * root_scale(field) * gain_out[0:1]).astype(narrow)

    each_tile(first_norm)

    def project(target, weight):
        def body(span, at):
            target[span] = product(normed_one[span], weight[...]).astype(narrow)

        each_tile(body)

    project(query, query_weight)
    gather.advance(SECOND, 4)
    project(key, key_weight)
    gather.start(THIRD)
    project(value, value_weight)
    gather.advance(SECOND, 5)
    for source, target in (
        (normed_one, normed_one_out), (query, query_out), (key, key_out), (value, value_out),
    ):
        save(source, target)
    for i in range(4):
        save(held[i], weight_outs[i])

    def share_copy(at):
        return pltpu.make_async_copy(
            shares.at[lax.rem(at, 2)],
            share_out.at[at // pairs, lax.rem(at, pairs)],
            share_sem.at[lax.rem(at, 2)],
        )

    def attend_pair(at, carry):
        row, pair, buffer = at // pairs, lax.rem(at, pairs), lax.rem(at, 2)

        for turn, group, step in (
            (1, THIRD, 1), (2, SECOND, 6), (4, THIRD, 2), (5, SECOND, 7), (7, THIRD, 3),
            (8, SECOND, 8), (10, THIRD, 4),
        ):

            @pl.when(at == turn)
            def _():
                gather.advance(group, step)

        @pl.when(at >= 2)
        def _():
            share_copy(at - 2).wait()

        bias = bias_block(bases[pair, 0:2])
        columns = rows_of(pair, 2 * KV)

        def span(begin, size):
            return pl.ds(pl.multiple_of(row * length + begin, BLOCK), size)

        for block in range(blocks):
            keys, places = reach(block, blocks)
            own = span(block * BLOCK, BLOCK)
            near = span(keys.start, keys.stop - keys.start)
            scores = product_right(wide_heads(query[own, columns]), key[near, columns])
            scores = scores + bias[:, places]
            allowed = column[own, :1] == lines[row, 0:1, keys]
            scores = jnp.where(jnp.concatenate([allowed, allowed], axis=0), scores, negative_fill)
            powers = jnp.exp(scores - jnp.max(scores, axis=1, keepdims=True))
            part = powers * (1.0 / jnp.sum(powers, axis=1, keepdims=True))
            part = part.astype(narrow)
            shares[buffer, block, :, places] = part
            mixed = product(part, value[near, columns])
            context[own, columns] = narrow_heads(mixed).astype(narrow)
        share_copy(at).start()
        return carry

    lax.fori_loop(0, rows * pairs, attend_pair, 0)
    save(context, context_out)

    def second_norm(span, at):
        field = tokens[span].astype(jnp.float32) + product(context[span], output_weight[...])
        hidden[span] = field
        normed_two[span] = (field * root_scale(field) * gain_out[1:2]).astype(narrow)

    each_tile(second_norm)
    save(hidden, hidden_out)
    save(normed_two, normed_two_out)
    gather.advance(THIRD, 5)
    gather.arrive(SECOND)
    for i in range(4, 8):
        save(held[i], weight_outs[i])
    chunk = tokens.shape[1]

    def feed(span, at):
        @pl.when(at == 1)
        def _():
            gather.advance(THIRD, 6)

        @pl.when(at == 3)
        def _():
            gather.advance(THIRD, 7)

        for begin in range(0, active.shape[1], chunk):
            part = slice(begin, begin + chunk)
            level, slope = gelu_parts(product(normed_two[span], inner_weight[:, part]))
            active[span, part] = level.astype(narrow)
            rise[span, part] = slope.astype(narrow)
        full = hidden[span] + product(active[span], outer_weight[...])
        memory[span] = full.astype(narrow)

    each_tile(feed)
    save(active, active_out)
    save(rise, rise_out)
    save(memory, memory_out)

    def cross(span, at):
        cross_keys[span] = product(memory[span], cross_key_weight[...]).astype(narrow)
        cross_values[span] = product(memory[span], cross_value_weight[...]).astype(narrow)

    each_tile(cross)
    save(cross_keys, cross_key_out)
    save(cross_values, cross_value_out)
    gather.advance(THIRD, count)
    gather.arrive(THIRD)
    for group in (FIRST, SECOND, THIRD):
        gather.settle(group)
    for copy in saves:
        copy.wait()
    for at in range(rows * pairs - 2, rows * pairs):
        share_copy(at).wait()


def forward(count, shards, tokens, segment_index, base):
    rows, length = segment_index.shape
    many, width = tokens.shape
    hidden_width = shards[4].shape[1]
    narrow, wide = jnp.bfloat16, jnp.float32
    pairs, total = HEADS // 2, len(shards)
    split = sum(kind in ("wide", "tall") for kind in FORWARD_KINDS)
    weights = [(count * s.shape[0], s.shape[1]) for s in shards]
    few, much = (many, width), (many, hidden_width)
    share_shape = (rows, pairs, length // BLOCK, 2 * BLOCK, 3 * BLOCK)
    shapes = [(w, narrow) for w in weights[:14]] + [((16, width), wide)]
    shapes += [
        (few, narrow), (few, narrow), (few, narrow), (share_shape, narrow), (few, narrow),
        (few, wide), (few, narrow), (much, narrow), (much, narrow), (few, narrow), (few, narrow),
        (few, narrow), (few, narrow),
    ]
    dma = pltpu.SemaphoreType.DMA
    scratch = [pltpu.VMEM(w, narrow) for w in weights[:8]] + [pltpu.VMEM(weights[14], narrow)]
    scratch += [pltpu.VMEM(few, narrow)] * 5
    scratch += [
        pltpu.VMEM(few, wide), pltpu.VMEM(few, narrow), pltpu.VMEM(much, narrow),
        pltpu.VMEM(much, narrow), pltpu.VMEM(few, narrow), pltpu.VMEM(few, narrow),
        pltpu.VMEM(few, narrow), pltpu.VMEM((2,) + share_shape[2:], narrow),
    ]
    scratch += [pltpu.VMEM((many, BLOCK), wide), pltpu.VMEM((rows, 8, length), wide)]
    scratch += [pltpu.VMEM((pairs, 8, base.shape[1]), wide)]
    scratch += [pltpu.VMEM(shards[i].shape, narrow) for i in THIRD]
    scratch += [dma((total, count))] * 4 + [dma((split, count))] * 4
    scratch += [dma((total + len(THIRD),)), dma((24,)), dma((2,))]
    anywhere = pl.BlockSpec(memory_space=pl.ANY)
    local = pl.BlockSpec(memory_space=pltpu.VMEM)
    got = pl.pallas_call(
        functools.partial(forward_kernel, count, rows),
        out_shape=[jax.ShapeDtypeStruct(s, d) for s, d in shapes],
        in_specs=[anywhere] * total + [local] * 3,
        out_specs=[anywhere] * 14 + [local] + [anywhere] * 13,
        scratch_shapes=scratch,
        compiler_params=pltpu.CompilerParams(
            collective_id=2, has_side_effects=True, vmem_limit_bytes=62 * 2**20
        ),
        name="forward",
    )(*shards, tokens, segment_index, base)
    return got[:14], got[14], got[15:]


def forward_apart(count, shards, tokens, segment_index, base):
    rows, length = segment_index.shape
    narrow = jnp.bfloat16
    whole = gather_weights(count, shards, KINDS)
    depth, many = shards[0].shape[0], tokens.shape[0]
    gains = whole[14][:, :, :depth].astype(jnp.float32)
    gains = gains.transpose(1, 0, 2).reshape(16, count * depth)
    base = base.reshape(HEADS // 2, 2, 3 * BLOCK)
    column = jnp.broadcast_to(segment_index.reshape(-1, 1), (many, BLOCK))
    whole = [part.reshape(-1, part.shape[2]) for part in whole[:14]]
    field = tokens.astype(jnp.float32)
    normed_one = (field * root_scale(field) * gains[0]).astype(narrow)
    query, key, value = [product(normed_one, weight).astype(narrow) for weight in whole[:3]]
    context, shares = attend_rows(
        rows, length, column, segment_index, base, query, key, value
    )
    hidden = field + product(context, whole[3])
    normed_two = (hidden * root_scale(hidden) * gains[1]).astype(narrow)
    active, rise = gelu_parts(product(normed_two, whole[4]))
    active = active.astype(narrow)
    memory = (hidden + product(active, whole[5])).astype(narrow)
    cross_keys, cross_values = [product(memory, weight).astype(narrow) for weight in whole[6:8]]
    return whole, gains, (
        query, key, value, shares, context, hidden, normed_two,
        active, rise, memory, cross_keys, cross_values, normed_one,
    )


INNER, OUTER = 0, 1
SPLITS = {INNER: 2}


def backward_kernel(count, rows, spans, *refs):
    refs = list(refs)

    def take(size):
        got = refs[:size]
        del refs[:size]
        return got

    (
        inner_hbm, outer_hbm, query_weight_hbm, key_weight_hbm, value_weight_hbm,
        output_weight_hbm, cross_key_weight_hbm, cross_value_weight_hbm,
        active_hbm, rise_hbm, normed_two_hbm, context_hbm, query_hbm, key_hbm, value_hbm,
        normed_one_hbm, tokens_hbm, memory_hbm, grad_keys_hbm, grad_values_hbm, cotangent_hbm,
        hidden_hbm, shares_hbm,
    ) = take(23)
    left_part, right_part, gain, decoder_gains = take(4)
    sums, pairs = take(8), len(spans)
    pair_sums = take(pairs)
    small_sum, tokens_grad_hbm = take(2)
    big, flat, half, work, final, far = take(1)[0], take(2), take(8), take(8), take(8), take(1)[0]
    left_all, right_all = take(2)
    pair_work, pair_half, pair_far = take(pairs), take(pairs), take(pairs)
    small, small_near, small_mid, small_far, small_all = take(5)
    pool, level, weights, shares, bias_acc, key_acc, value_acc = take(7)
    (
        near_sem, ring_out, ring_in, far_sem, end_sem, left_out, left_in,
        right_out, right_in, pair_sem, small_sem, small_out, small_in, load_sem, share_sem,
    ) = take(15)
    spot = Spot(count)
    core, plane = spot.core, spot.plane
    narrow = jnp.bfloat16
    many, width = level.shape[1:]
    tiles, length = many // TILE, many // rows
    blocks = length // BLOCK
    depth = width // count
    products = {2: big.at[0], 3: big.at[1], 4: big.at[2], 5: flat[0], 6: flat[0], 7: flat[1]}

    def peer(k):
        return (spot.dp, lax.rem(spot.fsdp + k, count))

    def slot_at(way, step):
        turn = step + 1 if way else count - 1 - step
        return ring_index(spot.place + turn, count)

    def near_copy(i):
        if i == INNER:
            source = big.at[pl.ds(2 * (1 - core), 2)]
        elif i == OUTER:
            source = big.at[:, :, half_of(1 - core, width)]
        else:
            source = products[i].at[:, half_of(1 - core, width)]
        return send(source, half[i], near_sem.at[0, i], near_sem.at[1, i], spot.sibling)

    def part_of(i, slot, side, way):
        rows_own = work[i].shape[2]
        if i == INNER:
            return half[i].at[way, pl.ds(pl.multiple_of(slot * depth, 16), depth)]
        if i == OUTER:
            begin = lax.rem(slot, 2) * 4 * depth + (2 * side + way) * rows_own
            return half[i].at[slot // 2, pl.ds(pl.multiple_of(begin, 16), rows_own)]
        begin = slot * depth + way * rows_own
        return half[i].at[pl.ds(pl.multiple_of(begin, 16), rows_own)]

    def far_copy(i, way, step):
        return send(
            part_of(i, slot_at(way, step), 1 - plane, way), far.at[way, step],
            far_sem.at[0, way, step], far_sem.at[1, way, step], spot.opposite,
        )

    def join(i):
        near_copy(i).wait()
        if i == INNER:

            def one(at, carry):
                side, span = at // 3, rows_of(lax.rem(at, 3))
                mine = big[2 * core + side, span]
                half[i][side, span] = plus(half[i][side, span], mine).astype(narrow)
                return carry

            lax.fori_loop(0, 6, one, 0)
        elif i == OUTER:

            def one(at, carry):
                side, span = at // 3, rows_of(lax.rem(at, 3))
                mine = big[side, span, half_of(core, width)]
                half[i][side, span] = plus(half[i][side, span], mine).astype(narrow)
                return carry

            lax.fori_loop(0, 12, one, 0)
        else:

            def one(at, carry):
                span = rows_of(at)
                mine = products[i][span, half_of(core, width)]
                half[i][span] = plus(half[i][span], mine).astype(narrow)
                return carry

            lax.fori_loop(0, 3, one, 0)
        if i == OUTER:

            def far_start(step, carry):
                for way in range(2):
                    far_copy(i, way, step).start()
                return carry

            lax.fori_loop(0, count, far_start, 0)

    def spans_of(i):
        rows_own = work[i].shape[2]
        parts = SPLITS.get(i, 1)
        size = rows_own // parts
        return [slice(at * size, (at + 1) * size) for at in range(parts)]

    def ring_copy(i, way, step, at):
        span = spans_of(i)[at]
        return send(
            work[i].at[way, step, span], work[i].at[way, step + 1, span],
            ring_out.at[i, at, way, step], ring_in.at[i, at, way, step],
            spot.before if way else spot.after,
        )

    def advance(group, step):
        for i in group:
            for way in range(2):
                if i == OUTER:
                    far_copy(i, way, step).wait_recv()
                block = part_of(i, slot_at(way, step), plane, way)
                for at, span in enumerate(spans_of(i)):
                    value = block[span].astype(jnp.float32)
                    if i == OUTER:
                        value = value + far[way, step, span].astype(jnp.float32)

                    @pl.when(step > 0)
                    def _():
                        ring_copy(i, way, step - 1, at).wait_recv()
                        total = plus(value, work[i][way, step, span])
                        work[i][way, step, span] = total.astype(narrow)

                    @pl.when(step == 0)
                    def _():
                        work[i][way, step, span] = value.astype(narrow)

                    @pl.when(step < count - 1)
                    def _():
                        ring_copy(i, way, step, at).start()

    def run(group, first, last):
        def one(step, carry):
            advance(group, step)
            return carry

        lax.fori_loop(first, last, one, 0)

    def end_across(i):
        return send(
            work[i].at[:, count - 1], final[i], end_sem.at[0, i], end_sem.at[1, i], spot.opposite
        )

    def end_piece(i, side):
        if i == OUTER:
            return cut("tall", sums[i], side, core)
        return sums[i].at[:, half_of(core, sums[i].shape[1])]

    def end_near(i):
        here = end_piece(i, plane)
        return send(here, here, end_sem.at[2, i], end_sem.at[3, i], spot.sibling)

    def end_far(i):
        here = end_piece(i, plane)
        return send(here, here, end_sem.at[4, i], end_sem.at[5, i], spot.opposite)

    def end_relay(i):
        here = end_piece(i, 1 - plane)
        return send(here, here, end_sem.at[6, i], end_sem.at[7, i], spot.sibling)

    def close(i):
        if i != OUTER:
            end_across(i).wait()
        here, rows_own = end_piece(i, plane), work[i].shape[2]
        for way in range(2):
            value = work[i][way, count - 1]
            if i != OUTER:
                value = plus(value, final[i][way]).astype(narrow)
            if i == INNER:
                here[:, way * width : (way + 1) * width] = value
            else:
                here[way * rows_own : (way + 1) * rows_own] = value
        if i == OUTER:
            end_far(i).start()
        end_near(i).start()

    def left_copy(k):
        other = lax.rem(spot.fsdp + k, count)
        return send(
            left_part.at[other], left_all.at[spot.fsdp], left_out.at[k], left_in.at[k], peer(k)
        )

    def right_copy(way, step):
        turn = step if way else count - step
        slot = ring_index(spot.place + turn, count)
        wide = right_part.shape[1] // 2
        here = right_all.at[slot, :, way * wide : (way + 1) * wide]
        return send(
            here, here, right_out.at[way, step], right_in.at[way, step],
            spot.before if way else spot.after,
        )

    def right_step(step):
        for way in range(2):
            right_copy(way, step - 1).wait_recv()
            if step < count - 1:
                right_copy(way, step).start()

    def pair_near(j):
        columns = pair_sums[j].shape[1]
        return send(
            pair_work[j].at[:, half_of(1 - core, columns)], pair_half[j],
            pair_sem.at[0, j], pair_sem.at[1, j], spot.sibling,
        )

    def pair_across(j):
        return send(
            pair_half[j], pair_far[j], pair_sem.at[2, j], pair_sem.at[3, j], spot.opposite
        )

    def pair_end(j):
        here = pair_sums[j].at[:, half_of(core, pair_sums[j].shape[1])]
        return send(here, here, pair_sem.at[4, j], pair_sem.at[5, j], spot.sibling)

    def small_copy(k):
        here = small_all.at[spot.fsdp]
        return send(here, here, small_out.at[k], small_in.at[k], peer(k))

    def each_peer(body):
        def one(k, carry):
            body(k)
            return carry

        lax.fori_loop(1, count, one, 0)

    def each_tile(body):
        def one(at, carry):
            body(rows_of(at))
            return carry

        lax.fori_loop(0, tiles, one, 0)

    used = []

    def load(source, target):
        copy = pltpu.make_async_copy(source, target, load_sem.at[len(used)])
        copy.start()
        used.append(copy)
        return copy

    def fold(target, left, right):
        def one(at, carry):
            span = rows_of(at)
            target[span] = product_left(left[:, span], right[...]).astype(narrow)
            return carry

        lax.fori_loop(0, width // TILE, one, 0)

    loads = [
        load(grad_keys_hbm, pool.at[4]), load(cross_key_weight_hbm, weights.at[0]),
        load(grad_values_hbm, pool.at[5]), load(cross_value_weight_hbm, weights.at[1]),
        load(cotangent_hbm, pool.at[2]), load(memory_hbm, pool.at[1]),
    ]

    def chunk_of(source, at):
        return source.at[:, pl.ds(at * width, width)]

    active_loads = {1: load(chunk_of(active_hbm, 1), pool.at[3])}
    hidden_load = load(hidden_hbm, level.at[2])
    out_loads = {0: load(outer_hbm.at[pl.ds(0, width)], weights.at[2])}
    barrier = pltpu.get_barrier_semaphore()
    for partner in (spot.sibling, spot.opposite):
        pl.semaphore_signal(barrier, inc=1, device_id=partner, device_id_type=MESH)
    each_peer(
        lambda k: pl.semaphore_signal(barrier, inc=1, device_id=peer(k), device_id_type=MESH)
    )
    pl.semaphore_wait(barrier, count + 1)
    each_peer(lambda k: left_copy(k).start())
    right_all[spot.fsdp] = right_part[...]
    left_all[spot.fsdp] = left_part[spot.fsdp]
    for way in range(2):
        right_copy(way, 0).start()
    small[...] = jnp.zeros_like(small)
    small[2:5] = decoder_gains[...]
    for copy in loads:
        copy.wait()

    def enter(span):
        value = pool[2, span].astype(jnp.float32)
        value = value + product_right(pool[4, span], weights[0])
        value = value + product_right(pool[5, span], weights[1])
        level[0, span] = value
        pool[0, span] = value.astype(narrow)

    each_tile(enter)
    active_loads[0] = load(chunk_of(active_hbm, 0), pool.at[2])
    in_loads = {
        at: load(chunk_of(inner_hbm, at), weights.at[at]) for at in range(2)
    }
    fold(flat[0], pool.at[1], pool.at[4])
    near_copy(6).start()
    fold(flat[1], pool.at[1], pool.at[5])
    near_copy(7).start()
    normed_load = load(normed_two_hbm, pool.at[1])
    context_load = load(context_hbm, pool.at[4])
    right_step(1)

    rise_loads = {}
    for at in range(4):
        buffer = 2 + at % 2
        active_loads[at].wait()
        fold(big.at[at], pool.at[buffer], pool.at[0])
        if at < 2:
            active_loads[at + 2] = load(chunk_of(active_hbm, at + 2), pool.at[buffer])
        else:
            rise_loads[at - 2] = load(chunk_of(rise_hbm, at - 2), pool.at[buffer])
        if at == 1:
            right_step(2)
            join(6)
            join(7)
        elif at == 2:
            advance((6, 7), 0)
        elif at == 3:
            right_step(3)
    near_copy(OUTER).start()
    out_loads[1] = load(outer_hbm.at[pl.ds(width, width)], weights.at[3])

    normed_load.wait()
    for at in range(4):
        buffer = 2 + at % 2
        rise_loads[at].wait()
        out_loads[at].wait()
        in_loads[at].wait()

        def back(span):
            before = product_right(pool[0, span], weights[2 + at % 2])
            before = (before * pool[buffer, span].astype(jnp.float32)).astype(narrow)
            pool[buffer, span] = before
            moved = product_right(before, weights[at % 2])
            level[1, span] = moved if at == 0 else level[1, span] + moved

        each_tile(back)
        if at < 2:
            span = pl.ds((at + 2) * width, width)
            out_loads[at + 2] = load(outer_hbm.at[span], weights.at[2 + at % 2])
            in_loads[at + 2] = load(chunk_of(inner_hbm, at + 2), weights.at[at % 2])
        right_step(at + 4)
        advance((6, 7), at + 1)
        if at == 0:
            join(OUTER)
        else:
            advance((OUTER,), at - 1)
        fold(big.at[at], pool.at[1], pool.at[buffer])
        if at < 2:
            rise_loads[at + 2] = load(chunk_of(rise_hbm, at + 2), pool.at[buffer])
    near_copy(INNER).start()
    query_load = load(query_hbm, pool.at[1])
    key_load, value_load = load(key_hbm, pool.at[2]), load(value_hbm, pool.at[3])
    late_loads = [
        load(query_weight_hbm, weights.at[0]), load(key_weight_hbm, weights.at[1]),
        load(value_weight_hbm, weights.at[2]),
    ]
    output_load = load(output_weight_hbm, weights.at[3])

    def back_norm(field, moved, gain_row, at):
        scale = root_scale(field)
        small[at : at + 1] += jnp.sum(moved * field * scale, axis=0, keepdims=True)
        weighted = moved * gain_row
        mean = jnp.mean(weighted * field, axis=-1, keepdims=True)
        return scale * weighted - field * (scale * scale * scale) * mean

    hidden_load.wait()

    def second(span):
        value = level[0, span] + back_norm(level[2, span], level[1, span], gain[1:2], 1)
        level[0, span] = value
        pool[0, span] = value.astype(narrow)

    each_tile(second)
    advance((6, 7), 5)
    advance((OUTER,), 3)
    context_load.wait()
    fold(flat[0], pool.at[4], pool.at[0])
    near_copy(5).start()
    normed_one_load = load(normed_one_hbm, pool.at[4])
    output_load.wait()

    def third(span):
        pool[5, span] = product_right(pool[0, span], weights[3]).astype(narrow)

    each_tile(third)
    tokens_load = load(tokens_hbm, pool.at[0])
    advance((6, 7), 6)
    advance((OUTER,), 4)
    join(INNER)
    join(5)
    for copy in (query_load, key_load, value_load):
        copy.wait()

    def pair_products():
        each_peer(lambda k: left_copy(k).wait_recv())
        for j, (left_at, right_at) in enumerate(spans):
            own, columns = pair_sums[j].shape
            wide = -(-own // 128) * 128
            left = left_all[:, :, left_at : left_at + wide].reshape(-1, wide)
            for begin in range(0, columns, width):
                right = right_all[:, :, right_at + begin : right_at + begin + width]
                block = product_left(left, right.reshape(-1, width))
                pair_work[j][:, begin : begin + width] = block[:own].astype(narrow)
            pair_near(j).start()

    def pair_cross():
        for j in range(pairs):
            pair_near(j).wait()
            mine = pair_work[j][:, half_of(core, pair_sums[j].shape[1])]
            pair_half[j][...] = plus(pair_half[j][...], mine).astype(narrow)
            pair_across(j).start()

    def share_copy(at):
        return pltpu.make_async_copy(
            shares_hbm.at[lax.rem(at, rows), at // rows],
            shares.at[lax.rem(at, 2)],
            share_sem.at[lax.rem(at, 2)],
        )

    turns = rows * (HEADS // 2)
    share_copy(0).start()

    def attend_pair(at, carry):
        pair, row, buffer = at // rows, lax.rem(at, rows), lax.rem(at, 2)
        share_copy(at).wait()

        @pl.when(at + 1 < turns)
        def _():
            share_copy(at + 1).start()

        @pl.when(lax.rem(at, 2) == 1)
        def _():
            advance((INNER,), at // 2)

        @pl.when((at > 0) & (lax.rem(at, 2) == 0))
        def _():
            advance((5,), at // 2 - 1)

        @pl.when(at == 2)
        def _():
            advance((6, 7), 7)
            for i in (6, 7):
                end_across(i).start()

        for turn, step in ((1, 5), (3, 6), (5, 7)):

            @pl.when(at == turn)
            def _():
                advance((OUTER,), step)

        @pl.when(at == 2)
        def _():
            pair_products()

        @pl.when(at == 4)
        def _():
            pair_cross()

        @pl.when(row == 0)
        def _():
            bias_acc[...] = jnp.zeros_like(bias_acc)

        key_acc[...] = jnp.zeros_like(key_acc)
        value_acc[...] = jnp.zeros_like(value_acc)
        columns = rows_of(pair, 2 * KV)

        def span(begin, size):
            return pl.ds(pl.multiple_of(row * length + begin, BLOCK), size)

        for block in range(blocks):
            keys, places = reach(block, blocks)
            own = span(block * BLOCK, BLOCK)
            near = span(keys.start, keys.stop - keys.start)
            query, grad = wide_heads(pool[1, own, columns]), wide_heads(pool[5, own, columns])
            narrow_shares = shares[buffer, block, :, places]
            part = narrow_shares.astype(jnp.float32)
            value_acc[keys] += product_left(narrow_shares, grad)
            moved = part * product_right(grad, pool[3, near, columns])
            grad_scores = moved - part * jnp.sum(moved, axis=1, keepdims=True)
            bias_acc[:, places] += grad_scores
            low = grad_scores.astype(narrow)
            key_acc[keys] += product_left(low, query)
            mixed = product(low, pool[2, near, columns])
            pool[1, own, columns] = narrow_heads(mixed).astype(narrow)
        pool[2, span(0, length), columns] = key_acc[...].astype(narrow)
        pool[3, span(0, length), columns] = value_acc[...].astype(narrow)

        @pl.when(row == rows - 1)
        def _():
            for head in range(2):
                block = bias_acc[head * BLOCK : (head + 1) * BLOCK]
                place = slice(head * 3 * BLOCK, (head + 1) * 3 * BLOCK)
                small[pl.ds(5 + pair, 1), place] = offset_sums(block)

        return carry

    lax.fori_loop(0, turns, attend_pair, 0)
    advance((5,), 5)
    normed_one_load.wait()
    fold(big.at[0], pool.at[4], pool.at[1])
    near_copy(2).start()
    advance((INNER,), 6)
    advance((5,), 6)
    fold(big.at[1], pool.at[4], pool.at[2])
    near_copy(3).start()
    join(2)
    advance((2,), 0)
    fold(big.at[2], pool.at[4], pool.at[3])
    near_copy(4).start()
    join(3)
    advance((3,), 0)
    advance((INNER,), 7)
    advance((5,), 7)
    for i in (INNER, 5):
        end_across(i).start()
    join(4)
    advance((4,), 0)
    close(OUTER)
    for i in (6, 7):
        close(i)
    tokens_load.wait()
    for copy in late_loads:
        copy.wait()

    def save(at):
        span = rows_of(at)
        return pltpu.make_async_copy(
            level.at[1, span], tokens_grad_hbm.at[span], share_sem.at[2 + at]
        )

    def last(at, carry):
        span = rows_of(at)
        moved = product_right(pool[1, span], weights[0])
        moved = moved + product_right(pool[2, span], weights[1])
        moved = moved + product_right(pool[3, span], weights[2])
        field = pool[0, span].astype(jnp.float32)
        level[1, span] = level[0, span] + back_norm(field, moved, gain[0:1], 0)
        save(at).start()
        advance((2, 3, 4), at + 1)
        return carry

    lax.fori_loop(0, tiles, last, 0)
    near_small = send(small, small_near, small_sem.at[0], small_sem.at[1], spot.sibling)
    near_small.start()
    advance((2, 3, 4), tiles + 1)
    near_small.wait()
    small_mid[...] = small[...] + small_near[...]
    far_small = send(small_mid, small_far, small_sem.at[2], small_sem.at[3], spot.opposite)
    far_small.start()
    advance((2, 3, 4), tiles + 2)
    far_small.wait()
    small_all[spot.fsdp] = small_mid[...] + small_far[...]
    each_peer(lambda k: small_copy(k).start())
    run((2, 3, 4), tiles + 3, count)
    for i in (2, 3, 4):
        end_across(i).start()
    for j in range(pairs):
        pair_across(j).wait()
        here = half_of(core, pair_sums[j].shape[1])
        pair_sums[j][:, here] = plus(pair_half[j][...], pair_far[j][...]).astype(narrow)
        pair_end(j).start()
    close(INNER)
    close(5)
    end_far(OUTER).wait()
    end_relay(OUTER).start()
    each_peer(lambda k: small_copy(k).wait_recv())
    small_sum[...] = lax.fori_loop(
        1, count, lambda k, so_far: so_far + small_all[k], small_all[0]
    )
    for i in (2, 3, 4):
        close(i)
    for i in range(8):
        end_near(i).wait()
    end_relay(OUTER).wait()
    for j in range(pairs):
        pair_end(j).wait()
    for at in range(tiles):
        save(at).wait()

    def drain(step, carry):
        for way in range(2):
            far_copy(OUTER, way, step).wait_send()
        return carry

    lax.fori_loop(0, count, drain, 0)

    def drain_ring(step, carry):
        for way in range(2):
            for i in range(8):
                for at in range(SPLITS.get(i, 1)):
                    ring_copy(i, way, step, at).wait_send()
            right_copy(way, step).wait_send()
        left_copy(step + 1).wait_send()
        small_copy(step + 1).wait_send()
        return carry

    lax.fori_loop(0, count - 1, drain_ring, 0)


def backward(
    count, rows, whole, kept, tokens, cotangent, grad_keys, grad_values,
    left_part, right_part, pair_shapes, gains, decoder_gains,
):
    (
        query, key, value, shares, context, hidden, normed_two,
        active, rise, memory, unused_keys, unused_values, normed_one,
    ) = kept
    many, width = tokens.shape
    depth, narrow, wide = width // count, jnp.bfloat16, jnp.float32
    pairs = len(pair_shapes)
    spans, left_at, right_at = [], 0, 0
    for own, columns in pair_shapes:
        spans.append((left_at, right_at))
        left_at, right_at = left_at + -(-own // 128) * 128, right_at + columns
    dma, vmem = pltpu.SemaphoreType.DMA, pltpu.VMEM
    pieces = [(depth, width), (depth, width // 2)] + [(depth // 2, width // 2)] * 6
    outs = [(depth, 4 * width), (4 * depth, width)] + [(depth, width)] * 6
    little = (16, width)
    scratch = [vmem((4, width, width), narrow)] + [vmem((width, width), narrow)] * 2
    scratch += [vmem((2, width, width), narrow), vmem((4, width, width // 2), narrow)]
    scratch += [vmem((width, width // 2), narrow)] * 6
    scratch += [vmem((2, count) + piece, narrow) for piece in pieces]
    scratch += [vmem((2,) + piece, narrow) for piece in pieces]
    scratch += [vmem((2, count) + pieces[1], narrow)]
    scratch += [vmem(left_part.shape, narrow), vmem((count,) + right_part.shape, narrow)]
    scratch += [vmem(s, narrow) for s in pair_shapes]
    scratch += [vmem((r, c // 2), narrow) for r, c in pair_shapes] * 2
    scratch += [vmem(little, wide)] * 4 + [vmem((count,) + little, wide)]
    scratch += [
        vmem((6, many, width), narrow), vmem((3, many, width), wide),
        vmem((4, width, width), narrow), vmem((2,) + shares.shape[2:], narrow),
        vmem((2 * BLOCK, 3 * BLOCK), wide),
    ]
    scratch += [vmem((many // rows, 2 * KV), wide)] * 2
    scratch += [
        dma((2, 8)), dma((8, 2, 2, count)), dma((8, 2, 2, count)), dma((2, 2, count)), dma((8, 8)),
        dma((count,)), dma((count,)), dma((2, count)), dma((2, count)), dma((6, pairs)),
        dma((4,)), dma((count,)), dma((count,)), dma((48,)), dma((2 + many // TILE,)),
    ]
    shapes = [jax.ShapeDtypeStruct(s, narrow) for s in outs + list(pair_shapes)]
    shapes += [jax.ShapeDtypeStruct(little, wide), jax.ShapeDtypeStruct((many, width), wide)]
    anywhere = pl.BlockSpec(memory_space=pl.ANY)
    local = pl.BlockSpec(memory_space=pltpu.VMEM)
    got = pl.pallas_call(
        functools.partial(backward_kernel, count, rows, spans),
        out_shape=shapes,
        in_specs=[anywhere] * 23 + [local] * 4,
        out_specs=[local] * (len(shapes) - 1) + [anywhere],
        scratch_shapes=scratch,
        compiler_params=pltpu.CompilerParams(
            collective_id=3, has_side_effects=True, vmem_limit_bytes=63 * 2**20
        ),
        name="backward",
    )(
        whole[4], whole[5], whole[0], whole[1], whole[2], whole[3], whole[6], whole[7],
        active, rise, normed_two, context, query, key, value, normed_one, tokens, memory,
        grad_keys, grad_values, cotangent, hidden, shares,
        left_part, right_part, gains, decoder_gains,
    )
    return got[:8], got[8 : 8 + pairs], got[-2], got[-1]


def backward_apart(
    count, rows, whole, kept, tokens, cotangent, grad_cross_keys, grad_cross_values,
    left_part, right_part, pair_shapes, gains, decoder_gains,
):
    (
        query_full, key_full, value_full, output_full, inner_full, outer_full, cross_key_full,
        cross_value_full,
    ) = whole[:8]
    (
        query_all, key_all, value_all, shares, context, hidden, normed_two,
        active, rise, memory, unused_keys, unused_values, normed_one,
    ) = kept
    row_count, length = rows, tokens.shape[0] // rows
    gain_one, gain_two = gains[0], gains[1]
    field = tokens.astype(jnp.float32)
    scale_one, scale_two = root_scale(field), root_scale(hidden)
    grad_cross_key = product_left(memory, grad_cross_keys)
    grad_cross_value = product_left(memory, grad_cross_values)
    grad_memory = product_right(grad_cross_keys, cross_key_full) + product_right(
        grad_cross_values, cross_value_full
    )
    grad_encoded = cotangent.astype(jnp.float32) + grad_memory
    grad_branch = grad_encoded.astype(jnp.bfloat16)
    grad_outer = product_left(active, grad_branch)
    grad_active = product_right(grad_branch, outer_full)
    grad_before = (grad_active * rise).astype(jnp.bfloat16)
    grad_inner = product_left(normed_two, grad_before)
    grad_normed = product_right(grad_before, inner_full)
    field_part, grad_gain_two = norm_back(
        grad_normed, hidden, scale_two, gain_two
    )
    grad_hidden = grad_encoded + field_part
    grad_branch = grad_hidden.astype(jnp.bfloat16)
    grad_output = product_left(context, grad_branch)
    grad_context = product_right(grad_branch, output_full).astype(jnp.bfloat16)
    grad_query_all, grad_key_all, grad_value_all, bias_sums = attend_rows_back(
        row_count, length, query_all, key_all, value_all, grad_context, shares
    )
    grad_query = product_left(normed_one, grad_query_all)
    grad_key = product_left(normed_one, grad_key_all)
    grad_value = product_left(normed_one, grad_value_all)
    grad_normed = (
        product_right(grad_query_all, query_full)
        + product_right(grad_key_all, key_full)
        + product_right(grad_value_all, value_full)
    )
    field_part, grad_gain_one = norm_back(
        grad_normed, field, scale_one, gain_one
    )
    tokens_grad = grad_hidden + field_part
    small = jnp.concatenate([
        jnp.stack([grad_gain_one, grad_gain_two]),
        decoder_gains,
        bias_sums.reshape(HEADS // 2, -1),
        jnp.zeros((5, tokens.shape[1]), jnp.float32),
    ])
    encoder_grads = (
        grad_inner, grad_outer, grad_query, grad_key, grad_value, grad_output,
        grad_cross_key, grad_cross_value,
    )
    encoder_sums, decoder_sums, small_sum = reduce_grads(
        count,
        ENCODER_KINDS,
        [
            g.astype(jnp.bfloat16).reshape(count, g.shape[0] // count, g.shape[1])
            for g in encoder_grads
        ],
        left_part,
        right_part,
        pair_shapes,
        small,
    )
    return encoder_sums, decoder_sums, small_sum, tokens_grad


def widen_kernel(total, *refs):
    sources, targets = refs[:total], refs[total : 2 * total]
    held, wide, sems = refs[2 * total : 3 * total], list(refs[3 * total : -1]), refs[-1]
    ready = [part if part.dtype == jnp.float32 else wide.pop(0) for part in held]
    loads = [pltpu.make_async_copy(sources[at], held[at], sems.at[at]) for at in range(total)]
    stores = [
        pltpu.make_async_copy(ready[at], targets[at], sems.at[total + at]) for at in range(total)
    ]
    for copy in loads:
        copy.start()
    for at in range(total):
        loads[at].wait()
        if held[at] is not ready[at]:
            ready[at][...] = held[at][...].astype(jnp.float32)
        stores[at].start()
    for copy in stores:
        copy.wait()


def widen(parts):
    anywhere, total = pl.BlockSpec(memory_space=pl.ANY), len(parts)
    return pl.pallas_call(
        functools.partial(widen_kernel, total),
        out_shape=[jax.ShapeDtypeStruct(part.shape, jnp.float32) for part in parts],
        in_specs=[anywhere] * total,
        out_specs=[anywhere] * total,
        scratch_shapes=[pltpu.VMEM(part.shape, part.dtype) for part in parts]
        + [
            pltpu.VMEM(part.shape, jnp.float32) for part in parts if part.dtype != jnp.float32
        ]
        + [pltpu.SemaphoreType.DMA((2 * total,))],
        compiler_params=pltpu.CompilerParams(vmem_limit_bytes=63 * 2**20),
        name="widen",
    )(*parts)


def on_device(
    tokens,
    segment_index,
    start_vectors,
    first_gain,
    query_weight,
    key_weight,
    value_weight,
    output_weight,
    position_table,
    second_gain,
    inner_weight,
    outer_weight,
    start_gain,
    self_value,
    self_output,
    middle_gain,
    cross_query,
    cross_key,
    cross_value,
    cross_output,
    final_gain,
    decoder_inner,
    decoder_outer,
    encoded_cotangent,
    decoded_cotangent,
):
    row_count = segment_index.shape[0]
    length = segment_index.shape[1]
    slot_count = start_vectors.shape[1]
    width = tokens.shape[1]
    count = lax.axis_size("fsdp")
    depth = first_gain.shape[0]
    choices = jnp.arange(position_table.shape[0], dtype=jnp.int32)
    onehot = (offset_buckets()[None, :] == choices[:, None]).astype(jnp.float32)
    base = jnp.dot(position_table.T, onehot, precision=lax.Precision.HIGHEST)
    gains = jnp.stack([first_gain, second_gain, start_gain, middle_gain, final_gain])
    gains = jnp.pad(gains, ((0, 11), (0, BLOCK - depth)))
    shards = (
        query_weight, key_weight, value_weight, output_weight, inner_weight, outer_weight,
        cross_key, cross_value, self_value, self_output, cross_query, cross_output,
        decoder_inner, decoder_outer, gains,
    )
    fused = count == 8 and depth % 32 == 0 and (row_count, length) == (2, 512)
    plan = forward if fused else forward_apart
    whole, all_gains, kept = plan(count, shards, tokens, segment_index, base)
    memory, cross_keys, cross_values = kept[9:12]
    token_count = row_count * slot_count
    (
        decoded, start_grad, decoder_gain_grads,
        normed_fin, decoder_active, normed_start, own_value, normed_mid, cross_context,
        decoder_before_grad, last_branch, grad_own, self_branch, grad_asking, cross_branch,
        grad_cross_keys, grad_cross_values, encoded,
    ) = decode(
        segment_index,
        start_vectors.reshape(token_count, width),
        decoded_cotangent.reshape(token_count, width),
        all_gains,
        cross_keys,
        cross_values,
        memory,
        whole[8:14],
    )
    lefts = (normed_fin, decoder_active, normed_start, own_value, normed_mid, cross_context)
    rights = (decoder_before_grad, last_branch, grad_own, self_branch, grad_asking, cross_branch)
    pair_shapes = [(left.shape[1] // count, right.shape[1]) for left, right in zip(lefts, rights)]
    left_cols = []
    for left, (rows, unused) in zip(lefts, pair_shapes):
        columns = left.reshape(token_count, count, rows).transpose(1, 0, 2)
        left_cols.append(jnp.pad(columns, ((0, 0), (0, 0), (0, -rows % 128))))
    turn_back = backward if fused else backward_apart
    encoder_sums, decoder_sums, small_sum, tokens_grad = turn_back(
        count, row_count, whole, kept, tokens, encoded_cotangent,
        grad_cross_keys, grad_cross_values,
        jnp.concatenate(left_cols, axis=2),
        jnp.concatenate(rights, axis=1),
        pair_shapes, all_gains, decoder_gain_grads,
    )
    (
        inner_weight_grad, outer_weight_grad, query_weight_grad, key_weight_grad,
        value_weight_grad, output_weight_grad, cross_key_grad, cross_value_grad,
        decoder_inner_grad, decoder_outer_grad, self_value_grad, self_output_grad,
        cross_query_grad, cross_output_grad, tokens_grad,
    ) = widen([*encoder_sums, *decoder_sums, tokens_grad])
    position_table_grad = lax.dot_general(
        onehot,
        small_sum[5:11].reshape(HEADS, 3 * BLOCK),
        (((1,), (1,)), ((), ())),
        precision=lax.Precision.HIGHEST,
    )
    own_gains = lax.dynamic_slice_in_dim(
        small_sum[:5], lax.axis_index("fsdp") * depth, depth, axis=1
    )
    first_gain_grad, second_gain_grad, start_gain_grad, middle_gain_grad, final_gain_grad = own_gains
    decoded = decoded.reshape(start_vectors.shape)
    start_grad = start_grad.reshape(start_vectors.shape)
    return (
        encoded,
        decoded,
        tokens_grad,
        start_grad,
        first_gain_grad,
        query_weight_grad,
        key_weight_grad,
        value_weight_grad,
        output_weight_grad,
        position_table_grad,
        second_gain_grad,
        inner_weight_grad,
        outer_weight_grad,
        start_gain_grad,
        self_value_grad,
        self_output_grad,
        middle_gain_grad,
        cross_query_grad,
        cross_key_grad,
        cross_value_grad,
        cross_output_grad,
        final_gain_grad,
        decoder_inner_grad,
        decoder_outer_grad,
    )


def solution(mesh):
    placed = (
        P(("dp", "fsdp"), None),
        P(("dp", "fsdp"), None),
        P(("dp", "fsdp"), None, None),
        P("fsdp"),
        P("fsdp", None),
        P("fsdp", None),
        P("fsdp", None),
        P("fsdp", None),
        P(),
        P("fsdp"),
        P("fsdp", None),
        P("fsdp", None),
        P("fsdp"),
        P("fsdp", None),
        P("fsdp", None),
        P("fsdp"),
        P("fsdp", None),
        P("fsdp", None),
        P("fsdp", None),
        P("fsdp", None),
        P("fsdp"),
        P("fsdp", None),
        P("fsdp", None),
        P(("dp", "fsdp"), None),
        P(("dp", "fsdp"), None, None),
    )
    return jax.shard_map(
        on_device,
        mesh=mesh,
        in_specs=placed,
        out_specs=(
            P(("dp", "fsdp"), None),
            P(("dp", "fsdp"), None, None),
            P(("dp", "fsdp"), None),
            P(("dp", "fsdp"), None, None),
            P("fsdp"),
            P("fsdp", None),
            P("fsdp", None),
            P("fsdp", None),
            P("fsdp", None),
            P(),
            P("fsdp"),
            P("fsdp", None),
            P("fsdp", None),
            P("fsdp"),
            P("fsdp", None),
            P("fsdp", None),
            P("fsdp"),
            P("fsdp", None),
            P("fsdp", None),
            P("fsdp", None),
            P("fsdp", None),
            P("fsdp"),
            P("fsdp", None),
            P("fsdp", None),
        ),
        check_vma=False,
    )
```

```python
import functools

import jax
import jax.numpy as jnp
from jax import lax
from jax.experimental import pallas as pl
from jax.experimental.pallas import tpu as pltpu
from jax.sharding import PartitionSpec as P

HEADS = 12
KV = 64
BLOCK = 128


epsilon = 1e-06
negative_fill = -1e30
bucket_edges = (12, 16, 23, 32, 46, 64, 91)


MESH = pl.DeviceIdType.MESH
KINDS = (
    "square", "square", "square", "square", "wide", "tall", "square", "square",
    "square", "square", "square", "square", "wide", "tall", "small",
)


def ring_position(index, count):
    if count == 64:
        slow, rest = index // 32, index % 32
        row, column = rest // 8, rest % 8
        place = row * 8 + column + (row % 2) * (7 - 2 * column)
        return place + slow * (count - 1 - 2 * place)
    across, along = index % 2, index // 2
    return along + across * (count - 1 - 2 * along)


def ring_index(position, count):
    position = lax.rem(position, count)
    across = position // (count // 2)
    along = position + across * (count - 1 - 2 * position)
    if count == 64:
        row, column = along // 8, along % 8
        return across * 32 + row * 8 + column + (row % 2) * (7 - 2 * column)
    return 2 * along + across


class Spot:
    def __init__(self, count):
        self.count = count
        self.dp = lax.axis_index("dp")
        self.fsdp = lax.axis_index("fsdp")
        self.core = lax.rem(self.dp, 2)
        self.plane = self.dp // 2
        self.place = ring_position(self.fsdp, count)
        self.sibling = (self.dp + 1 - 2 * self.core, self.fsdp)
        self.opposite = (lax.rem(self.dp + 2, 4), self.fsdp)
        self.after = (self.dp, ring_index(self.place + 1, count))
        self.before = (self.dp, ring_index(self.place + count - 1, count))

    def greet(self, others=()):
        barrier = pltpu.get_barrier_semaphore()
        partners = (self.sibling, self.opposite, self.after, self.before) + tuple(others)
        for partner in partners:
            pl.semaphore_signal(barrier, inc=1, device_id=partner, device_id_type=MESH)
        pl.semaphore_wait(barrier, len(partners))


def cut(kind, ref, plane, core):
    rows, columns = ref.shape
    if kind == "small":
        return ref
    if kind == "square":
        half = columns // 2
        return ref.at[:, pl.ds(pl.multiple_of(core * half, 128), half)]
    if kind == "wide":
        quarter = columns // 4
        return ref.at[:, pl.ds(pl.multiple_of((core * 2 + plane) * quarter, 128), quarter)]
    half, upper = columns // 2, rows // 2
    return ref.at[
        pl.ds(pl.multiple_of(plane * upper, 8), upper),
        pl.ds(pl.multiple_of(core * half, 128), half),
    ]


def send(source, target, send_sem, recv_sem, device):
    return pltpu.make_async_remote_copy(
        src_ref=source,
        dst_ref=target,
        send_sem=send_sem,
        recv_sem=recv_sem,
        device_id=device,
        device_id_type=MESH,
    )


def gather_kernel(count, kinds, *refs):
    total = len(kinds)
    shards, fulls = refs[:total], refs[total : 2 * total]
    ring_out, ring_in, near_out, near_in, far_out, far_in, last_out, last_in, own_sem = refs[
        2 * total :
    ]
    spot = Spot(count)
    split = [i for i in range(total) if kinds[i] in ("wide", "tall")]

    window = min(count, 8)

    def slot_of(i, step):
        turn = step if i % 2 else count - step
        return ring_index(spot.place + turn, count)

    def ring_copy(i, step, source=None):
        here = cut(kinds[i], fulls[i].at[slot_of(i, step)], spot.plane, spot.core)
        return send(
            here if source is None else source,
            here,
            ring_out.at[i, lax.rem(step, window)],
            ring_in.at[i, step],
            spot.before if i % 2 else spot.after,
        )

    def near_copy(i, step):
        here = cut(kinds[i], fulls[i].at[slot_of(i, step)], spot.plane, spot.core)
        out = near_out.at[i, lax.rem(step, window)]
        return send(here, here, out, near_in.at[i, step], spot.sibling)

    def far_copy(i, step):
        here = cut(kinds[i], fulls[i].at[slot_of(i, step)], spot.plane, spot.core)
        at = split.index(i)
        out = far_out.at[at, lax.rem(step, window)]
        return send(here, here, out, far_in.at[at, step], spot.opposite)

    def last_copy(i, step):
        here = cut(kinds[i], fulls[i].at[slot_of(i, step)], 1 - spot.plane, spot.core)
        at = split.index(i)
        out = last_out.at[at, lax.rem(step, window)]
        return send(here, here, out, last_in.at[at, step], spot.sibling)

    def start(copy, i, step, first):
        if window < count:

            @pl.when(step >= first + window)
            def _():
                copy(i, step - window).wait_send()

        copy(i, step).start()

    def finish(copy, i, first, end):
        def one(step, carry):
            copy(i, step).wait_send()
            return carry

        lax.fori_loop(max(first, end - window), end, one, 0)

    owns = []
    for i in range(total):
        owns.append(pltpu.make_async_copy(shards[i], fulls[i].at[spot.fsdp], own_sem.at[i]))
        owns[-1].start()
    spot.greet()
    for i in range(total):
        ring_copy(i, 0, cut(kinds[i], shards[i], spot.plane, spot.core)).start()

    def one_step(step, carry):
        for i in range(total):
            ring_copy(i, step - 1).wait_recv()

            @pl.when(step < count - 1)
            def _():
                start(ring_copy, i, step, 0)

            if kinds[i] != "small":
                start(near_copy, i, step, 1)
            if i in split:
                start(far_copy, i, step, 1)

        @pl.when(step > 1)
        def _():
            for i in split:
                far_copy(i, step - 1).wait_recv()
                start(last_copy, i, step - 1, 1)

        return carry

    lax.fori_loop(1, count, one_step, 0)
    for i in split:
        far_copy(i, count - 1).wait_recv()
        start(last_copy, i, count - 1, 1)

    def settle(step, carry):
        for i in range(total):
            if kinds[i] != "small":
                near_copy(i, step).wait_recv()
            if i in split:
                last_copy(i, step).wait_recv()
        return carry

    lax.fori_loop(1, count, settle, 0)
    for i in range(total):
        finish(ring_copy, i, 0, count - 1)
        if kinds[i] != "small":
            finish(near_copy, i, 1, count)
        if i in split:
            finish(far_copy, i, 1, count)
            finish(last_copy, i, 1, count)
    for copy in owns:
        copy.wait()


def gather_weights(count, shards, kinds):
    total = len(shards)
    split = sum(kind in ("wide", "tall") for kind in kinds)
    window = min(count, 8)
    many, few = [
        [pltpu.SemaphoreType.DMA((rows, window)), pltpu.SemaphoreType.DMA((rows, count))] * 2
        for rows in (total, split)
    ]
    return pl.pallas_call(
        functools.partial(gather_kernel, count, kinds),
        out_shape=[jax.ShapeDtypeStruct((count,) + s.shape, s.dtype) for s in shards],
        in_specs=[pl.BlockSpec(memory_space=pl.ANY)] * total,
        out_specs=[pl.BlockSpec(memory_space=pl.ANY)] * total,
        scratch_shapes=many + few + [pltpu.SemaphoreType.DMA((total,))],
        compiler_params=pltpu.CompilerParams(collective_id=0, has_side_effects=True),
        name="gather_weights",
    )(*shards)

def plus(*terms):
    total = terms[0].astype(jnp.float32)
    for term in terms[1:]:
        total = total + term.astype(jnp.float32)
    return total


def half_of(core, columns):
    half = columns // 2
    return pl.ds(pl.multiple_of(core * half, 128), half)


def plane_part(kind, plane, rows, columns):
    if kind == "wide":
        return slice(None), pl.ds(pl.multiple_of(plane * (columns // 2), 128), columns // 2)
    if kind == "tall":
        return pl.ds(pl.multiple_of(plane * (rows // 2), 8), rows // 2), slice(None)
    return slice(None), slice(None)


ENCODER_KINDS = ("wide", "tall", "square", "square", "square", "square", "square", "square")


def reduce_kernel(count, kinds, spans, *refs):
    total, pairs = len(kinds), len(spans)
    refs = list(refs)

    def take(size):
        got = refs[:size]
        del refs[:size]
        return got

    grads = take(total)
    left_part, right_part, small = take(3)
    sums = take(total)
    pair_sums = take(pairs)
    (small_sum,) = take(1)
    half, work, final = take(total), take(total), take(total)
    split = [i for i in range(total) if kinds[i] != "square"]
    far = take(len(split))
    left_all, right_all = take(2)
    pair_half, pair_far, pair_work = take(pairs), take(pairs), take(pairs)
    small_near, small_mid, small_far, small_all = take(4)
    (
        near_sem, ring_out, ring_in, far_sem, end_sem, left_out, left_in,
        right_out, right_in, pair_sem, small_sem, small_out, small_in,
    ) = take(13)
    spot = Spot(count)
    core, plane = spot.core, spot.plane
    diagonal = (lax.rem(spot.dp + 2, 4) + 1 - 2 * core, spot.fsdp)

    def peer(k):
        return (spot.dp, lax.rem(spot.fsdp + k, count))

    barrier = pltpu.get_barrier_semaphore()
    for partner in (spot.sibling, spot.opposite, diagonal):
        pl.semaphore_signal(barrier, inc=1, device_id=partner, device_id_type=MESH)

    def greet(k, carry):
        pl.semaphore_signal(barrier, inc=1, device_id=peer(k), device_id_type=MESH)
        return carry

    lax.fori_loop(1, count, greet, 0)
    pl.semaphore_wait(barrier, count + 2)

    def near_copy(i):
        columns = grads[i].shape[2]
        return send(
            grads[i].at[:, :, half_of(1 - core, columns)], half[i],
            near_sem.at[0, i], near_sem.at[1, i], spot.sibling,
        )

    def slot_at(i, step):
        turn = step + 1 if i % 2 else count - 1 - step
        return ring_index(spot.place + turn, count)

    def far_copy(i, step):
        at = split.index(i)
        rows, columns = half[i].shape[1:]
        part = plane_part(kinds[i], 1 - plane, rows, columns)
        return send(
            half[i].at[(slot_at(i, step),) + part], far[at].at[step],
            far_sem.at[0, at, step], far_sem.at[1, at, step], spot.opposite,
        )

    def ring_copy(i, step):
        return send(
            work[i].at[step], work[i].at[step + 1], ring_out.at[i, step], ring_in.at[i, step],
            spot.before if i % 2 else spot.after,
        )

    def left_copy(k):
        other = lax.rem(spot.fsdp + k, count)
        return send(
            left_part.at[other], left_all.at[spot.fsdp], left_out.at[k], left_in.at[k], peer(k)
        )

    def right_copy(way, step):
        turn = step if way else count - step
        slot = ring_index(spot.place + turn, count)
        width = right_part.shape[1] // 2
        here = right_all.at[slot, :, way * width : (way + 1) * width]
        return send(
            here, here, right_out.at[way, step], right_in.at[way, step],
            spot.before if way else spot.after,
        )

    for i in range(total):
        near_copy(i).start()
    near_small = send(small, small_near, small_sem.at[0], small_sem.at[1], spot.sibling)
    near_small.start()

    def left_start(k, carry):
        left_copy(k).start()
        return carry

    lax.fori_loop(1, count, left_start, 0)
    right_all[spot.fsdp] = right_part[...]
    left_all[spot.fsdp] = left_part[spot.fsdp]
    for way in range(2):
        right_copy(way, 0).start()
    near_small.wait()
    small_mid[...] = small[...] + small_near[...]
    far_small = send(small_mid, small_far, small_sem.at[2], small_sem.at[3], spot.opposite)
    far_small.start()

    for i in range(total):
        near_copy(i).wait_recv()

        def join(slot, carry):
            mine = grads[i][slot, :, half_of(core, grads[i].shape[2])]
            half[i][slot] = plus(half[i][slot], mine).astype(jnp.bfloat16)
            return carry

        lax.fori_loop(0, count, join, 0)
        if i in split:

            def far_start(step, carry):
                far_copy(i, step).start()
                return carry

            lax.fori_loop(0, count, far_start, 0)

    far_small.wait()
    small_all[spot.fsdp] = small_mid[...] + small_far[...]

    def small_copy(k):
        here = small_all.at[spot.fsdp]
        return send(here, here, small_out.at[k], small_in.at[k], peer(k))

    def small_start(k, carry):
        small_copy(k).start()
        return carry

    lax.fori_loop(1, count, small_start, 0)

    def right_step(step, carry):
        for way in range(2):
            right_copy(way, step - 1).wait_recv()

            @pl.when(step < count - 1)
            def _():
                right_copy(way, step).start()

        return carry

    lax.fori_loop(1, count, right_step, 0)

    def left_wait(k, carry):
        left_copy(k).wait_recv()
        return carry

    lax.fori_loop(1, count, left_wait, 0)

    def pair_near(j):
        columns = pair_sums[j].shape[1]
        return send(
            pair_work[j].at[:, half_of(1 - core, columns)], pair_half[j],
            pair_sem.at[0, j], pair_sem.at[1, j], spot.sibling,
        )

    def pair_across(j):
        return send(
            pair_half[j], pair_far[j], pair_sem.at[2, j], pair_sem.at[3, j], spot.opposite
        )

    def pair_end(j):
        here = pair_sums[j].at[:, half_of(core, pair_sums[j].shape[1])]
        return send(here, here, pair_sem.at[4, j], pair_sem.at[5, j], spot.sibling)

    for j, (left_at, right_at) in enumerate(spans):
        rows, columns = pair_sums[j].shape
        span = -(-rows // 128) * 128
        left = left_all[:, :, left_at : left_at + span].reshape(-1, span)
        for begin in range(0, columns, 768):
            right = right_all[:, :, right_at + begin : right_at + begin + 768].reshape(-1, 768)
            block = lax.dot_general(
                left, right, (((0,), (0,)), ((), ())), preferred_element_type=jnp.float32
            )
            pair_work[j][:, begin : begin + 768] = block[:rows].astype(jnp.bfloat16)
        pair_near(j).start()
    for j in range(pairs):
        pair_near(j).wait()
        mine = pair_work[j][:, half_of(core, pair_sums[j].shape[1])]
        pair_half[j][...] = plus(pair_half[j][...], mine).astype(jnp.bfloat16)
        pair_across(j).start()

    def one_step(step, carry):
        for i in range(total):
            rows, columns = half[i].shape[1:]
            slot = slot_at(i, step)
            value = half[i][(slot,) + plane_part(kinds[i], plane, rows, columns)]
            value = value.astype(jnp.float32)
            if i in split:
                far_copy(i, step).wait_recv()
                value = value + far[split.index(i)][step].astype(jnp.float32)

            @pl.when(step > 0)
            def _():
                ring_copy(i, step - 1).wait_recv()
                work[i][step] = plus(value, work[i][step]).astype(jnp.bfloat16)

            @pl.when(step == 0)
            def _():
                work[i][step] = value.astype(jnp.bfloat16)

            @pl.when(step < count - 1)
            def _():
                ring_copy(i, step).start()

        return carry

    lax.fori_loop(0, count, one_step, 0)

    def end_across(i):
        return send(
            work[i].at[count - 1], final[i], end_sem.at[0, i], end_sem.at[1, i], spot.opposite
        )

    def end_piece(i, mine_plane):
        rows, columns = sums[i].shape
        wide = half_of(core, columns)
        if kinds[i] == "square":
            return sums[i].at[:, wide]
        return cut(kinds[i], sums[i], mine_plane, core)

    def end_copies(i):
        here = end_piece(i, plane)
        copies = [send(here, here, end_sem.at[2, i], end_sem.at[3, i], spot.sibling)]
        if i in split:
            copies.append(send(here, here, end_sem.at[4, i], end_sem.at[5, i], spot.opposite))
            copies.append(send(here, here, end_sem.at[6, i], end_sem.at[7, i], diagonal))
        return copies

    for i in range(total):
        if i not in split:
            end_across(i).start()
    for i in split:
        end_piece(i, plane)[...] = work[i][count - 1]
        for copy in end_copies(i):
            copy.start()
    for j in range(pairs):
        pair_across(j).wait()
        here = half_of(core, pair_sums[j].shape[1])
        pair_sums[j][:, here] = plus(pair_half[j][...], pair_far[j][...]).astype(jnp.bfloat16)
        pair_end(j).start()
    for i in range(total):
        if i not in split:
            end_across(i).wait()
            value = plus(work[i][count - 1], final[i][...]).astype(jnp.bfloat16)
            end_piece(i, plane)[...] = value
            for copy in end_copies(i):
                copy.start()

    def small_wait(k, carry):
        small_copy(k).wait_recv()
        return carry

    lax.fori_loop(1, count, small_wait, 0)
    small_sum[...] = lax.fori_loop(
        1, count, lambda k, so_far: so_far + small_all[k], small_all[0]
    )
    for i in range(total):
        for copy in end_copies(i):
            copy.wait()
    for j in range(pairs):
        pair_end(j).wait()
    for i in range(total):
        near_copy(i).wait_send()

    def drain(step, carry):
        for i in split:
            far_copy(i, step).wait_send()
        return carry

    lax.fori_loop(0, count, drain, 0)

    def drain_ring(step, carry):
        for i in range(total):
            ring_copy(i, step).wait_send()
        for way in range(2):
            right_copy(way, step).wait_send()
        left_copy(step + 1).wait_send()
        small_copy(step + 1).wait_send()
        return carry

    lax.fori_loop(0, count - 1, drain_ring, 0)


def reduce_grads(count, kinds, grads, left_part, right_part, pair_shapes, small):
    total, pairs = len(kinds), len(pair_shapes)
    spans, left_at, right_at = [], 0, 0
    for rows, columns in pair_shapes:
        spans.append((left_at, right_at))
        left_at, right_at = left_at + -(-rows // 128) * 128, right_at + columns
    narrow = jnp.bfloat16
    blocks = [g.shape[1:] for g in grads]
    pieces = []
    for kind, (rows, columns) in zip(kinds, blocks):
        if kind == "wide":
            pieces.append((rows, columns // 4))
        elif kind == "tall":
            pieces.append((rows // 2, columns // 2))
        else:
            pieces.append((rows, columns // 2))
    split = [i for i in range(total) if kinds[i] != "square"]
    dma = pltpu.SemaphoreType.DMA
    scratch = [pltpu.VMEM((count, r, c // 2), narrow) for r, c in blocks]
    scratch += [pltpu.VMEM((count, r, c), narrow) for r, c in pieces]
    scratch += [pltpu.VMEM((r, c), narrow) for r, c in pieces]
    scratch += [pltpu.VMEM((count,) + pieces[i], narrow) for i in split]
    scratch += [
        pltpu.VMEM(left_part.shape, narrow),
        pltpu.VMEM((count,) + right_part.shape, narrow),
    ]
    scratch += [pltpu.VMEM((r, c // 2), narrow) for r, c in pair_shapes] * 2
    scratch += [pltpu.VMEM((r, c), narrow) for r, c in pair_shapes]
    scratch += [pltpu.VMEM(small.shape, jnp.float32)] * 3
    scratch += [pltpu.VMEM((count,) + small.shape, jnp.float32)]
    scratch += [
        dma((2, total)), dma((total, count)), dma((total, count)), dma((2, len(split), count)),
        dma((8, total)), dma((count,)), dma((count,)), dma((2, count)), dma((2, count)),
        dma((6, pairs)), dma((4,)), dma((count,)), dma((count,)),
    ]
    outs = [jax.ShapeDtypeStruct(b, narrow) for b in blocks]
    outs += [jax.ShapeDtypeStruct(s, narrow) for s in pair_shapes]
    outs += [jax.ShapeDtypeStruct(small.shape, jnp.float32)]
    got = pl.pallas_call(
        functools.partial(reduce_kernel, count, kinds, spans),
        out_shape=outs,
        in_specs=[pl.BlockSpec(memory_space=pltpu.VMEM)] * (total + 3),
        out_specs=[pl.BlockSpec(memory_space=pltpu.VMEM)] * len(outs),
        scratch_shapes=scratch,
        compiler_params=pltpu.CompilerParams(
            collective_id=1, has_side_effects=True, vmem_limit_bytes=62 * 2**20
        ),
        name="reduce_grads",
    )(*grads, left_part, right_part, small)
    return got[:total], got[total : total + pairs], got[-1]


def product(left, right):
    return jnp.dot(left, right, preferred_element_type=jnp.float32)


def product_left(left, right):
    return lax.dot_general(
        left, right, (((0,), (0,)), ((), ())), preferred_element_type=jnp.float32
    )


def product_right(left, right):
    return lax.dot_general(
        left, right, (((1,), (1,)), ((), ())), preferred_element_type=jnp.float32
    )


def root_scale(field):
    return lax.rsqrt(jnp.mean(field * field, axis=-1, keepdims=True) + epsilon)


def norm_back(grad_normed, field, scale, gain):
    gain_grad = jnp.sum(grad_normed * field * scale, axis=0)
    weighted = grad_normed * gain
    field_grad = scale * weighted - field * (scale * scale * scale) * jnp.mean(
        weighted * field, axis=-1, keepdims=True
    )
    return (field_grad, gain_grad)


def wide_heads(block):
    first = lax.broadcasted_iota(jnp.int32, block.shape, 1) < KV
    none = jnp.zeros_like(block)
    return jnp.concatenate([jnp.where(first, block, none), jnp.where(first, none, block)], axis=0)


def narrow_heads(stacked):
    half = stacked.shape[0] // 2
    first = lax.broadcasted_iota(jnp.int32, (half, stacked.shape[1]), 1) < KV
    return jnp.where(first, stacked[:half], stacked[half:])


def reach(at, blocks):
    low, high = max(0, at - 1), min(blocks, at + 2)
    begin = (low - at + 1) * BLOCK
    return slice(low * BLOCK, high * BLOCK), slice(begin, begin + (high - low) * BLOCK)


def bias_block(base):
    heads = []
    for at in range(2):
        level = jnp.broadcast_to(base[at : at + 1], (BLOCK, base.shape[1]))
        heads.append(pltpu.roll(level, 0, axis=1, stride=1, stride_axis=0))
    return jnp.concatenate(heads, axis=0)


def offset_sums(block):
    rows, width = block.shape
    while rows > 8:
        rows = rows // 2
        block = block[:rows] + pltpu.roll(block[rows:], width - rows, axis=1)
    place = lax.broadcasted_iota(jnp.int32, block.shape, 0)
    for bit in (4, 2, 1):
        block = jnp.where((place & bit) > 0, pltpu.roll(block, width - bit, axis=1), block)
    return jnp.sum(block, axis=0, keepdims=True)


def attend_kernel(column_ref, row_ref, base_ref, query_ref, key_ref, value_ref, out_ref, share_ref):
    blocks = query_ref.shape[0] // BLOCK
    bias = bias_block(base_ref[0])
    for at in range(blocks):
        keys, places = reach(at, blocks)
        own = slice(at * BLOCK, (at + 1) * BLOCK)
        scores = product_right(wide_heads(query_ref[own]), key_ref[keys]) + bias[:, places]
        allowed = column_ref[own, :1] == row_ref[0, :1, keys]
        scores = jnp.where(jnp.concatenate([allowed, allowed], axis=0), scores, negative_fill)
        powers = jnp.exp(scores - jnp.max(scores, axis=1, keepdims=True))
        shares = powers * (1.0 / jnp.sum(powers, axis=1, keepdims=True))
        shares = shares.astype(jnp.bfloat16)
        share_ref[0, 0, at, :, places] = shares
        mixed = product(shares, value_ref[keys])
        out_ref[own] = narrow_heads(mixed).astype(jnp.bfloat16)


def attend_back_kernel(
    query_ref, key_ref, value_ref, grad_ref, share_ref,
    grad_query_ref, grad_key_ref, grad_value_ref, sums_ref, bias_acc, key_acc, value_acc,
):
    blocks = query_ref.shape[0] // BLOCK

    @pl.when(pl.program_id(1) == 0)
    def _():
        bias_acc[...] = jnp.zeros_like(bias_acc)

    key_acc[...] = jnp.zeros_like(key_acc)
    value_acc[...] = jnp.zeros_like(value_acc)
    for at in range(blocks):
        keys, places = reach(at, blocks)
        own = slice(at * BLOCK, (at + 1) * BLOCK)
        query, grad = wide_heads(query_ref[own]), wide_heads(grad_ref[own])
        narrow_shares = share_ref[0, 0, at, :, places]
        shares = narrow_shares.astype(jnp.float32)
        value_acc[keys] += product_left(narrow_shares, grad)
        moved = shares * product_right(grad, value_ref[keys])
        grad_scores = moved - shares * jnp.sum(moved, axis=1, keepdims=True)
        bias_acc[:, places] += grad_scores
        narrow = grad_scores.astype(jnp.bfloat16)
        grad_query_ref[own] = narrow_heads(product(narrow, key_ref[keys])).astype(jnp.bfloat16)
        key_acc[keys] += product_left(narrow, query)
    grad_key_ref[...] = key_acc[...].astype(jnp.bfloat16)
    grad_value_ref[...] = value_acc[...].astype(jnp.bfloat16)

    @pl.when(pl.program_id(1) == pl.num_programs(1) - 1)
    def _():
        sums_ref[0] = jnp.concatenate(
            [offset_sums(bias_acc[:BLOCK]), offset_sums(bias_acc[BLOCK:])], axis=0
        )


def offset_buckets():
    offset = jnp.arange(3 * BLOCK, dtype=jnp.int32) - BLOCK
    distance = jnp.abs(offset)
    far_bucket = 8 + sum(((distance >= boundary).astype(jnp.int32) for boundary in bucket_edges))
    near_bucket = jnp.where(distance < 8, distance, far_bucket)
    return jnp.where(offset > 0, 16, 0) + near_bucket


def attend_rows(rows, length, column, segment_index, base, query, key, value):
    pairs = HEADS // 2
    part = pl.BlockSpec((length, 2 * KV), lambda r, p: (r, p))
    return pl.pallas_call(
        attend_kernel,
        grid=(rows, pairs),
        out_shape=[
            jax.ShapeDtypeStruct(query.shape, jnp.bfloat16),
            jax.ShapeDtypeStruct(
                (rows, pairs, length // BLOCK, 2 * BLOCK, 3 * BLOCK), jnp.bfloat16
            ),
        ],
        in_specs=[
            pl.BlockSpec((length, BLOCK), lambda r, p: (r, 0)),
            pl.BlockSpec((1, 1, length), lambda r, p: (r, 0, 0)),
            pl.BlockSpec((1, 2, 3 * BLOCK), lambda r, p: (p, 0, 0)),
            part, part, part,
        ],
        out_specs=[
            part,
            pl.BlockSpec(
                (1, 1, length // BLOCK, 2 * BLOCK, 3 * BLOCK), lambda r, p: (r, p, 0, 0, 0)
            ),
        ],
        compiler_params=pltpu.CompilerParams(vmem_limit_bytes=48 * 2**20),
        name="attend",
    )(column, segment_index.reshape(rows, 1, length), base, query, key, value)


def attend_rows_back(rows, length, query, key, value, grad, shares):
    pairs = HEADS // 2
    part = pl.BlockSpec((length, 2 * KV), lambda p, r: (r, p))
    return pl.pallas_call(
        attend_back_kernel,
        grid=(pairs, rows),
        out_shape=[jax.ShapeDtypeStruct(query.shape, jnp.bfloat16)] * 3
        + [jax.ShapeDtypeStruct((pairs, 2, 3 * BLOCK), jnp.float32)],
        in_specs=[
            part, part, part, part,
            pl.BlockSpec(
                (1, 1, length // BLOCK, 2 * BLOCK, 3 * BLOCK), lambda p, r: (r, p, 0, 0, 0)
            ),
        ],
        out_specs=[part, part, part, pl.BlockSpec((1, 2, 3 * BLOCK), lambda p, r: (p, 0, 0))],
        scratch_shapes=[
            pltpu.VMEM((2 * BLOCK, 3 * BLOCK), jnp.float32),
            pltpu.VMEM((length, 2 * KV), jnp.float32),
            pltpu.VMEM((length, 2 * KV), jnp.float32),
        ],
        compiler_params=pltpu.CompilerParams(vmem_limit_bytes=48 * 2**20),
        name="attend_back",
    )(query, key, value, grad, shares)


def gelu_parts(before):
    slope = 0.7978845608028654
    square = before * before
    bend = jnp.tanh(slope * (before + 0.044715 * before * square))
    half = 0.5 * (1.0 + bend)
    rise = half + 0.5 * before * (1.0 - bend * bend) * slope * (1.0 + 3 * 0.044715 * square)
    return before * half, rise


def slots_of(stacked, count):
    rows, columns = stacked.shape
    own = lax.broadcasted_iota(jnp.int32, (rows, columns), 0) // count
    head = lax.broadcasted_iota(jnp.int32, (rows, columns), 1) // KV
    return jnp.where(own == head, stacked, 0.0)


LEFTS = ("normed_fin", "active", "normed_start", "own", "normed_mid", "context")
RIGHTS = ("before_grad", "last_branch", "grad_own", "self_branch", "grad_asking", "cross_branch")


def decoder_kernel(rows, slots, count, *refs):
    refs = list(refs)
    packed = count > 0
    factors = refs[16 : 18 if packed else 28]
    del refs[16 : 18 if packed else 28]
    (
        segment_ref, start_ref, cotangent_ref, gain_ref, keys_hbm, values_hbm, memory_hbm,
        self_value_hbm, self_output_hbm, cross_query_hbm, cross_output_hbm,
        inner_hbm, outer_hbm,
        decoded_ref, start_grad_ref, gain_grad_ref,
        grad_keys_hbm, grad_values_hbm, encoded_hbm,
        keys_ref, values_ref, grad_keys_ref, grad_values_ref, memory_ref,
        self_value, self_output, cross_query, cross_output, inner, outer, sems,
    ) = refs

    def keep(name, value):
        names = LEFTS if name in LEFTS else RIGHTS
        at, columns = names.index(name), value.shape[1]
        if not packed:
            factors[at + (0 if names is LEFTS else 6)][...] = value
        elif names is RIGHTS:
            begin = at * start_ref.shape[1] + (0 if at == 0 else inner.shape[1] - start_ref.shape[1])
            factors[1][:, begin : begin + columns] = value
        else:
            own = columns // count
            span = -(-own // 128) * 128
            begin = at * 128 + (0 if at < 2 else -(-inner.shape[1] // count // 128) * 128 - 128)
            wide = value.astype(jnp.float32)
            for slot in range(count):
                turn = (columns - slot * own) % columns
                part = (pltpu.roll(wide, turn, axis=1) if turn else wide)[:, :span]
                lanes = lax.broadcasted_iota(jnp.int32, part.shape, 1)
                part = jnp.where(lanes < own, part, 0.0).astype(value.dtype)
                factors[0][slot, :, begin : begin + span] = part

    loads = []
    for at, (source, target) in enumerate((
        (self_value_hbm, self_value), (self_output_hbm, self_output),
        (cross_query_hbm, cross_query), (cross_output_hbm, cross_output),
        (inner_hbm, inner), (outer_hbm, outer), (keys_hbm, keys_ref), (values_hbm, values_ref),
        (memory_hbm, memory_ref),
    )):
        loads.append(pltpu.make_async_copy(source, target, sems.at[at]))
    for at in (0, 1, 2, 6, 7):
        loads[at].start()
    narrow = jnp.bfloat16
    length = keys_ref.shape[0] // rows
    start_gain, middle_gain, final_gain = gain_ref[2:3], gain_ref[3:4], gain_ref[4:5]

    start_field = start_ref[...].astype(jnp.float32)
    scale_start = root_scale(start_field)
    normed_start = (start_field * scale_start * start_gain).astype(narrow)
    keep("normed_start", normed_start)
    loads[0].wait()
    for at in (3, 4, 5, 8):
        loads[at].start()
    own = product(normed_start, self_value[...]).astype(narrow)
    keep("own", own)
    loads[1].wait()
    first_field = start_field + product(own, self_output[...])
    scale_mid = root_scale(first_field)
    normed_mid = (first_field * scale_mid * middle_gain).astype(narrow)
    keep("normed_mid", normed_mid)
    loads[2].wait()
    asking = product(normed_mid, cross_query[...]).astype(narrow).astype(jnp.float32)
    loads[6].wait()
    loads[7].wait()
    wides, all_shares, contexts = [], [], []
    for row in range(rows):
        part = asking[row * slots : (row + 1) * slots]
        wide = slots_of(jnp.concatenate([part] * HEADS, axis=0), slots).astype(narrow)
        span = slice(row * length, (row + 1) * length)
        scores = product_right(wide, keys_ref[span])
        slot = lax.rem(lax.broadcasted_iota(jnp.int32, scores.shape, 0), slots)
        scores = jnp.where(slot == segment_ref[row : row + 1], scores, negative_fill)
        powers = jnp.exp(scores - jnp.max(scores, axis=1, keepdims=True))
        shares = powers * (1.0 / jnp.sum(powers, axis=1, keepdims=True))
        mixed = slots_of(product(shares.astype(narrow), values_ref[span]), slots)
        contexts.append(jnp.sum(mixed.reshape(HEADS, slots, -1), axis=0))
        wides.append(wide)
        all_shares.append(shares)
    context = jnp.concatenate(contexts, axis=0).astype(narrow)
    keep("context", context)
    loads[3].wait()
    second_field = first_field + product(context, cross_output[...])
    scale_fin = root_scale(second_field)
    normed_fin = (second_field * scale_fin * final_gain).astype(narrow)
    keep("normed_fin", normed_fin)
    loads[4].wait()
    active, rise = gelu_parts(product(normed_fin, inner[...]))
    active = active.astype(narrow)
    keep("active", active)
    loads[5].wait()
    decoded_ref[...] = (second_field + product(active, outer[...])).astype(narrow)

    branch = cotangent_ref[...]
    keep("last_branch", branch)
    grad_second = branch.astype(jnp.float32)
    before_grad = (product_right(branch, outer[...]) * rise).astype(narrow)
    keep("before_grad", before_grad)
    grad_normed = product_right(before_grad, inner[...])
    moved, final_gain_grad = norm_back(grad_normed, second_field, scale_fin, final_gain)
    grad_second = grad_second + moved
    branch = grad_second.astype(narrow)
    keep("cross_branch", branch)
    grad_context = product_right(branch, cross_output[...]).astype(narrow).astype(jnp.float32)
    askings = []
    for row in range(rows):
        part = grad_context[row * slots : (row + 1) * slots]
        wide = slots_of(jnp.concatenate([part] * HEADS, axis=0), slots).astype(narrow)
        span = slice(row * length, (row + 1) * length)
        shares = all_shares[row]
        moved = shares * product_right(wide, values_ref[span])
        grad_scores = moved - shares * jnp.sum(moved, axis=1, keepdims=True)
        grad_scores = grad_scores.astype(narrow)
        grad_values_ref[span] = product_left(shares.astype(narrow), wide).astype(narrow)
        grad_keys_ref[span] = product_left(grad_scores, wides[row]).astype(narrow)
        mixed = slots_of(product(grad_scores, keys_ref[span]), slots)
        askings.append(jnp.sum(mixed.reshape(HEADS, slots, -1), axis=0))
    loads[8].wait()
    stores = [pltpu.make_async_copy(memory_ref, encoded_hbm, sems.at[11])]
    stores.append(pltpu.make_async_copy(grad_keys_ref, grad_keys_hbm, sems.at[9]))
    stores.append(pltpu.make_async_copy(grad_values_ref, grad_values_hbm, sems.at[10]))
    for copy in stores:
        copy.start()
    grad_asking = jnp.concatenate(askings, axis=0).astype(narrow)
    keep("grad_asking", grad_asking)
    grad_normed = product_right(grad_asking, cross_query[...])
    moved, middle_gain_grad = norm_back(grad_normed, first_field, scale_mid, middle_gain)
    grad_first = grad_second + moved
    branch = grad_first.astype(narrow)
    keep("self_branch", branch)
    grad_own = product_right(branch, self_output[...]).astype(narrow)
    keep("grad_own", grad_own)
    grad_normed = product_right(grad_own, self_value[...])
    moved, start_gain_grad = norm_back(grad_normed, start_field, scale_start, start_gain)
    start_grad_ref[...] = grad_first + moved
    gain_grad_ref[...] = jnp.concatenate(
        [start_gain_grad[None], middle_gain_grad[None], final_gain_grad[None]], axis=0
    )
    for copy in stores:
        copy.wait()


def decode(count, segment_index, start, cotangent, gains, keys, values, memory, weights):
    rows, tokens, width = segment_index.shape[0], start.shape[0], start.shape[1]
    narrow, hidden = jnp.bfloat16, weights[4].shape[1]
    few = jax.ShapeDtypeStruct((tokens, width), narrow)
    many = jax.ShapeDtypeStruct((tokens, hidden), narrow)
    factors = [few, many, few, few, few, few, many, few, few, few, few, few]
    if count:
        span = 5 * 128 + hidden // count
        factors = [
            jax.ShapeDtypeStruct((count, tokens, span), narrow),
            jax.ShapeDtypeStruct((tokens, hidden + 5 * width), narrow),
        ]
    outs = [
        few,
        jax.ShapeDtypeStruct((tokens, width), jnp.float32),
        jax.ShapeDtypeStruct((3, width), jnp.float32),
        *factors,
        jax.ShapeDtypeStruct(keys.shape, narrow),
        jax.ShapeDtypeStruct(values.shape, narrow),
        jax.ShapeDtypeStruct(memory.shape, narrow),
    ]
    anywhere = pl.BlockSpec(memory_space=pl.ANY)
    local = pl.BlockSpec(memory_space=pltpu.VMEM)
    return pl.pallas_call(
        functools.partial(decoder_kernel, rows, tokens // rows, count),
        out_shape=outs,
        in_specs=[local] * 4 + [anywhere] * 9,
        out_specs=[local] * (len(outs) - 3) + [anywhere] * 3,
        scratch_shapes=[pltpu.VMEM(keys.shape, narrow)] * 5
        + [pltpu.VMEM(w.shape, narrow) for w in weights]
        + [pltpu.SemaphoreType.DMA((12,))],
        compiler_params=pltpu.CompilerParams(vmem_limit_bytes=63 * 2**20),
        name="decode",
    )(segment_index, start, cotangent, gains, keys, values, memory, *weights)


TILE = 256


def rows_of(at, size=TILE):
    return pl.ds(pl.multiple_of(at * size, size), size)


FORWARD_KINDS = (
    "tall", "tall", "square", "square", "wide", "tall", "square", "square",
    "square", "square", "square", "square", "wide", "tall", "small",
)


class Gather:
    def __init__(self, spot, kinds, shards, fulls, staged, sems):
        self.spot, self.kinds, self.shards, self.fulls = spot, kinds, shards, fulls
        self.staged = staged
        (
            self.ring_out, self.ring_in, self.near_out, self.near_in,
            self.far_out, self.far_in, self.last_out, self.last_in, self.own_sem,
        ) = sems
        self.split = [i for i in range(len(kinds)) if kinds[i] in ("wide", "tall")]

    def piece(self, i, step, plane):
        count = self.spot.count
        slot = ring_index(self.spot.place + (step if i % 2 else count - step), count)
        rows = self.shards[i].shape[0]
        block = self.fulls[i].at[pl.ds(pl.multiple_of(slot * rows, 16), rows)]
        return cut(self.kinds[i], block, plane, self.spot.core)

    def own_copy(self, i):
        rows = self.shards[i].shape[0]
        block = self.fulls[i].at[pl.ds(pl.multiple_of(self.spot.fsdp * rows, 16), rows)]
        return pltpu.make_async_copy(self.staged.get(i, self.shards[i]), block, self.own_sem.at[i])

    def stage_copy(self, i):
        at = len(self.kinds) + list(self.staged).index(i)
        return pltpu.make_async_copy(self.shards[i], self.staged[i], self.own_sem.at[at])

    def ring_copy(self, i, step, source=None):
        here = self.piece(i, step, self.spot.plane)
        return send(
            here if source is None else source, here,
            self.ring_out.at[i, step], self.ring_in.at[i, step],
            self.spot.before if i % 2 else self.spot.after,
        )

    def near_copy(self, i, step):
        here = self.piece(i, step, self.spot.plane)
        return send(
            here, here, self.near_out.at[i, step], self.near_in.at[i, step], self.spot.sibling
        )

    def far_copy(self, i, step):
        here, at = self.piece(i, step, self.spot.plane), self.split.index(i)
        return send(
            here, here, self.far_out.at[at, step], self.far_in.at[at, step], self.spot.opposite
        )

    def last_copy(self, i, step):
        here, at = self.piece(i, step, 1 - self.spot.plane), self.split.index(i)
        return send(
            here, here, self.last_out.at[at, step], self.last_in.at[at, step], self.spot.sibling
        )

    def start(self, group):
        for i in group:
            source = cut(self.kinds[i], self.shards[i], self.spot.plane, self.spot.core)
            self.ring_copy(i, 0, source).start()

    def advance(self, group, step):
        count = self.spot.count
        for i in group:
            if step < count:
                self.ring_copy(i, step - 1).wait_recv()
                if step < count - 1:
                    self.ring_copy(i, step).start()
                if self.kinds[i] != "small":
                    self.near_copy(i, step).start()
                if i in self.split:
                    self.far_copy(i, step).start()
        for i in group:
            if step > 1 and i in self.split:
                self.far_copy(i, step - 1).wait_recv()
                self.last_copy(i, step - 1).start()

    def arrive(self, group):
        def one(step, carry):
            for i in group:
                if self.kinds[i] != "small":
                    self.near_copy(i, step).wait_recv()
                if i in self.split:
                    self.last_copy(i, step).wait_recv()
            return carry

        lax.fori_loop(1, self.spot.count, one, 0)
        for i in group:
            self.own_copy(i).wait()

    def settle(self, group):
        def one(step, carry):
            for i in group:
                self.ring_copy(i, step - 1).wait_send()
                if self.kinds[i] != "small":
                    self.near_copy(i, step).wait_send()
                if i in self.split:
                    self.far_copy(i, step).wait_send()
                    self.last_copy(i, step).wait_send()
            return carry

        lax.fori_loop(1, self.spot.count, one, 0)


FIRST, SECOND, THIRD = (0, 1, 2, 3, 14), (4, 5, 6, 7), (8, 9, 10, 11, 12, 13)


def forward_kernel(count, rows, *refs):
    refs = list(refs)

    def take(size):
        got = refs[:size]
        del refs[:size]
        return got

    shards = take(15)
    tokens, segment, base = take(3)
    weight_outs = take(14)
    (gain_out,) = take(1)
    (
        query_out, key_out, value_out, share_out, context_out, hidden_out, normed_two_out,
        active_out, rise_out, memory_out, cross_key_out, cross_value_out, normed_one_out,
    ) = take(13)
    held = take(8)
    gain_all, normed_one, query, key, value, context = take(6)
    hidden, normed_two, active, rise, memory, cross_keys, cross_values, shares = take(8)
    column, lines, bases = take(3)
    staged = dict(zip(THIRD, take(len(THIRD))))
    gather_sems = take(9)
    save_sem, share_sem = take(2)
    spot = Spot(count)
    fulls = held + weight_outs[8:] + [gain_all]
    gather = Gather(spot, FORWARD_KINDS, shards, fulls, staged, gather_sems)
    tiles = tokens.shape[0] // TILE
    length = tokens.shape[0] // rows
    blocks, pairs = length // BLOCK, HEADS // 2
    narrow = jnp.bfloat16
    saves = []

    def save(source, target):
        copy = pltpu.make_async_copy(source, target, save_sem.at[len(saves)])
        copy.start()
        saves.append(copy)

    def each_tile(body):
        def one(at, carry):
            body(rows_of(at), at)
            return carry

        lax.fori_loop(0, tiles, one, 0)

    for i in FIRST:
        gather.own_copy(i).start()
    spot.greet()
    gather.start(FIRST)
    for i in SECOND:
        gather.own_copy(i).start()
    for i in THIRD:
        gather.stage_copy(i).start()
    for pair in range(pairs):
        bases[pair, 0:2] = base[2 * pair : 2 * pair + 2]
    for row in range(rows):
        lines[row, 0:1] = segment[row : row + 1].astype(jnp.float32)
        for block in range(blocks):
            line = segment[row : row + 1, block * BLOCK : (block + 1) * BLOCK].astype(jnp.float32)
            begin = row * length + block * BLOCK
            column[begin : begin + BLOCK] = jnp.broadcast_to(line, (BLOCK, BLOCK)).T
    for step in range(1, 5):
        gather.advance(FIRST, step)
    gather.start(SECOND)
    for i in THIRD:
        gather.stage_copy(i).wait()
        gather.own_copy(i).start()
    for step in range(5, count):
        gather.advance(FIRST, step)
        gather.advance(SECOND, step - 4)
    gather.advance(FIRST, count)
    gather.arrive(FIRST)
    gain, width = jnp.zeros(gain_out.shape, jnp.float32), tokens.shape[1]
    depth = width // count
    lanes = lax.broadcasted_iota(jnp.int32, gain.shape, 1)
    for slot in range(count):
        part = gain_all[slot * 16 : (slot + 1) * 16].astype(jnp.float32)
        part = jnp.concatenate([part, jnp.zeros((16, width - part.shape[1]), jnp.float32)], axis=1)
        part = pltpu.roll(part, slot * depth, axis=1)
        gain = gain + jnp.where(lanes // depth == slot, part, 0.0)
    gain_out[...] = gain
    query_weight, key_weight, value_weight, output_weight = held[:4]
    inner_weight, outer_weight, cross_key_weight, cross_value_weight = held[4:]

    def first_norm(span, at):
        field = tokens[span].astype(jnp.float32)
        normed_one[span] = (field * root_scale(field) * gain_out[0:1]).astype(narrow)

    each_tile(first_norm)

    def project(target, weight):
        def body(span, at):
            target[span] = product(normed_one[span], weight[...]).astype(narrow)

        each_tile(body)

    project(query, query_weight)
    gather.advance(SECOND, 4)
    project(key, key_weight)
    gather.start(THIRD)
    project(value, value_weight)
    gather.advance(SECOND, 5)
    for source, target in (
        (normed_one, normed_one_out), (query, query_out), (key, key_out), (value, value_out),
    ):
        save(source, target)
    for i in range(4):
        save(held[i], weight_outs[i])

    def share_copy(at):
        return pltpu.make_async_copy(
            shares.at[lax.rem(at, 2)],
            share_out.at[at // pairs, lax.rem(at, pairs)],
            share_sem.at[lax.rem(at, 2)],
        )

    def attend_pair(at, carry):
        row, pair, buffer = at // pairs, lax.rem(at, pairs), lax.rem(at, 2)

        for turn, group, step in (
            (1, THIRD, 1), (2, SECOND, 6), (4, THIRD, 2), (5, SECOND, 7), (7, THIRD, 3),
            (8, SECOND, 8), (10, THIRD, 4),
        ):

            @pl.when(at == turn)
            def _():
                gather.advance(group, step)

        @pl.when(at >= 2)
        def _():
            share_copy(at - 2).wait()

        bias = bias_block(bases[pair, 0:2])
        columns = rows_of(pair, 2 * KV)

        def span(begin, size):
            return pl.ds(pl.multiple_of(row * length + begin, BLOCK), size)

        for block in range(blocks):
            keys, places = reach(block, blocks)
            own = span(block * BLOCK, BLOCK)
            near = span(keys.start, keys.stop - keys.start)
            scores = product_right(wide_heads(query[own, columns]), key[near, columns])
            scores = scores + bias[:, places]
            allowed = column[own, :1] == lines[row, 0:1, keys]
            scores = jnp.where(jnp.concatenate([allowed, allowed], axis=0), scores, negative_fill)
            powers = jnp.exp(scores - jnp.max(scores, axis=1, keepdims=True))
            part = powers * (1.0 / jnp.sum(powers, axis=1, keepdims=True))
            part = part.astype(narrow)
            shares[buffer, block, :, places] = part
            mixed = product(part, value[near, columns])
            context[own, columns] = narrow_heads(mixed).astype(narrow)
        share_copy(at).start()
        return carry

    lax.fori_loop(0, rows * pairs, attend_pair, 0)
    save(context, context_out)

    def second_norm(span, at):
        field = tokens[span].astype(jnp.float32) + product(context[span], output_weight[...])
        hidden[span] = field
        normed_two[span] = (field * root_scale(field) * gain_out[1:2]).astype(narrow)

    each_tile(second_norm)
    save(hidden, hidden_out)
    save(normed_two, normed_two_out)
    gather.advance(THIRD, 5)
    gather.arrive(SECOND)
    for i in range(4, 8):
        save(held[i], weight_outs[i])
    chunk = tokens.shape[1]

    def feed(span, at):
        @pl.when(at == 1)
        def _():
            gather.advance(THIRD, 6)

        @pl.when(at == 3)
        def _():
            gather.advance(THIRD, 7)

        for begin in range(0, active.shape[1], chunk):
            part = slice(begin, begin + chunk)
            level, slope = gelu_parts(product(normed_two[span], inner_weight[:, part]))
            active[span, part] = level.astype(narrow)
            rise[span, part] = slope.astype(narrow)
        full = hidden[span] + product(active[span], outer_weight[...])
        memory[span] = full.astype(narrow)

    each_tile(feed)
    save(active, active_out)
    save(rise, rise_out)
    save(memory, memory_out)

    def cross(span, at):
        cross_keys[span] = product(memory[span], cross_key_weight[...]).astype(narrow)
        cross_values[span] = product(memory[span], cross_value_weight[...]).astype(narrow)

    each_tile(cross)
    save(cross_keys, cross_key_out)
    save(cross_values, cross_value_out)
    gather.advance(THIRD, count)
    gather.arrive(THIRD)
    for group in (FIRST, SECOND, THIRD):
        gather.settle(group)
    for copy in saves:
        copy.wait()
    for at in range(rows * pairs - 2, rows * pairs):
        share_copy(at).wait()


def forward(count, shards, tokens, segment_index, base):
    rows, length = segment_index.shape
    many, width = tokens.shape
    hidden_width = shards[4].shape[1]
    narrow, wide = jnp.bfloat16, jnp.float32
    pairs, total = HEADS // 2, len(shards)
    split = sum(kind in ("wide", "tall") for kind in FORWARD_KINDS)
    weights = [(count * s.shape[0], s.shape[1]) for s in shards]
    few, much = (many, width), (many, hidden_width)
    share_shape = (rows, pairs, length // BLOCK, 2 * BLOCK, 3 * BLOCK)
    shapes = [(w, narrow) for w in weights[:14]] + [((16, width), wide)]
    shapes += [
        (few, narrow), (few, narrow), (few, narrow), (share_shape, narrow), (few, narrow),
        (few, wide), (few, narrow), (much, narrow), (much, narrow), (few, narrow), (few, narrow),
        (few, narrow), (few, narrow),
    ]
    dma = pltpu.SemaphoreType.DMA
    scratch = [pltpu.VMEM(w, narrow) for w in weights[:8]] + [pltpu.VMEM(weights[14], narrow)]
    scratch += [pltpu.VMEM(few, narrow)] * 5
    scratch += [
        pltpu.VMEM(few, wide), pltpu.VMEM(few, narrow), pltpu.VMEM(much, narrow),
        pltpu.VMEM(much, narrow), pltpu.VMEM(few, narrow), pltpu.VMEM(few, narrow),
        pltpu.VMEM(few, narrow), pltpu.VMEM((2,) + share_shape[2:], narrow),
    ]
    scratch += [pltpu.VMEM((many, BLOCK), wide), pltpu.VMEM((rows, 8, length), wide)]
    scratch += [pltpu.VMEM((pairs, 8, base.shape[1]), wide)]
    scratch += [pltpu.VMEM(shards[i].shape, narrow) for i in THIRD]
    scratch += [dma((total, count))] * 4 + [dma((split, count))] * 4
    scratch += [dma((total + len(THIRD),)), dma((24,)), dma((2,))]
    anywhere = pl.BlockSpec(memory_space=pl.ANY)
    local = pl.BlockSpec(memory_space=pltpu.VMEM)
    got = pl.pallas_call(
        functools.partial(forward_kernel, count, rows),
        out_shape=[jax.ShapeDtypeStruct(s, d) for s, d in shapes],
        in_specs=[anywhere] * total + [local] * 3,
        out_specs=[anywhere] * 14 + [local] + [anywhere] * 13,
        scratch_shapes=scratch,
        compiler_params=pltpu.CompilerParams(
            collective_id=2, has_side_effects=True, vmem_limit_bytes=62 * 2**20
        ),
        name="forward",
    )(*shards, tokens, segment_index, base)
    return got[:14], got[14], got[15:]


def forward_apart(count, shards, tokens, segment_index, base):
    rows, length = segment_index.shape
    narrow = jnp.bfloat16
    whole = gather_weights(count, shards, KINDS)
    depth, many = shards[0].shape[0], tokens.shape[0]
    gains = whole[14][:, :, :depth].astype(jnp.float32)
    gains = gains.transpose(1, 0, 2).reshape(16, count * depth)
    base = base.reshape(HEADS // 2, 2, 3 * BLOCK)
    column = jnp.broadcast_to(segment_index.reshape(-1, 1), (many, BLOCK))
    whole = [part.reshape(-1, part.shape[2]) for part in whole[:14]]
    field = tokens.astype(jnp.float32)
    normed_one = (field * root_scale(field) * gains[0]).astype(narrow)
    query, key, value = [product(normed_one, weight).astype(narrow) for weight in whole[:3]]
    context, shares = attend_rows(
        rows, length, column, segment_index, base, query, key, value
    )
    hidden = field + product(context, whole[3])
    normed_two = (hidden * root_scale(hidden) * gains[1]).astype(narrow)
    active, rise = gelu_parts(product(normed_two, whole[4]))
    active = active.astype(narrow)
    memory = (hidden + product(active, whole[5])).astype(narrow)
    cross_keys, cross_values = [product(memory, weight).astype(narrow) for weight in whole[6:8]]
    return whole, gains, (
        query, key, value, shares, context, hidden, normed_two,
        active, rise, memory, cross_keys, cross_values, normed_one,
    )


INNER, OUTER = 0, 1
SPLITS = {INNER: 2}


def backward_kernel(count, rows, spans, *refs):
    refs = list(refs)

    def take(size):
        got = refs[:size]
        del refs[:size]
        return got

    (
        inner_hbm, outer_hbm, query_weight_hbm, key_weight_hbm, value_weight_hbm,
        output_weight_hbm, cross_key_weight_hbm, cross_value_weight_hbm,
        active_hbm, rise_hbm, normed_two_hbm, context_hbm, query_hbm, key_hbm, value_hbm,
        normed_one_hbm, tokens_hbm, memory_hbm, grad_keys_hbm, grad_values_hbm, cotangent_hbm,
        hidden_hbm, shares_hbm,
    ) = take(23)
    left_part, right_part, gain, decoder_gains = take(4)
    sums, pairs = take(8), len(spans)
    pair_sums = take(pairs)
    small_sum, tokens_grad_hbm = take(2)
    big, flat, half, work, final, far = take(1)[0], take(2), take(8), take(8), take(8), take(1)[0]
    left_all, right_all = take(2)
    pair_work, pair_half, pair_far = take(pairs), take(pairs), take(pairs)
    small, small_near, small_mid, small_far, small_all = take(5)
    pool, level, weights, shares, bias_acc, key_acc, value_acc = take(7)
    (
        near_sem, ring_out, ring_in, far_sem, end_sem, left_out, left_in,
        right_out, right_in, pair_sem, small_sem, small_out, small_in, load_sem, share_sem,
    ) = take(15)
    spot = Spot(count)
    core, plane = spot.core, spot.plane
    narrow = jnp.bfloat16
    many, width = level.shape[1:]
    tiles, length = many // TILE, many // rows
    blocks = length // BLOCK
    depth = width // count
    products = {2: big.at[0], 3: big.at[1], 4: big.at[2], 5: flat[0], 6: flat[0], 7: flat[1]}

    def peer(k):
        return (spot.dp, lax.rem(spot.fsdp + k, count))

    def slot_at(way, step):
        turn = step + 1 if way else count - 1 - step
        return ring_index(spot.place + turn, count)

    def near_copy(i):
        if i == INNER:
            source = big.at[pl.ds(2 * (1 - core), 2)]
        elif i == OUTER:
            source = big.at[:, :, half_of(1 - core, width)]
        else:
            source = products[i].at[:, half_of(1 - core, width)]
        return send(source, half[i], near_sem.at[0, i], near_sem.at[1, i], spot.sibling)

    def part_of(i, slot, side, way):
        rows_own = work[i].shape[2]
        if i == INNER:
            return half[i].at[way, pl.ds(pl.multiple_of(slot * depth, 16), depth)]
        if i == OUTER:
            begin = lax.rem(slot, 2) * 4 * depth + (2 * side + way) * rows_own
            return half[i].at[slot // 2, pl.ds(pl.multiple_of(begin, 16), rows_own)]
        begin = slot * depth + way * rows_own
        return half[i].at[pl.ds(pl.multiple_of(begin, 16), rows_own)]

    def far_copy(i, way, step):
        return send(
            part_of(i, slot_at(way, step), 1 - plane, way), far.at[way, step],
            far_sem.at[0, way, step], far_sem.at[1, way, step], spot.opposite,
        )

    def join(i):
        near_copy(i).wait()
        if i == INNER:

            def one(at, carry):
                side, span = at // 3, rows_of(lax.rem(at, 3))
                mine = big[2 * core + side, span]
                half[i][side, span] = plus(half[i][side, span], mine).astype(narrow)
                return carry

            lax.fori_loop(0, 6, one, 0)
        elif i == OUTER:

            def one(at, carry):
                side, span = at // 3, rows_of(lax.rem(at, 3))
                mine = big[side, span, half_of(core, width)]
                half[i][side, span] = plus(half[i][side, span], mine).astype(narrow)
                return carry

            lax.fori_loop(0, 12, one, 0)
        else:

            def one(at, carry):
                span = rows_of(at)
                mine = products[i][span, half_of(core, width)]
                half[i][span] = plus(half[i][span], mine).astype(narrow)
                return carry

            lax.fori_loop(0, 3, one, 0)
        if i == OUTER:

            def far_start(step, carry):
                for way in range(2):
                    far_copy(i, way, step).start()
                return carry

            lax.fori_loop(0, count, far_start, 0)

    def spans_of(i):
        rows_own = work[i].shape[2]
        parts = SPLITS.get(i, 1)
        size = rows_own // parts
        return [slice(at * size, (at + 1) * size) for at in range(parts)]

    def ring_copy(i, way, step, at):
        span = spans_of(i)[at]
        return send(
            work[i].at[way, step, span], work[i].at[way, step + 1, span],
            ring_out.at[i, at, way, step], ring_in.at[i, at, way, step],
            spot.before if way else spot.after,
        )

    def advance(group, step):
        for i in group:
            for way in range(2):
                if i == OUTER:
                    far_copy(i, way, step).wait_recv()
                block = part_of(i, slot_at(way, step), plane, way)
                for at, span in enumerate(spans_of(i)):
                    value = block[span].astype(jnp.float32)
                    if i == OUTER:
                        value = value + far[way, step, span].astype(jnp.float32)

                    @pl.when(step > 0)
                    def _():
                        ring_copy(i, way, step - 1, at).wait_recv()
                        total = plus(value, work[i][way, step, span])
                        work[i][way, step, span] = total.astype(narrow)

                    @pl.when(step == 0)
                    def _():
                        work[i][way, step, span] = value.astype(narrow)

                    @pl.when(step < count - 1)
                    def _():
                        ring_copy(i, way, step, at).start()

    def run(group, first, last):
        def one(step, carry):
            advance(group, step)
            return carry

        lax.fori_loop(first, last, one, 0)

    def end_across(i):
        return send(
            work[i].at[:, count - 1], final[i], end_sem.at[0, i], end_sem.at[1, i], spot.opposite
        )

    def end_piece(i, side):
        if i == OUTER:
            return cut("tall", sums[i], side, core)
        return sums[i].at[:, half_of(core, sums[i].shape[1])]

    def end_near(i):
        here = end_piece(i, plane)
        return send(here, here, end_sem.at[2, i], end_sem.at[3, i], spot.sibling)

    def end_far(i):
        here = end_piece(i, plane)
        return send(here, here, end_sem.at[4, i], end_sem.at[5, i], spot.opposite)

    def end_relay(i):
        here = end_piece(i, 1 - plane)
        return send(here, here, end_sem.at[6, i], end_sem.at[7, i], spot.sibling)

    def close(i):
        if i != OUTER:
            end_across(i).wait()
        here, rows_own = end_piece(i, plane), work[i].shape[2]
        for way in range(2):
            value = work[i][way, count - 1]
            if i != OUTER:
                value = plus(value, final[i][way]).astype(narrow)
            if i == INNER:
                here[:, way * width : (way + 1) * width] = value
            else:
                here[way * rows_own : (way + 1) * rows_own] = value
        if i == OUTER:
            end_far(i).start()
        end_near(i).start()

    def left_copy(k):
        other = lax.rem(spot.fsdp + k, count)
        return send(
            left_part.at[other], left_all.at[spot.fsdp], left_out.at[k], left_in.at[k], peer(k)
        )

    def right_copy(way, step):
        turn = step if way else count - step
        slot = ring_index(spot.place + turn, count)
        wide = right_part.shape[1] // 2
        here = right_all.at[slot, :, way * wide : (way + 1) * wide]
        return send(
            here, here, right_out.at[way, step], right_in.at[way, step],
            spot.before if way else spot.after,
        )

    def right_step(step):
        for way in range(2):
            right_copy(way, step - 1).wait_recv()
            if step < count - 1:
                right_copy(way, step).start()

    def pair_near(j):
        columns = pair_sums[j].shape[1]
        return send(
            pair_work[j].at[:, half_of(1 - core, columns)], pair_half[j],
            pair_sem.at[0, j], pair_sem.at[1, j], spot.sibling,
        )

    def pair_across(j):
        return send(
            pair_half[j], pair_far[j], pair_sem.at[2, j], pair_sem.at[3, j], spot.opposite
        )

    def pair_end(j):
        here = pair_sums[j].at[:, half_of(core, pair_sums[j].shape[1])]
        return send(here, here, pair_sem.at[4, j], pair_sem.at[5, j], spot.sibling)

    def small_copy(k):
        here = small_all.at[spot.fsdp]
        return send(here, here, small_out.at[k], small_in.at[k], peer(k))

    def each_peer(body):
        def one(k, carry):
            body(k)
            return carry

        lax.fori_loop(1, count, one, 0)

    def each_tile(body):
        def one(at, carry):
            body(rows_of(at))
            return carry

        lax.fori_loop(0, tiles, one, 0)

    used = []

    def load(source, target):
        copy = pltpu.make_async_copy(source, target, load_sem.at[len(used)])
        copy.start()
        used.append(copy)
        return copy

    def fold(target, left, right):
        def one(at, carry):
            span = rows_of(at)
            target[span] = product_left(left[:, span], right[...]).astype(narrow)
            return carry

        lax.fori_loop(0, width // TILE, one, 0)

    loads = [
        load(grad_keys_hbm, pool.at[4]), load(cross_key_weight_hbm, weights.at[0]),
        load(grad_values_hbm, pool.at[5]), load(cross_value_weight_hbm, weights.at[1]),
        load(cotangent_hbm, pool.at[2]), load(memory_hbm, pool.at[1]),
    ]

    def chunk_of(source, at):
        return source.at[:, pl.ds(at * width, width)]

    active_loads = {1: load(chunk_of(active_hbm, 1), pool.at[3])}
    hidden_load = load(hidden_hbm, level.at[2])
    out_loads = {0: load(outer_hbm.at[pl.ds(0, width)], weights.at[2])}
    barrier = pltpu.get_barrier_semaphore()
    for partner in (spot.sibling, spot.opposite):
        pl.semaphore_signal(barrier, inc=1, device_id=partner, device_id_type=MESH)
    each_peer(
        lambda k: pl.semaphore_signal(barrier, inc=1, device_id=peer(k), device_id_type=MESH)
    )
    pl.semaphore_wait(barrier, count + 1)
    each_peer(lambda k: left_copy(k).start())
    right_all[spot.fsdp] = right_part[...]
    left_all[spot.fsdp] = left_part[spot.fsdp]
    for way in range(2):
        right_copy(way, 0).start()
    small[...] = jnp.zeros_like(small)
    small[2:5] = decoder_gains[...]
    for copy in loads:
        copy.wait()

    def enter(span):
        value = pool[2, span].astype(jnp.float32)
        value = value + product_right(pool[4, span], weights[0])
        value = value + product_right(pool[5, span], weights[1])
        level[0, span] = value
        pool[0, span] = value.astype(narrow)

    each_tile(enter)
    active_loads[0] = load(chunk_of(active_hbm, 0), pool.at[2])
    in_loads = {
        at: load(chunk_of(inner_hbm, at), weights.at[at]) for at in range(2)
    }
    fold(flat[0], pool.at[1], pool.at[4])
    near_copy(6).start()
    fold(flat[1], pool.at[1], pool.at[5])
    near_copy(7).start()
    normed_load = load(normed_two_hbm, pool.at[1])
    context_load = load(context_hbm, pool.at[4])
    right_step(1)

    rise_loads = {}
    for at in range(4):
        buffer = 2 + at % 2
        active_loads[at].wait()
        fold(big.at[at], pool.at[buffer], pool.at[0])
        if at < 2:
            active_loads[at + 2] = load(chunk_of(active_hbm, at + 2), pool.at[buffer])
        else:
            rise_loads[at - 2] = load(chunk_of(rise_hbm, at - 2), pool.at[buffer])
        if at == 1:
            right_step(2)
            join(6)
            join(7)
        elif at == 2:
            advance((6, 7), 0)
        elif at == 3:
            right_step(3)
    near_copy(OUTER).start()
    out_loads[1] = load(outer_hbm.at[pl.ds(width, width)], weights.at[3])

    normed_load.wait()
    for at in range(4):
        buffer = 2 + at % 2
        rise_loads[at].wait()
        out_loads[at].wait()
        in_loads[at].wait()

        def back(span):
            before = product_right(pool[0, span], weights[2 + at % 2])
            before = (before * pool[buffer, span].astype(jnp.float32)).astype(narrow)
            pool[buffer, span] = before
            moved = product_right(before, weights[at % 2])
            level[1, span] = moved if at == 0 else level[1, span] + moved

        each_tile(back)
        if at < 2:
            span = pl.ds((at + 2) * width, width)
            out_loads[at + 2] = load(outer_hbm.at[span], weights.at[2 + at % 2])
            in_loads[at + 2] = load(chunk_of(inner_hbm, at + 2), weights.at[at % 2])
        right_step(at + 4)
        advance((6, 7), at + 1)
        if at == 0:
            join(OUTER)
        else:
            advance((OUTER,), at - 1)
        fold(big.at[at], pool.at[1], pool.at[buffer])
        if at < 2:
            rise_loads[at + 2] = load(chunk_of(rise_hbm, at + 2), pool.at[buffer])
    near_copy(INNER).start()
    query_load = load(query_hbm, pool.at[1])
    key_load, value_load = load(key_hbm, pool.at[2]), load(value_hbm, pool.at[3])
    late_loads = [
        load(query_weight_hbm, weights.at[0]), load(key_weight_hbm, weights.at[1]),
        load(value_weight_hbm, weights.at[2]),
    ]
    output_load = load(output_weight_hbm, weights.at[3])

    def back_norm(field, moved, gain_row, at):
        scale = root_scale(field)
        small[at : at + 1] += jnp.sum(moved * field * scale, axis=0, keepdims=True)
        weighted = moved * gain_row
        mean = jnp.mean(weighted * field, axis=-1, keepdims=True)
        return scale * weighted - field * (scale * scale * scale) * mean

    hidden_load.wait()

    def second(span):
        value = level[0, span] + back_norm(level[2, span], level[1, span], gain[1:2], 1)
        level[0, span] = value
        pool[0, span] = value.astype(narrow)

    each_tile(second)
    advance((6, 7), 5)
    advance((OUTER,), 3)
    context_load.wait()
    fold(flat[0], pool.at[4], pool.at[0])
    near_copy(5).start()
    normed_one_load = load(normed_one_hbm, pool.at[4])
    output_load.wait()

    def third(span):
        pool[5, span] = product_right(pool[0, span], weights[3]).astype(narrow)

    each_tile(third)
    tokens_load = load(tokens_hbm, pool.at[0])
    advance((6, 7), 6)
    advance((OUTER,), 4)
    join(INNER)
    join(5)
    for copy in (query_load, key_load, value_load):
        copy.wait()

    def pair_products():
        each_peer(lambda k: left_copy(k).wait_recv())
        for j, (left_at, right_at) in enumerate(spans):
            own, columns = pair_sums[j].shape
            wide = -(-own // 128) * 128
            left = left_all[:, :, left_at : left_at + wide].reshape(-1, wide)
            for begin in range(0, columns, width):
                right = right_all[:, :, right_at + begin : right_at + begin + width]
                block = product_left(left, right.reshape(-1, width))
                pair_work[j][:, begin : begin + width] = block[:own].astype(narrow)
            pair_near(j).start()

    def pair_cross():
        for j in range(pairs):
            pair_near(j).wait()
            mine = pair_work[j][:, half_of(core, pair_sums[j].shape[1])]
            pair_half[j][...] = plus(pair_half[j][...], mine).astype(narrow)
            pair_across(j).start()

    def share_copy(at):
        return pltpu.make_async_copy(
            shares_hbm.at[lax.rem(at, rows), at // rows],
            shares.at[lax.rem(at, 2)],
            share_sem.at[lax.rem(at, 2)],
        )

    turns = rows * (HEADS // 2)
    share_copy(0).start()

    def attend_pair(at, carry):
        pair, row, buffer = at // rows, lax.rem(at, rows), lax.rem(at, 2)
        share_copy(at).wait()

        @pl.when(at + 1 < turns)
        def _():
            share_copy(at + 1).start()

        @pl.when(lax.rem(at, 2) == 1)
        def _():
            advance((INNER,), at // 2)

        @pl.when((at > 0) & (lax.rem(at, 2) == 0))
        def _():
            advance((5,), at // 2 - 1)

        @pl.when(at == 2)
        def _():
            advance((6, 7), 7)
            for i in (6, 7):
                end_across(i).start()

        for turn, step in ((1, 5), (3, 6), (5, 7)):

            @pl.when(at == turn)
            def _():
                advance((OUTER,), step)

        @pl.when(at == 2)
        def _():
            pair_products()

        @pl.when(at == 4)
        def _():
            pair_cross()

        @pl.when(row == 0)
        def _():
            bias_acc[...] = jnp.zeros_like(bias_acc)

        key_acc[...] = jnp.zeros_like(key_acc)
        value_acc[...] = jnp.zeros_like(value_acc)
        columns = rows_of(pair, 2 * KV)

        def span(begin, size):
            return pl.ds(pl.multiple_of(row * length + begin, BLOCK), size)

        for block in range(blocks):
            keys, places = reach(block, blocks)
            own = span(block * BLOCK, BLOCK)
            near = span(keys.start, keys.stop - keys.start)
            query, grad = wide_heads(pool[1, own, columns]), wide_heads(pool[5, own, columns])
            narrow_shares = shares[buffer, block, :, places]
            part = narrow_shares.astype(jnp.float32)
            value_acc[keys] += product_left(narrow_shares, grad)
            moved = part * product_right(grad, pool[3, near, columns])
            grad_scores = moved - part * jnp.sum(moved, axis=1, keepdims=True)
            bias_acc[:, places] += grad_scores
            low = grad_scores.astype(narrow)
            key_acc[keys] += product_left(low, query)
            mixed = product(low, pool[2, near, columns])
            pool[1, own, columns] = narrow_heads(mixed).astype(narrow)
        pool[2, span(0, length), columns] = key_acc[...].astype(narrow)
        pool[3, span(0, length), columns] = value_acc[...].astype(narrow)

        @pl.when(row == rows - 1)
        def _():
            for head in range(2):
                block = bias_acc[head * BLOCK : (head + 1) * BLOCK]
                place = slice(head * 3 * BLOCK, (head + 1) * 3 * BLOCK)
                small[pl.ds(5 + pair, 1), place] = offset_sums(block)

        return carry

    lax.fori_loop(0, turns, attend_pair, 0)
    advance((5,), 5)
    normed_one_load.wait()
    fold(big.at[0], pool.at[4], pool.at[1])
    near_copy(2).start()
    advance((INNER,), 6)
    advance((5,), 6)
    fold(big.at[1], pool.at[4], pool.at[2])
    near_copy(3).start()
    join(2)
    advance((2,), 0)
    fold(big.at[2], pool.at[4], pool.at[3])
    near_copy(4).start()
    join(3)
    advance((3,), 0)
    advance((INNER,), 7)
    advance((5,), 7)
    for i in (INNER, 5):
        end_across(i).start()
    join(4)
    advance((4,), 0)
    close(OUTER)
    for i in (6, 7):
        close(i)
    tokens_load.wait()
    for copy in late_loads:
        copy.wait()

    def save(at):
        span = rows_of(at)
        return pltpu.make_async_copy(
            level.at[1, span], tokens_grad_hbm.at[span], share_sem.at[2 + at]
        )

    def last(at, carry):
        span = rows_of(at)
        moved = product_right(pool[1, span], weights[0])
        moved = moved + product_right(pool[2, span], weights[1])
        moved = moved + product_right(pool[3, span], weights[2])
        field = pool[0, span].astype(jnp.float32)
        level[1, span] = level[0, span] + back_norm(field, moved, gain[0:1], 0)
        save(at).start()
        advance((2, 3, 4), at + 1)
        return carry

    lax.fori_loop(0, tiles, last, 0)
    near_small = send(small, small_near, small_sem.at[0], small_sem.at[1], spot.sibling)
    near_small.start()
    advance((2, 3, 4), tiles + 1)
    near_small.wait()
    small_mid[...] = small[...] + small_near[...]
    far_small = send(small_mid, small_far, small_sem.at[2], small_sem.at[3], spot.opposite)
    far_small.start()
    advance((2, 3, 4), tiles + 2)
    far_small.wait()
    small_all[spot.fsdp] = small_mid[...] + small_far[...]
    each_peer(lambda k: small_copy(k).start())
    run((2, 3, 4), tiles + 3, count)
    for i in (2, 3, 4):
        end_across(i).start()
    for j in range(pairs):
        pair_across(j).wait()
        here = half_of(core, pair_sums[j].shape[1])
        pair_sums[j][:, here] = plus(pair_half[j][...], pair_far[j][...]).astype(narrow)
        pair_end(j).start()
    close(INNER)
    close(5)
    end_far(OUTER).wait()
    end_relay(OUTER).start()
    each_peer(lambda k: small_copy(k).wait_recv())
    small_sum[...] = lax.fori_loop(
        1, count, lambda k, so_far: so_far + small_all[k], small_all[0]
    )
    for i in (2, 3, 4):
        close(i)
    for i in range(8):
        end_near(i).wait()
    end_relay(OUTER).wait()
    for j in range(pairs):
        pair_end(j).wait()
    for at in range(tiles):
        save(at).wait()

    def drain(step, carry):
        for way in range(2):
            far_copy(OUTER, way, step).wait_send()
        return carry

    lax.fori_loop(0, count, drain, 0)

    def drain_ring(step, carry):
        for way in range(2):
            for i in range(8):
                for at in range(SPLITS.get(i, 1)):
                    ring_copy(i, way, step, at).wait_send()
            right_copy(way, step).wait_send()
        left_copy(step + 1).wait_send()
        small_copy(step + 1).wait_send()
        return carry

    lax.fori_loop(0, count - 1, drain_ring, 0)


def backward(
    count, rows, whole, kept, tokens, cotangent, grad_keys, grad_values,
    left_part, right_part, pair_shapes, gains, decoder_gains,
):
    (
        query, key, value, shares, context, hidden, normed_two,
        active, rise, memory, unused_keys, unused_values, normed_one,
    ) = kept
    many, width = tokens.shape
    depth, narrow, wide = width // count, jnp.bfloat16, jnp.float32
    pairs = len(pair_shapes)
    spans, left_at, right_at = [], 0, 0
    for own, columns in pair_shapes:
        spans.append((left_at, right_at))
        left_at, right_at = left_at + -(-own // 128) * 128, right_at + columns
    dma, vmem = pltpu.SemaphoreType.DMA, pltpu.VMEM
    pieces = [(depth, width), (depth, width // 2)] + [(depth // 2, width // 2)] * 6
    outs = [(depth, 4 * width), (4 * depth, width)] + [(depth, width)] * 6
    little = (16, width)
    scratch = [vmem((4, width, width), narrow)] + [vmem((width, width), narrow)] * 2
    scratch += [vmem((2, width, width), narrow), vmem((4, width, width // 2), narrow)]
    scratch += [vmem((width, width // 2), narrow)] * 6
    scratch += [vmem((2, count) + piece, narrow) for piece in pieces]
    scratch += [vmem((2,) + piece, narrow) for piece in pieces]
    scratch += [vmem((2, count) + pieces[1], narrow)]
    scratch += [vmem(left_part.shape, narrow), vmem((count,) + right_part.shape, narrow)]
    scratch += [vmem(s, narrow) for s in pair_shapes]
    scratch += [vmem((r, c // 2), narrow) for r, c in pair_shapes] * 2
    scratch += [vmem(little, wide)] * 4 + [vmem((count,) + little, wide)]
    scratch += [
        vmem((6, many, width), narrow), vmem((3, many, width), wide),
        vmem((4, width, width), narrow), vmem((2,) + shares.shape[2:], narrow),
        vmem((2 * BLOCK, 3 * BLOCK), wide),
    ]
    scratch += [vmem((many // rows, 2 * KV), wide)] * 2
    scratch += [
        dma((2, 8)), dma((8, 2, 2, count)), dma((8, 2, 2, count)), dma((2, 2, count)), dma((8, 8)),
        dma((count,)), dma((count,)), dma((2, count)), dma((2, count)), dma((6, pairs)),
        dma((4,)), dma((count,)), dma((count,)), dma((48,)), dma((2 + many // TILE,)),
    ]
    shapes = [jax.ShapeDtypeStruct(s, narrow) for s in outs + list(pair_shapes)]
    shapes += [jax.ShapeDtypeStruct(little, wide), jax.ShapeDtypeStruct((many, width), wide)]
    anywhere = pl.BlockSpec(memory_space=pl.ANY)
    local = pl.BlockSpec(memory_space=pltpu.VMEM)
    got = pl.pallas_call(
        functools.partial(backward_kernel, count, rows, spans),
        out_shape=shapes,
        in_specs=[anywhere] * 23 + [local] * 4,
        out_specs=[local] * (len(shapes) - 1) + [anywhere],
        scratch_shapes=scratch,
        compiler_params=pltpu.CompilerParams(
            collective_id=3, has_side_effects=True, vmem_limit_bytes=63 * 2**20
        ),
        name="backward",
    )(
        whole[4], whole[5], whole[0], whole[1], whole[2], whole[3], whole[6], whole[7],
        active, rise, normed_two, context, query, key, value, normed_one, tokens, memory,
        grad_keys, grad_values, cotangent, hidden, shares,
        left_part, right_part, gains, decoder_gains,
    )
    return got[:8], got[8 : 8 + pairs], got[-2], got[-1]


def backward_apart(
    count, rows, whole, kept, tokens, cotangent, grad_cross_keys, grad_cross_values,
    left_part, right_part, pair_shapes, gains, decoder_gains,
):
    (
        query_full, key_full, value_full, output_full, inner_full, outer_full, cross_key_full,
        cross_value_full,
    ) = whole[:8]
    (
        query_all, key_all, value_all, shares, context, hidden, normed_two,
        active, rise, memory, unused_keys, unused_values, normed_one,
    ) = kept
    row_count, length = rows, tokens.shape[0] // rows
    gain_one, gain_two = gains[0], gains[1]
    field = tokens.astype(jnp.float32)
    scale_one, scale_two = root_scale(field), root_scale(hidden)
    grad_cross_key = product_left(memory, grad_cross_keys)
    grad_cross_value = product_left(memory, grad_cross_values)
    grad_memory = product_right(grad_cross_keys, cross_key_full) + product_right(
        grad_cross_values, cross_value_full
    )
    grad_encoded = cotangent.astype(jnp.float32) + grad_memory
    grad_branch = grad_encoded.astype(jnp.bfloat16)
    grad_outer = product_left(active, grad_branch)
    grad_active = product_right(grad_branch, outer_full)
    grad_before = (grad_active * rise).astype(jnp.bfloat16)
    grad_inner = product_left(normed_two, grad_before)
    grad_normed = product_right(grad_before, inner_full)
    field_part, grad_gain_two = norm_back(
        grad_normed, hidden, scale_two, gain_two
    )
    grad_hidden = grad_encoded + field_part
    grad_branch = grad_hidden.astype(jnp.bfloat16)
    grad_output = product_left(context, grad_branch)
    grad_context = product_right(grad_branch, output_full).astype(jnp.bfloat16)
    grad_query_all, grad_key_all, grad_value_all, bias_sums = attend_rows_back(
        row_count, length, query_all, key_all, value_all, grad_context, shares
    )
    grad_query = product_left(normed_one, grad_query_all)
    grad_key = product_left(normed_one, grad_key_all)
    grad_value = product_left(normed_one, grad_value_all)
    grad_normed = (
        product_right(grad_query_all, query_full)
        + product_right(grad_key_all, key_full)
        + product_right(grad_value_all, value_full)
    )
    field_part, grad_gain_one = norm_back(
        grad_normed, field, scale_one, gain_one
    )
    tokens_grad = grad_hidden + field_part
    small = jnp.concatenate([
        jnp.stack([grad_gain_one, grad_gain_two]),
        decoder_gains,
        bias_sums.reshape(HEADS // 2, -1),
        jnp.zeros((5, tokens.shape[1]), jnp.float32),
    ])
    encoder_grads = (
        grad_inner, grad_outer, grad_query, grad_key, grad_value, grad_output,
        grad_cross_key, grad_cross_value,
    )
    encoder_sums, decoder_sums, small_sum = reduce_grads(
        count,
        ENCODER_KINDS,
        [
            g.astype(jnp.bfloat16).reshape(count, g.shape[0] // count, g.shape[1])
            for g in encoder_grads
        ],
        left_part,
        right_part,
        pair_shapes,
        small,
    )
    return encoder_sums, decoder_sums, small_sum, tokens_grad


def widen_kernel(total, *refs):
    sources, targets = refs[:total], refs[total : 2 * total]
    held, wide, sems = refs[2 * total : 3 * total], list(refs[3 * total : -1]), refs[-1]
    ready = [part if part.dtype == jnp.float32 else wide.pop(0) for part in held]
    loads = [pltpu.make_async_copy(sources[at], held[at], sems.at[at]) for at in range(total)]
    stores = [
        pltpu.make_async_copy(ready[at], targets[at], sems.at[total + at]) for at in range(total)
    ]
    for copy in loads:
        copy.start()
    for at in range(total):
        loads[at].wait()
        if held[at] is not ready[at]:
            ready[at][...] = held[at][...].astype(jnp.float32)
        stores[at].start()
    for copy in stores:
        copy.wait()


def widen(parts):
    anywhere, total = pl.BlockSpec(memory_space=pl.ANY), len(parts)
    return pl.pallas_call(
        functools.partial(widen_kernel, total),
        out_shape=[jax.ShapeDtypeStruct(part.shape, jnp.float32) for part in parts],
        in_specs=[anywhere] * total,
        out_specs=[anywhere] * total,
        scratch_shapes=[pltpu.VMEM(part.shape, part.dtype) for part in parts]
        + [
            pltpu.VMEM(part.shape, jnp.float32) for part in parts if part.dtype != jnp.float32
        ]
        + [pltpu.SemaphoreType.DMA((2 * total,))],
        compiler_params=pltpu.CompilerParams(vmem_limit_bytes=63 * 2**20),
        name="widen",
    )(*parts)


def on_device(
    tokens,
    segment_index,
    start_vectors,
    first_gain,
    query_weight,
    key_weight,
    value_weight,
    output_weight,
    position_table,
    second_gain,
    inner_weight,
    outer_weight,
    start_gain,
    self_value,
    self_output,
    middle_gain,
    cross_query,
    cross_key,
    cross_value,
    cross_output,
    final_gain,
    decoder_inner,
    decoder_outer,
    encoded_cotangent,
    decoded_cotangent,
):
    row_count = segment_index.shape[0]
    length = segment_index.shape[1]
    slot_count = start_vectors.shape[1]
    width = tokens.shape[1]
    count = lax.axis_size("fsdp")
    depth = first_gain.shape[0]
    choices = jnp.arange(position_table.shape[0], dtype=jnp.int32)
    onehot = (offset_buckets()[None, :] == choices[:, None]).astype(jnp.float32)
    base = jnp.dot(position_table.T, onehot, precision=lax.Precision.HIGHEST)
    gains = jnp.stack([first_gain, second_gain, start_gain, middle_gain, final_gain])
    gains = jnp.pad(gains, ((0, 11), (0, BLOCK - depth)))
    shards = (
        query_weight, key_weight, value_weight, output_weight, inner_weight, outer_weight,
        cross_key, cross_value, self_value, self_output, cross_query, cross_output,
        decoder_inner, decoder_outer, gains,
    )
    fused = count == 8 and depth % 32 == 0 and (row_count, length) == (2, 512)
    plan = forward if fused else forward_apart
    whole, all_gains, kept = plan(count, shards, tokens, segment_index, base)
    memory, cross_keys, cross_values = kept[9:12]
    token_count = row_count * slot_count
    (
        decoded, start_grad, decoder_gain_grads, *factors,
        grad_cross_keys, grad_cross_values, encoded,
    ) = decode(
        count if fused else 0,
        segment_index,
        start_vectors.reshape(token_count, width),
        decoded_cotangent.reshape(token_count, width),
        all_gains,
        cross_keys,
        cross_values,
        memory,
        whole[8:14],
    )
    hidden_width = decoder_inner.shape[1]
    pair_shapes = [(depth, hidden_width), (hidden_width // count, width)] + [(depth, width)] * 4
    if not fused:
        left_cols = []
        for left, (rows, unused) in zip(factors[:6], pair_shapes):
            columns = left.reshape(token_count, count, rows).transpose(1, 0, 2)
            left_cols.append(jnp.pad(columns, ((0, 0), (0, 0), (0, -rows % 128))))
        factors = (jnp.concatenate(left_cols, axis=2), jnp.concatenate(factors[6:], axis=1))
    turn_back = backward if fused else backward_apart
    encoder_sums, decoder_sums, small_sum, tokens_grad = turn_back(
        count, row_count, whole, kept, tokens, encoded_cotangent,
        grad_cross_keys, grad_cross_values,
        *factors, pair_shapes, all_gains, decoder_gain_grads,
    )
    (
        inner_weight_grad, outer_weight_grad, query_weight_grad, key_weight_grad,
        value_weight_grad, output_weight_grad, cross_key_grad, cross_value_grad,
        decoder_inner_grad, decoder_outer_grad, self_value_grad, self_output_grad,
        cross_query_grad, cross_output_grad, tokens_grad,
    ) = widen([*encoder_sums, *decoder_sums, tokens_grad])
    position_table_grad = lax.dot_general(
        onehot,
        small_sum[5:11].reshape(HEADS, 3 * BLOCK),
        (((1,), (1,)), ((), ())),
        precision=lax.Precision.HIGHEST,
    )
    own_gains = lax.dynamic_slice_in_dim(
        small_sum[:5], lax.axis_index("fsdp") * depth, depth, axis=1
    )
    first_gain_grad, second_gain_grad, start_gain_grad, middle_gain_grad, final_gain_grad = own_gains
    decoded = decoded.reshape(start_vectors.shape)
    start_grad = start_grad.reshape(start_vectors.shape)
    return (
        encoded,
        decoded,
        tokens_grad,
        start_grad,
        first_gain_grad,
        query_weight_grad,
        key_weight_grad,
        value_weight_grad,
        output_weight_grad,
        position_table_grad,
        second_gain_grad,
        inner_weight_grad,
        outer_weight_grad,
        start_gain_grad,
        self_value_grad,
        self_output_grad,
        middle_gain_grad,
        cross_query_grad,
        cross_key_grad,
        cross_value_grad,
        cross_output_grad,
        final_gain_grad,
        decoder_inner_grad,
        decoder_outer_grad,
    )


def solution(mesh):
    placed = (
        P(("dp", "fsdp"), None),
        P(("dp", "fsdp"), None),
        P(("dp", "fsdp"), None, None),
        P("fsdp"),
        P("fsdp", None),
        P("fsdp", None),
        P("fsdp", None),
        P("fsdp", None),
        P(),
        P("fsdp"),
        P("fsdp", None),
        P("fsdp", None),
        P("fsdp"),
        P("fsdp", None),
        P("fsdp", None),
        P("fsdp"),
        P("fsdp", None),
        P("fsdp", None),
        P("fsdp", None),
        P("fsdp", None),
        P("fsdp"),
        P("fsdp", None),
        P("fsdp", None),
        P(("dp", "fsdp"), None),
        P(("dp", "fsdp"), None, None),
    )
    return jax.shard_map(
        on_device,
        mesh=mesh,
        in_specs=placed,
        out_specs=(
            P(("dp", "fsdp"), None),
            P(("dp", "fsdp"), None, None),
            P(("dp", "fsdp"), None),
            P(("dp", "fsdp"), None, None),
            P("fsdp"),
            P("fsdp", None),
            P("fsdp", None),
            P("fsdp", None),
            P("fsdp", None),
            P(),
            P("fsdp"),
            P("fsdp", None),
            P("fsdp", None),
            P("fsdp"),
            P("fsdp", None),
            P("fsdp", None),
            P("fsdp"),
            P("fsdp", None),
            P("fsdp", None),
            P("fsdp", None),
            P("fsdp", None),
            P("fsdp"),
            P("fsdp", None),
            P("fsdp", None),
        ),
        check_vma=False,
    )
```

```python
import functools

import jax
import jax.numpy as jnp
from jax import lax
from jax.experimental import pallas as pl
from jax.experimental.pallas import tpu as pltpu
from jax.sharding import PartitionSpec as P

HEADS = 12
KV = 64
BLOCK = 128


epsilon = 1e-06
negative_fill = -1e30
bucket_edges = (12, 16, 23, 32, 46, 64, 91)


MESH = pl.DeviceIdType.MESH
KINDS = (
    "square", "square", "square", "square", "wide", "tall", "square", "square",
    "square", "square", "square", "square", "wide", "tall", "small",
)


def ring_position(index, count):
    if count == 64:
        slow, rest = index // 32, index % 32
        row, column = rest // 8, rest % 8
        place = row * 8 + column + (row % 2) * (7 - 2 * column)
        return place + slow * (count - 1 - 2 * place)
    across, along = index % 2, index // 2
    return along + across * (count - 1 - 2 * along)


def ring_index(position, count):
    position = lax.rem(position, count)
    across = position // (count // 2)
    along = position + across * (count - 1 - 2 * position)
    if count == 64:
        row, column = along // 8, along % 8
        return across * 32 + row * 8 + column + (row % 2) * (7 - 2 * column)
    return 2 * along + across


class Spot:
    def __init__(self, count):
        self.count = count
        self.dp = lax.axis_index("dp")
        self.fsdp = lax.axis_index("fsdp")
        self.core = lax.rem(self.dp, 2)
        self.plane = self.dp // 2
        self.place = ring_position(self.fsdp, count)
        self.sibling = (self.dp + 1 - 2 * self.core, self.fsdp)
        self.opposite = (lax.rem(self.dp + 2, 4), self.fsdp)
        self.after = (self.dp, ring_index(self.place + 1, count))
        self.before = (self.dp, ring_index(self.place + count - 1, count))

    def greet(self, others=()):
        barrier = pltpu.get_barrier_semaphore()
        partners = (self.sibling, self.opposite, self.after, self.before) + tuple(others)
        for partner in partners:
            pl.semaphore_signal(barrier, inc=1, device_id=partner, device_id_type=MESH)
        pl.semaphore_wait(barrier, len(partners))


def cut(kind, ref, plane, core):
    rows, columns = ref.shape
    if kind == "small":
        return ref
    if kind == "square":
        half = columns // 2
        return ref.at[:, pl.ds(pl.multiple_of(core * half, 128), half)]
    if kind == "wide":
        quarter = columns // 4
        return ref.at[:, pl.ds(pl.multiple_of((core * 2 + plane) * quarter, 128), quarter)]
    half, upper = columns // 2, rows // 2
    return ref.at[
        pl.ds(pl.multiple_of(plane * upper, 8), upper),
        pl.ds(pl.multiple_of(core * half, 128), half),
    ]


def send(source, target, send_sem, recv_sem, device):
    return pltpu.make_async_remote_copy(
        src_ref=source,
        dst_ref=target,
        send_sem=send_sem,
        recv_sem=recv_sem,
        device_id=device,
        device_id_type=MESH,
    )


def gather_kernel(count, kinds, *refs):
    total = len(kinds)
    shards, fulls = refs[:total], refs[total : 2 * total]
    ring_out, ring_in, near_out, near_in, far_out, far_in, last_out, last_in, own_sem = refs[
        2 * total :
    ]
    spot = Spot(count)
    split = [i for i in range(total) if kinds[i] in ("wide", "tall")]

    window = min(count, 8)

    def slot_of(i, step):
        turn = step if i % 2 else count - step
        return ring_index(spot.place + turn, count)

    def ring_copy(i, step, source=None):
        here = cut(kinds[i], fulls[i].at[slot_of(i, step)], spot.plane, spot.core)
        return send(
            here if source is None else source,
            here,
            ring_out.at[i, lax.rem(step, window)],
            ring_in.at[i, step],
            spot.before if i % 2 else spot.after,
        )

    def near_copy(i, step):
        here = cut(kinds[i], fulls[i].at[slot_of(i, step)], spot.plane, spot.core)
        out = near_out.at[i, lax.rem(step, window)]
        return send(here, here, out, near_in.at[i, step], spot.sibling)

    def far_copy(i, step):
        here = cut(kinds[i], fulls[i].at[slot_of(i, step)], spot.plane, spot.core)
        at = split.index(i)
        out = far_out.at[at, lax.rem(step, window)]
        return send(here, here, out, far_in.at[at, step], spot.opposite)

    def last_copy(i, step):
        here = cut(kinds[i], fulls[i].at[slot_of(i, step)], 1 - spot.plane, spot.core)
        at = split.index(i)
        out = last_out.at[at, lax.rem(step, window)]
        return send(here, here, out, last_in.at[at, step], spot.sibling)

    def start(copy, i, step, first):
        if window < count:

            @pl.when(step >= first + window)
            def _():
                copy(i, step - window).wait_send()

        copy(i, step).start()

    def finish(copy, i, first, end):
        def one(step, carry):
            copy(i, step).wait_send()
            return carry

        lax.fori_loop(max(first, end - window), end, one, 0)

    owns = []
    for i in range(total):
        owns.append(pltpu.make_async_copy(shards[i], fulls[i].at[spot.fsdp], own_sem.at[i]))
        owns[-1].start()
    spot.greet()
    for i in range(total):
        ring_copy(i, 0, cut(kinds[i], shards[i], spot.plane, spot.core)).start()

    def one_step(step, carry):
        for i in range(total):
            ring_copy(i, step - 1).wait_recv()

            @pl.when(step < count - 1)
            def _():
                start(ring_copy, i, step, 0)

            if kinds[i] != "small":
                start(near_copy, i, step, 1)
            if i in split:
                start(far_copy, i, step, 1)

        @pl.when(step > 1)
        def _():
            for i in split:
                far_copy(i, step - 1).wait_recv()
                start(last_copy, i, step - 1, 1)

        return carry

    lax.fori_loop(1, count, one_step, 0)
    for i in split:
        far_copy(i, count - 1).wait_recv()
        start(last_copy, i, count - 1, 1)

    def settle(step, carry):
        for i in range(total):
            if kinds[i] != "small":
                near_copy(i, step).wait_recv()
            if i in split:
                last_copy(i, step).wait_recv()
        return carry

    lax.fori_loop(1, count, settle, 0)
    for i in range(total):
        finish(ring_copy, i, 0, count - 1)
        if kinds[i] != "small":
            finish(near_copy, i, 1, count)
        if i in split:
            finish(far_copy, i, 1, count)
            finish(last_copy, i, 1, count)
    for copy in owns:
        copy.wait()


def gather_weights(count, shards, kinds):
    total = len(shards)
    split = sum(kind in ("wide", "tall") for kind in kinds)
    window = min(count, 8)
    many, few = [
        [pltpu.SemaphoreType.DMA((rows, window)), pltpu.SemaphoreType.DMA((rows, count))] * 2
        for rows in (total, split)
    ]
    return pl.pallas_call(
        functools.partial(gather_kernel, count, kinds),
        out_shape=[jax.ShapeDtypeStruct((count,) + s.shape, s.dtype) for s in shards],
        in_specs=[pl.BlockSpec(memory_space=pl.ANY)] * total,
        out_specs=[pl.BlockSpec(memory_space=pl.ANY)] * total,
        scratch_shapes=many + few + [pltpu.SemaphoreType.DMA((total,))],
        compiler_params=pltpu.CompilerParams(collective_id=0, has_side_effects=True),
        name="gather_weights",
    )(*shards)

def plus(*terms):
    total = terms[0].astype(jnp.float32)
    for term in terms[1:]:
        total = total + term.astype(jnp.float32)
    return total


def half_of(core, columns):
    half = columns // 2
    return pl.ds(pl.multiple_of(core * half, 128), half)


def plane_part(kind, plane, rows, columns):
    if kind == "wide":
        return slice(None), pl.ds(pl.multiple_of(plane * (columns // 2), 128), columns // 2)
    if kind == "tall":
        return pl.ds(pl.multiple_of(plane * (rows // 2), 8), rows // 2), slice(None)
    return slice(None), slice(None)


ENCODER_KINDS = ("wide", "tall", "square", "square", "square", "square", "square", "square")


def reduce_kernel(count, kinds, spans, *refs):
    total, pairs = len(kinds), len(spans)
    refs = list(refs)

    def take(size):
        got = refs[:size]
        del refs[:size]
        return got

    grads = take(total)
    left_part, right_part, small = take(3)
    sums = take(total)
    pair_sums = take(pairs)
    (small_sum,) = take(1)
    half, work, final = take(total), take(total), take(total)
    split = [i for i in range(total) if kinds[i] != "square"]
    far = take(len(split))
    left_all, right_all = take(2)
    pair_half, pair_far, pair_work = take(pairs), take(pairs), take(pairs)
    small_near, small_mid, small_far, small_all = take(4)
    (
        near_sem, ring_out, ring_in, far_sem, end_sem, left_out, left_in,
        right_out, right_in, pair_sem, small_sem, small_out, small_in,
    ) = take(13)
    spot = Spot(count)
    core, plane = spot.core, spot.plane
    diagonal = (lax.rem(spot.dp + 2, 4) + 1 - 2 * core, spot.fsdp)

    def peer(k):
        return (spot.dp, lax.rem(spot.fsdp + k, count))

    barrier = pltpu.get_barrier_semaphore()
    for partner in (spot.sibling, spot.opposite, diagonal):
        pl.semaphore_signal(barrier, inc=1, device_id=partner, device_id_type=MESH)

    def greet(k, carry):
        pl.semaphore_signal(barrier, inc=1, device_id=peer(k), device_id_type=MESH)
        return carry

    lax.fori_loop(1, count, greet, 0)
    pl.semaphore_wait(barrier, count + 2)

    def near_copy(i):
        columns = grads[i].shape[2]
        return send(
            grads[i].at[:, :, half_of(1 - core, columns)], half[i],
            near_sem.at[0, i], near_sem.at[1, i], spot.sibling,
        )

    def slot_at(i, step):
        turn = step + 1 if i % 2 else count - 1 - step
        return ring_index(spot.place + turn, count)

    def far_copy(i, step):
        at = split.index(i)
        rows, columns = half[i].shape[1:]
        part = plane_part(kinds[i], 1 - plane, rows, columns)
        return send(
            half[i].at[(slot_at(i, step),) + part], far[at].at[step],
            far_sem.at[0, at, step], far_sem.at[1, at, step], spot.opposite,
        )

    def ring_copy(i, step):
        return send(
            work[i].at[step], work[i].at[step + 1], ring_out.at[i, step], ring_in.at[i, step],
            spot.before if i % 2 else spot.after,
        )

    def left_copy(k):
        other = lax.rem(spot.fsdp + k, count)
        return send(
            left_part.at[other], left_all.at[spot.fsdp], left_out.at[k], left_in.at[k], peer(k)
        )

    def right_copy(way, step):
        turn = step if way else count - step
        slot = ring_index(spot.place + turn, count)
        width = right_part.shape[1] // 2
        here = right_all.at[slot, :, way * width : (way + 1) * width]
        return send(
            here, here, right_out.at[way, step], right_in.at[way, step],
            spot.before if way else spot.after,
        )

    for i in range(total):
        near_copy(i).start()
    near_small = send(small, small_near, small_sem.at[0], small_sem.at[1], spot.sibling)
    near_small.start()

    def left_start(k, carry):
        left_copy(k).start()
        return carry

    lax.fori_loop(1, count, left_start, 0)
    right_all[spot.fsdp] = right_part[...]
    left_all[spot.fsdp] = left_part[spot.fsdp]
    for way in range(2):
        right_copy(way, 0).start()
    near_small.wait()
    small_mid[...] = small[...] + small_near[...]
    far_small = send(small_mid, small_far, small_sem.at[2], small_sem.at[3], spot.opposite)
    far_small.start()

    for i in range(total):
        near_copy(i).wait_recv()

        def join(slot, carry):
            mine = grads[i][slot, :, half_of(core, grads[i].shape[2])]
            half[i][slot] = plus(half[i][slot], mine).astype(jnp.bfloat16)
            return carry

        lax.fori_loop(0, count, join, 0)
        if i in split:

            def far_start(step, carry):
                far_copy(i, step).start()
                return carry

            lax.fori_loop(0, count, far_start, 0)

    far_small.wait()
    small_all[spot.fsdp] = small_mid[...] + small_far[...]

    def small_copy(k):
        here = small_all.at[spot.fsdp]
        return send(here, here, small_out.at[k], small_in.at[k], peer(k))

    def small_start(k, carry):
        small_copy(k).start()
        return carry

    lax.fori_loop(1, count, small_start, 0)

    def right_step(step, carry):
        for way in range(2):
            right_copy(way, step - 1).wait_recv()

            @pl.when(step < count - 1)
            def _():
                right_copy(way, step).start()

        return carry

    lax.fori_loop(1, count, right_step, 0)

    def left_wait(k, carry):
        left_copy(k).wait_recv()
        return carry

    lax.fori_loop(1, count, left_wait, 0)

    def pair_near(j):
        columns = pair_sums[j].shape[1]
        return send(
            pair_work[j].at[:, half_of(1 - core, columns)], pair_half[j],
            pair_sem.at[0, j], pair_sem.at[1, j], spot.sibling,
        )

    def pair_across(j):
        return send(
            pair_half[j], pair_far[j], pair_sem.at[2, j], pair_sem.at[3, j], spot.opposite
        )

    def pair_end(j):
        here = pair_sums[j].at[:, half_of(core, pair_sums[j].shape[1])]
        return send(here, here, pair_sem.at[4, j], pair_sem.at[5, j], spot.sibling)

    for j, (left_at, right_at) in enumerate(spans):
        rows, columns = pair_sums[j].shape
        span = -(-rows // 128) * 128
        left = left_all[:, :, left_at : left_at + span].reshape(-1, span)
        for begin in range(0, columns, 768):
            right = right_all[:, :, right_at + begin : right_at + begin + 768].reshape(-1, 768)
            block = lax.dot_general(
                left, right, (((0,), (0,)), ((), ())), preferred_element_type=jnp.float32
            )
            pair_work[j][:, begin : begin + 768] = block[:rows].astype(jnp.bfloat16)
        pair_near(j).start()
    for j in range(pairs):
        pair_near(j).wait()
        mine = pair_work[j][:, half_of(core, pair_sums[j].shape[1])]
        pair_half[j][...] = plus(pair_half[j][...], mine).astype(jnp.bfloat16)
        pair_across(j).start()

    def one_step(step, carry):
        for i in range(total):
            rows, columns = half[i].shape[1:]
            slot = slot_at(i, step)
            value = half[i][(slot,) + plane_part(kinds[i], plane, rows, columns)]
            value = value.astype(jnp.float32)
            if i in split:
                far_copy(i, step).wait_recv()
                value = value + far[split.index(i)][step].astype(jnp.float32)

            @pl.when(step > 0)
            def _():
                ring_copy(i, step - 1).wait_recv()
                work[i][step] = plus(value, work[i][step]).astype(jnp.bfloat16)

            @pl.when(step == 0)
            def _():
                work[i][step] = value.astype(jnp.bfloat16)

            @pl.when(step < count - 1)
            def _():
                ring_copy(i, step).start()

        return carry

    lax.fori_loop(0, count, one_step, 0)

    def end_across(i):
        return send(
            work[i].at[count - 1], final[i], end_sem.at[0, i], end_sem.at[1, i], spot.opposite
        )

    def end_piece(i, mine_plane):
        rows, columns = sums[i].shape
        wide = half_of(core, columns)
        if kinds[i] == "square":
            return sums[i].at[:, wide]
        return cut(kinds[i], sums[i], mine_plane, core)

    def end_copies(i):
        here = end_piece(i, plane)
        copies = [send(here, here, end_sem.at[2, i], end_sem.at[3, i], spot.sibling)]
        if i in split:
            copies.append(send(here, here, end_sem.at[4, i], end_sem.at[5, i], spot.opposite))
            copies.append(send(here, here, end_sem.at[6, i], end_sem.at[7, i], diagonal))
        return copies

    for i in range(total):
        if i not in split:
            end_across(i).start()
    for i in split:
        end_piece(i, plane)[...] = work[i][count - 1]
        for copy in end_copies(i):
            copy.start()
    for j in range(pairs):
        pair_across(j).wait()
        here = half_of(core, pair_sums[j].shape[1])
        pair_sums[j][:, here] = plus(pair_half[j][...], pair_far[j][...]).astype(jnp.bfloat16)
        pair_end(j).start()
    for i in range(total):
        if i not in split:
            end_across(i).wait()
            value = plus(work[i][count - 1], final[i][...]).astype(jnp.bfloat16)
            end_piece(i, plane)[...] = value
            for copy in end_copies(i):
                copy.start()

    def small_wait(k, carry):
        small_copy(k).wait_recv()
        return carry

    lax.fori_loop(1, count, small_wait, 0)
    small_sum[...] = lax.fori_loop(
        1, count, lambda k, so_far: so_far + small_all[k], small_all[0]
    )
    for i in range(total):
        for copy in end_copies(i):
            copy.wait()
    for j in range(pairs):
        pair_end(j).wait()
    for i in range(total):
        near_copy(i).wait_send()

    def drain(step, carry):
        for i in split:
            far_copy(i, step).wait_send()
        return carry

    lax.fori_loop(0, count, drain, 0)

    def drain_ring(step, carry):
        for i in range(total):
            ring_copy(i, step).wait_send()
        for way in range(2):
            right_copy(way, step).wait_send()
        left_copy(step + 1).wait_send()
        small_copy(step + 1).wait_send()
        return carry

    lax.fori_loop(0, count - 1, drain_ring, 0)


def reduce_grads(count, kinds, grads, left_part, right_part, pair_shapes, small):
    total, pairs = len(kinds), len(pair_shapes)
    spans, left_at, right_at = [], 0, 0
    for rows, columns in pair_shapes:
        spans.append((left_at, right_at))
        left_at, right_at = left_at + -(-rows // 128) * 128, right_at + columns
    narrow = jnp.bfloat16
    blocks = [g.shape[1:] for g in grads]
    pieces = []
    for kind, (rows, columns) in zip(kinds, blocks):
        if kind == "wide":
            pieces.append((rows, columns // 4))
        elif kind == "tall":
            pieces.append((rows // 2, columns // 2))
        else:
            pieces.append((rows, columns // 2))
    split = [i for i in range(total) if kinds[i] != "square"]
    dma = pltpu.SemaphoreType.DMA
    scratch = [pltpu.VMEM((count, r, c // 2), narrow) for r, c in blocks]
    scratch += [pltpu.VMEM((count, r, c), narrow) for r, c in pieces]
    scratch += [pltpu.VMEM((r, c), narrow) for r, c in pieces]
    scratch += [pltpu.VMEM((count,) + pieces[i], narrow) for i in split]
    scratch += [
        pltpu.VMEM(left_part.shape, narrow),
        pltpu.VMEM((count,) + right_part.shape, narrow),
    ]
    scratch += [pltpu.VMEM((r, c // 2), narrow) for r, c in pair_shapes] * 2
    scratch += [pltpu.VMEM((r, c), narrow) for r, c in pair_shapes]
    scratch += [pltpu.VMEM(small.shape, jnp.float32)] * 3
    scratch += [pltpu.VMEM((count,) + small.shape, jnp.float32)]
    scratch += [
        dma((2, total)), dma((total, count)), dma((total, count)), dma((2, len(split), count)),
        dma((8, total)), dma((count,)), dma((count,)), dma((2, count)), dma((2, count)),
        dma((6, pairs)), dma((4,)), dma((count,)), dma((count,)),
    ]
    outs = [jax.ShapeDtypeStruct(b, narrow) for b in blocks]
    outs += [jax.ShapeDtypeStruct(s, narrow) for s in pair_shapes]
    outs += [jax.ShapeDtypeStruct(small.shape, jnp.float32)]
    got = pl.pallas_call(
        functools.partial(reduce_kernel, count, kinds, spans),
        out_shape=outs,
        in_specs=[pl.BlockSpec(memory_space=pltpu.VMEM)] * (total + 3),
        out_specs=[pl.BlockSpec(memory_space=pltpu.VMEM)] * len(outs),
        scratch_shapes=scratch,
        compiler_params=pltpu.CompilerParams(
            collective_id=1, has_side_effects=True, vmem_limit_bytes=62 * 2**20
        ),
        name="reduce_grads",
    )(*grads, left_part, right_part, small)
    return got[:total], got[total : total + pairs], got[-1]


def product(left, right):
    return jnp.dot(left, right, preferred_element_type=jnp.float32)


def product_left(left, right):
    return lax.dot_general(
        left, right, (((0,), (0,)), ((), ())), preferred_element_type=jnp.float32
    )


def product_right(left, right):
    return lax.dot_general(
        left, right, (((1,), (1,)), ((), ())), preferred_element_type=jnp.float32
    )


def root_scale(field):
    return lax.rsqrt(jnp.mean(field * field, axis=-1, keepdims=True) + epsilon)


def norm_back(grad_normed, field, scale, gain):
    gain_grad = jnp.sum(grad_normed * field * scale, axis=0)
    weighted = grad_normed * gain
    field_grad = scale * weighted - field * (scale * scale * scale) * jnp.mean(
        weighted * field, axis=-1, keepdims=True
    )
    return (field_grad, gain_grad)


def wide_heads(block):
    first = lax.broadcasted_iota(jnp.int32, block.shape, 1) < KV
    none = jnp.zeros_like(block)
    return jnp.concatenate([jnp.where(first, block, none), jnp.where(first, none, block)], axis=0)


def narrow_heads(stacked):
    half = stacked.shape[0] // 2
    first = lax.broadcasted_iota(jnp.int32, (half, stacked.shape[1]), 1) < KV
    return jnp.where(first, stacked[:half], stacked[half:])


def reach(at, blocks):
    low, high = max(0, at - 1), min(blocks, at + 2)
    begin = (low - at + 1) * BLOCK
    return slice(low * BLOCK, high * BLOCK), slice(begin, begin + (high - low) * BLOCK)


def bias_block(base):
    heads = []
    for at in range(2):
        level = jnp.broadcast_to(base[at : at + 1], (BLOCK, base.shape[1]))
        heads.append(pltpu.roll(level, 0, axis=1, stride=1, stride_axis=0))
    return jnp.concatenate(heads, axis=0)


def offset_sums(block):
    rows, width = block.shape
    while rows > 8:
        rows = rows // 2
        block = block[:rows] + pltpu.roll(block[rows:], width - rows, axis=1)
    place = lax.broadcasted_iota(jnp.int32, block.shape, 0)
    for bit in (4, 2, 1):
        block = jnp.where((place & bit) > 0, pltpu.roll(block, width - bit, axis=1), block)
    return jnp.sum(block, axis=0, keepdims=True)


def attend_kernel(column_ref, row_ref, base_ref, query_ref, key_ref, value_ref, out_ref, share_ref):
    blocks = query_ref.shape[0] // BLOCK
    bias = bias_block(base_ref[0])
    for at in range(blocks):
        keys, places = reach(at, blocks)
        own = slice(at * BLOCK, (at + 1) * BLOCK)
        scores = product_right(wide_heads(query_ref[own]), key_ref[keys]) + bias[:, places]
        allowed = column_ref[own, :1] == row_ref[0, :1, keys]
        scores = jnp.where(jnp.concatenate([allowed, allowed], axis=0), scores, negative_fill)
        powers = jnp.exp(scores - jnp.max(scores, axis=1, keepdims=True))
        shares = powers * (1.0 / jnp.sum(powers, axis=1, keepdims=True))
        shares = shares.astype(jnp.bfloat16)
        share_ref[0, 0, at, :, places] = shares
        mixed = product(shares, value_ref[keys])
        out_ref[own] = narrow_heads(mixed).astype(jnp.bfloat16)


def attend_back_kernel(
    query_ref, key_ref, value_ref, grad_ref, share_ref,
    grad_query_ref, grad_key_ref, grad_value_ref, sums_ref, bias_acc, key_acc, value_acc,
):
    blocks = query_ref.shape[0] // BLOCK

    @pl.when(pl.program_id(1) == 0)
    def _():
        bias_acc[...] = jnp.zeros_like(bias_acc)

    key_acc[...] = jnp.zeros_like(key_acc)
    value_acc[...] = jnp.zeros_like(value_acc)
    for at in range(blocks):
        keys, places = reach(at, blocks)
        own = slice(at * BLOCK, (at + 1) * BLOCK)
        query, grad = wide_heads(query_ref[own]), wide_heads(grad_ref[own])
        narrow_shares = share_ref[0, 0, at, :, places]
        shares = narrow_shares.astype(jnp.float32)
        value_acc[keys] += product_left(narrow_shares, grad)
        moved = shares * product_right(grad, value_ref[keys])
        grad_scores = moved - shares * jnp.sum(moved, axis=1, keepdims=True)
        bias_acc[:, places] += grad_scores
        narrow = grad_scores.astype(jnp.bfloat16)
        grad_query_ref[own] = narrow_heads(product(narrow, key_ref[keys])).astype(jnp.bfloat16)
        key_acc[keys] += product_left(narrow, query)
    grad_key_ref[...] = key_acc[...].astype(jnp.bfloat16)
    grad_value_ref[...] = value_acc[...].astype(jnp.bfloat16)

    @pl.when(pl.program_id(1) == pl.num_programs(1) - 1)
    def _():
        sums_ref[0] = jnp.concatenate(
            [offset_sums(bias_acc[:BLOCK]), offset_sums(bias_acc[BLOCK:])], axis=0
        )


def offset_buckets():
    offset = jnp.arange(3 * BLOCK, dtype=jnp.int32) - BLOCK
    distance = jnp.abs(offset)
    far_bucket = 8 + sum(((distance >= boundary).astype(jnp.int32) for boundary in bucket_edges))
    near_bucket = jnp.where(distance < 8, distance, far_bucket)
    return jnp.where(offset > 0, 16, 0) + near_bucket


def attend_rows(rows, length, column, segment_index, base, query, key, value):
    pairs = HEADS // 2
    part = pl.BlockSpec((length, 2 * KV), lambda r, p: (r, p))
    return pl.pallas_call(
        attend_kernel,
        grid=(rows, pairs),
        out_shape=[
            jax.ShapeDtypeStruct(query.shape, jnp.bfloat16),
            jax.ShapeDtypeStruct(
                (rows, pairs, length // BLOCK, 2 * BLOCK, 3 * BLOCK), jnp.bfloat16
            ),
        ],
        in_specs=[
            pl.BlockSpec((length, BLOCK), lambda r, p: (r, 0)),
            pl.BlockSpec((1, 1, length), lambda r, p: (r, 0, 0)),
            pl.BlockSpec((1, 2, 3 * BLOCK), lambda r, p: (p, 0, 0)),
            part, part, part,
        ],
        out_specs=[
            part,
            pl.BlockSpec(
                (1, 1, length // BLOCK, 2 * BLOCK, 3 * BLOCK), lambda r, p: (r, p, 0, 0, 0)
            ),
        ],
        compiler_params=pltpu.CompilerParams(vmem_limit_bytes=48 * 2**20),
        name="attend",
    )(column, segment_index.reshape(rows, 1, length), base, query, key, value)


def attend_rows_back(rows, length, query, key, value, grad, shares):
    pairs = HEADS // 2
    part = pl.BlockSpec((length, 2 * KV), lambda p, r: (r, p))
    return pl.pallas_call(
        attend_back_kernel,
        grid=(pairs, rows),
        out_shape=[jax.ShapeDtypeStruct(query.shape, jnp.bfloat16)] * 3
        + [jax.ShapeDtypeStruct((pairs, 2, 3 * BLOCK), jnp.float32)],
        in_specs=[
            part, part, part, part,
            pl.BlockSpec(
                (1, 1, length // BLOCK, 2 * BLOCK, 3 * BLOCK), lambda p, r: (r, p, 0, 0, 0)
            ),
        ],
        out_specs=[part, part, part, pl.BlockSpec((1, 2, 3 * BLOCK), lambda p, r: (p, 0, 0))],
        scratch_shapes=[
            pltpu.VMEM((2 * BLOCK, 3 * BLOCK), jnp.float32),
            pltpu.VMEM((length, 2 * KV), jnp.float32),
            pltpu.VMEM((length, 2 * KV), jnp.float32),
        ],
        compiler_params=pltpu.CompilerParams(vmem_limit_bytes=48 * 2**20),
        name="attend_back",
    )(query, key, value, grad, shares)


def gelu_parts(before):
    slope = 0.7978845608028654
    square = before * before
    bend = jnp.tanh(slope * (before + 0.044715 * before * square))
    half = 0.5 * (1.0 + bend)
    rise = half + 0.5 * before * (1.0 - bend * bend) * slope * (1.0 + 3 * 0.044715 * square)
    return before * half, rise


def slots_of(stacked, count):
    rows, columns = stacked.shape
    own = lax.broadcasted_iota(jnp.int32, (rows, columns), 0) // count
    head = lax.broadcasted_iota(jnp.int32, (rows, columns), 1) // KV
    return jnp.where(own == head, stacked, 0.0)


LEFTS = ("normed_fin", "active", "normed_start", "own", "normed_mid", "context")
RIGHTS = ("before_grad", "last_branch", "grad_own", "self_branch", "grad_asking", "cross_branch")


def decoder_kernel(rows, slots, count, *refs):
    refs = list(refs)
    packed = count > 0
    factors = refs[16 : 18 if packed else 28]
    del refs[16 : 18 if packed else 28]
    (
        segment_ref, start_ref, cotangent_ref, gain_ref, keys_hbm, values_hbm, memory_hbm,
        self_value_hbm, self_output_hbm, cross_query_hbm, cross_output_hbm,
        inner_hbm, outer_hbm,
        decoded_ref, start_grad_ref, gain_grad_ref,
        grad_keys_hbm, grad_values_hbm, encoded_hbm,
        keys_ref, values_ref, grad_keys_ref, grad_values_ref, memory_ref,
        self_value, self_output, cross_query, cross_output, inner, outer, sems,
    ) = refs

    def keep(name, value):
        names = LEFTS if name in LEFTS else RIGHTS
        at, columns = names.index(name), value.shape[1]
        if not packed:
            factors[at + (0 if names is LEFTS else 6)][...] = value
        elif names is RIGHTS:
            begin = at * start_ref.shape[1] + (0 if at == 0 else inner.shape[1] - start_ref.shape[1])
            factors[1][:, begin : begin + columns] = value
        else:
            own = columns // count
            span = -(-own // 128) * 128
            begin = at * 128 + (0 if at < 2 else -(-inner.shape[1] // count // 128) * 128 - 128)
            wide = value.astype(jnp.float32)
            for slot in range(count):
                turn = (columns - slot * own) % columns
                part = (pltpu.roll(wide, turn, axis=1) if turn else wide)[:, :span]
                lanes = lax.broadcasted_iota(jnp.int32, part.shape, 1)
                part = jnp.where(lanes < own, part, 0.0).astype(value.dtype)
                factors[0][slot, :, begin : begin + span] = part

    loads = []
    for at, (source, target) in enumerate((
        (self_value_hbm, self_value), (self_output_hbm, self_output),
        (cross_query_hbm, cross_query), (cross_output_hbm, cross_output),
        (inner_hbm, inner), (outer_hbm, outer), (keys_hbm, keys_ref), (values_hbm, values_ref),
        (memory_hbm, memory_ref),
    )):
        loads.append(pltpu.make_async_copy(source, target, sems.at[at]))
    for at in (0, 1, 2, 6, 7):
        loads[at].start()
    narrow = jnp.bfloat16
    length = keys_ref.shape[0] // rows
    start_gain, middle_gain, final_gain = gain_ref[2:3], gain_ref[3:4], gain_ref[4:5]

    start_field = start_ref[...].astype(jnp.float32)
    scale_start = root_scale(start_field)
    normed_start = (start_field * scale_start * start_gain).astype(narrow)
    keep("normed_start", normed_start)
    loads[0].wait()
    for at in (3, 4, 5, 8):
        loads[at].start()
    own = product(normed_start, self_value[...]).astype(narrow)
    keep("own", own)
    loads[1].wait()
    first_field = start_field + product(own, self_output[...])
    scale_mid = root_scale(first_field)
    normed_mid = (first_field * scale_mid * middle_gain).astype(narrow)
    keep("normed_mid", normed_mid)
    loads[2].wait()
    asking = product(normed_mid, cross_query[...]).astype(narrow).astype(jnp.float32)
    loads[6].wait()
    loads[7].wait()
    wides, all_shares, contexts = [], [], []
    for row in range(rows):
        part = asking[row * slots : (row + 1) * slots]
        wide = slots_of(jnp.concatenate([part] * HEADS, axis=0), slots).astype(narrow)
        span = slice(row * length, (row + 1) * length)
        scores = product_right(wide, keys_ref[span])
        slot = lax.rem(lax.broadcasted_iota(jnp.int32, scores.shape, 0), slots)
        scores = jnp.where(slot == segment_ref[row : row + 1], scores, negative_fill)
        powers = jnp.exp(scores - jnp.max(scores, axis=1, keepdims=True))
        shares = powers * (1.0 / jnp.sum(powers, axis=1, keepdims=True))
        mixed = slots_of(product(shares.astype(narrow), values_ref[span]), slots)
        contexts.append(jnp.sum(mixed.reshape(HEADS, slots, -1), axis=0))
        wides.append(wide)
        all_shares.append(shares)
    context = jnp.concatenate(contexts, axis=0).astype(narrow)
    keep("context", context)
    loads[3].wait()
    second_field = first_field + product(context, cross_output[...])
    scale_fin = root_scale(second_field)
    normed_fin = (second_field * scale_fin * final_gain).astype(narrow)
    keep("normed_fin", normed_fin)
    loads[4].wait()
    active, rise = gelu_parts(product(normed_fin, inner[...]))
    active = active.astype(narrow)
    keep("active", active)
    loads[5].wait()
    decoded_ref[...] = (second_field + product(active, outer[...])).astype(narrow)

    branch = cotangent_ref[...]
    keep("last_branch", branch)
    grad_second = branch.astype(jnp.float32)
    before_grad = (product_right(branch, outer[...]) * rise).astype(narrow)
    keep("before_grad", before_grad)
    grad_normed = product_right(before_grad, inner[...])
    moved, final_gain_grad = norm_back(grad_normed, second_field, scale_fin, final_gain)
    grad_second = grad_second + moved
    branch = grad_second.astype(narrow)
    keep("cross_branch", branch)
    grad_context = product_right(branch, cross_output[...]).astype(narrow).astype(jnp.float32)
    askings = []
    for row in range(rows):
        part = grad_context[row * slots : (row + 1) * slots]
        wide = slots_of(jnp.concatenate([part] * HEADS, axis=0), slots).astype(narrow)
        span = slice(row * length, (row + 1) * length)
        shares = all_shares[row]
        moved = shares * product_right(wide, values_ref[span])
        grad_scores = moved - shares * jnp.sum(moved, axis=1, keepdims=True)
        grad_scores = grad_scores.astype(narrow)
        grad_values_ref[span] = product_left(shares.astype(narrow), wide).astype(narrow)
        grad_keys_ref[span] = product_left(grad_scores, wides[row]).astype(narrow)
        mixed = slots_of(product(grad_scores, keys_ref[span]), slots)
        askings.append(jnp.sum(mixed.reshape(HEADS, slots, -1), axis=0))
    loads[8].wait()
    stores = [pltpu.make_async_copy(memory_ref, encoded_hbm, sems.at[11])]
    stores.append(pltpu.make_async_copy(grad_keys_ref, grad_keys_hbm, sems.at[9]))
    stores.append(pltpu.make_async_copy(grad_values_ref, grad_values_hbm, sems.at[10]))
    for copy in stores:
        copy.start()
    grad_asking = jnp.concatenate(askings, axis=0).astype(narrow)
    keep("grad_asking", grad_asking)
    grad_normed = product_right(grad_asking, cross_query[...])
    moved, middle_gain_grad = norm_back(grad_normed, first_field, scale_mid, middle_gain)
    grad_first = grad_second + moved
    branch = grad_first.astype(narrow)
    keep("self_branch", branch)
    grad_own = product_right(branch, self_output[...]).astype(narrow)
    keep("grad_own", grad_own)
    grad_normed = product_right(grad_own, self_value[...])
    moved, start_gain_grad = norm_back(grad_normed, start_field, scale_start, start_gain)
    start_grad_ref[...] = grad_first + moved
    gain_grad_ref[...] = jnp.concatenate(
        [start_gain_grad[None], middle_gain_grad[None], final_gain_grad[None]], axis=0
    )
    for copy in stores:
        copy.wait()


def decode(count, segment_index, start, cotangent, gains, keys, values, memory, weights):
    rows, tokens, width = segment_index.shape[0], start.shape[0], start.shape[1]
    narrow, hidden = jnp.bfloat16, weights[4].shape[1]
    few = jax.ShapeDtypeStruct((tokens, width), narrow)
    many = jax.ShapeDtypeStruct((tokens, hidden), narrow)
    factors = [few, many, few, few, few, few, many, few, few, few, few, few]
    if count:
        span = 5 * 128 + hidden // count
        factors = [
            jax.ShapeDtypeStruct((count, tokens, span), narrow),
            jax.ShapeDtypeStruct((tokens, hidden + 5 * width), narrow),
        ]
    outs = [
        few,
        jax.ShapeDtypeStruct((tokens, width), jnp.float32),
        jax.ShapeDtypeStruct((3, width), jnp.float32),
        *factors,
        jax.ShapeDtypeStruct(keys.shape, narrow),
        jax.ShapeDtypeStruct(values.shape, narrow),
        jax.ShapeDtypeStruct(memory.shape, narrow),
    ]
    anywhere = pl.BlockSpec(memory_space=pl.ANY)
    local = pl.BlockSpec(memory_space=pltpu.VMEM)
    return pl.pallas_call(
        functools.partial(decoder_kernel, rows, tokens // rows, count),
        out_shape=outs,
        in_specs=[local] * 4 + [anywhere] * 9,
        out_specs=[local] * (len(outs) - 3) + [anywhere] * 3,
        scratch_shapes=[pltpu.VMEM(keys.shape, narrow)] * 5
        + [pltpu.VMEM(w.shape, narrow) for w in weights]
        + [pltpu.SemaphoreType.DMA((12,))],
        compiler_params=pltpu.CompilerParams(vmem_limit_bytes=63 * 2**20),
        name="decode",
    )(segment_index, start, cotangent, gains, keys, values, memory, *weights)


TILE = 256


def rows_of(at, size=TILE):
    return pl.ds(pl.multiple_of(at * size, size), size)


FORWARD_KINDS = (
    "tall", "tall", "square", "square", "wide", "tall", "square", "square",
    "square", "square", "square", "square", "wide", "tall", "small",
)


class Gather:
    def __init__(self, spot, kinds, shards, fulls, staged, sems):
        self.spot, self.kinds, self.shards, self.fulls = spot, kinds, shards, fulls
        self.staged = staged
        (
            self.ring_out, self.ring_in, self.near_out, self.near_in,
            self.far_out, self.far_in, self.last_out, self.last_in, self.own_sem,
        ) = sems
        self.split = [i for i in range(len(kinds)) if kinds[i] in ("wide", "tall")]

    def piece(self, i, step, plane):
        count = self.spot.count
        slot = ring_index(self.spot.place + (step if i % 2 else count - step), count)
        rows = self.shards[i].shape[0]
        block = self.fulls[i].at[pl.ds(pl.multiple_of(slot * rows, 16), rows)]
        return cut(self.kinds[i], block, plane, self.spot.core)

    def own_copy(self, i):
        rows = self.shards[i].shape[0]
        block = self.fulls[i].at[pl.ds(pl.multiple_of(self.spot.fsdp * rows, 16), rows)]
        return pltpu.make_async_copy(self.staged.get(i, self.shards[i]), block, self.own_sem.at[i])

    def stage_copy(self, i):
        at = len(self.kinds) + list(self.staged).index(i)
        return pltpu.make_async_copy(self.shards[i], self.staged[i], self.own_sem.at[at])

    def ring_copy(self, i, step, source=None):
        here = self.piece(i, step, self.spot.plane)
        return send(
            here if source is None else source, here,
            self.ring_out.at[i, step], self.ring_in.at[i, step],
            self.spot.before if i % 2 else self.spot.after,
        )

    def near_copy(self, i, step):
        here = self.piece(i, step, self.spot.plane)
        return send(
            here, here, self.near_out.at[i, step], self.near_in.at[i, step], self.spot.sibling
        )

    def far_copy(self, i, step):
        here, at = self.piece(i, step, self.spot.plane), self.split.index(i)
        return send(
            here, here, self.far_out.at[at, step], self.far_in.at[at, step], self.spot.opposite
        )

    def last_copy(self, i, step):
        here, at = self.piece(i, step, 1 - self.spot.plane), self.split.index(i)
        return send(
            here, here, self.last_out.at[at, step], self.last_in.at[at, step], self.spot.sibling
        )

    def start(self, group):
        for i in group:
            source = cut(self.kinds[i], self.shards[i], self.spot.plane, self.spot.core)
            self.ring_copy(i, 0, source).start()

    def advance(self, group, step):
        count = self.spot.count
        for i in group:
            if step < count:
                self.ring_copy(i, step - 1).wait_recv()
                if step < count - 1:
                    self.ring_copy(i, step).start()
                if i in self.split:
                    self.far_copy(i, step).start()
        for i in group:
            if step < count and self.kinds[i] != "small":
                self.near_copy(i, step).start()
        for i in group:
            if step > 1 and i in self.split:
                self.far_copy(i, step - 1).wait_recv()
                self.last_copy(i, step - 1).start()

    def arrive(self, group):
        def one(step, carry):
            for i in group:
                if self.kinds[i] != "small":
                    self.near_copy(i, step).wait_recv()
                if i in self.split:
                    self.last_copy(i, step).wait_recv()
            return carry

        lax.fori_loop(1, self.spot.count, one, 0)
        for i in group:
            self.own_copy(i).wait()

    def settle(self, group):
        def one(step, carry):
            for i in group:
                self.ring_copy(i, step - 1).wait_send()
                if self.kinds[i] != "small":
                    self.near_copy(i, step).wait_send()
                if i in self.split:
                    self.far_copy(i, step).wait_send()
                    self.last_copy(i, step).wait_send()
            return carry

        lax.fori_loop(1, self.spot.count, one, 0)


FIRST, SECOND, THIRD = (0, 1, 2, 3, 14), (4, 5, 6, 7), (12, 13, 8, 9, 10, 11)


def forward_kernel(count, rows, *refs):
    refs = list(refs)

    def take(size):
        got = refs[:size]
        del refs[:size]
        return got

    shards = take(15)
    tokens, segment, base = take(3)
    weight_outs = take(14)
    (gain_out,) = take(1)
    (
        query_out, key_out, value_out, share_out, context_out, hidden_out, normed_two_out,
        active_out, rise_out, memory_out, cross_key_out, cross_value_out, normed_one_out,
    ) = take(13)
    held = take(8)
    gain_all, normed_one, query, key, value, context = take(6)
    hidden, normed_two, active, rise, memory, cross_keys, cross_values, shares = take(8)
    column, lines, bases = take(3)
    staged = dict(zip(THIRD, take(len(THIRD))))
    gather_sems = take(9)
    save_sem, share_sem = take(2)
    spot = Spot(count)
    fulls = held + weight_outs[8:] + [gain_all]
    gather = Gather(spot, FORWARD_KINDS, shards, fulls, staged, gather_sems)
    tiles = tokens.shape[0] // TILE
    length = tokens.shape[0] // rows
    blocks, pairs = length // BLOCK, HEADS // 2
    narrow = jnp.bfloat16
    saves = []

    def save(source, target):
        copy = pltpu.make_async_copy(source, target, save_sem.at[len(saves)])
        copy.start()
        saves.append(copy)

    def each_tile(body):
        def one(at, carry):
            body(rows_of(at), at)
            return carry

        lax.fori_loop(0, tiles, one, 0)

    for i in FIRST:
        gather.own_copy(i).start()
    spot.greet()
    gather.start(FIRST)
    for i in SECOND:
        gather.own_copy(i).start()
    for i in THIRD:
        gather.stage_copy(i).start()
    for pair in range(pairs):
        bases[pair, 0:2] = base[2 * pair : 2 * pair + 2]
    for row in range(rows):
        lines[row, 0:1] = segment[row : row + 1].astype(jnp.float32)
        for block in range(blocks):
            line = segment[row : row + 1, block * BLOCK : (block + 1) * BLOCK].astype(jnp.float32)
            begin = row * length + block * BLOCK
            column[begin : begin + BLOCK] = jnp.broadcast_to(line, (BLOCK, BLOCK)).T
    for step in range(1, 5):
        gather.advance(FIRST, step)
    gather.start(SECOND)
    for i in THIRD:
        gather.stage_copy(i).wait()
        gather.own_copy(i).start()
    for step in range(5, count):
        gather.advance(FIRST, step)
        gather.advance(SECOND, step - 4)
    gather.advance(FIRST, count)
    gather.arrive(FIRST)
    gain, width = jnp.zeros(gain_out.shape, jnp.float32), tokens.shape[1]
    depth = width // count
    lanes = lax.broadcasted_iota(jnp.int32, gain.shape, 1)
    for slot in range(count):
        part = gain_all[slot * 16 : (slot + 1) * 16].astype(jnp.float32)
        part = jnp.concatenate([part, jnp.zeros((16, width - part.shape[1]), jnp.float32)], axis=1)
        part = pltpu.roll(part, slot * depth, axis=1)
        gain = gain + jnp.where(lanes // depth == slot, part, 0.0)
    gain_out[...] = gain
    query_weight, key_weight, value_weight, output_weight = held[:4]
    inner_weight, outer_weight, cross_key_weight, cross_value_weight = held[4:]

    def first_norm(span, at):
        field = tokens[span].astype(jnp.float32)
        normed_one[span] = (field * root_scale(field) * gain_out[0:1]).astype(narrow)

    each_tile(first_norm)

    def project(target, weight):
        def body(span, at):
            target[span] = product(normed_one[span], weight[...]).astype(narrow)

        each_tile(body)

    project(query, query_weight)
    gather.advance(SECOND, 4)
    project(key, key_weight)
    gather.start(THIRD)
    project(value, value_weight)
    gather.advance(SECOND, 5)
    for source, target in (
        (normed_one, normed_one_out), (query, query_out), (key, key_out), (value, value_out),
    ):
        save(source, target)
    for i in range(4):
        save(held[i], weight_outs[i])

    def share_copy(at):
        return pltpu.make_async_copy(
            shares.at[lax.rem(at, 2)],
            share_out.at[at // pairs, lax.rem(at, pairs)],
            share_sem.at[lax.rem(at, 2)],
        )

    def attend_pair(at, carry):
        row, pair, buffer = at // pairs, lax.rem(at, pairs), lax.rem(at, 2)

        for turn, group, step in (
            (1, THIRD, 1), (2, SECOND, 6), (4, THIRD, 2), (5, SECOND, 7), (7, THIRD, 3),
            (8, SECOND, 8), (10, THIRD, 4),
        ):

            @pl.when(at == turn)
            def _():
                gather.advance(group, step)

        @pl.when(at >= 2)
        def _():
            share_copy(at - 2).wait()

        bias = bias_block(bases[pair, 0:2])
        columns = rows_of(pair, 2 * KV)

        def span(begin, size):
            return pl.ds(pl.multiple_of(row * length + begin, BLOCK), size)

        for block in range(blocks):
            keys, places = reach(block, blocks)
            own = span(block * BLOCK, BLOCK)
            near = span(keys.start, keys.stop - keys.start)
            scores = product_right(wide_heads(query[own, columns]), key[near, columns])
            scores = scores + bias[:, places]
            allowed = column[own, :1] == lines[row, 0:1, keys]
            scores = jnp.where(jnp.concatenate([allowed, allowed], axis=0), scores, negative_fill)
            powers = jnp.exp(scores - jnp.max(scores, axis=1, keepdims=True))
            part = powers * (1.0 / jnp.sum(powers, axis=1, keepdims=True))
            part = part.astype(narrow)
            shares[buffer, block, :, places] = part
            mixed = product(part, value[near, columns])
            context[own, columns] = narrow_heads(mixed).astype(narrow)
        share_copy(at).start()
        return carry

    lax.fori_loop(0, rows * pairs, attend_pair, 0)
    save(context, context_out)

    def second_norm(span, at):
        field = tokens[span].astype(jnp.float32) + product(context[span], output_weight[...])
        hidden[span] = field
        normed_two[span] = (field * root_scale(field) * gain_out[1:2]).astype(narrow)

    each_tile(second_norm)
    save(hidden, hidden_out)
    save(normed_two, normed_two_out)
    gather.advance(THIRD, 5)
    gather.arrive(SECOND)
    for i in range(4, 8):
        save(held[i], weight_outs[i])
    chunk = tokens.shape[1]

    def feed(span, at):
        @pl.when(at == 1)
        def _():
            gather.advance(THIRD, 6)

        @pl.when(at == 3)
        def _():
            gather.advance(THIRD, 7)

        for begin in range(0, active.shape[1], chunk):
            part = slice(begin, begin + chunk)
            level, slope = gelu_parts(product(normed_two[span], inner_weight[:, part]))
            active[span, part] = level.astype(narrow)
            rise[span, part] = slope.astype(narrow)
        full = hidden[span] + product(active[span], outer_weight[...])
        memory[span] = full.astype(narrow)

    each_tile(feed)
    save(active, active_out)
    save(rise, rise_out)
    save(memory, memory_out)

    def cross(span, at):
        cross_keys[span] = product(memory[span], cross_key_weight[...]).astype(narrow)
        cross_values[span] = product(memory[span], cross_value_weight[...]).astype(narrow)

    each_tile(cross)
    save(cross_keys, cross_key_out)
    save(cross_values, cross_value_out)
    for group in (FIRST, SECOND):
        gather.settle(group)
    for copy in saves:
        copy.wait()
    for at in range(rows * pairs - 2, rows * pairs):
        share_copy(at).wait()
    gather.advance(THIRD, count)
    gather.arrive(THIRD)
    gather.settle(THIRD)


def forward(count, shards, tokens, segment_index, base):
    rows, length = segment_index.shape
    many, width = tokens.shape
    hidden_width = shards[4].shape[1]
    narrow, wide = jnp.bfloat16, jnp.float32
    pairs, total = HEADS // 2, len(shards)
    split = sum(kind in ("wide", "tall") for kind in FORWARD_KINDS)
    weights = [(count * s.shape[0], s.shape[1]) for s in shards]
    few, much = (many, width), (many, hidden_width)
    share_shape = (rows, pairs, length // BLOCK, 2 * BLOCK, 3 * BLOCK)
    shapes = [(w, narrow) for w in weights[:14]] + [((16, width), wide)]
    shapes += [
        (few, narrow), (few, narrow), (few, narrow), (share_shape, narrow), (few, narrow),
        (few, wide), (few, narrow), (much, narrow), (much, narrow), (few, narrow), (few, narrow),
        (few, narrow), (few, narrow),
    ]
    dma = pltpu.SemaphoreType.DMA
    scratch = [pltpu.VMEM(w, narrow) for w in weights[:8]] + [pltpu.VMEM(weights[14], narrow)]
    scratch += [pltpu.VMEM(few, narrow)] * 5
    scratch += [
        pltpu.VMEM(few, wide), pltpu.VMEM(few, narrow), pltpu.VMEM(much, narrow),
        pltpu.VMEM(much, narrow), pltpu.VMEM(few, narrow), pltpu.VMEM(few, narrow),
        pltpu.VMEM(few, narrow), pltpu.VMEM((2,) + share_shape[2:], narrow),
    ]
    scratch += [pltpu.VMEM((many, BLOCK), wide), pltpu.VMEM((rows, 8, length), wide)]
    scratch += [pltpu.VMEM((pairs, 8, base.shape[1]), wide)]
    scratch += [pltpu.VMEM(shards[i].shape, narrow) for i in THIRD]
    scratch += [dma((total, count))] * 4 + [dma((split, count))] * 4
    scratch += [dma((total + len(THIRD),)), dma((24,)), dma((2,))]
    anywhere = pl.BlockSpec(memory_space=pl.ANY)
    local = pl.BlockSpec(memory_space=pltpu.VMEM)
    got = pl.pallas_call(
        functools.partial(forward_kernel, count, rows),
        out_shape=[jax.ShapeDtypeStruct(s, d) for s, d in shapes],
        in_specs=[anywhere] * total + [local] * 3,
        out_specs=[anywhere] * 14 + [local] + [anywhere] * 13,
        scratch_shapes=scratch,
        compiler_params=pltpu.CompilerParams(
            collective_id=2, has_side_effects=True, vmem_limit_bytes=62 * 2**20
        ),
        name="forward",
    )(*shards, tokens, segment_index, base)
    return got[:14], got[14], got[15:]


def forward_apart(count, shards, tokens, segment_index, base):
    rows, length = segment_index.shape
    narrow = jnp.bfloat16
    whole = gather_weights(count, shards, KINDS)
    depth, many = shards[0].shape[0], tokens.shape[0]
    gains = whole[14][:, :, :depth].astype(jnp.float32)
    gains = gains.transpose(1, 0, 2).reshape(16, count * depth)
    base = base.reshape(HEADS // 2, 2, 3 * BLOCK)
    column = jnp.broadcast_to(segment_index.reshape(-1, 1), (many, BLOCK))
    whole = [part.reshape(-1, part.shape[2]) for part in whole[:14]]
    field = tokens.astype(jnp.float32)
    normed_one = (field * root_scale(field) * gains[0]).astype(narrow)
    query, key, value = [product(normed_one, weight).astype(narrow) for weight in whole[:3]]
    context, shares = attend_rows(
        rows, length, column, segment_index, base, query, key, value
    )
    hidden = field + product(context, whole[3])
    normed_two = (hidden * root_scale(hidden) * gains[1]).astype(narrow)
    active, rise = gelu_parts(product(normed_two, whole[4]))
    active = active.astype(narrow)
    memory = (hidden + product(active, whole[5])).astype(narrow)
    cross_keys, cross_values = [product(memory, weight).astype(narrow) for weight in whole[6:8]]
    return whole, gains, (
        query, key, value, shares, context, hidden, normed_two,
        active, rise, memory, cross_keys, cross_values, normed_one,
    )


INNER, OUTER = 0, 1
SPLITS = {INNER: 2}


def backward_kernel(count, rows, spans, *refs):
    refs = list(refs)

    def take(size):
        got = refs[:size]
        del refs[:size]
        return got

    (
        inner_hbm, outer_hbm, query_weight_hbm, key_weight_hbm, value_weight_hbm,
        output_weight_hbm, cross_key_weight_hbm, cross_value_weight_hbm,
        active_hbm, rise_hbm, normed_two_hbm, context_hbm, query_hbm, key_hbm, value_hbm,
        normed_one_hbm, tokens_hbm, memory_hbm, grad_keys_hbm, grad_values_hbm, cotangent_hbm,
        hidden_hbm, shares_hbm,
    ) = take(23)
    left_part, right_part, gain, decoder_gains = take(4)
    sums, pairs = take(8), len(spans)
    pair_sums = take(pairs)
    small_sum, tokens_grad_hbm = take(2)
    big, flat, half, work, final, far = take(1)[0], take(2), take(8), take(8), take(8), take(1)[0]
    left_all, right_all = take(2)
    pair_work, pair_half, pair_far = take(pairs), take(pairs), take(pairs)
    small, small_near, small_mid, small_far, small_all = take(5)
    pool, level, weights, shares, bias_acc, key_acc, value_acc = take(7)
    (
        near_sem, ring_out, ring_in, far_sem, end_sem, left_out, left_in,
        right_out, right_in, pair_sem, small_sem, small_out, small_in, load_sem, share_sem,
    ) = take(15)
    spot = Spot(count)
    core, plane = spot.core, spot.plane
    narrow = jnp.bfloat16
    many, width = level.shape[1:]
    tiles, length = many // TILE, many // rows
    blocks = length // BLOCK
    depth = width // count
    products = {2: big.at[0], 3: big.at[1], 4: big.at[2], 5: flat[0], 6: flat[0], 7: flat[1]}

    def peer(k):
        return (spot.dp, lax.rem(spot.fsdp + k, count))

    def slot_at(way, step):
        turn = step + 1 if way else count - 1 - step
        return ring_index(spot.place + turn, count)

    def near_copy(i):
        if i == INNER:
            source = big.at[pl.ds(2 * (1 - core), 2)]
        elif i == OUTER:
            source = big.at[:, :, half_of(1 - core, width)]
        else:
            source = products[i].at[:, half_of(1 - core, width)]
        return send(source, half[i], near_sem.at[0, i], near_sem.at[1, i], spot.sibling)

    def part_of(i, slot, side, way):
        rows_own = work[i].shape[2]
        if i == INNER:
            return half[i].at[way, pl.ds(pl.multiple_of(slot * depth, 16), depth)]
        if i == OUTER:
            begin = lax.rem(slot, 2) * 4 * depth + (2 * side + way) * rows_own
            return half[i].at[slot // 2, pl.ds(pl.multiple_of(begin, 16), rows_own)]
        begin = slot * depth + way * rows_own
        return half[i].at[pl.ds(pl.multiple_of(begin, 16), rows_own)]

    def far_copy(i, way, step):
        return send(
            part_of(i, slot_at(way, step), 1 - plane, way), far.at[way, step],
            far_sem.at[0, way, step], far_sem.at[1, way, step], spot.opposite,
        )

    def join(i):
        near_copy(i).wait()
        if i == INNER:

            def one(at, carry):
                side, span = at // 3, rows_of(lax.rem(at, 3))
                mine = big[2 * core + side, span]
                half[i][side, span] = plus(half[i][side, span], mine).astype(narrow)
                return carry

            lax.fori_loop(0, 6, one, 0)
        elif i == OUTER:

            def one(at, carry):
                side, span = at // 3, rows_of(lax.rem(at, 3))
                mine = big[side, span, half_of(core, width)]
                half[i][side, span] = plus(half[i][side, span], mine).astype(narrow)
                return carry

            lax.fori_loop(0, 12, one, 0)
        else:

            def one(at, carry):
                span = rows_of(at)
                mine = products[i][span, half_of(core, width)]
                half[i][span] = plus(half[i][span], mine).astype(narrow)
                return carry

            lax.fori_loop(0, 3, one, 0)
        if i == OUTER:

            def far_start(step, carry):
                for way in range(2):
                    far_copy(i, way, step).start()
                return carry

            lax.fori_loop(0, count, far_start, 0)

    def spans_of(i):
        rows_own = work[i].shape[2]
        parts = SPLITS.get(i, 1)
        size = rows_own // parts
        return [slice(at * size, (at + 1) * size) for at in range(parts)]

    def ring_copy(i, way, step, at):
        span = spans_of(i)[at]
        return send(
            work[i].at[way, step, span], work[i].at[way, step + 1, span],
            ring_out.at[i, at, way, step], ring_in.at[i, at, way, step],
            spot.before if way else spot.after,
        )

    def advance(group, step):
        for i in group:
            for way in range(2):
                if i == OUTER:
                    far_copy(i, way, step).wait_recv()
                block = part_of(i, slot_at(way, step), plane, way)
                for at, span in enumerate(spans_of(i)):
                    value = block[span].astype(jnp.float32)
                    if i == OUTER:
                        value = value + far[way, step, span].astype(jnp.float32)

                    @pl.when(step > 0)
                    def _():
                        ring_copy(i, way, step - 1, at).wait_recv()
                        total = plus(value, work[i][way, step, span])
                        work[i][way, step, span] = total.astype(narrow)

                    @pl.when(step == 0)
                    def _():
                        work[i][way, step, span] = value.astype(narrow)

                    @pl.when(step < count - 1)
                    def _():
                        ring_copy(i, way, step, at).start()

    def run(group, first, last):
        def one(step, carry):
            advance(group, step)
            return carry

        lax.fori_loop(first, last, one, 0)

    def end_across(i):
        return send(
            work[i].at[:, count - 1], final[i], end_sem.at[0, i], end_sem.at[1, i], spot.opposite
        )

    def end_piece(i, side):
        if i == OUTER:
            return cut("tall", sums[i], side, core)
        return sums[i].at[:, half_of(core, sums[i].shape[1])]

    def end_near(i):
        here = end_piece(i, plane)
        return send(here, here, end_sem.at[2, i], end_sem.at[3, i], spot.sibling)

    def end_far(i):
        here = end_piece(i, plane)
        return send(here, here, end_sem.at[4, i], end_sem.at[5, i], spot.opposite)

    def end_relay(i):
        here = end_piece(i, 1 - plane)
        return send(here, here, end_sem.at[6, i], end_sem.at[7, i], spot.sibling)

    def close(i):
        if i != OUTER:
            end_across(i).wait()
        here, rows_own = end_piece(i, plane), work[i].shape[2]
        for way in range(2):
            value = work[i][way, count - 1]
            if i != OUTER:
                value = plus(value, final[i][way]).astype(narrow)
            if i == INNER:
                here[:, way * width : (way + 1) * width] = value
            else:
                here[way * rows_own : (way + 1) * rows_own] = value
        if i == OUTER:
            end_far(i).start()
        end_near(i).start()

    def left_copy(k):
        other = lax.rem(spot.fsdp + k, count)
        return send(
            left_part.at[other], left_all.at[spot.fsdp], left_out.at[k], left_in.at[k], peer(k)
        )

    def right_copy(way, step):
        turn = step if way else count - step
        slot = ring_index(spot.place + turn, count)
        wide = right_part.shape[1] // 2
        here = right_all.at[slot, :, way * wide : (way + 1) * wide]
        return send(
            here, here, right_out.at[way, step], right_in.at[way, step],
            spot.before if way else spot.after,
        )

    def right_step(step):
        for way in range(2):
            right_copy(way, step - 1).wait_recv()
            if step < count - 1:
                right_copy(way, step).start()

    def pair_near(j):
        columns = pair_sums[j].shape[1]
        return send(
            pair_work[j].at[:, half_of(1 - core, columns)], pair_half[j],
            pair_sem.at[0, j], pair_sem.at[1, j], spot.sibling,
        )

    def pair_across(j):
        return send(
            pair_half[j], pair_far[j], pair_sem.at[2, j], pair_sem.at[3, j], spot.opposite
        )

    def pair_end(j):
        here = pair_sums[j].at[:, half_of(core, pair_sums[j].shape[1])]
        return send(here, here, pair_sem.at[4, j], pair_sem.at[5, j], spot.sibling)

    def small_copy(k):
        here = small_all.at[spot.fsdp]
        return send(here, here, small_out.at[k], small_in.at[k], peer(k))

    def each_peer(body):
        def one(k, carry):
            body(k)
            return carry

        lax.fori_loop(1, count, one, 0)

    def each_tile(body):
        def one(at, carry):
            body(rows_of(at))
            return carry

        lax.fori_loop(0, tiles, one, 0)

    used = []

    def load(source, target):
        copy = pltpu.make_async_copy(source, target, load_sem.at[len(used)])
        copy.start()
        used.append(copy)
        return copy

    def fold(target, left, right):
        def one(at, carry):
            span = rows_of(at)
            target[span] = product_left(left[:, span], right[...]).astype(narrow)
            return carry

        lax.fori_loop(0, width // TILE, one, 0)

    loads = [
        load(grad_keys_hbm, pool.at[4]), load(cross_key_weight_hbm, weights.at[0]),
        load(grad_values_hbm, pool.at[5]), load(cross_value_weight_hbm, weights.at[1]),
        load(cotangent_hbm, pool.at[2]), load(memory_hbm, pool.at[1]),
    ]

    def chunk_of(source, at):
        return source.at[:, pl.ds(at * width, width)]

    active_loads = {1: load(chunk_of(active_hbm, 1), pool.at[3])}
    hidden_load = load(hidden_hbm, level.at[2])
    out_loads = {0: load(outer_hbm.at[pl.ds(0, width)], weights.at[2])}
    barrier = pltpu.get_barrier_semaphore()
    for partner in (spot.sibling, spot.opposite):
        pl.semaphore_signal(barrier, inc=1, device_id=partner, device_id_type=MESH)
    each_peer(
        lambda k: pl.semaphore_signal(barrier, inc=1, device_id=peer(k), device_id_type=MESH)
    )
    pl.semaphore_wait(barrier, count + 1)
    each_peer(lambda k: left_copy(k).start())
    right_all[spot.fsdp] = right_part[...]
    left_all[spot.fsdp] = left_part[spot.fsdp]
    for way in range(2):
        right_copy(way, 0).start()
    small[...] = jnp.zeros_like(small)
    small[2:5] = decoder_gains[...]
    for copy in loads:
        copy.wait()

    def enter(span):
        value = pool[2, span].astype(jnp.float32)
        value = value + product_right(pool[4, span], weights[0])
        value = value + product_right(pool[5, span], weights[1])
        level[0, span] = value
        pool[0, span] = value.astype(narrow)

    each_tile(enter)
    active_loads[0] = load(chunk_of(active_hbm, 0), pool.at[2])
    in_loads = {
        at: load(chunk_of(inner_hbm, at), weights.at[at]) for at in range(2)
    }
    fold(flat[0], pool.at[1], pool.at[4])
    near_copy(6).start()
    fold(flat[1], pool.at[1], pool.at[5])
    near_copy(7).start()
    normed_load = load(normed_two_hbm, pool.at[1])
    context_load = load(context_hbm, pool.at[4])
    right_step(1)

    rise_loads = {}
    for at in range(4):
        buffer = 2 + at % 2
        active_loads[at].wait()
        fold(big.at[at], pool.at[buffer], pool.at[0])
        if at < 2:
            active_loads[at + 2] = load(chunk_of(active_hbm, at + 2), pool.at[buffer])
        else:
            rise_loads[at - 2] = load(chunk_of(rise_hbm, at - 2), pool.at[buffer])
        if at == 1:
            right_step(2)
            join(6)
            join(7)
        elif at == 2:
            advance((6, 7), 0)
        elif at == 3:
            right_step(3)
    near_copy(OUTER).start()
    out_loads[1] = load(outer_hbm.at[pl.ds(width, width)], weights.at[3])

    normed_load.wait()
    for at in range(4):
        buffer = 2 + at % 2
        rise_loads[at].wait()
        out_loads[at].wait()
        in_loads[at].wait()

        def back(span):
            before = product_right(pool[0, span], weights[2 + at % 2])
            before = (before * pool[buffer, span].astype(jnp.float32)).astype(narrow)
            pool[buffer, span] = before
            moved = product_right(before, weights[at % 2])
            level[1, span] = moved if at == 0 else level[1, span] + moved

        each_tile(back)
        if at < 2:
            span = pl.ds((at + 2) * width, width)
            out_loads[at + 2] = load(outer_hbm.at[span], weights.at[2 + at % 2])
            in_loads[at + 2] = load(chunk_of(inner_hbm, at + 2), weights.at[at % 2])
        right_step(at + 4)
        advance((6, 7), at + 1)
        if at == 0:
            join(OUTER)
        else:
            advance((OUTER,), at - 1)
        fold(big.at[at], pool.at[1], pool.at[buffer])
        if at < 2:
            rise_loads[at + 2] = load(chunk_of(rise_hbm, at + 2), pool.at[buffer])
    near_copy(INNER).start()
    query_load = load(query_hbm, pool.at[1])
    key_load, value_load = load(key_hbm, pool.at[2]), load(value_hbm, pool.at[3])
    late_loads = [
        load(query_weight_hbm, weights.at[0]), load(key_weight_hbm, weights.at[1]),
        load(value_weight_hbm, weights.at[2]),
    ]
    output_load = load(output_weight_hbm, weights.at[3])

    def back_norm(field, moved, gain_row, at):
        scale = root_scale(field)
        small[at : at + 1] += jnp.sum(moved * field * scale, axis=0, keepdims=True)
        weighted = moved * gain_row
        mean = jnp.mean(weighted * field, axis=-1, keepdims=True)
        return scale * weighted - field * (scale * scale * scale) * mean

    hidden_load.wait()

    def second(span):
        value = level[0, span] + back_norm(level[2, span], level[1, span], gain[1:2], 1)
        level[0, span] = value
        pool[0, span] = value.astype(narrow)

    each_tile(second)
    advance((6, 7), 5)
    advance((OUTER,), 3)
    context_load.wait()
    fold(flat[0], pool.at[4], pool.at[0])
    near_copy(5).start()
    normed_one_load = load(normed_one_hbm, pool.at[4])
    output_load.wait()

    def third(span):
        pool[5, span] = product_right(pool[0, span], weights[3]).astype(narrow)

    each_tile(third)
    tokens_load = load(tokens_hbm, pool.at[0])
    advance((6, 7), 6)
    advance((OUTER,), 4)
    join(INNER)
    join(5)
    for copy in (query_load, key_load, value_load):
        copy.wait()

    def pair_products():
        each_peer(lambda k: left_copy(k).wait_recv())
        for j, (left_at, right_at) in enumerate(spans):
            own, columns = pair_sums[j].shape
            wide = -(-own // 128) * 128
            left = left_all[:, :, left_at : left_at + wide].reshape(-1, wide)
            for begin in range(0, columns, width):
                right = right_all[:, :, right_at + begin : right_at + begin + width]
                block = product_left(left, right.reshape(-1, width))
                pair_work[j][:, begin : begin + width] = block[:own].astype(narrow)
            pair_near(j).start()

    def pair_cross():
        for j in range(pairs):
            pair_near(j).wait()
            mine = pair_work[j][:, half_of(core, pair_sums[j].shape[1])]
            pair_half[j][...] = plus(pair_half[j][...], mine).astype(narrow)
            pair_across(j).start()

    def share_copy(at):
        return pltpu.make_async_copy(
            shares_hbm.at[lax.rem(at, rows), at // rows],
            shares.at[lax.rem(at, 2)],
            share_sem.at[lax.rem(at, 2)],
        )

    turns = rows * (HEADS // 2)
    share_copy(0).start()

    def attend_pair(at, carry):
        pair, row, buffer = at // rows, lax.rem(at, rows), lax.rem(at, 2)
        share_copy(at).wait()

        @pl.when(at + 1 < turns)
        def _():
            share_copy(at + 1).start()

        @pl.when(lax.rem(at, 2) == 1)
        def _():
            advance((INNER,), at // 2)

        @pl.when((at > 0) & (lax.rem(at, 2) == 0))
        def _():
            advance((5,), at // 2 - 1)

        @pl.when(at == 2)
        def _():
            advance((6, 7), 7)
            for i in (6, 7):
                end_across(i).start()

        for turn, step in ((1, 5), (3, 6), (5, 7)):

            @pl.when(at == turn)
            def _():
                advance((OUTER,), step)

        @pl.when(at == 2)
        def _():
            pair_products()

        @pl.when(at == 4)
        def _():
            pair_cross()

        @pl.when(row == 0)
        def _():
            bias_acc[...] = jnp.zeros_like(bias_acc)

        key_acc[...] = jnp.zeros_like(key_acc)
        value_acc[...] = jnp.zeros_like(value_acc)
        columns = rows_of(pair, 2 * KV)

        def span(begin, size):
            return pl.ds(pl.multiple_of(row * length + begin, BLOCK), size)

        for block in range(blocks):
            keys, places = reach(block, blocks)
            own = span(block * BLOCK, BLOCK)
            near = span(keys.start, keys.stop - keys.start)
            query, grad = wide_heads(pool[1, own, columns]), wide_heads(pool[5, own, columns])
            narrow_shares = shares[buffer, block, :, places]
            part = narrow_shares.astype(jnp.float32)
            value_acc[keys] += product_left(narrow_shares, grad)
            moved = part * product_right(grad, pool[3, near, columns])
            grad_scores = moved - part * jnp.sum(moved, axis=1, keepdims=True)
            bias_acc[:, places] += grad_scores
            low = grad_scores.astype(narrow)
            key_acc[keys] += product_left(low, query)
            mixed = product(low, pool[2, near, columns])
            pool[1, own, columns] = narrow_heads(mixed).astype(narrow)
        pool[2, span(0, length), columns] = key_acc[...].astype(narrow)
        pool[3, span(0, length), columns] = value_acc[...].astype(narrow)

        @pl.when(row == rows - 1)
        def _():
            for head in range(2):
                block = bias_acc[head * BLOCK : (head + 1) * BLOCK]
                place = slice(head * 3 * BLOCK, (head + 1) * 3 * BLOCK)
                small[pl.ds(5 + pair, 1), place] = offset_sums(block)

        return carry

    lax.fori_loop(0, turns, attend_pair, 0)
    advance((5,), 5)
    normed_one_load.wait()
    fold(big.at[0], pool.at[4], pool.at[1])
    near_copy(2).start()
    advance((INNER,), 6)
    advance((5,), 6)
    fold(big.at[1], pool.at[4], pool.at[2])
    near_copy(3).start()
    join(2)
    advance((2,), 0)
    fold(big.at[2], pool.at[4], pool.at[3])
    near_copy(4).start()
    join(3)
    advance((3,), 0)
    advance((INNER,), 7)
    advance((5,), 7)
    for i in (INNER, 5):
        end_across(i).start()
    join(4)
    advance((4,), 0)
    close(OUTER)
    for i in (6, 7):
        close(i)
    tokens_load.wait()
    for copy in late_loads:
        copy.wait()

    def save(at):
        span = rows_of(at)
        return pltpu.make_async_copy(
            level.at[1, span], tokens_grad_hbm.at[span], share_sem.at[2 + at]
        )

    def last(at, carry):
        span = rows_of(at)
        moved = product_right(pool[1, span], weights[0])
        moved = moved + product_right(pool[2, span], weights[1])
        moved = moved + product_right(pool[3, span], weights[2])
        field = pool[0, span].astype(jnp.float32)
        level[1, span] = level[0, span] + back_norm(field, moved, gain[0:1], 0)
        save(at).start()
        advance((2, 3, 4), at + 1)
        return carry

    lax.fori_loop(0, tiles, last, 0)
    near_small = send(small, small_near, small_sem.at[0], small_sem.at[1], spot.sibling)
    near_small.start()
    advance((2, 3, 4), tiles + 1)
    near_small.wait()
    small_mid[...] = small[...] + small_near[...]
    far_small = send(small_mid, small_far, small_sem.at[2], small_sem.at[3], spot.opposite)
    far_small.start()
    advance((2, 3, 4), tiles + 2)
    far_small.wait()
    small_all[spot.fsdp] = small_mid[...] + small_far[...]
    each_peer(lambda k: small_copy(k).start())
    run((2, 3, 4), tiles + 3, count)
    for i in (2, 3, 4):
        end_across(i).start()
    for j in range(pairs):
        pair_across(j).wait()
        here = half_of(core, pair_sums[j].shape[1])
        pair_sums[j][:, here] = plus(pair_half[j][...], pair_far[j][...]).astype(narrow)
        pair_end(j).start()
    close(INNER)
    close(5)
    end_far(OUTER).wait()
    end_relay(OUTER).start()
    def drain(step, carry):
        for way in range(2):
            far_copy(OUTER, way, step).wait_send()
        return carry

    lax.fori_loop(0, count, drain, 0)

    def drain_ring(step, carry):
        for way in range(2):
            for i in range(8):
                for at in range(SPLITS.get(i, 1)):
                    ring_copy(i, way, step, at).wait_send()
            right_copy(way, step).wait_send()
        left_copy(step + 1).wait_send()
        small_copy(step + 1).wait_send()
        return carry

    lax.fori_loop(0, count - 1, drain_ring, 0)

    each_peer(lambda k: small_copy(k).wait_recv())
    small_sum[...] = lax.fori_loop(
        1, count, lambda k, so_far: so_far + small_all[k], small_all[0]
    )
    for i in (2, 3, 4):
        close(i)
    for i in range(8):
        end_near(i).wait()
    end_relay(OUTER).wait()
    for j in range(pairs):
        pair_end(j).wait()
    for at in range(tiles):
        save(at).wait()


def backward(
    count, rows, whole, kept, tokens, cotangent, grad_keys, grad_values,
    left_part, right_part, pair_shapes, gains, decoder_gains,
):
    (
        query, key, value, shares, context, hidden, normed_two,
        active, rise, memory, unused_keys, unused_values, normed_one,
    ) = kept
    many, width = tokens.shape
    depth, narrow, wide = width // count, jnp.bfloat16, jnp.float32
    pairs = len(pair_shapes)
    spans, left_at, right_at = [], 0, 0
    for own, columns in pair_shapes:
        spans.append((left_at, right_at))
        left_at, right_at = left_at + -(-own // 128) * 128, right_at + columns
    dma, vmem = pltpu.SemaphoreType.DMA, pltpu.VMEM
    pieces = [(depth, width), (depth, width // 2)] + [(depth // 2, width // 2)] * 6
    outs = [(depth, 4 * width), (4 * depth, width)] + [(depth, width)] * 6
    little = (16, width)
    scratch = [vmem((4, width, width), narrow)] + [vmem((width, width), narrow)] * 2
    scratch += [vmem((2, width, width), narrow), vmem((4, width, width // 2), narrow)]
    scratch += [vmem((width, width // 2), narrow)] * 6
    scratch += [vmem((2, count) + piece, narrow) for piece in pieces]
    scratch += [vmem((2,) + piece, narrow) for piece in pieces]
    scratch += [vmem((2, count) + pieces[1], narrow)]
    scratch += [vmem(left_part.shape, narrow), vmem((count,) + right_part.shape, narrow)]
    scratch += [vmem(s, narrow) for s in pair_shapes]
    scratch += [vmem((r, c // 2), narrow) for r, c in pair_shapes] * 2
    scratch += [vmem(little, wide)] * 4 + [vmem((count,) + little, wide)]
    scratch += [
        vmem((6, many, width), narrow), vmem((3, many, width), wide),
        vmem((4, width, width), narrow), vmem((2,) + shares.shape[2:], narrow),
        vmem((2 * BLOCK, 3 * BLOCK), wide),
    ]
    scratch += [vmem((many // rows, 2 * KV), wide)] * 2
    scratch += [
        dma((2, 8)), dma((8, 2, 2, count)), dma((8, 2, 2, count)), dma((2, 2, count)), dma((8, 8)),
        dma((count,)), dma((count,)), dma((2, count)), dma((2, count)), dma((6, pairs)),
        dma((4,)), dma((count,)), dma((count,)), dma((48,)), dma((2 + many // TILE,)),
    ]
    shapes = [jax.ShapeDtypeStruct(s, narrow) for s in outs + list(pair_shapes)]
    shapes += [jax.ShapeDtypeStruct(little, wide), jax.ShapeDtypeStruct((many, width), wide)]
    anywhere = pl.BlockSpec(memory_space=pl.ANY)
    local = pl.BlockSpec(memory_space=pltpu.VMEM)
    got = pl.pallas_call(
        functools.partial(backward_kernel, count, rows, spans),
        out_shape=shapes,
        in_specs=[anywhere] * 23 + [local] * 4,
        out_specs=[local] * (len(shapes) - 1) + [anywhere],
        scratch_shapes=scratch,
        compiler_params=pltpu.CompilerParams(
            collective_id=3, has_side_effects=True, vmem_limit_bytes=63 * 2**20
        ),
        name="backward",
    )(
        whole[4], whole[5], whole[0], whole[1], whole[2], whole[3], whole[6], whole[7],
        active, rise, normed_two, context, query, key, value, normed_one, tokens, memory,
        grad_keys, grad_values, cotangent, hidden, shares,
        left_part, right_part, gains, decoder_gains,
    )
    return got[:8], got[8 : 8 + pairs], got[-2], got[-1]


def backward_apart(
    count, rows, whole, kept, tokens, cotangent, grad_cross_keys, grad_cross_values,
    left_part, right_part, pair_shapes, gains, decoder_gains,
):
    (
        query_full, key_full, value_full, output_full, inner_full, outer_full, cross_key_full,
        cross_value_full,
    ) = whole[:8]
    (
        query_all, key_all, value_all, shares, context, hidden, normed_two,
        active, rise, memory, unused_keys, unused_values, normed_one,
    ) = kept
    row_count, length = rows, tokens.shape[0] // rows
    gain_one, gain_two = gains[0], gains[1]
    field = tokens.astype(jnp.float32)
    scale_one, scale_two = root_scale(field), root_scale(hidden)
    grad_cross_key = product_left(memory, grad_cross_keys)
    grad_cross_value = product_left(memory, grad_cross_values)
    grad_memory = product_right(grad_cross_keys, cross_key_full) + product_right(
        grad_cross_values, cross_value_full
    )
    grad_encoded = cotangent.astype(jnp.float32) + grad_memory
    grad_branch = grad_encoded.astype(jnp.bfloat16)
    grad_outer = product_left(active, grad_branch)
    grad_active = product_right(grad_branch, outer_full)
    grad_before = (grad_active * rise).astype(jnp.bfloat16)
    grad_inner = product_left(normed_two, grad_before)
    grad_normed = product_right(grad_before, inner_full)
    field_part, grad_gain_two = norm_back(
        grad_normed, hidden, scale_two, gain_two
    )
    grad_hidden = grad_encoded + field_part
    grad_branch = grad_hidden.astype(jnp.bfloat16)
    grad_output = product_left(context, grad_branch)
    grad_context = product_right(grad_branch, output_full).astype(jnp.bfloat16)
    grad_query_all, grad_key_all, grad_value_all, bias_sums = attend_rows_back(
        row_count, length, query_all, key_all, value_all, grad_context, shares
    )
    grad_query = product_left(normed_one, grad_query_all)
    grad_key = product_left(normed_one, grad_key_all)
    grad_value = product_left(normed_one, grad_value_all)
    grad_normed = (
        product_right(grad_query_all, query_full)
        + product_right(grad_key_all, key_full)
        + product_right(grad_value_all, value_full)
    )
    field_part, grad_gain_one = norm_back(
        grad_normed, field, scale_one, gain_one
    )
    tokens_grad = grad_hidden + field_part
    small = jnp.concatenate([
        jnp.stack([grad_gain_one, grad_gain_two]),
        decoder_gains,
        bias_sums.reshape(HEADS // 2, -1),
        jnp.zeros((5, tokens.shape[1]), jnp.float32),
    ])
    encoder_grads = (
        grad_inner, grad_outer, grad_query, grad_key, grad_value, grad_output,
        grad_cross_key, grad_cross_value,
    )
    encoder_sums, decoder_sums, small_sum = reduce_grads(
        count,
        ENCODER_KINDS,
        [
            g.astype(jnp.bfloat16).reshape(count, g.shape[0] // count, g.shape[1])
            for g in encoder_grads
        ],
        left_part,
        right_part,
        pair_shapes,
        small,
    )
    return encoder_sums, decoder_sums, small_sum, tokens_grad


def widen_kernel(total, *refs):
    sources, targets = refs[:total], refs[total : 2 * total]
    held, wide, sems = refs[2 * total : 3 * total], list(refs[3 * total : -1]), refs[-1]
    ready = [part if part.dtype == jnp.float32 else wide.pop(0) for part in held]
    loads = [pltpu.make_async_copy(sources[at], held[at], sems.at[at]) for at in range(total)]
    stores = [
        pltpu.make_async_copy(ready[at], targets[at], sems.at[total + at]) for at in range(total)
    ]
    for copy in loads:
        copy.start()
    for at in range(total):
        loads[at].wait()
        if held[at] is not ready[at]:
            ready[at][...] = held[at][...].astype(jnp.float32)
        stores[at].start()
    for copy in stores:
        copy.wait()


def widen(parts):
    anywhere, total = pl.BlockSpec(memory_space=pl.ANY), len(parts)
    return pl.pallas_call(
        functools.partial(widen_kernel, total),
        out_shape=[jax.ShapeDtypeStruct(part.shape, jnp.float32) for part in parts],
        in_specs=[anywhere] * total,
        out_specs=[anywhere] * total,
        scratch_shapes=[pltpu.VMEM(part.shape, part.dtype) for part in parts]
        + [
            pltpu.VMEM(part.shape, jnp.float32) for part in parts if part.dtype != jnp.float32
        ]
        + [pltpu.SemaphoreType.DMA((2 * total,))],
        compiler_params=pltpu.CompilerParams(vmem_limit_bytes=63 * 2**20),
        name="widen",
    )(*parts)


def on_device(
    tokens,
    segment_index,
    start_vectors,
    first_gain,
    query_weight,
    key_weight,
    value_weight,
    output_weight,
    position_table,
    second_gain,
    inner_weight,
    outer_weight,
    start_gain,
    self_value,
    self_output,
    middle_gain,
    cross_query,
    cross_key,
    cross_value,
    cross_output,
    final_gain,
    decoder_inner,
    decoder_outer,
    encoded_cotangent,
    decoded_cotangent,
):
    row_count = segment_index.shape[0]
    length = segment_index.shape[1]
    slot_count = start_vectors.shape[1]
    width = tokens.shape[1]
    count = lax.axis_size("fsdp")
    depth = first_gain.shape[0]
    choices = jnp.arange(position_table.shape[0], dtype=jnp.int32)
    onehot = (offset_buckets()[None, :] == choices[:, None]).astype(jnp.float32)
    base = jnp.dot(position_table.T, onehot, precision=lax.Precision.HIGHEST)
    gains = jnp.stack([first_gain, second_gain, start_gain, middle_gain, final_gain])
    gains = jnp.pad(gains, ((0, 11), (0, BLOCK - depth)))
    shards = (
        query_weight, key_weight, value_weight, output_weight, inner_weight, outer_weight,
        cross_key, cross_value, self_value, self_output, cross_query, cross_output,
        decoder_inner, decoder_outer, gains,
    )
    fused = count == 8 and depth % 32 == 0 and (row_count, length) == (2, 512)
    plan = forward if fused else forward_apart
    whole, all_gains, kept = plan(count, shards, tokens, segment_index, base)
    memory, cross_keys, cross_values = kept[9:12]
    token_count = row_count * slot_count
    (
        decoded, start_grad, decoder_gain_grads, *factors,
        grad_cross_keys, grad_cross_values, encoded,
    ) = decode(
        count if fused else 0,
        segment_index,
        start_vectors.reshape(token_count, width),
        decoded_cotangent.reshape(token_count, width),
        all_gains,
        cross_keys,
        cross_values,
        memory,
        whole[8:14],
    )
    hidden_width = decoder_inner.shape[1]
    pair_shapes = [(depth, hidden_width), (hidden_width // count, width)] + [(depth, width)] * 4
    if not fused:
        left_cols = []
        for left, (rows, unused) in zip(factors[:6], pair_shapes):
            columns = left.reshape(token_count, count, rows).transpose(1, 0, 2)
            left_cols.append(jnp.pad(columns, ((0, 0), (0, 0), (0, -rows % 128))))
        factors = (jnp.concatenate(left_cols, axis=2), jnp.concatenate(factors[6:], axis=1))
    turn_back = backward if fused else backward_apart
    encoder_sums, decoder_sums, small_sum, tokens_grad = turn_back(
        count, row_count, whole, kept, tokens, encoded_cotangent,
        grad_cross_keys, grad_cross_values,
        *factors, pair_shapes, all_gains, decoder_gain_grads,
    )
    (
        inner_weight_grad, outer_weight_grad, query_weight_grad, key_weight_grad,
        value_weight_grad, output_weight_grad, cross_key_grad, cross_value_grad,
        decoder_inner_grad, decoder_outer_grad, self_value_grad, self_output_grad,
        cross_query_grad, cross_output_grad, tokens_grad,
    ) = widen([*encoder_sums, *decoder_sums, tokens_grad])
    position_table_grad = lax.dot_general(
        onehot,
        small_sum[5:11].reshape(HEADS, 3 * BLOCK),
        (((1,), (1,)), ((), ())),
        precision=lax.Precision.HIGHEST,
    )
    own_gains = lax.dynamic_slice_in_dim(
        small_sum[:5], lax.axis_index("fsdp") * depth, depth, axis=1
    )
    first_gain_grad, second_gain_grad, start_gain_grad, middle_gain_grad, final_gain_grad = own_gains
    decoded = decoded.reshape(start_vectors.shape)
    start_grad = start_grad.reshape(start_vectors.shape)
    return (
        encoded,
        decoded,
        tokens_grad,
        start_grad,
        first_gain_grad,
        query_weight_grad,
        key_weight_grad,
        value_weight_grad,
        output_weight_grad,
        position_table_grad,
        second_gain_grad,
        inner_weight_grad,
        outer_weight_grad,
        start_gain_grad,
        self_value_grad,
        self_output_grad,
        middle_gain_grad,
        cross_query_grad,
        cross_key_grad,
        cross_value_grad,
        cross_output_grad,
        final_gain_grad,
        decoder_inner_grad,
        decoder_outer_grad,
    )


def solution(mesh):
    placed = (
        P(("dp", "fsdp"), None),
        P(("dp", "fsdp"), None),
        P(("dp", "fsdp"), None, None),
        P("fsdp"),
        P("fsdp", None),
        P("fsdp", None),
        P("fsdp", None),
        P("fsdp", None),
        P(),
        P("fsdp"),
        P("fsdp", None),
        P("fsdp", None),
        P("fsdp"),
        P("fsdp", None),
        P("fsdp", None),
        P("fsdp"),
        P("fsdp", None),
        P("fsdp", None),
        P("fsdp", None),
        P("fsdp", None),
        P("fsdp"),
        P("fsdp", None),
        P("fsdp", None),
        P(("dp", "fsdp"), None),
        P(("dp", "fsdp"), None, None),
    )
    return jax.shard_map(
        on_device,
        mesh=mesh,
        in_specs=placed,
        out_specs=(
            P(("dp", "fsdp"), None),
            P(("dp", "fsdp"), None, None),
            P(("dp", "fsdp"), None),
            P(("dp", "fsdp"), None, None),
            P("fsdp"),
            P("fsdp", None),
            P("fsdp", None),
            P("fsdp", None),
            P("fsdp", None),
            P(),
            P("fsdp"),
            P("fsdp", None),
            P("fsdp", None),
            P("fsdp"),
            P("fsdp", None),
            P("fsdp", None),
            P("fsdp"),
            P("fsdp", None),
            P("fsdp", None),
            P("fsdp", None),
            P("fsdp", None),
            P("fsdp"),
            P("fsdp", None),
            P("fsdp", None),
        ),
        check_vma=False,
    )
```
